32 devices in a mesh: query: 8 (over y, x, core), feat: 4 (over z).
Axes of the slice: x: 2, y: 2, z: 4, core: 2. Of those that a mesh axis runs over, the one named last changes fastest.
Arguments:
- scores: float32 [32768], P(('query', 'feat')), may hold values from -6 to 6
- labels: int32 [32768], P('query'), may hold values from 0 to 4
- leaves: int32 [32768], P(('query', 'feat')), may hold values from 0 to 1023
- bins: int32 [32768, 256], P(('query', 'feat')), may hold values from 0 to 255
- lengths: int32 [8, 16], P('query'), may hold values from 1 to 1024, 4096 in all within a row
- owner: int32 [256], replicated, may hold values from 0 to 255, each once
Outputs:
- lambdas: float32 [2, 32768], P(None, ('query', 'feat'))
- leaf_values: float32 [1024], replicated
- score_step: float32 [32768], P(('query', 'feat'))
- histograms: float32 [3, 65536], P(None, ('query', 'feat'))
The draws below stay inside these ranges and needn't reach their ends.
Inputs may be any that keep to these rules, and one draw needn't show every extreme that they name: `lengths`: each row sums to 4096. `owner`: a permutation; the p-th device of query+feat, in that order, holds the histograms of the features owner[j] for p * 8 <= j < (p + 1) * 8.
All inputs are finite; a program needn't handle non-finite values.
Results may differ from the reference program's by a relative error of at most 0.0003.
Values sent between devices are 32-bit elements; how exact they have to be, the bound alone decides.
No kernel may reach another device: no remote copies, remote signals or barrier semaphores. Data moves between devices by JAX's collectives and lax.ppermute only.
A program may use at most 128 MiB of HBM per device.

```python
import math
import jax
import jax.numpy as jnp
import numpy as np
from jax import lax

FEATURES = 256
BINS = 256
LEAVES = 1024
MAX_LEN = 1024
TILE_ROWS = 512
DOCS_DEV = 1024
BLOCK_DOCS = 4096
QUERIES_BLOCK = 16
DOCS_ALL = 32768
WINDOW = 1536
LEAF_SPAN = 128
N_QUERY = 8


def grade_draw(key):
    return jax.random.randint(jax.random.fold_in(key, 101), (DOCS_ALL,), 0, 5, dtype=jnp.int32)


def draw_labels(key, part):
    return grade_draw(key).astype(jnp.int32)


def draw_leaves(key, part):
    grades = grade_draw(key)
    places = jnp.arange(DOCS_ALL, dtype=jnp.int32)
    jitter = jax.random.randint(jax.random.fold_in(key, 102), (DOCS_ALL,), 0, 16, dtype=jnp.int32)
    nearby = (places // BLOCK_DOCS * LEAF_SPAN + grades * 8 + jitter) % LEAVES
    anywhere = jax.random.randint(jax.random.fold_in(key, 103), (DOCS_ALL,), 0, LEAVES, dtype=jnp.int32)
    picked = jax.random.randint(jax.random.fold_in(key, 104), (DOCS_ALL,), 0, 10, dtype=jnp.int32) < 9
    chosen = jnp.where(picked, nearby, anywhere)
    chosen = chosen.at[0].set(0).at[DOCS_ALL - 1].set(LEAVES - 1)
    return chosen.astype(jnp.int32)


def plant(entries, rng, low, high):
    spot = [jax.random.randint(jax.random.fold_in(rng, axis), (), 0, length) for axis, length in enumerate(entries.shape)]
    widest = entries.shape.index(max(entries.shape))
    neighbour = spot[:widest] + [(spot[widest] + 1) % entries.shape[widest]] + spot[widest + 1:]
    return entries.at[tuple(spot)].set(low).at[tuple(neighbour)].set(high)


def level_of(rng, extent, cuts, smallest, top_value):
    def one(axis_at, shards_of):
        draws = jax.random.uniform(jax.random.fold_in(jax.random.fold_in(rng, 6), axis_at), (shards_of,), jnp.float32, smallest / len(cuts), top_value / len(cuts))
        return jnp.repeat(jnp.exp(draws), extent[axis_at] // shards_of).reshape((-1,) + (1,) * (len(extent) - axis_at - 1))

    loudness = one(*cuts[0])
    for cut in cuts[1:]:
        loudness = loudness * one(*cut)
    return loudness


def profile(count, total, bound, slope):
    loads = [(1 << 20) // math.isqrt(grade ** slope) + 1 for grade in range(2, count + 1)]
    spare, holding = total - bound - (count - 1), [1] * (count - 1)
    while spare > 0:
        movable = [i for i in range(count - 1) if holding[i] < bound]
        mass, budget = sum([loads[i] for i in movable]), spare
        for i in movable:
            more = min(bound - holding[i], max(1, budget * loads[i] // mass), spare)
            holding[i] = holding[i] + more
            spare = spare - more
    return np.array([bound] + holding)


def uneven(stream_key, amount, total, limit, slope):
    if amount == 2:
        one = jax.random.randint(stream_key, (), max(1, total - limit), min(limit, total - 1) + 1)
        return jnp.stack([one, total - one])
    sizes = jnp.asarray(profile(amount, total, limit, slope), jnp.int32)
    twos = (amount - 1) // 2
    donor, receiver = sizes[1:1 + 2 * twos:2], sizes[2:2 + 2 * twos:2]
    slack = jnp.minimum(donor - 1, limit - receiver)
    passed = jax.random.randint(jax.random.fold_in(stream_key, 1), (twos,), 0, 1 << 20) % (slack + 1)
    sizes = sizes.at[1:1 + 2 * twos:2].set(donor - passed).at[2:2 + 2 * twos:2].set(receiver + passed)
    return sizes[jax.random.permutation(jax.random.fold_in(stream_key, 2), amount)]


def gaussian(stream_key, dims, scale, reach, cuts=(), held_as=jnp.bfloat16):
    result = scale * jax.random.normal(stream_key, dims, jnp.float32)
    if cuts:
        result = result * level_of(stream_key, dims, cuts, -0.22, 0.18)
    return jnp.clip(result, -reach, reach).astype(held_as)


def setup_inputs(seed: int = 0) -> dict:
    streams_of = jax.random.split(jax.random.key(seed), 7)
    return {
        "scores": gaussian(streams_of[0], (DOCS_ALL,), 1.0, 6.0, ((0, 32),), jnp.float32),
        "labels": draw_labels(jax.random.fold_in(streams_of[6], 71), 0),
        "leaves": draw_leaves(jax.random.fold_in(streams_of[6], 71), 0),
        "bins": plant(jax.random.randint(streams_of[3], (DOCS_ALL, FEATURES), 0, BINS), jax.random.fold_in(streams_of[3], 1), 0, BINS - 1).astype(jnp.int32),
        "lengths": jax.vmap(lambda own: uneven(own, QUERIES_BLOCK, BLOCK_DOCS, MAX_LEN, 2))(jax.random.split(streams_of[4], N_QUERY)).reshape((N_QUERY, QUERIES_BLOCK)).astype(jnp.int32),
        "owner": jax.random.permutation(streams_of[5], FEATURES).astype(jnp.int32),
    }


lasso_penalty = 1.0
ridge_penalty = 1.0
shrinkage = 0.1


def query_of(lengths_row, count):
    bounds = jnp.cumsum(lengths_row)
    places = jnp.arange(count, dtype=jnp.int32)
    return jnp.searchsorted(bounds, places, side="right").astype(jnp.int32)


def place_in_query(sorted_ids):
    places = jnp.arange(sorted_ids.shape[0], dtype=jnp.int32)
    first = jnp.concatenate([jnp.ones((1,), dtype=jnp.bool_), sorted_ids[1:] != sorted_ids[:-1]])
    starts = lax.cummax(jnp.where(first, places, 0), axis=0)
    return places - starts


def query_stats(values, grades, query_ids, count):
    order = jnp.lexsort((-values, query_ids))
    ranked = place_in_query(query_ids[order])
    standing = jnp.zeros(values.shape, jnp.int32).at[order].set(ranked)
    discount = 1.0 / jnp.log2(2.0 + standing.astype(jnp.float32))
    ideal_order = jnp.lexsort((-grades, query_ids))
    ideal_ids = query_ids[ideal_order]
    ideal_place = place_in_query(ideal_ids)
    worth = jnp.exp2(grades[ideal_order].astype(jnp.float32)) - 1.0
    terms = worth / jnp.log2(2.0 + ideal_place.astype(jnp.float32))
    slots = jnp.where(ideal_ids >= 0, ideal_ids, count)
    ideal = jax.ops.segment_sum(terms, slots, num_segments=count + 1)
    usable = ideal > 0.5
    inverse = jnp.where(usable, 1.0 / jnp.where(usable, ideal, 1.0), 0.0)
    return discount, inverse[jnp.where(query_ids >= 0, query_ids, count)]


def pair_block(row_part, col_part, forward):
    row_score, row_grade, row_query, row_discount, row_inverse, row_place = row_part
    col_score, col_grade, col_query, col_discount, col_place = col_part
    keep = (row_query[:, None] == col_query[None, :]) & (row_query[:, None] >= 0)
    if forward:
        keep = keep & (col_place[None, :] > row_place[:, None])
    else:
        keep = keep & (col_place[None, :] != row_place[:, None])
    row_worth = jnp.exp2(row_grade.astype(jnp.float32))
    col_worth = jnp.exp2(col_grade.astype(jnp.float32))
    signs = jnp.sign(row_grade[:, None] - col_grade[None, :]).astype(jnp.float32)
    change = jnp.abs(row_worth[:, None] - col_worth[None, :]) * jnp.abs(row_discount[:, None] - col_discount[None, :]) * row_inverse[:, None]
    chance = jax.nn.sigmoid(-signs * (row_score[:, None] - col_score[None, :]))
    push = jnp.where(keep, change * chance, 0.0) * signs
    bend = jnp.where(keep, change * chance * (1.0 - chance), 0.0)
    return -jnp.sum(push, axis=1), jnp.sum(bend, axis=1), jnp.sum(push, axis=0), jnp.sum(bend, axis=0)


def add_into(total, piece, start):
    current = lax.dynamic_slice_in_dim(total, start, piece.shape[0])
    return lax.dynamic_update_slice_in_dim(total, current + piece, start, 0)


def leaf_newton(sums):
    total_grad = sums[0]
    total_curv = sums[1]
    return -jnp.sign(total_grad) * jnp.maximum(jnp.abs(total_grad) - lasso_penalty, 0.0) / (total_curv + ridge_penalty)


def histogram_of(gradient, curvature, bins, slot):
    cells = (slot[None, :] * BINS + bins).reshape(-1)
    weights = jnp.stack([gradient, curvature, jnp.ones_like(gradient)])
    spread = jnp.repeat(weights, FEATURES, axis=1)

    def one_stat(column):
        return jax.ops.segment_sum(column, cells, num_segments=FEATURES * BINS)

    return jax.vmap(one_stat)(spread)


def reference(scores, labels, leaves, bins, lengths, owner):
    def block_query(lengths_row):
        return query_of(lengths_row, BLOCK_DOCS)

    local_ids = jax.vmap(block_query)(lengths)
    query_ids = (local_ids + (jnp.arange(N_QUERY, dtype=jnp.int32) * QUERIES_BLOCK)[:, None]).reshape(-1)
    total_queries = N_QUERY * QUERIES_BLOCK
    discount, inverse = query_stats(scores, labels, query_ids, total_queries)
    padded = (jnp.pad(scores, (0, WINDOW)), jnp.pad(labels, (0, WINDOW)),
              jnp.pad(query_ids, (0, WINDOW), constant_values=-1), jnp.pad(discount, (0, WINDOW)),
              jnp.pad(inverse, (0, WINDOW)), jnp.arange(DOCS_ALL + WINDOW, dtype=jnp.int32))

    def visit(carry, tile_index):
        acc_grad, acc_curv = carry
        start = tile_index * TILE_ROWS
        row_part = tuple(lax.dynamic_slice_in_dim(item, start, TILE_ROWS) for item in padded)
        col_part = tuple(lax.dynamic_slice_in_dim(padded[which], start, WINDOW) for which in (0, 1, 2, 3, 5))
        row_grad, row_curv, col_grad, col_curv = pair_block(row_part, col_part, True)
        acc_grad = add_into(add_into(acc_grad, col_grad, start), row_grad, start)
        acc_curv = add_into(add_into(acc_curv, col_curv, start), row_curv, start)
        return (acc_grad, acc_curv), None

    empty = jnp.zeros((DOCS_ALL + WINDOW,), jnp.float32)
    (acc_grad, acc_curv), unused = lax.scan(visit, (empty, empty), jnp.arange(DOCS_ALL // TILE_ROWS, dtype=jnp.int32))
    gradient = acc_grad[:DOCS_ALL]
    curvature = acc_curv[:DOCS_ALL]
    lambdas = jnp.stack([gradient, curvature])
    leaf_sums = jnp.stack([jax.ops.segment_sum(gradient, leaves, num_segments=LEAVES),
                           jax.ops.segment_sum(curvature, leaves, num_segments=LEAVES)])
    leaf_values = leaf_newton(leaf_sums)
    score_step = shrinkage * leaf_values[leaves]
    slot = jnp.zeros((FEATURES,), jnp.int32).at[owner].set(jnp.arange(FEATURES, dtype=jnp.int32))

    def add_block(hist, block_index):
        start = block_index * DOCS_DEV
        block_bins = lax.dynamic_slice_in_dim(bins, start, DOCS_DEV, 0)
        part_grad = lax.dynamic_slice_in_dim(gradient, start, DOCS_DEV)
        part_curv = lax.dynamic_slice_in_dim(curvature, start, DOCS_DEV)
        return hist + histogram_of(part_grad, part_curv, block_bins, slot), None

    histograms, unused = lax.scan(add_block, jnp.zeros((3, FEATURES * BINS), jnp.float32),
                                  jnp.arange(DOCS_ALL // DOCS_DEV, dtype=jnp.int32))
    return lambdas, leaf_values, score_step, histograms
```

```python
import functools

import jax
import jax.numpy as jnp
import numpy as np
from jax import lax
from jax.experimental import pallas as pl
from jax.experimental.pallas import tpu as pltpu
from jax.sharding import PartitionSpec as P

BINS = 256
LEAVES = 1024
LANES = 128
GRADES = 4
LOW = 32
HIGH = BINS // LOW
GROUP = 8
CHUNK = 64
MAX_LEN = 1024

lasso_penalty = 1.0
ridge_penalty = 1.0
shrinkage = 0.1

VMEM_LIMIT = 48 * 1024 * 1024
F32 = jnp.float32
BF16 = jnp.bfloat16
NT = (((1,), (1,)), ((), ()))


def iota(shape, axis):
    return lax.broadcasted_iota(jnp.int32, shape, axis)


def vmem():
    return pl.BlockSpec(memory_space=pltpu.VMEM)


def smem():
    return pl.BlockSpec(memory_space=pltpu.SMEM)


def prepare_kernel(len_ref, pos_ref, perm_ref, bins_ref, lab_ref, bins_t_ref, qid_ref, inv_ref, bounds_ref):
    queries = len_ref.shape[1]
    rows = lab_ref.shape[0]
    own = inv_ref.shape[0]
    bins = bins_ref[...].astype(F32).astype(BF16)
    bins_t_ref[...] = lax.dot_general(perm_ref[...], bins, NT, preferred_element_type=F32)

    place = iota((rows, LANES), 0) * LANES + iota((rows, LANES), 1)
    qid = jnp.zeros((rows, LANES), jnp.int32)
    begin = jnp.zeros((queries, LANES), jnp.int32)
    finish = jnp.zeros((queries, LANES), jnp.int32)
    which = iota((queries, LANES), 0)
    start = jnp.int32(0)
    for q in range(queries):
        end = start + len_ref[0, q]
        qid = qid + jnp.where(place >= end, 1, 0)
        begin = jnp.where(which == q, start, begin)
        finish = jnp.where(which == q, end, finish)

        def set_low(r, carry, start=start):
            bounds_ref[0, r] = start
            return carry

        def set_high(r, carry, end=end):
            bounds_ref[1, r] = end
            return carry

        lax.fori_loop((start + LANES - 1) // LANES, (end + LANES - 1) // LANES, set_low, 0)
        lax.fori_loop(start // LANES, end // LANES, set_high, 0)
        start = end
    qid_ref[...] = qid

    counts = [jnp.zeros((queries, LANES), F32) for _ in range(GRADES)]
    lane = iota((queries, LANES), 1)
    for r in range(rows):
        at = lane + r * LANES
        inside = (at >= begin) & (at < finish)
        grade = jnp.where(inside, jnp.broadcast_to(lab_ref[r:r + 1, :], (queries, LANES)), 0)
        for g in range(GRADES):
            counts[g] = counts[g] + jnp.where(grade > g, 1.0, 0.0)
    position = iota((queries, MAX_LEN), 1).astype(F32)
    worth = jnp.zeros((queries, MAX_LEN), F32)
    for g in range(GRADES):
        held = jnp.sum(counts[g], axis=1, keepdims=True)
        worth = worth + jnp.where(position < held, float(2 ** g), 0.0)
    ideal = jnp.sum(worth / jnp.log2(2.0 + position), axis=1, keepdims=True)
    usable = ideal > 0.5
    inverse = jnp.where(usable, 1.0 / jnp.where(usable, ideal, 1.0), 0.0)
    first = pos_ref[0] * own
    for t in range(own):
        at = lane + (first + t) * LANES
        inside = (at >= begin) & (at < finish)
        inv_ref[t:t + 1, :] = jnp.sum(jnp.where(inside, inverse, 0.0), axis=0, keepdims=True)


def prepare(lengths, pos, perm, bins, labels):
    rows = labels.shape[0]
    own = bins.shape[0] // LANES
    features = bins.shape[1]
    return pl.pallas_call(
        prepare_kernel,
        out_shape=(
            jax.ShapeDtypeStruct((features, bins.shape[0]), F32),
            jax.ShapeDtypeStruct((rows, LANES), jnp.int32),
            jax.ShapeDtypeStruct((own, LANES), F32),
            jax.ShapeDtypeStruct((2, rows), jnp.int32),
        ),
        in_specs=[smem(), smem(), vmem(), vmem(), vmem()],
        out_specs=(vmem(), vmem(), vmem(), smem()),
        compiler_params=pltpu.CompilerParams(vmem_limit_bytes=VMEM_LIMIT),
        cost_estimate=pl.CostEstimate(flops=200_000_000, bytes_accessed=3_000_000, transcendentals=20_000),
        name="prepare",
    )(lengths, pos, perm, bins, labels)


def split_terms(value, terms):
    parts = []
    rest = value
    for _ in range(terms):
        part = rest.astype(BF16)
        parts.append(part)
        rest = rest - part.astype(F32)
    return parts


def widen(ref, source, rows):
    turned = jnp.transpose(source)
    for r in range(rows):
        ref[r * LANES:(r + 1) * LANES, :] = jnp.broadcast_to(turned[:, r:r + 1], (LANES, LANES))


def pairs_kernel(parts, bounds_ref, pos_ref, *refs):
    score_refs = refs[:parts]
    (lab_ref, qid_ref, inv_ref, leaf_ref, lam_ref, sums_ref,
     s_row, a_row, w_row, d_row, s_col, a_col, w_col, q_col, d_col, grad, curv) = refs[parts:]
    rows = lab_ref.shape[0]
    own = inv_ref.shape[0]
    me = pos_ref[0]
    for k in range(parts):
        s_row[pl.ds(pl.multiple_of((me ^ k) * own, own), own), :] = score_refs[k][...]
    a_row[...] = jnp.exp(s_row[...])
    w_row[...] = jnp.left_shift(1, lab_ref[...]).astype(F32)
    d_row[...] = jnp.zeros((rows, LANES), F32)
    widen(s_col, s_row[...], rows)
    widen(q_col, qid_ref[...], rows)
    widen(a_col, a_row[...], rows)
    widen(w_col, w_row[...], rows)

    first = me * own
    window_low = bounds_ref[0, first] // LANES
    window_high = (bounds_ref[1, first + own - 1] + LANES - 1) // LANES

    def row_of(ref, r):
        return jnp.broadcast_to(ref[pl.ds(r, 1), :], (8, LANES))

    def rank_group(r, carry):
        score = row_of(s_row, r)
        query = row_of(qid_ref, r)

        def sweep(ahead):
            def step(c, acc):
                base = pl.multiple_of(c * CHUNK, CHUNK)
                acc = list(acc)
                for u in range(CHUNK // 8):
                    other = s_col[pl.ds(base + 8 * u, 8), :]
                    above = (other >= score) if ahead else (other > score)
                    hit = above & (q_col[pl.ds(base + 8 * u, 8), :] == query)
                    acc[u % 4] = acc[u % 4] + jnp.where(hit, 1.0, 0.0)
                return tuple(acc)
            return step

        acc = tuple(jnp.zeros((8, LANES), F32) for _ in range(4))
        low = bounds_ref[0, r] // CHUNK
        high = (bounds_ref[1, r] + CHUNK - 1) // CHUNK
        per = LANES // CHUNK
        acc = lax.fori_loop(low, r * per, sweep(True), acc)
        acc = list(lax.fori_loop((r + 1) * per, high, sweep(False), acc))
        base = pl.multiple_of(r * LANES, LANES)
        for u in range(LANES // 8):
            other = s_col[pl.ds(base + 8 * u, 8), :]
            earlier = iota((8, LANES), 0) + 8 * u < iota((8, LANES), 1)
            above = (other > score) | ((other == score) & earlier)
            hit = above & (q_col[pl.ds(base + 8 * u, 8), :] == query)
            acc[u % 4] = acc[u % 4] + jnp.where(hit, 1.0, 0.0)
        total = (acc[0] + acc[1]) + (acc[2] + acc[3])
        d_row[pl.ds(r, 1), :] = jnp.sum(total, axis=0, keepdims=True)
        return carry

    lax.fori_loop(window_low, window_high, rank_group, 0)
    d_row[...] = 1.0 / jnp.log2(2.0 + d_row[...])
    widen(d_col, d_row[...], rows)

    def pair_group(t, carry):
        r = first + t
        a_i = row_of(a_row, r)
        w_i = row_of(w_row, r)
        d_i = row_of(d_row, r)
        query = row_of(qid_ref, r)

        def step(c, acc):
            base = pl.multiple_of(c * CHUNK, CHUNK)
            push = list(acc[:2])
            bend = list(acc[2:])
            for u in range(CHUNK // 8):
                at = pl.ds(base + 8 * u, 8)
                a_j = a_col[at, :]
                total = a_i + a_j
                rough = pl.reciprocal(total, approx=True)
                recip = rough * (2.0 - total * rough)
                gap = jnp.abs(d_i - d_col[at, :])
                lift = w_i - w_col[at, :]
                weight = jnp.where(q_col[at, :] == query, gap * recip, 0.0) * lift
                push[u % 2] = push[u % 2] + weight * jnp.where(lift > 0.0, a_j, a_i)
                bend[u % 2] = bend[u % 2] + jnp.abs(weight) * (recip * a_j)
            return tuple(push + bend)

        acc = tuple(jnp.zeros((8, LANES), F32) for _ in range(4))
        low = bounds_ref[0, r] // CHUNK
        high = (bounds_ref[1, r] + CHUNK - 1) // CHUNK
        acc = lax.fori_loop(low, high, step, acc)
        inverse = inv_ref[pl.ds(t, 1), :]
        grad[pl.ds(t, 1), :] = -inverse * jnp.sum(acc[0] + acc[1], axis=0, keepdims=True)
        curv[pl.ds(t, 1), :] = inverse * a_row[pl.ds(r, 1), :] * jnp.sum(acc[2] + acc[3], axis=0, keepdims=True)
        return carry

    lax.fori_loop(0, own, pair_group, 0)
    for t in range(own):
        lam_ref[0:1, t * LANES:(t + 1) * LANES] = grad[t:t + 1, :]
        lam_ref[1:2, t * LANES:(t + 1) * LANES] = curv[t:t + 1, :]

    docs = own * LANES
    leaf = leaf_ref[...]
    highs = LEAVES // LANES
    top = jnp.broadcast_to(leaf // LANES, (highs, docs)) == iota((highs, docs), 0)
    spots = jnp.where(jnp.broadcast_to(leaf % LANES, (LANES, docs)) == iota((LANES, docs), 0), 1.0, 0.0).astype(BF16)
    pieces = []
    for c in range(2):
        for part in split_terms(lam_ref[c:c + 1, :], 3):
            pieces.append(jnp.where(top, jnp.broadcast_to(part.astype(F32), (highs, docs)), 0.0))
    stacked = jnp.concatenate(pieces, axis=0).astype(BF16)
    sums = lax.dot_general(stacked, spots, NT, preferred_element_type=F32)
    for c in range(2):
        base = c * 3 * highs
        sums_ref[c * highs:(c + 1) * highs, :] = (
            sums[base:base + highs] + (sums[base + highs:base + 2 * highs] + sums[base + 2 * highs:base + 3 * highs])
        )


def pair_terms(bounds, pos, scores, labels, qid, inverse, leaves):
    rows = labels.shape[0]
    own = inverse.shape[0]
    block = rows * LANES
    row = pltpu.VMEM((rows, LANES), F32)
    col = pltpu.VMEM((block, LANES), F32)
    return pl.pallas_call(
        functools.partial(pairs_kernel, len(scores)),
        out_shape=(
            jax.ShapeDtypeStruct((2, own * LANES), F32),
            jax.ShapeDtypeStruct((2 * LEAVES // LANES, LANES), F32),
        ),
        in_specs=[smem(), smem()] + [vmem()] * (len(scores) + 4),
        out_specs=(vmem(), vmem()),
        scratch_shapes=[row, row, row, row, col, col, col, pltpu.VMEM((block, LANES), jnp.int32), col,
                        pltpu.VMEM((own, LANES), F32), pltpu.VMEM((own, LANES), F32)],
        compiler_params=pltpu.CompilerParams(vmem_limit_bytes=VMEM_LIMIT),
        cost_estimate=pl.CostEstimate(flops=40_000_000, bytes_accessed=200_000, transcendentals=2_000_000),
        name="pair_terms",
    )(bounds, pos, *scores, labels, qid, inverse, leaves)


def histogram_kernel(first, groups, lam_ref, bins_ref, out_ref, weights):
    docs = lam_ref.shape[1]
    depth = 256
    rows = 16
    for c in range(2):
        fine = split_terms(lam_ref[c:c + 1, :], 2)
        tile = jnp.concatenate([jnp.broadcast_to(part.astype(F32), (HIGH, docs)) for part in fine], axis=0)
        weights[c * rows:(c + 1) * rows, :] = tile.astype(BF16)

    row = iota((rows, depth), 0)
    low_level = [(row + rows * k).astype(F32).astype(BF16) for k in range(LOW // rows)]
    high_level = (row % HIGH).astype(F32).astype(BF16)
    upper = row < HIGH
    zero = jnp.zeros((rows, depth), BF16)
    one = jnp.ones((rows, depth), BF16)
    lane_owner = iota((1, GROUP * LOW), 1) // LOW

    def one_group(g, carry):
        base = pl.multiple_of((first + g) * GROUP, GROUP)
        acc = None
        for k in range(docs // depth):
            span = slice(k * depth, (k + 1) * depth)
            code = bins_ref[pl.ds(base, GROUP), span]
            high = jnp.floor(code * (1.0 / LOW))
            low = code - high * LOW
            left, right, count = [], [], []
            wide = []
            for f in range(GROUP):
                high_f = jnp.broadcast_to(high[f:f + 1, :], (rows, depth))
                low_f = jnp.broadcast_to(low[f:f + 1, :], (rows, depth)).astype(BF16)
                wide.append(high_f)
                match = high_f.astype(BF16) == high_level
                for c in range(2):
                    left.append(jnp.where(match, weights[c * rows:(c + 1) * rows, span], zero))
                for level in low_level:
                    right.append(jnp.where(low_f == level, one, zero))
            for f in range(0, GROUP, 2):
                both = jnp.where(upper, wide[f], wide[f + 1]).astype(BF16)
                count.append(jnp.where(both == high_level, one, zero))
            part = lax.dot_general(
                jnp.concatenate(left + count, axis=0), jnp.concatenate(right, axis=0), NT,
                preferred_element_type=F32,
            )
            acc = part if acc is None else acc + part
        stats = jnp.zeros((2 * rows, GROUP * LOW), F32)
        counts = jnp.zeros((HIGH, GROUP * LOW), F32)
        for f in range(GROUP):
            mine = lane_owner == f
            stats = jnp.where(mine, acc[f * 2 * rows:(f + 1) * 2 * rows], stats)
            at = GROUP * 2 * rows + f * HIGH
            counts = jnp.where(mine, acc[at:at + HIGH], counts)
        out_ref[g] = jnp.concatenate(
            [stats[0:HIGH] + stats[HIGH:2 * HIGH], stats[2 * HIGH:3 * HIGH] + stats[3 * HIGH:4 * HIGH], counts], axis=0)
        return carry

    lax.fori_loop(0, groups, one_group, 0)


def histogram_part(first, groups, lambdas, bins_t):
    docs = lambdas.shape[1]
    return pl.pallas_call(
        functools.partial(histogram_kernel, first, groups),
        out_shape=jax.ShapeDtypeStruct((groups, 3 * HIGH, GROUP * LOW), F32),
        in_specs=[vmem(), vmem()],
        out_specs=vmem(),
        scratch_shapes=[pltpu.VMEM((4 * HIGH, docs), BF16)],
        compiler_params=pltpu.CompilerParams(vmem_limit_bytes=VMEM_LIMIT),
        cost_estimate=pl.CostEstimate(flops=groups * 330_000_000, bytes_accessed=groups * 60_000, transcendentals=0),
        name="histogram_part",
    )(lambdas, bins_t)


def finish_kernel(parts, per_dev, *refs):
    sum_refs = refs[:parts]
    leaf_ref = refs[parts]
    hist_refs = refs[parts + 1:parts + 1 + parts]
    value_ref, step_ref, hist_ref = refs[2 * parts + 1:]
    totals = add_up([ref[...] for ref in sum_refs])
    highs = LEAVES // LANES
    grad, curv = totals[:highs], totals[highs:]
    shrunk = jnp.maximum(jnp.abs(grad) - lasso_penalty, 0.0)
    values = jnp.where(grad > 0.0, -shrunk, shrunk) / (curv + ridge_penalty)
    value_ref[...] = values
    leaf = leaf_ref[...]
    top, spot = leaf // LANES, leaf % LANES
    step = jnp.zeros(leaf.shape, F32)
    for h in range(highs):
        row = jnp.broadcast_to(values[h:h + 1, :], leaf.shape)
        step = jnp.where(top == h, jnp.take_along_axis(row, spot, axis=1), step)
    step_ref[...] = shrinkage * step
    hist = add_up([ref[...] for ref in hist_refs])
    if per_dev == GROUP:
        for c in range(3):
            for f in range(GROUP):
                line = [hist[c * HIGH + h:c * HIGH + h + 1, f * LOW:(f + 1) * LOW] for h in range(HIGH)]
                hist_ref[c:c + 1, f * BINS:(f + 1) * BINS] = jnp.concatenate(line, axis=1)
    else:
        hist_ref[...] = hist


def finish(sums, leaves, hists, per_dev):
    out = (3, per_dev * BINS) if per_dev == GROUP else hists[0].shape
    return pl.pallas_call(
        functools.partial(finish_kernel, len(sums), per_dev),
        out_shape=(
            jax.ShapeDtypeStruct((LEAVES // LANES, LANES), F32),
            jax.ShapeDtypeStruct(leaves.shape, F32),
            jax.ShapeDtypeStruct(out, F32),
        ),
        in_specs=[vmem()] * (2 * len(sums) + 1),
        out_specs=(vmem(), vmem(), vmem()),
        compiler_params=pltpu.CompilerParams(vmem_limit_bytes=VMEM_LIMIT),
        name="finish",
    )(*sums, leaves, *hists)


def add_up(parts):
    while len(parts) > 1:
        parts = [parts[k] + parts[k + 1] for k in range(0, len(parts), 2)]
    return parts[0]


def exchange_rounds(query_count, feat_count):
    feat_bits = [1 << b for b in range(feat_count.bit_length() - 1)]
    query_bits = [feat_count << b for b in range(query_count.bit_length() - 1)]
    rounds = [query_bits[:1]] if query_bits else []
    for bits in (query_bits[1:], feat_bits):
        rounds += [bits[k:k + 2] for k in range(0, len(bits), 2)]
    return [[0] + bits if len(bits) == 1 else [0, bits[0], bits[1], bits[0] | bits[1]] for bits in rounds]


def local(scores, labels, leaves, bins, lengths, owner):
    query_count = lax.axis_size("query")
    feat_count = lax.axis_size("feat")
    count = query_count * feat_count
    feat_pos = lax.axis_index("feat").astype(jnp.int32)
    place = lax.axis_index("query").astype(jnp.int32) * feat_count + feat_pos
    docs = scores.shape[0]
    own = docs // LANES
    features = owner.shape[0]
    per_dev = features // count
    axes = ("query", "feat")
    rounds = exchange_rounds(query_count, feat_count)

    def swap(value, mask):
        return lax.ppermute(value, axes, [(p, p ^ mask) for p in range(count)])

    own_scores = scores.reshape(own, LANES)
    score_parts = [own_scores] + [
        lax.ppermute(own_scores, "feat", [(p, p ^ k) for p in range(feat_count)]) for k in range(1, feat_count)]

    order = [0]
    for masks in reversed(rounds):
        order = [mask | rest for mask in masks for rest in order]
    relative = jnp.asarray(np.array(order, np.int32)) ^ place
    held = owner.reshape(count, per_dev)
    pick = relative[:, None, None] == jnp.arange(count, dtype=jnp.int32)[None, :, None]
    turned = jnp.sum(jnp.where(pick, held[None], 0), axis=1).reshape(features)
    perm = (turned[:, None] == jnp.arange(features, dtype=jnp.int32)[None, :]).astype(BF16)

    pos = feat_pos.reshape(1)
    label_rows = labels.reshape(-1, LANES)
    bins_t, qid, inverse, bounds = prepare(lengths, pos, perm, bins, label_rows)
    lambdas, sums = pair_terms(bounds, pos, score_parts, label_rows, qid, inverse, leaves.reshape(1, docs))

    def blocks(part):
        if per_dev == GROUP:
            return part
        groups = part.shape[0]
        wide = part.reshape(groups, 3, HIGH, GROUP // per_dev, per_dev, LOW)
        return wide.transpose(0, 3, 1, 4, 2, 5).reshape(groups * GROUP // per_dev, 3, per_dev * BINS)

    total_groups = features // GROUP
    fan = len(rounds[1])
    cuts = [total_groups // 2, total_groups // (2 * fan), 0]
    tops = [total_groups, total_groups // 2, total_groups // (2 * fan)]
    pieces = [blocks(histogram_part(cut, top - cut, lambdas, bins_t)) for cut, top in zip(cuts, tops)]

    arrived = swap(pieces[0], rounds[0][1])
    edge = pieces[2].shape[0]
    current = [pieces[2] + arrived[:edge]]
    for k in range(fan - 1):
        span = slice(k * edge, (k + 1) * edge)
        current.append(pieces[1][span] + arrived[edge:][span])
    for k in range(1, len(rounds)):
        masks = rounds[k]
        received = [current[0]] + [swap(current[m], masks[m]) for m in range(1, len(masks))]
        if k + 1 < len(rounds):
            merged = add_up(received)
            step = merged.shape[0] // len(rounds[k + 1])
            current = [merged[m * step:(m + 1) * step] for m in range(len(rounds[k + 1]))]

    for k, masks in enumerate(rounds):
        sums_parts = [sums] + [swap(sums, mask) for mask in masks[1:]]
        if k + 1 < len(rounds):
            sums = add_up(sums_parts)

    values, step, histograms = finish(
        sums_parts, leaves.reshape(own, LANES), [part[0] for part in received], per_dev)
    return lambdas, values.reshape(LEAVES), step.reshape(docs), histograms


def solution(mesh):
    in_specs = (
        P(("query", "feat")),
        P("query"),
        P(("query", "feat")),
        P(("query", "feat"), None),
        P("query", None),
        P(),
    )
    out_specs = (P(None, ("query", "feat")), P(), P(("query", "feat")), P(None, ("query", "feat")))
    return jax.shard_map(local, mesh=mesh, in_specs=in_specs, out_specs=out_specs, check_vma=False)
```

```python
import functools

import jax
import jax.numpy as jnp
from jax import lax
from jax.experimental import pallas as pl
from jax.experimental.pallas import tpu as pltpu
from jax.sharding import PartitionSpec as P

BINS = 256
LEAVES = 1024
LANES = 128
GRADES = 4
LOW = 32
HIGH = BINS // LOW
GROUP = 8
CHUNK = 64
MAX_LEN = 1024

lasso_penalty = 1.0
ridge_penalty = 1.0
shrinkage = 0.1

VMEM_LIMIT = 48 * 1024 * 1024
F32 = jnp.float32
BF16 = jnp.bfloat16
NT = (((1,), (1,)), ((), ()))


def iota(shape, axis):
    return lax.broadcasted_iota(jnp.int32, shape, axis)


def vmem():
    return pl.BlockSpec(memory_space=pltpu.VMEM)


def smem():
    return pl.BlockSpec(memory_space=pltpu.SMEM)


def prepare_kernel(feat_count, masks, len_ref, pos_ref, owner_hbm, bins_hbm, lab_hbm, leaf_hbm,
                   bins_t_ref, qid_ref, worth_ref, inv_ref, leaf_ref, bounds_ref, bins_ref, lab_ref, owner_ref, sems):
    queries = len_ref.shape[1]
    rows = lab_ref.shape[0]
    own = inv_ref.shape[0]
    features = bins_ref.shape[1]
    place = pos_ref[0]
    copies = [pltpu.make_async_copy(source, target, sems.at[k]) for k, (source, target) in enumerate(
        ((lab_hbm, lab_ref), (owner_hbm, owner_ref), (bins_hbm, bins_ref), (leaf_hbm, leaf_ref)))]
    for copy in copies:
        copy.start()

    spot = iota((rows, LANES), 0) * LANES + iota((rows, LANES), 1)
    qid = jnp.zeros((rows, LANES), jnp.int32)
    begin = jnp.zeros((queries, LANES), jnp.int32)
    finish = jnp.zeros((queries, LANES), jnp.int32)
    which = iota((queries, LANES), 0)
    start = jnp.int32(0)
    for q in range(queries):
        end = start + len_ref[0, q]
        qid = qid + jnp.where(spot >= end, 1, 0)
        begin = jnp.where(which == q, start, begin)
        finish = jnp.where(which == q, end, finish)

        def set_low(r, carry, start=start):
            bounds_ref[0, r] = start
            return carry

        def set_high(r, carry, end=end):
            bounds_ref[1, r] = end
            return carry

        lax.fori_loop((start + LANES - 1) // LANES, (end + LANES - 1) // LANES, set_low, 0)
        lax.fori_loop(start // LANES, end // LANES, set_high, 0)
        start = end
    qid_ref[...] = qid

    copies[0].wait()
    worth_ref[...] = jnp.left_shift(1, lab_ref[...]).astype(F32)
    counts = [jnp.zeros((queries, LANES), F32) for _ in range(GRADES)]
    lane = iota((queries, LANES), 1)
    for r in range(rows):
        at = lane + r * LANES
        inside = (at >= begin) & (at < finish)
        grade = jnp.where(inside, jnp.broadcast_to(lab_ref[r:r + 1, :], (queries, LANES)), 0)
        for g in range(GRADES):
            counts[g] = counts[g] + jnp.where(grade > g, 1.0, 0.0)
    position = iota((queries, MAX_LEN), 1).astype(F32)
    gain = jnp.zeros((queries, MAX_LEN), F32)
    for g in range(GRADES):
        held = jnp.sum(counts[g], axis=1, keepdims=True)
        gain = gain + jnp.where(position < held, float(2 ** g), 0.0)
    level = 1.0 / jnp.log2(2.0 + position[0:1, :])
    ideal = jnp.sum(gain * level, axis=1, keepdims=True)
    usable = ideal > 0.5
    inverse = jnp.where(usable, 1.0 / jnp.where(usable, ideal, 1.0), 0.0)
    first = place % feat_count * own
    for t in range(own):
        at = lane + (first + t) * LANES
        inside = (at >= begin) & (at < finish)
        inv_ref[t:t + 1, :] = jnp.sum(jnp.where(inside, inverse, 0.0), axis=0, keepdims=True)

    copies[1].wait()
    per_dev = features >> len(masks)
    owner = jnp.concatenate([owner_ref[k:k + 1, :] for k in range(features // LANES)], axis=1)
    square = (features, features)
    down, across = iota(square, 0), iota(square, 1)
    index = down // per_dev
    target = jnp.zeros(square, jnp.int32)
    for b, mask in enumerate(masks):
        target = target + ((index >> b) & 1) * mask
    target = (target ^ place) * per_dev + down % per_dev
    pick = jnp.where(target == across, 1.0, 0.0).astype(BF16)
    holds = jnp.where(jnp.broadcast_to(owner, square) == down, 1.0, 0.0).astype(BF16)
    perm = lax.dot_general(pick, holds, NT, preferred_element_type=F32).astype(BF16)
    copies[2].wait()
    bins = bins_ref[...].astype(F32).astype(BF16)
    bins_t_ref[...] = lax.dot_general(perm, bins, NT, preferred_element_type=F32)
    copies[3].wait()


def prepare(feat_count, masks, lengths, pos, owner, bins, labels, leaves):
    rows = labels.shape[0]
    own = leaves.shape[0]
    docs, features = bins.shape
    hbm = pl.BlockSpec(memory_space=pltpu.HBM)
    return pl.pallas_call(
        functools.partial(prepare_kernel, feat_count, masks),
        out_shape=(
            jax.ShapeDtypeStruct((features, docs), F32),
            jax.ShapeDtypeStruct((rows, LANES), jnp.int32),
            jax.ShapeDtypeStruct((rows, LANES), F32),
            jax.ShapeDtypeStruct((own, LANES), F32),
            jax.ShapeDtypeStruct((own, LANES), jnp.int32),
            jax.ShapeDtypeStruct((2, rows), jnp.int32),
        ),
        in_specs=[smem(), smem(), hbm, hbm, hbm, hbm],
        out_specs=(vmem(), vmem(), vmem(), vmem(), vmem(), smem()),
        scratch_shapes=[pltpu.VMEM((docs, features), jnp.int32), pltpu.VMEM((rows, LANES), jnp.int32),
                        pltpu.VMEM((features // LANES, LANES), jnp.int32), pltpu.SemaphoreType.DMA((4,))],
        compiler_params=pltpu.CompilerParams(vmem_limit_bytes=VMEM_LIMIT),
        cost_estimate=pl.CostEstimate(flops=200_000_000, bytes_accessed=3_000_000, transcendentals=20_000),
        name="prepare",
    )(lengths, pos, owner, bins, labels, leaves)


def split_terms(value, terms):
    parts = []
    rest = value
    for _ in range(terms):
        part = rest.astype(BF16)
        parts.append(part)
        rest = rest - part.astype(F32)
    return parts


def widen(ref, source):
    turned = jnp.transpose(source)
    for r in range(source.shape[0]):
        ref[r * LANES:(r + 1) * LANES, :] = jnp.broadcast_to(turned[:, r:r + 1], (LANES, LANES))


def pairs_kernel(parts, bounds_ref, pos_ref, *refs):
    score_refs = refs[:parts]
    (worth_ref, qid_ref, inv_ref, leaf_ref, lam_ref, tile_ref, sums_ref,
     s_row, a_row, d_row, s_turn, q_turn, s_col, q_col, a_own, w_own, d_own, push_own, bend_own) = refs[parts:]
    rows = worth_ref.shape[0]
    own = inv_ref.shape[0]
    docs = own * LANES
    me = pos_ref[0] % parts
    for k in range(parts):
        s_row[pl.ds(pl.multiple_of((me ^ k) * own, own), own), :] = score_refs[k][...]
    a_row[...] = jnp.exp(s_row[...])
    d_row[...] = jnp.zeros((rows, LANES), F32)
    first = pl.multiple_of(me * own, own)
    window_low = bounds_ref[0, first] // LANES
    window_high = (bounds_ref[1, first + own - 1] + LANES - 1) // LANES
    s_turn[...] = jnp.transpose(s_row[...])
    q_turn[...] = jnp.transpose(qid_ref[...])
    for r in range(rows):
        @pl.when((r >= window_low) & (r < window_high))
        def _(r=r):
            at = slice(r * LANES, (r + 1) * LANES)
            s_col[at, :] = jnp.broadcast_to(s_turn[:, r:r + 1], (LANES, LANES))
            q_col[at, :] = jnp.broadcast_to(q_turn[:, r:r + 1], (LANES, LANES))
    widen(a_own, a_row[pl.ds(first, own), :])
    widen(w_own, worth_ref[pl.ds(first, own), :])

    def row_of(ref, r):
        return jnp.broadcast_to(ref[pl.ds(r, 1), :], (8, LANES))

    def rank_group(r, carry):
        score = row_of(s_row, r)
        query = row_of(qid_ref, r)

        def sweep(ahead):
            def step(c, acc):
                base = pl.multiple_of(c * CHUNK, CHUNK)
                acc = list(acc)
                for u in range(CHUNK // 8):
                    other = s_col[pl.ds(base + 8 * u, 8), :]
                    above = (other >= score) if ahead else (other > score)
                    hit = above & (q_col[pl.ds(base + 8 * u, 8), :] == query)
                    acc[u % 4] = acc[u % 4] + jnp.where(hit, 1.0, 0.0)
                return tuple(acc)
            return step

        acc = tuple(jnp.zeros((8, LANES), F32) for _ in range(4))
        per = LANES // CHUNK
        low = jnp.maximum(bounds_ref[0, r] // CHUNK, window_low * per)
        high = jnp.minimum((bounds_ref[1, r] + CHUNK - 1) // CHUNK, window_high * per)
        acc = lax.fori_loop(low, r * per, sweep(True), acc)
        acc = list(lax.fori_loop((r + 1) * per, high, sweep(False), acc))
        base = pl.multiple_of(r * LANES, LANES)
        for u in range(LANES // 8):
            other = s_col[pl.ds(base + 8 * u, 8), :]
            earlier = iota((8, LANES), 0) + 8 * u < iota((8, LANES), 1)
            above = (other > score) | ((other == score) & earlier)
            hit = above & (q_col[pl.ds(base + 8 * u, 8), :] == query)
            acc[u % 4] = acc[u % 4] + jnp.where(hit, 1.0, 0.0)
        total = (acc[0] + acc[1]) + (acc[2] + acc[3])
        d_row[pl.ds(r, 1), :] = jnp.sum(total, axis=0, keepdims=True)
        return carry

    lax.fori_loop(window_low, window_high, rank_group, 0)
    d_row[...] = 1.0 / jnp.log2(2.0 + d_row[...])
    widen(d_own, d_row[pl.ds(first, own), :])

    def pair_block(b, carry):
        base = pl.multiple_of(b * CHUNK, CHUNK)
        r = first + b // (LANES // CHUNK)
        count = CHUNK // 8
        queries = pl.multiple_of(first * LANES + base, CHUNK)

        def step(c, acc):
            acc = list(acc)
            a_j = row_of(a_row, c)
            w_j = row_of(worth_ref, c)
            d_j = row_of(d_row, c)
            query = row_of(qid_ref, c)
            for u in range(count):
                at = pl.ds(base + 8 * u, 8)
                a_i = a_own[at, :]
                total = a_i + a_j
                rough = pl.reciprocal(total, approx=True)
                recip = rough * (2.0 - total * rough)
                gap = jnp.abs(d_own[at, :] - d_j)
                lift = w_own[at, :] - w_j
                weight = jnp.where(q_col[pl.ds(queries + 8 * u, 8), :] == query, gap * recip, 0.0) * lift
                acc[u] = acc[u] + weight * jnp.where(lift > 0.0, a_j, a_i)
                acc[count + u] = acc[count + u] + jnp.abs(weight) * (recip * a_j)
            return tuple(acc)

        acc = tuple(jnp.zeros((8, LANES), F32) for _ in range(2 * count))
        acc = lax.fori_loop(bounds_ref[0, r] // LANES, (bounds_ref[1, r] + LANES - 1) // LANES, step, acc)
        for u in range(count):
            push_own[pl.ds(base + 8 * u, 8), :] = acc[u]
            bend_own[pl.ds(base + 8 * u, 8), :] = acc[count + u]
        return carry

    lax.fori_loop(0, docs // CHUNK, pair_block, 0)
    for t in range(own):
        at = slice(t * LANES, (t + 1) * LANES)
        inverse = inv_ref[t:t + 1, :]
        lam_ref[0:1, at] = -inverse * jnp.sum(jnp.transpose(push_own[at, :]), axis=0, keepdims=True)
        lam_ref[1:2, at] = (inverse * a_row[pl.ds(first + t, 1), :]
                            * jnp.sum(jnp.transpose(bend_own[at, :]), axis=0, keepdims=True))

    leaf = jnp.concatenate([leaf_ref[t:t + 1, :] for t in range(own)], axis=1)
    highs = LEAVES // LANES
    top = jnp.broadcast_to(leaf // LANES, (highs, docs)) == iota((highs, docs), 0)
    spots = jnp.where(jnp.broadcast_to(leaf % LANES, (LANES, docs)) == iota((LANES, docs), 0), 1.0, 0.0).astype(BF16)
    pieces, tiles = [], []
    for c in range(2):
        for k, part in enumerate(split_terms(lam_ref[c:c + 1, :], 3)):
            wide = jnp.broadcast_to(part.astype(F32), (highs, docs))
            pieces.append(jnp.where(top, wide, 0.0))
            if k < 2:
                tiles.append(wide)
    tile_ref[...] = jnp.concatenate(tiles, axis=0).astype(BF16)
    stacked = jnp.concatenate(pieces, axis=0).astype(BF16)
    sums = lax.dot_general(stacked, spots, NT, preferred_element_type=F32)
    for c in range(2):
        base = c * 3 * highs
        sums_ref[:, c * LANES:(c + 1) * LANES] = (
            sums[base:base + highs] + (sums[base + highs:base + 2 * highs] + sums[base + 2 * highs:base + 3 * highs])
        )


def pair_terms(bounds, pos, scores, worth, qid, inverse, leaves):
    rows = worth.shape[0]
    own = inverse.shape[0]
    docs = own * LANES
    highs = LEAVES // LANES
    row = pltpu.VMEM((rows, LANES), F32)
    mine = pltpu.VMEM((docs, LANES), F32)
    return pl.pallas_call(
        functools.partial(pairs_kernel, len(scores)),
        out_shape=(
            jax.ShapeDtypeStruct((2, docs), F32),
            jax.ShapeDtypeStruct((4 * HIGH, docs), BF16),
            jax.ShapeDtypeStruct((highs, 2 * LANES), F32),
        ),
        in_specs=[smem(), smem()] + [vmem()] * (len(scores) + 4),
        out_specs=(vmem(), vmem(), vmem()),
        scratch_shapes=[row, row, row, pltpu.VMEM((LANES, rows), F32), pltpu.VMEM((LANES, rows), jnp.int32),
                        pltpu.VMEM((rows * LANES, LANES), F32), pltpu.VMEM((rows * LANES, LANES), jnp.int32),
                        mine, mine, mine, mine, mine],
        compiler_params=pltpu.CompilerParams(vmem_limit_bytes=VMEM_LIMIT),
        cost_estimate=pl.CostEstimate(flops=40_000_000, bytes_accessed=200_000, transcendentals=2_000_000),
        name="pair_terms",
    )(bounds, pos, *scores, worth, qid, inverse, leaves)


def histogram_kernel(first, groups, tile_ref, bins_ref, *refs):
    out_ref = refs[-1]
    docs = tile_ref.shape[1]
    depth = 256
    rows = 16
    row = iota((rows, depth), 0)
    low_level = [(row + rows * k).astype(F32).astype(BF16) for k in range(LOW // rows)]
    high_level = (row % HIGH).astype(F32).astype(BF16)
    upper = row < HIGH
    zero = jnp.zeros((rows, depth), BF16)
    one = jnp.ones((rows, depth), BF16)
    lane_owner = iota((1, GROUP * LOW), 1) // LOW

    def one_group(g, carry):
        base = pl.multiple_of((first + g) * GROUP, GROUP)
        acc = None
        for k in range(docs // depth):
            span = slice(k * depth, (k + 1) * depth)
            code = bins_ref[pl.ds(base, GROUP), span]
            high = jnp.floor(code * (1.0 / LOW))
            low = code - high * LOW
            left, right, count = [], [], []
            wide = []
            for f in range(GROUP):
                high_f = jnp.broadcast_to(high[f:f + 1, :], (rows, depth))
                low_f = jnp.broadcast_to(low[f:f + 1, :], (rows, depth)).astype(BF16)
                wide.append(high_f)
                match = high_f.astype(BF16) == high_level
                for c in range(2):
                    left.append(jnp.where(match, tile_ref[c * rows:(c + 1) * rows, span], zero))
                for level in low_level:
                    right.append(jnp.where(low_f == level, one, zero))
            for f in range(0, GROUP, 2):
                both = jnp.where(upper, wide[f], wide[f + 1]).astype(BF16)
                count.append(jnp.where(both == high_level, one, zero))
            part = lax.dot_general(
                jnp.concatenate(left + count, axis=0), jnp.concatenate(right, axis=0), NT,
                preferred_element_type=F32,
            )
            acc = part if acc is None else acc + part
        stats = jnp.zeros((2 * rows, GROUP * LOW), F32)
        counts = jnp.zeros((HIGH, GROUP * LOW), F32)
        for f in range(GROUP):
            mine = lane_owner == f
            stats = jnp.where(mine, acc[f * 2 * rows:(f + 1) * 2 * rows], stats)
            at = GROUP * 2 * rows + f * HIGH
            counts = jnp.where(mine, acc[at:at + HIGH], counts)
        out_ref[pl.ds(pl.multiple_of(g * 3 * HIGH, 3 * HIGH), 3 * HIGH), :] = jnp.concatenate(
            [stats[0:HIGH] + stats[HIGH:2 * HIGH], stats[2 * HIGH:3 * HIGH] + stats[3 * HIGH:4 * HIGH], counts], axis=0)
        return carry

    if len(refs) > 1:
        out_ref[groups * 3 * HIGH:, :] = refs[0][...]
    lax.fori_loop(0, groups, one_group, 0, unroll=2)


def histogram_part(first, groups, tiles, bins_t, *tail):
    rows = groups * 3 * HIGH + sum(piece.shape[0] for piece in tail)
    return pl.pallas_call(
        functools.partial(histogram_kernel, first, groups),
        out_shape=jax.ShapeDtypeStruct((rows, GROUP * LOW), F32),
        in_specs=[vmem()] * (2 + len(tail)),
        out_specs=vmem(),
        compiler_params=pltpu.CompilerParams(vmem_limit_bytes=VMEM_LIMIT),
        cost_estimate=pl.CostEstimate(flops=groups * 330_000_000, bytes_accessed=groups * 60_000, transcendentals=0),
        name="histogram_part",
    )(tiles, bins_t, *tail)


def finish_kernel(per_dev, leaf_ref, kept_ref, sums_ref, *refs):
    arrived = refs[:-3]
    value_ref, step_ref, hist_ref = refs[-3:]
    unit = kept_ref.shape[0]
    totals = add_up([sums_ref[...]] + [ref[unit:, :] for ref in arrived])
    highs = LEAVES // LANES
    grad, curv = totals[:, :LANES], totals[:, LANES:]
    shrunk = jnp.maximum(jnp.abs(grad) - lasso_penalty, 0.0)
    values = jnp.where(grad > 0.0, -shrunk, shrunk) / (curv + ridge_penalty)
    value_ref[...] = values
    leaf = leaf_ref[...]
    top, spot = leaf // LANES, leaf % LANES
    step = jnp.zeros(leaf.shape, F32)
    for h in range(highs):
        row = jnp.broadcast_to(values[h:h + 1, :], leaf.shape)
        step = jnp.where(top == h, jnp.take_along_axis(row, spot, axis=1), step)
    step_ref[...] = shrinkage * step
    hist = add_up([kept_ref[...]] + [ref[:unit, :] for ref in arrived])
    if per_dev == GROUP:
        for c in range(3):
            for f in range(GROUP):
                line = [hist[c * HIGH + h:c * HIGH + h + 1, f * LOW:(f + 1) * LOW] for h in range(HIGH)]
                hist_ref[c:c + 1, f * BINS:(f + 1) * BINS] = jnp.concatenate(line, axis=1)
    else:
        hist_ref[...] = hist


def finish(per_dev, leaves, kept, sums, arrived):
    out = (3, per_dev * BINS) if per_dev == GROUP else kept.shape
    return pl.pallas_call(
        functools.partial(finish_kernel, per_dev),
        out_shape=(
            jax.ShapeDtypeStruct((LEAVES // LANES, LANES), F32),
            jax.ShapeDtypeStruct(leaves.shape, F32),
            jax.ShapeDtypeStruct(out, F32),
        ),
        in_specs=[vmem()] * (3 + len(arrived)),
        out_specs=(vmem(), vmem(), vmem()),
        compiler_params=pltpu.CompilerParams(vmem_limit_bytes=VMEM_LIMIT),
        name="finish",
    )(leaves, kept, sums, *arrived)


def add_up(parts):
    while len(parts) > 1:
        parts = [parts[k] + parts[k + 1] for k in range(0, len(parts), 2)]
    return parts[0]


def exchange_rounds(query_count, feat_count):
    feat_bits = [1 << b for b in range(feat_count.bit_length() - 1)]
    query_bits = [feat_count << b for b in range(query_count.bit_length() - 1)]
    rounds = [query_bits[:1]]
    for bits in (query_bits[1:], feat_bits):
        rounds += [bits[k:k + 2] for k in range(0, len(bits), 2)]
    return rounds


def local(scores, labels, leaves, bins, lengths, owner):
    query_count = lax.axis_size("query")
    feat_count = lax.axis_size("feat")
    count = query_count * feat_count
    place = lax.axis_index("query").astype(jnp.int32) * feat_count + lax.axis_index("feat").astype(jnp.int32)
    docs = scores.shape[0]
    own = docs // LANES
    features = owner.shape[0]
    per_dev = features // count
    unit = 3 * per_dev
    axes = ("query", "feat")
    rounds = exchange_rounds(query_count, feat_count)
    bit_masks = [bit for bits in reversed(rounds) for bit in bits]
    fans = [[0, bits[0]] if len(bits) == 1 else [0, bits[0], bits[1], bits[0] | bits[1]] for bits in rounds]

    def swap(value, mask):
        return lax.ppermute(value, axes, [(p, p ^ mask) for p in range(count)])

    own_scores = scores.reshape(own, LANES)
    score_parts = [own_scores] + [
        lax.ppermute(own_scores, "feat", [(p, p ^ k) for p in range(feat_count)]) for k in range(1, feat_count)]

    pos = place.reshape(1)
    bins_t, qid, worth, inverse, leaf_rows, bounds = prepare(
        feat_count, bit_masks, lengths, pos, owner.reshape(-1, LANES), bins, labels.reshape(-1, LANES),
        leaves.reshape(own, LANES))
    lambdas, tiles, sums = pair_terms(bounds, pos, score_parts, worth, qid, inverse, leaf_rows)

    def part(low, high, *tail):
        if per_dev == GROUP:
            return histogram_part(low, high - low, tiles, bins_t, *tail)
        groups = high - low
        wide = histogram_part(low, groups, tiles, bins_t)
        wide = wide.reshape(groups, 3, HIGH, GROUP // per_dev, per_dev, LOW).transpose(0, 3, 1, 4, 2, 5)
        return jnp.concatenate([wide.reshape(groups * GROUP // per_dev * unit, BINS), *tail], axis=0)

    fan = fans[1]
    half = features // GROUP // 2
    quarter = half // len(fan)
    edge = count // 2 // len(fan) * unit
    far_rest = swap(part(half + quarter, 2 * half, sums), fans[0][1])
    near_rest = part(quarter, half)
    far_first = swap(part(half, half + quarter), fans[0][1])
    near_first = part(0, quarter)

    sums = sums + far_rest[edge * (len(fan) - 1):]
    sent = [near_rest[k * edge:(k + 1) * edge] + far_rest[k * edge:(k + 1) * edge] for k in range(len(fan) - 1)]
    kept = near_first + far_first
    for k in range(1, len(rounds)):
        arrived = [swap(jnp.concatenate([block, sums], axis=0), mask) for block, mask in zip(sent, fans[k][1:])]
        if k + 1 < len(rounds):
            sums = add_up([sums] + [block[edge:] for block in arrived])
            merged = add_up([kept] + [block[:edge] for block in arrived])
            edge = edge // len(fans[k + 1])
            kept = merged[:edge]
            sent = [merged[m * edge:(m + 1) * edge] for m in range(1, len(fans[k + 1]))]

    values, step, histograms = finish(per_dev, leaf_rows, kept, sums, arrived)
    return lambdas, values.reshape(LEAVES), step.reshape(docs), histograms.reshape(3, per_dev * BINS)


def solution(mesh):
    in_specs = (
        P(("query", "feat")),
        P("query"),
        P(("query", "feat")),
        P(("query", "feat"), None),
        P("query", None),
        P(),
    )
    out_specs = (P(None, ("query", "feat")), P(), P(("query", "feat")), P(None, ("query", "feat")))
    return jax.shard_map(local, mesh=mesh, in_specs=in_specs, out_specs=out_specs, check_vma=False)
```

```python
import functools

import jax
import jax.numpy as jnp
from jax import lax
from jax.experimental import pallas as pl
from jax.experimental.pallas import tpu as pltpu
from jax.sharding import PartitionSpec as P

BINS = 256
LEAVES = 1024
LANES = 128
GRADES = 4
LOW = 32
HIGH = BINS // LOW
GROUP = 8
CHUNK = 64
MAX_LEN = 1024

lasso_penalty = 1.0
ridge_penalty = 1.0
shrinkage = 0.1

VMEM_LIMIT = 48 * 1024 * 1024
F32 = jnp.float32
BF16 = jnp.bfloat16
NT = (((1,), (1,)), ((), ()))


def iota(shape, axis):
    return lax.broadcasted_iota(jnp.int32, shape, axis)


def vmem():
    return pl.BlockSpec(memory_space=pltpu.VMEM)


def smem():
    return pl.BlockSpec(memory_space=pltpu.SMEM)


def prepare_kernel(feat_count, masks, len_ref, pos_ref, owner_hbm, bins_hbm, lab_hbm, leaf_hbm,
                   bins_t_ref, qid_ref, worth_ref, inv_ref, leaf_ref, bounds_ref, bins_ref, lab_ref, owner_ref, sems):
    queries = len_ref.shape[1]
    rows = lab_ref.shape[0]
    own = inv_ref.shape[0]
    features = bins_ref.shape[1]
    place = pos_ref[0]
    copies = [pltpu.make_async_copy(source, target, sems.at[k]) for k, (source, target) in enumerate(
        ((lab_hbm, lab_ref), (owner_hbm, owner_ref), (bins_hbm, bins_ref), (leaf_hbm, leaf_ref)))]
    for copy in copies:
        copy.start()

    spot = iota((rows, LANES), 0) * LANES + iota((rows, LANES), 1)
    qid = jnp.zeros((rows, LANES), jnp.int32)
    begin = jnp.zeros((queries, LANES), jnp.int32)
    finish = jnp.zeros((queries, LANES), jnp.int32)
    which = iota((queries, LANES), 0)
    start = jnp.int32(0)
    for q in range(queries):
        end = start + len_ref[0, q]
        qid = qid + jnp.where(spot >= end, 1, 0)
        begin = jnp.where(which == q, start, begin)
        finish = jnp.where(which == q, end, finish)

        def set_low(r, carry, start=start):
            bounds_ref[0, r] = start
            return carry

        def set_high(r, carry, end=end):
            bounds_ref[1, r] = end
            return carry

        lax.fori_loop((start + LANES - 1) // LANES, (end + LANES - 1) // LANES, set_low, 0)
        lax.fori_loop(start // LANES, end // LANES, set_high, 0)
        start = end
    qid_ref[...] = qid

    copies[0].wait()
    worth_ref[...] = jnp.left_shift(1, lab_ref[...]).astype(F32)
    counts = [jnp.zeros((queries, LANES), F32) for _ in range(GRADES)]
    lane = iota((queries, LANES), 1)
    for r in range(rows):
        at = lane + r * LANES
        inside = (at >= begin) & (at < finish)
        grade = jnp.where(inside, jnp.broadcast_to(lab_ref[r:r + 1, :], (queries, LANES)), 0)
        for g in range(GRADES):
            counts[g] = counts[g] + jnp.where(grade > g, 1.0, 0.0)
    position = iota((queries, MAX_LEN), 1).astype(F32)
    gain = jnp.zeros((queries, MAX_LEN), F32)
    for g in range(GRADES):
        held = jnp.sum(counts[g], axis=1, keepdims=True)
        gain = gain + jnp.where(position < held, float(2 ** g), 0.0)
    level = 1.0 / jnp.log2(2.0 + position[0:1, :])
    ideal = jnp.sum(gain * level, axis=1, keepdims=True)
    usable = ideal > 0.5
    inverse = jnp.where(usable, 1.0 / jnp.where(usable, ideal, 1.0), 0.0)
    first = place % feat_count * own
    for t in range(own):
        at = lane + (first + t) * LANES
        inside = (at >= begin) & (at < finish)
        inv_ref[t:t + 1, :] = jnp.sum(jnp.where(inside, inverse, 0.0), axis=0, keepdims=True)

    copies[1].wait()
    per_dev = features >> len(masks)
    owner = jnp.concatenate([owner_ref[k:k + 1, :] for k in range(features // LANES)], axis=1)
    square = (features, features)
    down, across = iota(square, 0), iota(square, 1)
    index = down // per_dev
    target = jnp.zeros(square, jnp.int32)
    for b, mask in enumerate(masks):
        target = target + ((index >> b) & 1) * mask
    target = (target ^ (place - place % feat_count)) * per_dev + down % per_dev
    pick = jnp.where(target == across, 1.0, 0.0).astype(BF16)
    holds = jnp.where(jnp.broadcast_to(owner, square) == down, 1.0, 0.0).astype(BF16)
    perm = lax.dot_general(pick, holds, NT, preferred_element_type=F32).astype(BF16)
    copies[2].wait()
    bins = bins_ref[...].astype(F32).astype(BF16)
    bins_t_ref[...] = lax.dot_general(perm, bins, NT, preferred_element_type=F32)
    copies[3].wait()


def prepare(feat_count, masks, lengths, pos, owner, bins, labels, leaves):
    rows = labels.shape[0]
    own = leaves.shape[0]
    docs, features = bins.shape
    hbm = pl.BlockSpec(memory_space=pltpu.HBM)
    return pl.pallas_call(
        functools.partial(prepare_kernel, feat_count, masks),
        out_shape=(
            jax.ShapeDtypeStruct((features, docs), F32),
            jax.ShapeDtypeStruct((rows, LANES), jnp.int32),
            jax.ShapeDtypeStruct((rows, LANES), F32),
            jax.ShapeDtypeStruct((own, LANES), F32),
            jax.ShapeDtypeStruct((own, LANES), jnp.int32),
            jax.ShapeDtypeStruct((2, rows), jnp.int32),
        ),
        in_specs=[smem(), smem(), hbm, hbm, hbm, hbm],
        out_specs=(vmem(), vmem(), vmem(), vmem(), vmem(), smem()),
        scratch_shapes=[pltpu.VMEM((docs, features), jnp.int32), pltpu.VMEM((rows, LANES), jnp.int32),
                        pltpu.VMEM((features // LANES, LANES), jnp.int32), pltpu.SemaphoreType.DMA((4,))],
        compiler_params=pltpu.CompilerParams(vmem_limit_bytes=VMEM_LIMIT),
        cost_estimate=pl.CostEstimate(flops=200_000_000, bytes_accessed=3_000_000, transcendentals=20_000),
        name="prepare",
    )(lengths, pos, owner, bins, labels, leaves)


def split_terms(value, terms):
    parts = []
    rest = value
    for _ in range(terms):
        part = rest.astype(BF16)
        parts.append(part)
        rest = rest - part.astype(F32)
    return parts


def widen(ref, source):
    turned = jnp.transpose(source)
    for r in range(source.shape[0]):
        ref[r * LANES:(r + 1) * LANES, :] = jnp.broadcast_to(turned[:, r:r + 1], (LANES, LANES))


def pairs_kernel(parts, bounds_ref, pos_ref, s_row, worth_ref, qid_ref, inv_ref, leaf_ref, lam_ref, tile_ref, sums_ref,
                 a_row, d_row, s_turn, q_turn, s_col, q_col, a_own, w_own, d_own, push_own, bend_own):
    rows = worth_ref.shape[0]
    own = inv_ref.shape[0]
    docs = own * LANES
    me = pos_ref[0] % parts
    a_row[...] = jnp.exp(s_row[...])
    d_row[...] = jnp.zeros((rows, LANES), F32)
    first = pl.multiple_of(me * own, own)
    window_low = bounds_ref[0, first] // LANES
    window_high = (bounds_ref[1, first + own - 1] + LANES - 1) // LANES
    s_turn[...] = jnp.transpose(s_row[...])
    q_turn[...] = jnp.transpose(qid_ref[...])
    for r in range(rows):
        @pl.when((r >= window_low) & (r < window_high))
        def _(r=r):
            at = slice(r * LANES, (r + 1) * LANES)
            s_col[at, :] = jnp.broadcast_to(s_turn[:, r:r + 1], (LANES, LANES))
            q_col[at, :] = jnp.broadcast_to(q_turn[:, r:r + 1], (LANES, LANES))
    widen(a_own, a_row[pl.ds(first, own), :])
    widen(w_own, worth_ref[pl.ds(first, own), :])

    def row_of(ref, r):
        return jnp.broadcast_to(ref[pl.ds(r, 1), :], (8, LANES))

    def rank_group(r, carry):
        score = row_of(s_row, r)
        query = row_of(qid_ref, r)

        def sweep(ahead):
            def step(c, acc):
                base = pl.multiple_of(c * CHUNK, CHUNK)
                acc = list(acc)
                for u in range(CHUNK // 8):
                    other = s_col[pl.ds(base + 8 * u, 8), :]
                    above = (other >= score) if ahead else (other > score)
                    hit = above & (q_col[pl.ds(base + 8 * u, 8), :] == query)
                    acc[u % 4] = acc[u % 4] + jnp.where(hit, 1.0, 0.0)
                return tuple(acc)
            return step

        acc = tuple(jnp.zeros((8, LANES), F32) for _ in range(4))
        per = LANES // CHUNK
        low = jnp.maximum(bounds_ref[0, r] // CHUNK, window_low * per)
        high = jnp.minimum((bounds_ref[1, r] + CHUNK - 1) // CHUNK, window_high * per)
        acc = lax.fori_loop(low, r * per, sweep(True), acc)
        acc = list(lax.fori_loop((r + 1) * per, high, sweep(False), acc))
        base = pl.multiple_of(r * LANES, LANES)
        for u in range(LANES // 8):
            other = s_col[pl.ds(base + 8 * u, 8), :]
            earlier = iota((8, LANES), 0) + 8 * u < iota((8, LANES), 1)
            above = (other > score) | ((other == score) & earlier)
            hit = above & (q_col[pl.ds(base + 8 * u, 8), :] == query)
            acc[u % 4] = acc[u % 4] + jnp.where(hit, 1.0, 0.0)
        total = (acc[0] + acc[1]) + (acc[2] + acc[3])
        d_row[pl.ds(r, 1), :] = jnp.sum(total, axis=0, keepdims=True)
        return carry

    lax.fori_loop(window_low, window_high, rank_group, 0)
    d_row[...] = 1.0 / jnp.log2(2.0 + d_row[...])
    widen(d_own, d_row[pl.ds(first, own), :])

    def pair_block(b, carry):
        base = pl.multiple_of(b * CHUNK, CHUNK)
        r = first + b // (LANES // CHUNK)
        count = CHUNK // 8
        queries = pl.multiple_of(first * LANES + base, CHUNK)

        def step(c, acc):
            acc = list(acc)
            a_j = row_of(a_row, c)
            w_j = row_of(worth_ref, c)
            d_j = row_of(d_row, c)
            query = row_of(qid_ref, c)
            for u in range(count):
                at = pl.ds(base + 8 * u, 8)
                a_i = a_own[at, :]
                total = a_i + a_j
                rough = pl.reciprocal(total, approx=True)
                recip = rough * (2.0 - total * rough)
                gap = jnp.abs(d_own[at, :] - d_j)
                lift = w_own[at, :] - w_j
                weight = jnp.where(q_col[pl.ds(queries + 8 * u, 8), :] == query, gap * recip, 0.0) * lift
                acc[u] = acc[u] + weight * jnp.where(lift > 0.0, a_j, a_i)
                acc[count + u] = acc[count + u] + jnp.abs(weight) * (recip * a_j)
            return tuple(acc)

        acc = tuple(jnp.zeros((8, LANES), F32) for _ in range(2 * count))
        acc = lax.fori_loop(bounds_ref[0, r] // LANES, (bounds_ref[1, r] + LANES - 1) // LANES, step, acc)
        for u in range(count):
            push_own[pl.ds(base + 8 * u, 8), :] = acc[u]
            bend_own[pl.ds(base + 8 * u, 8), :] = acc[count + u]
        return carry

    lax.fori_loop(0, docs // CHUNK, pair_block, 0)
    for t in range(own):
        at = slice(t * LANES, (t + 1) * LANES)
        inverse = inv_ref[t:t + 1, :]
        lam_ref[0:1, at] = -inverse * jnp.sum(jnp.transpose(push_own[at, :]), axis=0, keepdims=True)
        lam_ref[1:2, at] = (inverse * a_row[pl.ds(first + t, 1), :]
                            * jnp.sum(jnp.transpose(bend_own[at, :]), axis=0, keepdims=True))

    leaf = jnp.concatenate([leaf_ref[t:t + 1, :] for t in range(own)], axis=1)
    highs = LEAVES // LANES
    top = jnp.broadcast_to(leaf // LANES, (highs, docs)) == iota((highs, docs), 0)
    spots = jnp.where(jnp.broadcast_to(leaf % LANES, (LANES, docs)) == iota((LANES, docs), 0), 1.0, 0.0).astype(BF16)
    pieces, tiles = [], []
    for c in range(2):
        for k, part in enumerate(split_terms(lam_ref[c:c + 1, :], 3)):
            wide = jnp.broadcast_to(part.astype(F32), (highs, docs))
            pieces.append(jnp.where(top, wide, 0.0))
            if k < 2:
                tiles.append(wide)
    tile_ref[...] = jnp.concatenate(tiles, axis=0).astype(BF16)
    stacked = jnp.concatenate(pieces, axis=0).astype(BF16)
    sums = lax.dot_general(stacked, spots, NT, preferred_element_type=F32)
    for c in range(2):
        base = c * 3 * highs
        sums_ref[:, c * LANES:(c + 1) * LANES] = (
            sums[base:base + highs] + (sums[base + highs:base + 2 * highs] + sums[base + 2 * highs:base + 3 * highs])
        )


def pair_terms(parts, bounds, pos, scores, worth, qid, inverse, leaves):
    rows = worth.shape[0]
    own = inverse.shape[0]
    docs = own * LANES
    highs = LEAVES // LANES
    row = pltpu.VMEM((rows, LANES), F32)
    mine = pltpu.VMEM((docs, LANES), F32)
    return pl.pallas_call(
        functools.partial(pairs_kernel, parts),
        out_shape=(
            jax.ShapeDtypeStruct((2, docs), F32),
            jax.ShapeDtypeStruct((4 * HIGH, docs), BF16),
            jax.ShapeDtypeStruct((highs, 2 * LANES), F32),
        ),
        in_specs=[smem(), smem()] + [vmem()] * 5,
        out_specs=(vmem(), vmem(), vmem()),
        scratch_shapes=[row, row, pltpu.VMEM((LANES, rows), F32), pltpu.VMEM((LANES, rows), jnp.int32),
                        pltpu.VMEM((rows * LANES, LANES), F32), pltpu.VMEM((rows * LANES, LANES), jnp.int32),
                        mine, mine, mine, mine, mine],
        compiler_params=pltpu.CompilerParams(vmem_limit_bytes=VMEM_LIMIT),
        cost_estimate=pl.CostEstimate(flops=40_000_000, bytes_accessed=200_000, transcendentals=2_000_000),
        name="pair_terms",
    )(bounds, pos, scores, worth, qid, inverse, leaves)


def histogram_kernel(first, groups, tile_ref, bins_ref, *refs):
    out_ref = refs[-1]
    docs = tile_ref.shape[1]
    depth = 256
    rows = 16
    row = iota((rows, depth), 0)
    low_level = [(row + rows * k).astype(F32).astype(BF16) for k in range(LOW // rows)]
    high_level = (row % HIGH).astype(F32).astype(BF16)
    upper = row < HIGH
    zero = jnp.zeros((rows, depth), BF16)
    one = jnp.ones((rows, depth), BF16)
    lane_owner = iota((1, GROUP * LOW), 1) // LOW

    def one_group(g, carry):
        base = pl.multiple_of((first + g) * GROUP, GROUP)
        acc = None
        for k in range(docs // depth):
            span = slice(k * depth, (k + 1) * depth)
            code = bins_ref[pl.ds(base, GROUP), span]
            high = jnp.floor(code * (1.0 / LOW))
            low = code - high * LOW
            left, right, count = [], [], []
            wide = []
            for f in range(GROUP):
                high_f = jnp.broadcast_to(high[f:f + 1, :], (rows, depth))
                low_f = jnp.broadcast_to(low[f:f + 1, :], (rows, depth)).astype(BF16)
                wide.append(high_f)
                match = high_f.astype(BF16) == high_level
                for c in range(2):
                    left.append(jnp.where(match, tile_ref[c * rows:(c + 1) * rows, span], zero))
                for level in low_level:
                    right.append(jnp.where(low_f == level, one, zero))
            for f in range(0, GROUP, 2):
                both = jnp.where(upper, wide[f], wide[f + 1]).astype(BF16)
                count.append(jnp.where(both == high_level, one, zero))
            part = lax.dot_general(
                jnp.concatenate(left + count, axis=0), jnp.concatenate(right, axis=0), NT,
                preferred_element_type=F32,
            )
            acc = part if acc is None else acc + part
        stats = jnp.zeros((2 * rows, GROUP * LOW), F32)
        counts = jnp.zeros((HIGH, GROUP * LOW), F32)
        for f in range(GROUP):
            mine = lane_owner == f
            stats = jnp.where(mine, acc[f * 2 * rows:(f + 1) * 2 * rows], stats)
            at = GROUP * 2 * rows + f * HIGH
            counts = jnp.where(mine, acc[at:at + HIGH], counts)
        out_ref[pl.ds(pl.multiple_of(g * 3 * HIGH, 3 * HIGH), 3 * HIGH), :] = jnp.concatenate(
            [stats[0:HIGH] + stats[HIGH:2 * HIGH], stats[2 * HIGH:3 * HIGH] + stats[3 * HIGH:4 * HIGH], counts], axis=0)
        return carry

    if len(refs) > 1:
        out_ref[groups * 3 * HIGH:, :] = refs[0][...]
    lax.fori_loop(0, groups, one_group, 0, unroll=2)


def histogram_part(first, groups, tiles, bins_t, *tail):
    rows = groups * 3 * HIGH + sum(piece.shape[0] for piece in tail)
    return pl.pallas_call(
        functools.partial(histogram_kernel, first, groups),
        out_shape=jax.ShapeDtypeStruct((rows, GROUP * LOW), F32),
        in_specs=[vmem()] * (2 + len(tail)),
        out_specs=vmem(),
        compiler_params=pltpu.CompilerParams(vmem_limit_bytes=VMEM_LIMIT),
        cost_estimate=pl.CostEstimate(flops=groups * 330_000_000, bytes_accessed=groups * 60_000, transcendentals=0),
        name="histogram_part",
    )(tiles, bins_t, *tail)


def finish_kernel(per_dev, leaf_ref, arrived_ref, value_ref, step_ref, hist_ref):
    highs = LEAVES // LANES
    unit = arrived_ref.shape[1] - highs
    parts = range(arrived_ref.shape[0])
    totals = add_up([arrived_ref[k, unit:, :] for k in parts])
    grad, curv = totals[:, :LANES], totals[:, LANES:]
    shrunk = jnp.maximum(jnp.abs(grad) - lasso_penalty, 0.0)
    values = jnp.where(grad > 0.0, -shrunk, shrunk) / (curv + ridge_penalty)
    value_ref[...] = values
    leaf = leaf_ref[...]
    top, spot = leaf // LANES, leaf % LANES
    step = jnp.zeros(leaf.shape, F32)
    for h in range(highs):
        row = jnp.broadcast_to(values[h:h + 1, :], leaf.shape)
        step = jnp.where(top == h, jnp.take_along_axis(row, spot, axis=1), step)
    step_ref[...] = shrinkage * step
    hist = add_up([arrived_ref[k, :unit, :] for k in parts])
    if per_dev == GROUP:
        for c in range(3):
            for f in range(GROUP):
                line = [hist[c * HIGH + h:c * HIGH + h + 1, f * LOW:(f + 1) * LOW] for h in range(HIGH)]
                hist_ref[c:c + 1, f * BINS:(f + 1) * BINS] = jnp.concatenate(line, axis=1)
    else:
        hist_ref[...] = hist


def finish(per_dev, leaves, arrived):
    out = (3, per_dev * BINS) if per_dev == GROUP else (3 * per_dev, BINS)
    return pl.pallas_call(
        functools.partial(finish_kernel, per_dev),
        out_shape=(
            jax.ShapeDtypeStruct((LEAVES // LANES, LANES), F32),
            jax.ShapeDtypeStruct(leaves.shape, F32),
            jax.ShapeDtypeStruct(out, F32),
        ),
        in_specs=[vmem()] * 2,
        out_specs=(vmem(), vmem(), vmem()),
        compiler_params=pltpu.CompilerParams(vmem_limit_bytes=VMEM_LIMIT),
        name="finish",
    )(leaves, arrived)


def add_up(parts):
    while len(parts) > 1:
        parts = [parts[k] + parts[k + 1] for k in range(0, len(parts), 2)]
    return parts[0]


def exchange_rounds(query_count, feat_count):
    feat_bits = [1 << b for b in range(feat_count.bit_length() - 1)]
    query_bits = [feat_count << b for b in range(query_count.bit_length() - 1)]
    rounds = [query_bits[:1]]
    rounds += [query_bits[1:][k:k + 2] for k in range(0, len(query_bits) - 1, 2)]
    return rounds, feat_bits


def local(scores, labels, leaves, bins, lengths, owner):
    query_count = lax.axis_size("query")
    feat_count = lax.axis_size("feat")
    count = query_count * feat_count
    place = lax.axis_index("query").astype(jnp.int32) * feat_count + lax.axis_index("feat").astype(jnp.int32)
    docs = scores.shape[0]
    own = docs // LANES
    features = owner.shape[0]
    per_dev = features // count
    unit = 3 * per_dev
    axes = ("query", "feat")
    rounds, feat_bits = exchange_rounds(query_count, feat_count)
    bit_masks = feat_bits + [bit for bits in reversed(rounds) for bit in bits]
    fans = [[0, bits[0]] if len(bits) == 1 else [0, bits[0], bits[1], bits[0] | bits[1]] for bits in rounds]

    def swap(value, mask):
        return lax.ppermute(value, axes, [(p, p ^ mask) for p in range(count)])

    own_scores = scores.reshape(own, LANES)
    own_scores = jnp.broadcast_to(own_scores[None], (feat_count, own, LANES))
    gathered = lax.all_to_all(own_scores, "feat", 0, 0).reshape(feat_count * own, LANES)

    pos = place.reshape(1)
    bins_t, qid, worth, inverse, leaf_rows, bounds = prepare(
        feat_count, bit_masks, lengths, pos, owner.reshape(-1, LANES), bins, labels.reshape(-1, LANES),
        leaves.reshape(own, LANES))
    lambdas, tiles, sums = pair_terms(feat_count, bounds, pos, gathered, worth, qid, inverse, leaf_rows)

    def part(low, high, *tail):
        if per_dev == GROUP:
            return histogram_part(low, high - low, tiles, bins_t, *tail)
        groups = high - low
        wide = histogram_part(low, groups, tiles, bins_t)
        wide = wide.reshape(groups, 3, HIGH, GROUP // per_dev, per_dev, LOW).transpose(0, 3, 1, 4, 2, 5)
        return jnp.concatenate([wide.reshape(groups * GROUP // per_dev * unit, BINS), *tail], axis=0)

    fan = fans[1]
    half = features // GROUP // 2
    quarter = half // len(fan)
    edge = count // 2 // len(fan) * unit
    far_rest = swap(part(half + quarter, 2 * half, sums), fans[0][1])
    near_rest = part(quarter, half)
    far_first = swap(part(half, half + quarter), fans[0][1])
    near_first = part(0, quarter)

    sums = sums + far_rest[edge * (len(fan) - 1):]
    sent = [near_rest[k * edge:(k + 1) * edge] + far_rest[k * edge:(k + 1) * edge] for k in range(len(fan) - 1)]
    kept = near_first + far_first
    for k in range(1, len(rounds)):
        arrived = [swap(jnp.concatenate([block, sums], axis=0), mask) for block, mask in zip(sent, fans[k][1:])]
        sums = add_up([sums] + [block[edge:] for block in arrived])
        merged = add_up([kept] + [block[:edge] for block in arrived])
        if k + 1 < len(rounds):
            edge = edge // len(fans[k + 1])
            kept = merged[:edge]
            sent = [merged[m * edge:(m + 1) * edge] for m in range(1, len(fans[k + 1]))]
    merged = merged.reshape(feat_count, unit, BINS)
    sums = jnp.broadcast_to(sums[None], (feat_count,) + sums.shape)
    arrived = lax.all_to_all(jnp.concatenate([merged, sums], axis=1), "feat", 0, 0)

    values, step, histograms = finish(per_dev, leaf_rows, arrived)
    return lambdas, values.reshape(LEAVES), step.reshape(docs), histograms.reshape(3, per_dev * BINS)


def solution(mesh):
    in_specs = (
        P(("query", "feat")),
        P("query"),
        P(("query", "feat")),
        P(("query", "feat"), None),
        P("query", None),
        P(),
    )
    out_specs = (P(None, ("query", "feat")), P(), P(("query", "feat")), P(None, ("query", "feat")))
    return jax.shard_map(local, mesh=mesh, in_specs=in_specs, out_specs=out_specs, check_vma=False)
```

```python
import functools

import jax
import jax.numpy as jnp
from jax import lax
from jax.experimental import pallas as pl
from jax.experimental.pallas import tpu as pltpu
from jax.sharding import PartitionSpec as P

BINS = 256
LEAVES = 1024
LANES = 128
GRADES = 4
LOW = 32
HIGH = BINS // LOW
GROUP = 8
CHUNK = 64
MAX_LEN = 1024

lasso_penalty = 1.0
ridge_penalty = 1.0
shrinkage = 0.1

VMEM_LIMIT = 48 * 1024 * 1024
F32 = jnp.float32
BF16 = jnp.bfloat16
NT = (((1,), (1,)), ((), ()))


def iota(shape, axis):
    return lax.broadcasted_iota(jnp.int32, shape, axis)


def vmem():
    return pl.BlockSpec(memory_space=pltpu.VMEM)


def smem():
    return pl.BlockSpec(memory_space=pltpu.SMEM)


def label_kernel(feat_count, len_ref, pos_ref, lab_ref, qid_ref, worth_ref, inv_ref, bounds_ref):
    queries = len_ref.shape[1]
    rows = lab_ref.shape[0]
    own = inv_ref.shape[0]
    spot = iota((rows, LANES), 0) * LANES + iota((rows, LANES), 1)
    qid = jnp.zeros((rows, LANES), jnp.int32)
    begin = jnp.zeros((queries, LANES), jnp.int32)
    finish = jnp.zeros((queries, LANES), jnp.int32)
    which = iota((queries, LANES), 0)
    start = jnp.int32(0)
    for q in range(queries):
        end = start + len_ref[0, q]
        qid = qid + jnp.where(spot >= end, 1, 0)
        begin = jnp.where(which == q, start, begin)
        finish = jnp.where(which == q, end, finish)

        def set_low(r, carry, start=start):
            bounds_ref[0, r] = start
            return carry

        def set_high(r, carry, end=end):
            bounds_ref[1, r] = end
            return carry

        lax.fori_loop((start + LANES - 1) // LANES, (end + LANES - 1) // LANES, set_low, 0)
        lax.fori_loop(start // LANES, end // LANES, set_high, 0)
        start = end
    qid_ref[...] = qid
    worth_ref[...] = jnp.left_shift(1, lab_ref[...]).astype(F32)

    counts = [jnp.zeros((queries, LANES), F32) for _ in range(GRADES)]
    lane = iota((queries, LANES), 1)
    for r in range(rows):
        at = lane + r * LANES
        inside = (at >= begin) & (at < finish)
        grade = jnp.where(inside, jnp.broadcast_to(lab_ref[r:r + 1, :], (queries, LANES)), 0)
        for g in range(GRADES):
            counts[g] = counts[g] + jnp.where(grade > g, 1.0, 0.0)
    position = iota((queries, MAX_LEN), 1).astype(F32)
    gain = jnp.zeros((queries, MAX_LEN), F32)
    for g in range(GRADES):
        held = jnp.sum(counts[g], axis=1, keepdims=True)
        gain = gain + jnp.where(position < held, float(2 ** g), 0.0)
    level = 1.0 / jnp.log2(2.0 + position[0:1, :])
    ideal = jnp.sum(gain * level, axis=1, keepdims=True)
    usable = ideal > 0.5
    inverse = jnp.where(usable, 1.0 / jnp.where(usable, ideal, 1.0), 0.0)
    first = pos_ref[0] % feat_count * own
    for t in range(own):
        at = lane + (first + t) * LANES
        inside = (at >= begin) & (at < finish)
        inv_ref[t:t + 1, :] = jnp.sum(jnp.where(inside, inverse, 0.0), axis=0, keepdims=True)


def label_terms(feat_count, own, lengths, pos, labels):
    rows = labels.shape[0]
    return pl.pallas_call(
        functools.partial(label_kernel, feat_count),
        out_shape=(
            jax.ShapeDtypeStruct((rows, LANES), jnp.int32),
            jax.ShapeDtypeStruct((rows, LANES), F32),
            jax.ShapeDtypeStruct((own, LANES), F32),
            jax.ShapeDtypeStruct((2, rows), jnp.int32),
        ),
        in_specs=[smem(), smem(), vmem()],
        out_specs=(vmem(), vmem(), vmem(), smem()),
        compiler_params=pltpu.CompilerParams(vmem_limit_bytes=VMEM_LIMIT),
        cost_estimate=pl.CostEstimate(flops=10_000_000, bytes_accessed=3_000_000, transcendentals=20_000),
        name="label_terms",
    )(lengths, pos, labels)


def order_kernel(masks, pos_ref, owner_ref, bins_ref, out_ref):
    features = bins_ref.shape[1]
    per_dev = features >> len(masks)
    owner = jnp.concatenate([owner_ref[k:k + 1, :] for k in range(features // LANES)], axis=1)
    square = (features, features)
    down, across = iota(square, 0), iota(square, 1)
    index = down // per_dev
    target = jnp.zeros(square, jnp.int32)
    for b, mask in enumerate(masks):
        target = target + ((index >> b) & 1) * mask
    target = (target ^ pos_ref[0]) * per_dev + down % per_dev
    pick = jnp.where(target == across, 1.0, 0.0).astype(BF16)
    holds = jnp.where(jnp.broadcast_to(owner, square) == down, 1.0, 0.0).astype(BF16)
    perm = lax.dot_general(pick, holds, NT, preferred_element_type=F32).astype(BF16)
    bins = bins_ref[...].astype(F32).astype(BF16)
    out_ref[...] = lax.dot_general(perm, bins, NT, preferred_element_type=F32)


def order_bins(masks, pos, owner, bins):
    docs, features = bins.shape
    return pl.pallas_call(
        functools.partial(order_kernel, masks),
        out_shape=jax.ShapeDtypeStruct((features, docs), F32),
        in_specs=[smem(), vmem(), vmem()],
        out_specs=vmem(),
        compiler_params=pltpu.CompilerParams(vmem_limit_bytes=VMEM_LIMIT),
        cost_estimate=pl.CostEstimate(flops=200_000_000, bytes_accessed=3_000_000, transcendentals=0),
        name="order_bins",
    )(pos, owner, bins)


def split_terms(value, terms):
    parts = []
    rest = value
    for _ in range(terms):
        part = rest.astype(BF16)
        parts.append(part)
        rest = rest - part.astype(F32)
    return parts


def widen(ref, source):
    turned = jnp.transpose(source)
    for r in range(source.shape[0]):
        ref[r * LANES:(r + 1) * LANES, :] = jnp.broadcast_to(turned[:, r:r + 1], (LANES, LANES))


def pairs_kernel(parts, bounds_ref, pos_ref, *refs):
    score_refs = refs[:parts]
    (worth_ref, qid_ref, inv_ref, leaf_ref, lam_ref, tile_ref, sums_ref,
     s_row, a_row, d_row, s_turn, q_turn, s_col, q_col, a_own, w_own, d_own, push_own, bend_own) = refs[parts:]
    rows = worth_ref.shape[0]
    own = inv_ref.shape[0]
    docs = own * LANES
    me = pos_ref[0] % (rows // own)
    k = 0
    for ref in score_refs:
        for piece in range(ref.shape[0] // own):
            s_row[pl.ds(pl.multiple_of((me ^ k) * own, own), own), :] = ref[piece * own:(piece + 1) * own, :]
            k += 1
    a_row[...] = jnp.exp(s_row[...])
    d_row[...] = jnp.zeros((rows, LANES), F32)
    first = pl.multiple_of(me * own, own)
    window_low = bounds_ref[0, first] // LANES
    window_high = (bounds_ref[1, first + own - 1] + LANES - 1) // LANES
    s_turn[...] = jnp.transpose(s_row[...])
    q_turn[...] = jnp.transpose(qid_ref[...])
    for r in range(rows):
        @pl.when((r >= window_low) & (r < window_high))
        def _(r=r):
            at = slice(r * LANES, (r + 1) * LANES)
            s_col[at, :] = jnp.broadcast_to(s_turn[:, r:r + 1], (LANES, LANES))
            q_col[at, :] = jnp.broadcast_to(q_turn[:, r:r + 1], (LANES, LANES))
    widen(a_own, a_row[pl.ds(first, own), :])
    widen(w_own, worth_ref[pl.ds(first, own), :])

    def row_of(ref, r):
        return jnp.broadcast_to(ref[pl.ds(r, 1), :], (8, LANES))

    def rank_group(r, carry):
        score = row_of(s_row, r)
        query = row_of(qid_ref, r)

        def sweep(ahead):
            def step(c, acc):
                base = pl.multiple_of(c * CHUNK, CHUNK)
                acc = list(acc)
                for u in range(CHUNK // 8):
                    other = s_col[pl.ds(base + 8 * u, 8), :]
                    above = (other >= score) if ahead else (other > score)
                    hit = above & (q_col[pl.ds(base + 8 * u, 8), :] == query)
                    acc[u % 4] = acc[u % 4] + jnp.where(hit, 1.0, 0.0)
                return tuple(acc)
            return step

        acc = tuple(jnp.zeros((8, LANES), F32) for _ in range(4))
        per = LANES // CHUNK
        low = jnp.maximum(bounds_ref[0, r] // CHUNK, window_low * per)
        high = jnp.minimum((bounds_ref[1, r] + CHUNK - 1) // CHUNK, window_high * per)
        acc = lax.fori_loop(low, r * per, sweep(True), acc)
        acc = list(lax.fori_loop((r + 1) * per, high, sweep(False), acc))
        base = pl.multiple_of(r * LANES, LANES)
        for u in range(LANES // 8):
            other = s_col[pl.ds(base + 8 * u, 8), :]
            earlier = iota((8, LANES), 0) + 8 * u < iota((8, LANES), 1)
            above = (other > score) | ((other == score) & earlier)
            hit = above & (q_col[pl.ds(base + 8 * u, 8), :] == query)
            acc[u % 4] = acc[u % 4] + jnp.where(hit, 1.0, 0.0)
        total = (acc[0] + acc[1]) + (acc[2] + acc[3])
        d_row[pl.ds(r, 1), :] = jnp.sum(total, axis=0, keepdims=True)
        return carry

    lax.fori_loop(window_low, window_high, rank_group, 0)
    d_row[...] = 1.0 / jnp.log2(2.0 + d_row[...])
    widen(d_own, d_row[pl.ds(first, own), :])

    def pair_block(b, carry):
        base = pl.multiple_of(b * CHUNK, CHUNK)
        r = first + b // (LANES // CHUNK)
        count = CHUNK // 8
        queries = pl.multiple_of(first * LANES + base, CHUNK)

        def step(c, acc):
            acc = list(acc)
            a_j = row_of(a_row, c)
            w_j = row_of(worth_ref, c)
            d_j = row_of(d_row, c)
            query = row_of(qid_ref, c)
            for u in range(count):
                at = pl.ds(base + 8 * u, 8)
                a_i = a_own[at, :]
                total = a_i + a_j
                rough = pl.reciprocal(total, approx=True)
                recip = rough * (2.0 - total * rough)
                gap = jnp.abs(d_own[at, :] - d_j)
                lift = w_own[at, :] - w_j
                weight = jnp.where(q_col[pl.ds(queries + 8 * u, 8), :] == query, gap * recip, 0.0) * lift
                acc[u] = acc[u] + weight * jnp.where(lift > 0.0, a_j, a_i)
                acc[count + u] = acc[count + u] + jnp.abs(weight) * (recip * a_j)
            return tuple(acc)

        acc = tuple(jnp.zeros((8, LANES), F32) for _ in range(2 * count))
        acc = lax.fori_loop(bounds_ref[0, r] // LANES, (bounds_ref[1, r] + LANES - 1) // LANES, step, acc)
        for u in range(count):
            push_own[pl.ds(base + 8 * u, 8), :] = acc[u]
            bend_own[pl.ds(base + 8 * u, 8), :] = acc[count + u]
        return carry

    lax.fori_loop(0, docs // CHUNK, pair_block, 0)
    for t in range(own):
        at = slice(t * LANES, (t + 1) * LANES)
        inverse = inv_ref[t:t + 1, :]
        lam_ref[0:1, at] = -inverse * jnp.sum(jnp.transpose(push_own[at, :]), axis=0, keepdims=True)
        lam_ref[1:2, at] = (inverse * a_row[pl.ds(first + t, 1), :]
                            * jnp.sum(jnp.transpose(bend_own[at, :]), axis=0, keepdims=True))

    leaf = jnp.concatenate([leaf_ref[t:t + 1, :] for t in range(own)], axis=1)
    highs = LEAVES // LANES
    top = jnp.broadcast_to(leaf // LANES, (highs, docs)) == iota((highs, docs), 0)
    spots = jnp.where(jnp.broadcast_to(leaf % LANES, (LANES, docs)) == iota((LANES, docs), 0), 1.0, 0.0).astype(BF16)
    pieces, tiles = [], []
    for c in range(2):
        for k, part in enumerate(split_terms(lam_ref[c:c + 1, :], 3)):
            wide = jnp.broadcast_to(part.astype(F32), (highs, docs))
            pieces.append(jnp.where(top, wide, 0.0))
            if k < 2:
                tiles.append(wide)
    tile_ref[...] = jnp.concatenate(tiles, axis=0).astype(BF16)
    stacked = jnp.concatenate(pieces, axis=0).astype(BF16)
    sums = lax.dot_general(stacked, spots, NT, preferred_element_type=F32)
    for c in range(2):
        base = c * 3 * highs
        sums_ref[:, c * LANES:(c + 1) * LANES] = (
            sums[base:base + highs] + (sums[base + highs:base + 2 * highs] + sums[base + 2 * highs:base + 3 * highs])
        )


def pair_terms(bounds, pos, scores, worth, qid, inverse, leaves):
    rows = worth.shape[0]
    own = inverse.shape[0]
    docs = own * LANES
    highs = LEAVES // LANES
    row = pltpu.VMEM((rows, LANES), F32)
    mine = pltpu.VMEM((docs, LANES), F32)
    return pl.pallas_call(
        functools.partial(pairs_kernel, len(scores)),
        out_shape=(
            jax.ShapeDtypeStruct((2, docs), F32),
            jax.ShapeDtypeStruct((4 * HIGH, docs), BF16),
            jax.ShapeDtypeStruct((highs, 2 * LANES), F32),
        ),
        in_specs=[smem(), smem()] + [vmem()] * (len(scores) + 4),
        out_specs=(vmem(), vmem(), vmem()),
        scratch_shapes=[row, row, row, pltpu.VMEM((LANES, rows), F32), pltpu.VMEM((LANES, rows), jnp.int32),
                        pltpu.VMEM((rows * LANES, LANES), F32), pltpu.VMEM((rows * LANES, LANES), jnp.int32),
                        mine, mine, mine, mine, mine],
        compiler_params=pltpu.CompilerParams(vmem_limit_bytes=VMEM_LIMIT),
        cost_estimate=pl.CostEstimate(flops=40_000_000, bytes_accessed=200_000, transcendentals=2_000_000),
        name="pair_terms",
    )(bounds, pos, *scores, worth, qid, inverse, leaves)


def histogram_kernel(first, groups, tile_ref, bins_ref, *refs):
    out_ref = refs[-1]
    docs = tile_ref.shape[1]
    depth = 256
    rows = 16
    row = iota((rows, depth), 0)
    low_level = [(row + rows * k).astype(F32).astype(BF16) for k in range(LOW // rows)]
    high_level = (row % HIGH).astype(F32).astype(BF16)
    upper = row < HIGH
    zero = jnp.zeros((rows, depth), BF16)
    one = jnp.ones((rows, depth), BF16)
    lane_owner = iota((1, GROUP * LOW), 1) // LOW

    def one_group(g, carry):
        base = pl.multiple_of((first + g) * GROUP, GROUP)
        acc = None
        for k in range(docs // depth):
            span = slice(k * depth, (k + 1) * depth)
            code = bins_ref[pl.ds(base, GROUP), span]
            high = jnp.floor(code * (1.0 / LOW))
            low = code - high * LOW
            left, right, count = [], [], []
            wide = []
            for f in range(GROUP):
                high_f = jnp.broadcast_to(high[f:f + 1, :], (rows, depth))
                low_f = jnp.broadcast_to(low[f:f + 1, :], (rows, depth)).astype(BF16)
                wide.append(high_f)
                match = high_f.astype(BF16) == high_level
                for c in range(2):
                    left.append(jnp.where(match, tile_ref[c * rows:(c + 1) * rows, span], zero))
                for level in low_level:
                    right.append(jnp.where(low_f == level, one, zero))
            for f in range(0, GROUP, 2):
                both = jnp.where(upper, wide[f], wide[f + 1]).astype(BF16)
                count.append(jnp.where(both == high_level, one, zero))
            part = lax.dot_general(
                jnp.concatenate(left + count, axis=0), jnp.concatenate(right, axis=0), NT,
                preferred_element_type=F32,
            )
            acc = part if acc is None else acc + part
        stats = jnp.zeros((2 * rows, GROUP * LOW), F32)
        counts = jnp.zeros((HIGH, GROUP * LOW), F32)
        for f in range(GROUP):
            mine = lane_owner == f
            stats = jnp.where(mine, acc[f * 2 * rows:(f + 1) * 2 * rows], stats)
            at = GROUP * 2 * rows + f * HIGH
            counts = jnp.where(mine, acc[at:at + HIGH], counts)
        out_ref[pl.ds(pl.multiple_of(g * 3 * HIGH, 3 * HIGH), 3 * HIGH), :] = jnp.concatenate(
            [stats[0:HIGH] + stats[HIGH:2 * HIGH], stats[2 * HIGH:3 * HIGH] + stats[3 * HIGH:4 * HIGH], counts], axis=0)
        return carry

    if len(refs) > 1:
        out_ref[groups * 3 * HIGH:, :] = refs[0][...]
    lax.fori_loop(0, groups, one_group, 0, unroll=2)


def histogram_part(first, groups, tiles, bins_t, *tail):
    rows = groups * 3 * HIGH + sum(piece.shape[0] for piece in tail)
    return pl.pallas_call(
        functools.partial(histogram_kernel, first, groups),
        out_shape=jax.ShapeDtypeStruct((rows, GROUP * LOW), F32),
        in_specs=[vmem()] * (2 + len(tail)),
        out_specs=vmem(),
        compiler_params=pltpu.CompilerParams(vmem_limit_bytes=VMEM_LIMIT),
        cost_estimate=pl.CostEstimate(flops=groups * 330_000_000, bytes_accessed=groups * 60_000, transcendentals=0),
        name="histogram_part",
    )(tiles, bins_t, *tail)


def finish_kernel(per_dev, leaf_ref, kept_ref, sums_ref, *refs):
    arrived = refs[:-3]
    value_ref, step_ref, hist_ref = refs[-3:]
    unit = kept_ref.shape[0]
    totals = add_up([sums_ref[...]] + [ref[unit:, :] for ref in arrived])
    highs = LEAVES // LANES
    grad, curv = totals[:, :LANES], totals[:, LANES:]
    shrunk = jnp.maximum(jnp.abs(grad) - lasso_penalty, 0.0)
    values = jnp.where(grad > 0.0, -shrunk, shrunk) / (curv + ridge_penalty)
    value_ref[...] = values
    leaf = leaf_ref[...]
    top, spot = leaf // LANES, leaf % LANES
    step = jnp.zeros(leaf.shape, F32)
    for h in range(highs):
        row = jnp.broadcast_to(values[h:h + 1, :], leaf.shape)
        step = jnp.where(top == h, jnp.take_along_axis(row, spot, axis=1), step)
    step_ref[...] = shrinkage * step
    hist = add_up([kept_ref[...]] + [ref[:unit, :] for ref in arrived])
    if per_dev == GROUP:
        for c in range(3):
            for f in range(GROUP):
                line = [hist[c * HIGH + h:c * HIGH + h + 1, f * LOW:(f + 1) * LOW] for h in range(HIGH)]
                hist_ref[c:c + 1, f * BINS:(f + 1) * BINS] = jnp.concatenate(line, axis=1)
    else:
        hist_ref[...] = hist


def finish(per_dev, leaves, kept, sums, arrived):
    out = (3, per_dev * BINS) if per_dev == GROUP else kept.shape
    return pl.pallas_call(
        functools.partial(finish_kernel, per_dev),
        out_shape=(
            jax.ShapeDtypeStruct((LEAVES // LANES, LANES), F32),
            jax.ShapeDtypeStruct(leaves.shape, F32),
            jax.ShapeDtypeStruct(out, F32),
        ),
        in_specs=[vmem()] * (3 + len(arrived)),
        out_specs=(vmem(), vmem(), vmem()),
        compiler_params=pltpu.CompilerParams(vmem_limit_bytes=VMEM_LIMIT),
        name="finish",
    )(leaves, kept, sums, *arrived)


def add_up(parts):
    while len(parts) > 1:
        parts = [parts[k] + parts[k + 1] for k in range(0, len(parts), 2)]
    return parts[0]


def local(scores, labels, leaves, bins, lengths, owner):
    query_count = lax.axis_size("query")
    feat_count = lax.axis_size("feat")
    count = query_count * feat_count
    place = lax.axis_index("query").astype(jnp.int32) * feat_count + lax.axis_index("feat").astype(jnp.int32)
    docs = scores.shape[0]
    own = docs // LANES
    features = owner.shape[0]
    per_dev = features // count
    unit = 3 * per_dev
    axes = ("query", "feat")
    feat_masks = [1 << b for b in range(feat_count.bit_length() - 1)]
    masks = [feat_count << b for b in range(query_count.bit_length() - 1)] + feat_masks

    def swap(value, mask):
        return lax.ppermute(value, axes, [(p, p ^ mask) for p in range(count)])

    pos = place.reshape(1)
    leaf_rows = leaves.reshape(own, LANES)
    gathered = scores.reshape(own, LANES)
    score_parts = [gathered]
    for k, mask in enumerate(feat_masks):
        if k == 1:
            qid, worth, inverse, bounds = label_terms(feat_count, own, lengths, pos, labels.reshape(-1, LANES))
            gathered, inverse = lax.optimization_barrier((gathered, inverse))
        score_parts.append(swap(gathered, mask))
        gathered = jnp.concatenate([gathered, score_parts[-1]], axis=0)
    lambdas, tiles, sums = pair_terms(bounds, pos, score_parts, worth, qid, inverse, leaf_rows)
    pos, sums = lax.optimization_barrier((pos, sums))
    bins_t = order_bins(masks[::-1], pos, owner.reshape(-1, LANES), bins)

    def part(tiles, low, high, *tail):
        if per_dev == GROUP:
            return histogram_part(low, high - low, tiles, bins_t, *tail)
        groups = high - low
        wide = histogram_part(low, groups, tiles, bins_t)
        wide = wide.reshape(groups, 3, HIGH, GROUP // per_dev, per_dev, LOW).transpose(0, 3, 1, 4, 2, 5)
        return jnp.concatenate([wide.reshape(groups * GROUP // per_dev * unit, BINS), *tail], axis=0)

    def join(block, total):
        return jnp.concatenate([block, total], axis=0)

    quarter = features // GROUP // 4
    edge = count // 4 * unit
    arrived = swap(part(tiles, 3 * quarter, 4 * quarter, sums), masks[0])
    far = part(tiles, quarter, 2 * quarter) + arrived[:edge]
    sums = sums + arrived[edge:]
    message, tiles = lax.optimization_barrier((join(far, sums), tiles))
    crossed = swap(message, masks[1])
    arrived = swap(part(tiles, 2 * quarter, 3 * quarter), masks[0])
    kept = part(tiles, 0, quarter) + arrived + crossed[:edge]
    sums = sums + crossed[edge:]
    for mask in masks[2:-1]:
        edge = edge // 2
        arrived = swap(join(kept[edge:], sums), mask)
        kept = kept[:edge] + arrived[:edge]
        sums = sums + arrived[edge:]
    arrived = swap(join(kept[unit:], sums), masks[-1])
    values, step, histograms = finish(per_dev, leaf_rows, kept[:unit], sums, [arrived])
    return lambdas, values.reshape(LEAVES), step.reshape(docs), histograms.reshape(3, per_dev * BINS)


def solution(mesh):
    in_specs = (
        P(("query", "feat")),
        P("query"),
        P(("query", "feat")),
        P(("query", "feat"), None),
        P("query", None),
        P(),
    )
    out_specs = (P(None, ("query", "feat")), P(), P(("query", "feat")), P(None, ("query", "feat")))
    return jax.shard_map(local, mesh=mesh, in_specs=in_specs, out_specs=out_specs, check_vma=False)
```

```python
import functools

import jax
import jax.numpy as jnp
from jax import lax
from jax.experimental import pallas as pl
from jax.experimental.pallas import tpu as pltpu
from jax.sharding import PartitionSpec as P

BINS = 256
LEAVES = 1024
LANES = 128
GRADES = 4
LOW = 32
HIGH = BINS // LOW
GROUP = 8
CHUNK = 64
MAX_LEN = 1024

lasso_penalty = 1.0
ridge_penalty = 1.0
shrinkage = 0.1

VMEM_LIMIT = 48 * 1024 * 1024
F32 = jnp.float32
BF16 = jnp.bfloat16
NT = (((1,), (1,)), ((), ()))


def iota(shape, axis):
    return lax.broadcasted_iota(jnp.int32, shape, axis)


def vmem():
    return pl.BlockSpec(memory_space=pltpu.VMEM)


def smem():
    return pl.BlockSpec(memory_space=pltpu.SMEM)


def prepare_kernel(feat_count, masks, len_ref, pos_ref, lab_ref, owner_ref, leaf_ref, score_ref,
                   kept_ref, qid_ref, worth_ref, inv_ref, perm_ref, spot_ref, top_ref, bounds_ref):
    queries = len_ref.shape[1]
    rows = lab_ref.shape[0]
    own = leaf_ref.shape[0]
    docs = own * LANES
    kept_ref[...] = score_ref[...]
    spot = iota((rows, LANES), 0) * LANES + iota((rows, LANES), 1)
    qid = jnp.zeros((rows, LANES), jnp.int32)
    begin = jnp.zeros((queries, LANES), jnp.int32)
    finish = jnp.zeros((queries, LANES), jnp.int32)
    which = iota((queries, LANES), 0)
    start = jnp.int32(0)
    for q in range(queries):
        end = start + len_ref[0, q]
        qid = qid + jnp.where(spot >= end, 1, 0)
        begin = jnp.where(which == q, start, begin)
        finish = jnp.where(which == q, end, finish)

        def set_low(r, carry, start=start, end=end):
            bounds_ref[0, r] = start
            bounds_ref[2, r] = end
            return carry

        def set_high(r, carry, end=end):
            bounds_ref[1, r] = end
            return carry

        lax.fori_loop((start + LANES - 1) // LANES, (end + LANES - 1) // LANES, set_low, 0)
        lax.fori_loop(start // LANES, end // LANES, set_high, 0)
        start = end
    qid_ref[...] = qid
    worth_ref[...] = jnp.left_shift(1, lab_ref[...]).astype(F32)

    counts = [jnp.zeros((queries, LANES), F32) for _ in range(GRADES)]
    lane = iota((queries, LANES), 1)
    for r in range(rows):
        at = lane + r * LANES
        inside = (at >= begin) & (at < finish)
        grade = jnp.where(inside, jnp.broadcast_to(lab_ref[r:r + 1, :], (queries, LANES)), 0)
        for g in range(GRADES):
            counts[g] = counts[g] + jnp.where(grade > g, 1.0, 0.0)
    position = iota((queries, MAX_LEN), 1).astype(F32)
    gain = jnp.zeros((queries, MAX_LEN), F32)
    for g in range(GRADES):
        held = jnp.sum(counts[g], axis=1, keepdims=True)
        gain = gain + jnp.where(position < held, float(2 ** g), 0.0)
    level = 1.0 / jnp.log2(2.0 + position[0:1, :])
    ideal = jnp.sum(gain * level, axis=1, keepdims=True)
    usable = ideal > 0.5
    inverse = jnp.where(usable, 1.0 / jnp.where(usable, ideal, 1.0), 0.0)
    first = pos_ref[0] % feat_count * own
    for t in range(own):
        at = lane + (first + t) * LANES
        inside = (at >= begin) & (at < finish)
        inv_ref[0:1, t * LANES:(t + 1) * LANES] = jnp.sum(jnp.where(inside, inverse, 0.0), axis=0, keepdims=True)

    features = perm_ref.shape[0]
    per_dev = features >> len(masks)
    owner = jnp.concatenate([owner_ref[k:k + 1, :] for k in range(features // LANES)], axis=1)
    square = (features, features)
    down, across = iota(square, 0), iota(square, 1)
    index = iota((features, 1), 0) // per_dev
    target = jnp.zeros((features, 1), jnp.int32)
    for b, mask in enumerate(masks):
        target = target + ((index >> b) & 1) * mask
    target = (target ^ pos_ref[0]) * per_dev + iota((features, 1), 0) % per_dev
    pick = jnp.where(target == across, 1.0, 0.0).astype(BF16)
    holds = jnp.where(jnp.broadcast_to(owner, square) == down, 1.0, 0.0).astype(BF16)
    perm_ref[...] = lax.dot_general(pick, holds, NT, preferred_element_type=F32).astype(BF16)

    leaf = jnp.concatenate([leaf_ref[t:t + 1, :] for t in range(own)], axis=1)
    highs = LEAVES // LANES
    top_ref[...] = jnp.where(jnp.broadcast_to(leaf // LANES, (highs, docs)) == iota((highs, docs), 0), 1.0, 0.0)
    spot_ref[...] = jnp.where(
        jnp.broadcast_to(leaf % LANES, (LANES, docs)) == iota((LANES, docs), 0), 1.0, 0.0).astype(BF16)


def prepare(feat_count, masks, lengths, pos, labels, owner, leaves, scores):
    rows = labels.shape[0]
    docs = leaves.shape[0] * LANES
    features = owner.shape[0] * LANES
    return pl.pallas_call(
        functools.partial(prepare_kernel, feat_count, masks),
        out_shape=(
            jax.ShapeDtypeStruct(scores.shape, F32),
            jax.ShapeDtypeStruct((rows, LANES), jnp.int32),
            jax.ShapeDtypeStruct((rows, LANES), F32),
            jax.ShapeDtypeStruct((1, docs), F32),
            jax.ShapeDtypeStruct((features, features), BF16),
            jax.ShapeDtypeStruct((LANES, docs), BF16),
            jax.ShapeDtypeStruct((LEAVES // LANES, docs), F32),
            jax.ShapeDtypeStruct((3, rows), jnp.int32),
        ),
        in_specs=[smem(), smem()] + [vmem()] * 4,
        out_specs=(vmem(),) * 7 + (smem(),),
        compiler_params=pltpu.CompilerParams(vmem_limit_bytes=VMEM_LIMIT),
        cost_estimate=pl.CostEstimate(flops=50_000_000, bytes_accessed=3_000_000, transcendentals=20_000),
        name="prepare",
    )(lengths, pos, labels, owner, leaves, scores)


def order_kernel(perm_ref, bins_ref, out_ref):
    bins = bins_ref[...].astype(F32).astype(BF16)
    out_ref[...] = lax.dot_general(perm_ref[...], bins, NT, preferred_element_type=F32)


def order_bins(perm, bins):
    docs, features = bins.shape
    return pl.pallas_call(
        order_kernel,
        out_shape=jax.ShapeDtypeStruct((features, docs), F32),
        in_specs=[vmem(), vmem()],
        out_specs=vmem(),
        compiler_params=pltpu.CompilerParams(vmem_limit_bytes=VMEM_LIMIT),
        cost_estimate=pl.CostEstimate(flops=200_000_000, bytes_accessed=3_000_000, transcendentals=0),
        name="order_bins",
    )(perm, bins)


def split_terms(value, terms):
    parts = []
    rest = value
    for _ in range(terms):
        part = rest.astype(BF16)
        parts.append(part)
        rest = rest - part.astype(F32)
    return parts


def widen(ref, source):
    turned = jnp.transpose(source)
    for r in range(source.shape[0]):
        ref[r * LANES:(r + 1) * LANES, :] = jnp.broadcast_to(turned[:, r:r + 1], (LANES, LANES))


def lane_sums(source):
    parts = split_terms(source, 3)
    ones = jnp.ones((8, 2 * LANES), BF16)
    wide = lax.dot_general(ones, jnp.concatenate(parts[:2], axis=1), NT, preferred_element_type=F32)
    return (wide + lax.dot_general(ones[:, :LANES], parts[2], NT, preferred_element_type=F32))[0:1, :]


def pairs_kernel(feat_count, bounds_ref, pos_ref, *refs):
    scores = refs[:-21]
    (worth_ref, qid_ref, inv_ref, spot_ref, top_ref, lam_ref, tile_ref, sums_ref,
     s_row, a_row, d_row, w_row, q_row, s_turn, q_turn, s_col, q_col, a_own, w_own, d_own, sums_own) = refs[-21:]
    rows = worth_ref.shape[0]
    own = rows // feat_count
    docs = own * LANES
    me = pos_ref[0] % feat_count
    s_row[...] = jnp.zeros(s_row.shape, F32)
    near = [me, me ^ 1, ((me + 1) ^ 1) - 1]
    for where, ref in zip(near, scores):
        @pl.when((where >= 0) & (where < feat_count))
        def _(where=where, ref=ref):
            s_row[pl.ds(pl.multiple_of(where * own, own), own), :] = ref[...]
    a_row[...] = jnp.exp(s_row[...])
    d_row[...] = jnp.zeros(d_row.shape, F32)
    w_row[0:rows, :] = worth_ref[...]
    w_row[rows:, :] = jnp.zeros((8, LANES), F32)
    q_row[0:rows, :] = qid_ref[...]
    q_row[rows:, :] = jnp.full((8, LANES), -1, jnp.int32)
    first = pl.multiple_of(me * own, own)
    window_low = bounds_ref[0, first] // LANES
    window_high = (bounds_ref[1, first + own - 1] + LANES - 1) // LANES
    s_turn[...] = jnp.transpose(s_row[0:rows, :])
    q_turn[...] = jnp.transpose(qid_ref[...])
    for r in range(rows):
        @pl.when((r >= window_low) & (r < window_high))
        def _(r=r):
            at = slice(r * LANES, (r + 1) * LANES)
            s_col[at, :] = jnp.broadcast_to(s_turn[:, r:r + 1], (LANES, LANES))
            q_col[at, :] = jnp.broadcast_to(q_turn[:, r:r + 1], (LANES, LANES))
    widen(a_own, a_row[pl.ds(first, own), :])
    widen(w_own, w_row[pl.ds(first, own), :])

    def row_of(ref, r):
        return jnp.broadcast_to(ref[pl.ds(r, 1), :], (8, LANES))

    def rank_group(r, carry):
        score = row_of(s_row, r)
        query = row_of(q_row, r)

        def sweep(ahead, masked):
            def step(c, acc):
                base = pl.multiple_of(c * LANES, LANES)
                acc = list(acc)
                for u in range(LANES // 8):
                    other = s_col[pl.ds(base + 8 * u, 8), :]
                    hit = (other >= score) if ahead else (other > score)
                    if masked:
                        hit = hit & (q_col[pl.ds(base + 8 * u, 8), :] == query)
                    acc[u % 4] = acc[u % 4] + jnp.where(hit, 1.0, 0.0)
                return tuple(acc)
            return step

        acc = tuple(jnp.zeros((8, LANES), F32) for _ in range(4))
        start, end = bounds_ref[0, r], bounds_ref[1, r]
        low = jnp.maximum(start // LANES, window_low)
        high = jnp.minimum((end + LANES - 1) // LANES, window_high)
        single = bounds_ref[2, r] >= (r + 1) * LANES
        inner_low = jnp.where(single, jnp.maximum((start + LANES - 1) // LANES, window_low), r)
        inner_high = jnp.where(single, jnp.minimum(end // LANES, window_high), r + 1)
        acc = lax.fori_loop(low, inner_low, sweep(True, True), acc)
        acc = lax.fori_loop(inner_low, r, sweep(True, False), acc)
        acc = lax.fori_loop(r + 1, inner_high, sweep(False, False), acc)
        acc = list(lax.fori_loop(inner_high, high, sweep(False, True), acc))
        base = pl.multiple_of(r * LANES, LANES)
        for u in range(LANES // 8):
            other = s_col[pl.ds(base + 8 * u, 8), :]
            earlier = iota((8, LANES), 0) + 8 * u < iota((8, LANES), 1)
            above = (other > score) | ((other == score) & earlier)
            hit = above & (q_col[pl.ds(base + 8 * u, 8), :] == query)
            acc[u % 4] = acc[u % 4] + jnp.where(hit, 1.0, 0.0)
        total = (acc[0] + acc[1]) + (acc[2] + acc[3])
        d_row[pl.ds(r, 1), :] = jnp.sum(total, axis=0, keepdims=True)
        return carry

    lax.fori_loop(window_low, window_high, rank_group, 0)
    d_row[...] = 1.0 / jnp.log2(2.0 + d_row[...])
    widen(d_own, d_row[pl.ds(first, own), :])

    def pair_block(b, carry):
        base = pl.multiple_of(b * CHUNK, CHUNK)
        r = first + b // (LANES // CHUNK)
        count = CHUNK // 8
        queries = pl.multiple_of(first * LANES + base, CHUNK)

        def columns(width):
            def step(c, acc):
                acc = list(acc)
                other = []
                for k in range(width):
                    at = (r_low + width * c + k) if width > 1 else c
                    other.append([row_of(ref, at) for ref in (a_row, w_row, d_row, q_row)])
                for u in range(count):
                    at = pl.ds(base + 8 * u, 8)
                    a_i, w_i, d_i = a_own[at, :], w_own[at, :], d_own[at, :]
                    q_i = q_col[pl.ds(queries + 8 * u, 8), :]
                    for a_j, w_j, d_j, q_j in other:
                        recip = pl.reciprocal(a_i + a_j, approx=True)
                        lift = w_i - w_j
                        weight = jnp.where(q_i == q_j, jnp.abs(d_i - d_j) * recip, 0.0) * lift
                        acc[u] = acc[u] + weight * jnp.where(lift > 0.0, a_j, a_i)
                        acc[count + u] = acc[count + u] + jnp.abs(weight) * (recip * a_j)
                return tuple(acc)
            return step

        acc = tuple(jnp.zeros((8, LANES), F32) for _ in range(2 * count))
        r_low = bounds_ref[0, r] // LANES
        r_high = (bounds_ref[1, r] + LANES - 1) // LANES
        twos = (r_high - r_low) // 2
        acc = lax.fori_loop(0, twos, columns(2), acc)
        acc = lax.fori_loop(r_low + 2 * twos, r_high, columns(1), acc)
        for u in range(count):
            sums_own[pl.ds(base + 8 * u, 8), :] = acc[u]
            sums_own[pl.ds(docs + base + 8 * u, 8), :] = acc[count + u]
        return carry

    lax.fori_loop(0, docs // CHUNK, pair_block, 0)
    totals = lane_sums(sums_own[...])
    inverse = inv_ref[...]
    a_line = jnp.concatenate([a_row[pl.ds(first + t, 1), :] for t in range(own)], axis=1)
    terms = [-inverse * totals[:, :docs], inverse * a_line * totals[:, docs:]]

    highs = LEAVES // LANES
    top = top_ref[...] > 0.0
    pieces, tiles = [], []
    for c in range(2):
        lam_ref[c:c + 1, :] = terms[c]
        for k, part in enumerate(split_terms(terms[c], 3)):
            wide = jnp.broadcast_to(part.astype(F32), (highs, docs))
            pieces.append(jnp.where(top, wide, 0.0))
            if k < 2:
                tiles.append(wide)
    tile_ref[...] = jnp.concatenate(tiles, axis=0).astype(BF16)
    stacked = jnp.concatenate(pieces, axis=0).astype(BF16)
    sums = lax.dot_general(stacked, spot_ref[...], NT, preferred_element_type=F32)
    for c in range(2):
        base = c * 3 * highs
        sums_ref[:, c * LANES:(c + 1) * LANES] = (
            sums[base:base + highs] + (sums[base + highs:base + 2 * highs] + sums[base + 2 * highs:base + 3 * highs])
        )


def pair_terms(feat_count, bounds, pos, scores, worth, qid, inverse, spots, top):
    rows = worth.shape[0]
    docs = inverse.shape[1]
    highs = LEAVES // LANES
    row = pltpu.VMEM((rows + 8, LANES), F32)
    mine = pltpu.VMEM((docs, LANES), F32)
    return pl.pallas_call(
        functools.partial(pairs_kernel, feat_count),
        out_shape=(
            jax.ShapeDtypeStruct((2, docs), F32),
            jax.ShapeDtypeStruct((4 * HIGH, docs), BF16),
            jax.ShapeDtypeStruct((highs, 2 * LANES), F32),
        ),
        in_specs=[smem(), smem()] + [vmem()] * (len(scores) + 5),
        out_specs=(vmem(), vmem(), vmem()),
        scratch_shapes=[row, row, row, row, pltpu.VMEM((rows + 8, LANES), jnp.int32),
                        pltpu.VMEM((LANES, rows), F32), pltpu.VMEM((LANES, rows), jnp.int32),
                        pltpu.VMEM((rows * LANES, LANES), F32), pltpu.VMEM((rows * LANES, LANES), jnp.int32),
                        mine, mine, mine, pltpu.VMEM((2 * docs, LANES), F32)],
        compiler_params=pltpu.CompilerParams(vmem_limit_bytes=VMEM_LIMIT),
        cost_estimate=pl.CostEstimate(flops=40_000_000, bytes_accessed=200_000, transcendentals=2_000_000),
        name="pair_terms",
    )(bounds, pos, *scores, worth, qid, inverse, spots, top)


def histogram_kernel(first, groups, tile_ref, bins_ref, *refs):
    out_ref = refs[-1]
    docs = tile_ref.shape[1]
    depth = 256
    rows = 16
    row = iota((rows, depth), 0)
    low_level = [(row + rows * k).astype(F32).astype(BF16) for k in range(LOW // rows)]
    high_level = (row % HIGH).astype(F32).astype(BF16)
    upper = row < HIGH
    zero = jnp.zeros((rows, depth), BF16)
    one = jnp.ones((rows, depth), BF16)
    lane_owner = iota((1, GROUP * LOW), 1) // LOW

    def one_group(g, carry):
        base = pl.multiple_of((first + g) * GROUP, GROUP)
        acc = None
        for k in range(docs // depth):
            span = slice(k * depth, (k + 1) * depth)
            code = bins_ref[pl.ds(base, GROUP), span]
            high = jnp.floor(code * (1.0 / LOW))
            low = code - high * LOW
            left, right, count = [], [], []
            wide = []
            for f in range(GROUP):
                high_f = jnp.broadcast_to(high[f:f + 1, :], (rows, depth))
                low_f = jnp.broadcast_to(low[f:f + 1, :], (rows, depth)).astype(BF16)
                wide.append(high_f)
                match = high_f.astype(BF16) == high_level
                for c in range(2):
                    left.append(jnp.where(match, tile_ref[c * rows:(c + 1) * rows, span], zero))
                for level in low_level:
                    right.append(jnp.where(low_f == level, one, zero))
            for f in range(0, GROUP, 2):
                both = jnp.where(upper, wide[f], wide[f + 1]).astype(BF16)
                count.append(jnp.where(both == high_level, one, zero))
            part = lax.dot_general(
                jnp.concatenate(left + count, axis=0), jnp.concatenate(right, axis=0), NT,
                preferred_element_type=F32,
            )
            acc = part if acc is None else acc + part
        stats = jnp.zeros((2 * rows, GROUP * LOW), F32)
        counts = jnp.zeros((HIGH, GROUP * LOW), F32)
        for f in range(GROUP):
            mine = lane_owner == f
            stats = jnp.where(mine, acc[f * 2 * rows:(f + 1) * 2 * rows], stats)
            at = GROUP * 2 * rows + f * HIGH
            counts = jnp.where(mine, acc[at:at + HIGH], counts)
        out_ref[pl.ds(pl.multiple_of(g * 3 * HIGH, 3 * HIGH), 3 * HIGH), :] = jnp.concatenate(
            [stats[0:HIGH] + stats[HIGH:2 * HIGH], stats[2 * HIGH:3 * HIGH] + stats[3 * HIGH:4 * HIGH], counts], axis=0)
        return carry

    if len(refs) > 1:
        out_ref[groups * 3 * HIGH:, :] = refs[0][...]
    lax.fori_loop(0, groups, one_group, 0, unroll=2)


def histogram_part(first, groups, tiles, bins_t, *tail):
    rows = groups * 3 * HIGH + sum(piece.shape[0] for piece in tail)
    return pl.pallas_call(
        functools.partial(histogram_kernel, first, groups),
        out_shape=jax.ShapeDtypeStruct((rows, GROUP * LOW), F32),
        in_specs=[vmem()] * (2 + len(tail)),
        out_specs=vmem(),
        compiler_params=pltpu.CompilerParams(vmem_limit_bytes=VMEM_LIMIT),
        cost_estimate=pl.CostEstimate(flops=groups * 330_000_000, bytes_accessed=groups * 60_000, transcendentals=0),
        name="histogram_part",
    )(tiles, bins_t, *tail)


def finish_kernel(per_dev, leaf_ref, kept_ref, sums_ref, *refs):
    arrived = refs[:-3]
    value_ref, step_ref, hist_ref = refs[-3:]
    unit = kept_ref.shape[0]
    totals = add_up([sums_ref[...]] + [ref[unit:, :] for ref in arrived])
    highs = LEAVES // LANES
    grad, curv = totals[:, :LANES], totals[:, LANES:]
    shrunk = jnp.maximum(jnp.abs(grad) - lasso_penalty, 0.0)
    values = jnp.where(grad > 0.0, -shrunk, shrunk) / (curv + ridge_penalty)
    value_ref[...] = values
    leaf = leaf_ref[...]
    top, spot = leaf // LANES, leaf % LANES
    step = jnp.zeros(leaf.shape, F32)
    for h in range(highs):
        row = jnp.broadcast_to(values[h:h + 1, :], leaf.shape)
        step = jnp.where(top == h, jnp.take_along_axis(row, spot, axis=1), step)
    step_ref[...] = shrinkage * step
    hist = add_up([kept_ref[...]] + [ref[:unit, :] for ref in arrived])
    if per_dev == GROUP:
        for c in range(3):
            for f in range(GROUP):
                line = [hist[c * HIGH + h:c * HIGH + h + 1, f * LOW:(f + 1) * LOW] for h in range(HIGH)]
                hist_ref[c:c + 1, f * BINS:(f + 1) * BINS] = jnp.concatenate(line, axis=1)
    else:
        hist_ref[...] = hist


def finish(per_dev, leaves, kept, sums, arrived):
    out = (3, per_dev * BINS) if per_dev == GROUP else kept.shape
    return pl.pallas_call(
        functools.partial(finish_kernel, per_dev),
        out_shape=(
            jax.ShapeDtypeStruct((LEAVES // LANES, LANES), F32),
            jax.ShapeDtypeStruct(leaves.shape, F32),
            jax.ShapeDtypeStruct(out, F32),
        ),
        in_specs=[vmem()] * (3 + len(arrived)),
        out_specs=(vmem(), vmem(), vmem()),
        compiler_params=pltpu.CompilerParams(vmem_limit_bytes=VMEM_LIMIT),
        name="finish",
    )(leaves, kept, sums, *arrived)


def add_up(parts):
    while len(parts) > 1:
        parts = [parts[k] + parts[k + 1] for k in range(0, len(parts), 2)]
    return parts[0]


def local(scores, labels, leaves, bins, lengths, owner):
    query_count = lax.axis_size("query")
    feat_count = lax.axis_size("feat")
    count = query_count * feat_count
    place = lax.axis_index("query").astype(jnp.int32) * feat_count + lax.axis_index("feat").astype(jnp.int32)
    docs = scores.shape[0]
    own = docs // LANES
    features = owner.shape[0]
    per_dev = features // count
    unit = 3 * per_dev
    axes = ("query", "feat")
    feat_masks = [1 << b for b in range(feat_count.bit_length() - 1)]
    query_masks = [feat_count << b for b in range(query_count.bit_length() - 1)]

    def swap(value, mask):
        return lax.ppermute(value, axes, [(p, p ^ mask) for p in range(count)])

    pos = place.reshape(1)
    leaf_rows = leaves.reshape(own, LANES)
    own_scores = scores.reshape(own, LANES)
    score_parts = [own_scores]
    for begin in range(2):
        links = [(z, z + 1) for z in range(begin, feat_count - 1, 2)]
        score_parts.append(lax.ppermute(own_scores, "feat", links + [(b, a) for a, b in links]))
    score_parts[0], qid, worth, inverse, perm, spots, top, bounds = prepare(
        feat_count, feat_masks + query_masks[:0:-1] + query_masks[:1], lengths, pos, labels.reshape(-1, LANES),
        owner.reshape(-1, LANES), leaf_rows, own_scores)
    lambdas, tiles, sums = pair_terms(feat_count, bounds, pos, score_parts, worth, qid, inverse, spots, top)
    perm, sums = lax.optimization_barrier((perm, sums))
    bins_t = order_bins(perm, bins)

    def part(tiles, low, high, *tail):
        if per_dev == GROUP:
            return histogram_part(low, high - low, tiles, bins_t, *tail)
        groups = high - low
        wide = histogram_part(low, groups, tiles, bins_t)
        wide = wide.reshape(groups, 3, HIGH, GROUP // per_dev, per_dev, LOW).transpose(0, 3, 1, 4, 2, 5)
        return jnp.concatenate([wide.reshape(groups * GROUP // per_dev * unit, BINS), *tail], axis=0)

    def join(block, total):
        return jnp.concatenate([block, total], axis=0)

    quarter = features // GROUP // 4
    edge = count // 4 * unit
    arrived = swap(part(tiles, 3 * quarter, 4 * quarter, sums), query_masks[0])
    far = part(tiles, quarter, 2 * quarter) + arrived[:edge]
    sums = sums + arrived[edge:]
    message, tiles = lax.optimization_barrier((join(far, sums), tiles))
    crossed = swap(message, query_masks[1])
    arrived = swap(part(tiles, 2 * quarter, 3 * quarter), query_masks[0])
    kept = part(tiles, 0, quarter) + arrived + crossed[:edge]
    sums = sums + crossed[edge:]
    for mask in query_masks[2:]:
        edge = edge // 2
        arrived = swap(join(kept[edge:], sums), mask)
        kept = kept[:edge] + arrived[:edge]
        sums = sums + arrived[edge:]
    arrived = [swap(join(kept[m * unit:(m + 1) * unit], sums), m) for m in range(1, feat_count)]
    values, step, histograms = finish(per_dev, leaf_rows, kept[:unit], sums, arrived)
    return lambdas, values.reshape(LEAVES), step.reshape(docs), histograms.reshape(3, per_dev * BINS)


def solution(mesh):
    in_specs = (
        P(("query", "feat")),
        P("query"),
        P(("query", "feat")),
        P(("query", "feat"), None),
        P("query", None),
        P(),
    )
    out_specs = (P(None, ("query", "feat")), P(), P(("query", "feat")), P(None, ("query", "feat")))
    return jax.shard_map(local, mesh=mesh, in_specs=in_specs, out_specs=out_specs, check_vma=False)
```

```python
import functools

import jax
import jax.numpy as jnp
from jax import lax
from jax.experimental import pallas as pl
from jax.experimental.pallas import tpu as pltpu
from jax.sharding import PartitionSpec as P

BINS = 256
LEAVES = 1024
LANES = 128
GRADES = 4
LOW = 32
HIGH = BINS // LOW
GROUP = 8
CHUNK = 64
MAX_LEN = 1024

lasso_penalty = 1.0
ridge_penalty = 1.0
shrinkage = 0.1

VMEM_LIMIT = 48 * 1024 * 1024
F32 = jnp.float32
BF16 = jnp.bfloat16
NT = (((1,), (1,)), ((), ()))


def iota(shape, axis):
    return lax.broadcasted_iota(jnp.int32, shape, axis)


def vmem():
    return pl.BlockSpec(memory_space=pltpu.VMEM)


def smem():
    return pl.BlockSpec(memory_space=pltpu.SMEM)


def prepare_kernel(feat_count, masks, len_ref, pos_ref, lab_ref, owner_ref, score_ref,
                   kept_ref, qid_ref, worth_ref, inv_ref, perm_ref, bounds_ref):
    kept_ref[...] = score_ref[...]
    queries = len_ref.shape[1]
    rows = lab_ref.shape[0]
    own = rows // feat_count
    spot = iota((rows, LANES), 0) * LANES + iota((rows, LANES), 1)
    qid = jnp.zeros((rows, LANES), jnp.int32)
    begin = jnp.zeros((queries, LANES), jnp.int32)
    finish = jnp.zeros((queries, LANES), jnp.int32)
    which = iota((queries, LANES), 0)
    start = jnp.int32(0)
    for q in range(queries):
        end = start + len_ref[0, q]
        qid = qid + jnp.where(spot >= end, 1, 0)
        begin = jnp.where(which == q, start, begin)
        finish = jnp.where(which == q, end, finish)

        def set_low(r, carry, start=start, end=end):
            bounds_ref[0, r] = start
            bounds_ref[2, r] = end
            return carry

        def set_high(r, carry, end=end):
            bounds_ref[1, r] = end
            return carry

        lax.fori_loop((start + LANES - 1) // LANES, (end + LANES - 1) // LANES, set_low, 0)
        lax.fori_loop(start // LANES, end // LANES, set_high, 0)
        start = end
    qid_ref[...] = qid
    worth_ref[...] = jnp.left_shift(1, lab_ref[...]).astype(F32)

    counts = [jnp.zeros((queries, LANES), F32) for _ in range(GRADES)]
    lane = iota((queries, LANES), 1)
    for r in range(rows):
        at = lane + r * LANES
        inside = (at >= begin) & (at < finish)
        grade = jnp.where(inside, jnp.broadcast_to(lab_ref[r:r + 1, :], (queries, LANES)), 0)
        for g in range(GRADES):
            counts[g] = counts[g] + jnp.where(grade > g, 1.0, 0.0)
    position = iota((queries, MAX_LEN), 1).astype(F32)
    gain = jnp.zeros((queries, MAX_LEN), F32)
    for g in range(GRADES):
        held = jnp.sum(counts[g], axis=1, keepdims=True)
        gain = gain + jnp.where(position < held, float(2 ** g), 0.0)
    level = 1.0 / jnp.log2(2.0 + position[0:1, :])
    ideal = jnp.sum(gain * level, axis=1, keepdims=True)
    usable = ideal > 0.5
    inverse = jnp.where(usable, 1.0 / jnp.where(usable, ideal, 1.0), 0.0)
    first = pos_ref[0] % feat_count * own
    for t in range(own):
        at = lane + (first + t) * LANES
        inside = (at >= begin) & (at < finish)
        inv_ref[0:1, t * LANES:(t + 1) * LANES] = jnp.sum(jnp.where(inside, inverse, 0.0), axis=0, keepdims=True)

    features = perm_ref.shape[0]
    per_dev = features >> len(masks)
    owner = jnp.concatenate([owner_ref[k:k + 1, :] for k in range(features // LANES)], axis=1)
    square = (features, features)
    down, across = iota(square, 0), iota(square, 1)
    index = iota((features, 1), 0) // per_dev
    target = jnp.zeros((features, 1), jnp.int32)
    for b, mask in enumerate(masks):
        target = target + ((index >> b) & 1) * mask
    target = (target ^ pos_ref[0]) * per_dev + iota((features, 1), 0) % per_dev
    pick = jnp.where(target == across, 1.0, 0.0).astype(BF16)
    holds = jnp.where(jnp.broadcast_to(owner, square) == down, 1.0, 0.0).astype(BF16)
    perm_ref[...] = lax.dot_general(pick, holds, NT, preferred_element_type=F32).astype(BF16)


def prepare(feat_count, masks, lengths, pos, labels, owner, scores):
    rows = labels.shape[0]
    features = owner.shape[0] * LANES
    return pl.pallas_call(
        functools.partial(prepare_kernel, feat_count, masks),
        out_shape=(
            jax.ShapeDtypeStruct(scores.shape, F32),
            jax.ShapeDtypeStruct((rows, LANES), jnp.int32),
            jax.ShapeDtypeStruct((rows, LANES), F32),
            jax.ShapeDtypeStruct((1, rows // feat_count * LANES), F32),
            jax.ShapeDtypeStruct((features, features), BF16),
            jax.ShapeDtypeStruct((3, rows), jnp.int32),
        ),
        in_specs=[smem(), smem(), vmem(), vmem(), vmem()],
        out_specs=(vmem(),) * 5 + (smem(),),
        compiler_params=pltpu.CompilerParams(vmem_limit_bytes=VMEM_LIMIT),
        cost_estimate=pl.CostEstimate(flops=2_000_000_000, bytes_accessed=300_000, transcendentals=20_000),
        name="prepare",
    )(lengths, pos, labels, owner, scores)


def split_terms(value, terms):
    parts = []
    rest = value
    for _ in range(terms):
        part = rest.astype(BF16)
        parts.append(part)
        rest = rest - part.astype(F32)
    return parts


def pairs_kernel(feat_count, bounds_ref, pos_ref, *refs):
    scores = refs[:-20]
    (worth_ref, qid_ref, inv_ref, lam_ref, near_ref,
     s_row, a_row, d_row, s_turn, a_turn, w_turn, q_turn, d_turn, s_col, a_col, w_col, q_col, d_col, grad, curv) = refs[-20:]
    rows = worth_ref.shape[0]
    own = rows // feat_count
    docs = own * LANES
    me = pos_ref[0] % feat_count
    s_row[...] = jnp.zeros(s_row.shape, F32)
    near = [me, me ^ 1, ((me + 1) ^ 1) - 1]
    for where, ref in zip(near, scores):
        @pl.when((where >= 0) & (where < feat_count))
        def _(where=where, ref=ref):
            s_row[pl.ds(pl.multiple_of(where * own, own), own), :] = ref[...]
    a_row[...] = jnp.exp(s_row[...])
    d_row[...] = jnp.zeros(d_row.shape, F32)
    first = me * own
    window_low = bounds_ref[0, first] // LANES
    window_high = (bounds_ref[1, first + own - 1] + LANES - 1) // LANES

    def widen(pairs):
        for turn, source, _ in pairs:
            turn[...] = jnp.transpose(source[...])
        for r in range(rows):
            @pl.when((r >= window_low) & (r < window_high))
            def _(r=r):
                for turn, _, col in pairs:
                    col[r * LANES:(r + 1) * LANES, :] = jnp.broadcast_to(turn[:, r:r + 1], (LANES, LANES))

    widen([(s_turn, s_row, s_col), (q_turn, qid_ref, q_col), (a_turn, a_row, a_col), (w_turn, worth_ref, w_col)])

    def row_of(ref, r):
        return jnp.broadcast_to(ref[pl.ds(r, 1), :], (8, LANES))

    def spans(r):
        start, end = bounds_ref[0, r], bounds_ref[1, r]
        low = jnp.maximum(start // LANES, window_low)
        high = jnp.minimum((end + LANES - 1) // LANES, window_high)
        single = bounds_ref[2, r] >= (r + 1) * LANES
        inner_low = jnp.where(single, jnp.maximum((start + LANES - 1) // LANES, window_low), r)
        inner_high = jnp.where(single, jnp.minimum(end // LANES, window_high), r)
        return low, inner_low, inner_high, high

    def rank_group(r, carry):
        score = row_of(s_row, r)
        query = row_of(qid_ref, r)

        def sweep(ahead, masked):
            def step(c, acc):
                base = pl.multiple_of(c * LANES, LANES)
                acc = list(acc)
                for u in range(LANES // 8):
                    other = s_col[pl.ds(base + 8 * u, 8), :]
                    hit = (other >= score) if ahead else (other > score)
                    if masked:
                        hit = hit & (q_col[pl.ds(base + 8 * u, 8), :] == query)
                    acc[u % 4] = acc[u % 4] + jnp.where(hit, 1.0, 0.0)
                return tuple(acc)
            return step

        acc = tuple(jnp.zeros((8, LANES), F32) for _ in range(4))
        low, inner_low, inner_high, high = spans(r)
        after = jnp.maximum(inner_high, r + 1)
        acc = lax.fori_loop(low, inner_low, sweep(True, True), acc)
        acc = lax.fori_loop(inner_low, r, sweep(True, False), acc)
        acc = lax.fori_loop(r + 1, after, sweep(False, False), acc)
        acc = list(lax.fori_loop(after, high, sweep(False, True), acc))
        base = pl.multiple_of(r * LANES, LANES)
        for u in range(LANES // 8):
            other = s_col[pl.ds(base + 8 * u, 8), :]
            earlier = iota((8, LANES), 0) + 8 * u < iota((8, LANES), 1)
            above = (other > score) | ((other == score) & earlier)
            hit = above & (q_col[pl.ds(base + 8 * u, 8), :] == query)
            acc[u % 4] = acc[u % 4] + jnp.where(hit, 1.0, 0.0)
        total = (acc[0] + acc[1]) + (acc[2] + acc[3])
        d_row[pl.ds(r, 1), :] = jnp.sum(total, axis=0, keepdims=True)
        return carry

    lax.fori_loop(window_low, window_high, rank_group, 0)
    d_row[...] = 1.0 / jnp.log2(2.0 + d_row[...])
    widen([(d_turn, d_row, d_col)])

    def pair_group(t, carry):
        r = first + t
        a_i, w_i, d_i = row_of(a_row, r), row_of(worth_ref, r), row_of(d_row, r)
        query = row_of(qid_ref, r)

        def columns(masked):
            def step(c, acc):
                base = pl.multiple_of(c * LANES, LANES)
                acc = list(acc)
                for u in range(LANES // 8):
                    at = pl.ds(base + 8 * u, 8)
                    a_j = a_col[at, :]
                    recip = pl.reciprocal(a_i + a_j, approx=True)
                    lift = w_i - w_col[at, :]
                    weight = jnp.abs(d_i - d_col[at, :]) * recip
                    if masked:
                        weight = jnp.where(q_col[at, :] == query, weight, 0.0)
                    weight = weight * lift
                    acc[u % 2] = acc[u % 2] + weight * jnp.where(lift > 0.0, a_j, a_i)
                    acc[2 + u % 2] = acc[2 + u % 2] + jnp.abs(weight) * (recip * a_j)
                return tuple(acc)
            return step

        acc = tuple(jnp.zeros((8, LANES), F32) for _ in range(4))
        low, inner_low, inner_high, high = spans(r)
        acc = lax.fori_loop(low, inner_low, columns(True), acc)
        acc = lax.fori_loop(inner_low, inner_high, columns(False), acc)
        acc = lax.fori_loop(inner_high, high, columns(True), acc)
        grad[pl.ds(t, 1), :] = -jnp.sum(acc[0] + acc[1], axis=0, keepdims=True)
        curv[pl.ds(t, 1), :] = a_row[pl.ds(r, 1), :] * jnp.sum(acc[2] + acc[3], axis=0, keepdims=True)
        return carry

    lax.fori_loop(0, own, pair_group, 0)
    inverse = inv_ref[...]
    terms = [inverse * jnp.concatenate([ref[t:t + 1, :] for t in range(own)], axis=1) for ref in (grad, curv)]
    for c in range(2):
        lam_ref[c:c + 1, :] = terms[c]
        near_ref[c:c + 1, :] = terms[c]


def pair_terms(feat_count, bounds, pos, scores, worth, qid, inverse):
    rows = worth.shape[0]
    docs = inverse.shape[1]
    row = pltpu.VMEM((rows, LANES), F32)
    turn = pltpu.VMEM((LANES, rows), F32)
    col = pltpu.VMEM((rows * LANES, LANES), F32)
    mine = pltpu.VMEM((docs // LANES, LANES), F32)
    return pl.pallas_call(
        functools.partial(pairs_kernel, feat_count),
        out_shape=(jax.ShapeDtypeStruct((2, docs), F32), jax.ShapeDtypeStruct((2, docs), F32)),
        in_specs=[smem(), smem()] + [vmem()] * (len(scores) + 3),
        out_specs=(vmem(), vmem()),
        scratch_shapes=[row, row, row, turn, turn, turn, pltpu.VMEM((LANES, rows), jnp.int32), turn,
                        col, col, col, pltpu.VMEM((rows * LANES, LANES), jnp.int32), col, mine, mine],
        compiler_params=pltpu.CompilerParams(vmem_limit_bytes=VMEM_LIMIT),
        cost_estimate=pl.CostEstimate(flops=9_000_000_000, bytes_accessed=200_000, transcendentals=2_000_000),
        name="pair_terms",
    )(bounds, pos, *scores, worth, qid, inverse)


def leaf_kernel(perm_ref, bins_ref, leaf_ref, lam_ref, bins_t_ref, tile_ref, sums_ref):
    bins = bins_ref[...].astype(F32).astype(BF16)
    bins_t_ref[...] = lax.dot_general(perm_ref[...], bins, NT, preferred_element_type=F32)
    own = leaf_ref.shape[0]
    docs = own * LANES
    leaf = jnp.concatenate([leaf_ref[t:t + 1, :] for t in range(own)], axis=1)
    highs = LEAVES // LANES
    top = jnp.broadcast_to(leaf // LANES, (highs, docs)) == iota((highs, docs), 0)
    spots = jnp.where(jnp.broadcast_to(leaf % LANES, (LANES, docs)) == iota((LANES, docs), 0), 1.0, 0.0).astype(BF16)
    pieces, tiles = [], []
    for c in range(2):
        for k, part in enumerate(split_terms(lam_ref[c:c + 1, :], 3)):
            wide = jnp.broadcast_to(part.astype(F32), (highs, docs))
            pieces.append(jnp.where(top, wide, 0.0))
            if k < 2:
                tiles.append(wide)
    tile_ref[...] = jnp.concatenate(tiles, axis=0).astype(BF16)
    stacked = jnp.concatenate(pieces, axis=0).astype(BF16)
    sums = lax.dot_general(stacked, spots, NT, preferred_element_type=F32)
    for c in range(2):
        base = c * 3 * highs
        sums_ref[:, c * LANES:(c + 1) * LANES] = (
            sums[base:base + highs] + (sums[base + highs:base + 2 * highs] + sums[base + 2 * highs:base + 3 * highs])
        )


def leaf_terms(perm, bins, leaves, lambdas):
    docs, features = bins.shape
    return pl.pallas_call(
        leaf_kernel,
        out_shape=(
            jax.ShapeDtypeStruct((features, docs), F32),
            jax.ShapeDtypeStruct((4 * HIGH, docs), BF16),
            jax.ShapeDtypeStruct((LEAVES // LANES, 2 * LANES), F32),
        ),
        in_specs=[vmem()] * 4,
        out_specs=(vmem(), vmem(), vmem()),
        compiler_params=pltpu.CompilerParams(vmem_limit_bytes=VMEM_LIMIT),
        cost_estimate=pl.CostEstimate(flops=200_000_000, bytes_accessed=3_000_000, transcendentals=0),
        name="leaf_terms",
    )(perm, bins, leaves, lambdas)


def histogram_kernel(first, groups, tile_ref, bins_ref, *refs):
    out_ref = refs[-1]
    docs = tile_ref.shape[1]
    depth = 256
    rows = 16
    row = iota((rows, depth), 0)
    low_level = [(row + rows * k).astype(F32).astype(BF16) for k in range(LOW // rows)]
    high_level = (row % HIGH).astype(F32).astype(BF16)
    upper = row < HIGH
    zero = jnp.zeros((rows, depth), BF16)
    one = jnp.ones((rows, depth), BF16)
    lane_owner = iota((1, GROUP * LOW), 1) // LOW

    def one_group(g, carry):
        base = pl.multiple_of((first + g) * GROUP, GROUP)
        acc = None
        for k in range(docs // depth):
            span = slice(k * depth, (k + 1) * depth)
            code = bins_ref[pl.ds(base, GROUP), span]
            high = jnp.floor(code * (1.0 / LOW))
            low = code - high * LOW
            left, right, count = [], [], []
            wide = []
            for f in range(GROUP):
                high_f = jnp.broadcast_to(high[f:f + 1, :], (rows, depth))
                low_f = jnp.broadcast_to(low[f:f + 1, :], (rows, depth)).astype(BF16)
                wide.append(high_f)
                match = high_f.astype(BF16) == high_level
                for c in range(2):
                    left.append(jnp.where(match, tile_ref[c * rows:(c + 1) * rows, span], zero))
                for level in low_level:
                    right.append(jnp.where(low_f == level, one, zero))
            for f in range(0, GROUP, 2):
                both = jnp.where(upper, wide[f], wide[f + 1]).astype(BF16)
                count.append(jnp.where(both == high_level, one, zero))
            part = lax.dot_general(
                jnp.concatenate(left + count, axis=0), jnp.concatenate(right, axis=0), NT,
                preferred_element_type=F32,
            )
            acc = part if acc is None else acc + part
        stats = jnp.zeros((2 * rows, GROUP * LOW), F32)
        counts = jnp.zeros((HIGH, GROUP * LOW), F32)
        for f in range(GROUP):
            mine = lane_owner == f
            stats = jnp.where(mine, acc[f * 2 * rows:(f + 1) * 2 * rows], stats)
            at = GROUP * 2 * rows + f * HIGH
            counts = jnp.where(mine, acc[at:at + HIGH], counts)
        out_ref[pl.ds(pl.multiple_of(g * 3 * HIGH, 3 * HIGH), 3 * HIGH), :] = jnp.concatenate(
            [stats[0:HIGH] + stats[HIGH:2 * HIGH], stats[2 * HIGH:3 * HIGH] + stats[3 * HIGH:4 * HIGH], counts], axis=0)
        return carry

    if len(refs) > 1:
        out_ref[groups * 3 * HIGH:, :] = refs[0][...]
    lax.fori_loop(0, groups, one_group, 0, unroll=2)


def histogram_part(first, groups, tiles, bins_t, *tail):
    rows = groups * 3 * HIGH + sum(piece.shape[0] for piece in tail)
    return pl.pallas_call(
        functools.partial(histogram_kernel, first, groups),
        out_shape=jax.ShapeDtypeStruct((rows, GROUP * LOW), F32),
        in_specs=[vmem()] * (2 + len(tail)),
        out_specs=vmem(),
        compiler_params=pltpu.CompilerParams(vmem_limit_bytes=VMEM_LIMIT),
        cost_estimate=pl.CostEstimate(flops=groups * 330_000_000, bytes_accessed=groups * 60_000, transcendentals=0),
        name="histogram_part",
    )(tiles, bins_t, *tail)


def finish_kernel(per_dev, leaf_ref, kept_ref, sums_ref, *refs):
    arrived = refs[:-3]
    value_ref, step_ref, hist_ref = refs[-3:]
    unit = kept_ref.shape[0]
    totals = add_up([sums_ref[...]] + [ref[unit:, :] for ref in arrived])
    highs = LEAVES // LANES
    grad, curv = totals[:, :LANES], totals[:, LANES:]
    shrunk = jnp.maximum(jnp.abs(grad) - lasso_penalty, 0.0)
    values = jnp.where(grad > 0.0, -shrunk, shrunk) / (curv + ridge_penalty)
    value_ref[...] = values
    leaf = leaf_ref[...]
    top, spot = leaf // LANES, leaf % LANES
    step = jnp.zeros(leaf.shape, F32)
    for h in range(highs):
        row = jnp.broadcast_to(values[h:h + 1, :], leaf.shape)
        step = jnp.where(top == h, jnp.take_along_axis(row, spot, axis=1), step)
    step_ref[...] = shrinkage * step
    hist = add_up([kept_ref[...]] + [ref[:unit, :] for ref in arrived])
    if per_dev == GROUP:
        for c in range(3):
            for f in range(GROUP):
                line = [hist[c * HIGH + h:c * HIGH + h + 1, f * LOW:(f + 1) * LOW] for h in range(HIGH)]
                hist_ref[c:c + 1, f * BINS:(f + 1) * BINS] = jnp.concatenate(line, axis=1)
    else:
        hist_ref[...] = hist


def finish(per_dev, leaves, kept, sums, arrived):
    out = (3, per_dev * BINS) if per_dev == GROUP else kept.shape
    return pl.pallas_call(
        functools.partial(finish_kernel, per_dev),
        out_shape=(
            jax.ShapeDtypeStruct((LEAVES // LANES, LANES), F32),
            jax.ShapeDtypeStruct(leaves.shape, F32),
            jax.ShapeDtypeStruct(out, F32),
        ),
        in_specs=[vmem()] * (3 + len(arrived)),
        out_specs=(vmem(), vmem(), vmem()),
        compiler_params=pltpu.CompilerParams(vmem_limit_bytes=VMEM_LIMIT),
        name="finish",
    )(leaves, kept, sums, *arrived)


def add_up(parts):
    while len(parts) > 1:
        parts = [parts[k] + parts[k + 1] for k in range(0, len(parts), 2)]
    return parts[0]


def local(scores, labels, leaves, bins, lengths, owner):
    query_count = lax.axis_size("query")
    feat_count = lax.axis_size("feat")
    count = query_count * feat_count
    place = lax.axis_index("query").astype(jnp.int32) * feat_count + lax.axis_index("feat").astype(jnp.int32)
    docs = scores.shape[0]
    own = docs // LANES
    features = owner.shape[0]
    per_dev = features // count
    unit = 3 * per_dev
    axes = ("query", "feat")
    feat_masks = [1 << b for b in range(feat_count.bit_length() - 1)]
    query_masks = [feat_count << b for b in range(query_count.bit_length() - 1)]

    def swap(value, mask):
        return lax.ppermute(value, axes, [(p, p ^ mask) for p in range(count)])

    pos = place.reshape(1)
    leaf_rows = leaves.reshape(own, LANES)
    own_scores = scores.reshape(own, LANES)
    score_parts = [own_scores]
    for begin in range(2):
        links = [(z, z + 1) for z in range(begin, feat_count - 1, 2)]
        score_parts.append(lax.ppermute(own_scores, "feat", links + [(b, a) for a, b in links]))
    masks = feat_masks + query_masks[:0:-1] + query_masks[:1]
    score_parts[0], qid, worth, inverse, perm, bounds = prepare(
        feat_count, masks, lengths, pos, labels.reshape(-1, LANES), owner.reshape(-1, LANES), own_scores)
    lambdas, near_lambdas = pair_terms(feat_count, bounds, pos, score_parts, worth, qid, inverse)
    bins_t, tiles, sums = leaf_terms(perm, bins, leaf_rows, near_lambdas)

    def part(tiles, low, high, *tail):
        if per_dev == GROUP:
            return histogram_part(low, high - low, tiles, bins_t, *tail)
        groups = high - low
        wide = histogram_part(low, groups, tiles, bins_t)
        wide = wide.reshape(groups, 3, HIGH, GROUP // per_dev, per_dev, LOW).transpose(0, 3, 1, 4, 2, 5)
        return jnp.concatenate([wide.reshape(groups * GROUP // per_dev * unit, BINS), *tail], axis=0)

    def join(block, total):
        return jnp.concatenate([block, total], axis=0)

    quarter = features // GROUP // 4
    edge = count // 4 * unit
    arrived = swap(part(tiles, 3 * quarter, 4 * quarter, sums), query_masks[0])
    far = part(tiles, quarter, 2 * quarter) + arrived[:edge]
    sums = sums + arrived[edge:]
    message, tiles = lax.optimization_barrier((join(far, sums), tiles))
    crossed = swap(message, query_masks[1])
    arrived = swap(part(tiles, 2 * quarter, 3 * quarter), query_masks[0])
    kept = part(tiles, 0, quarter) + arrived + crossed[:edge]
    sums = sums + crossed[edge:]
    for mask in query_masks[2:]:
        edge = edge // 2
        arrived = swap(join(kept[edge:], sums), mask)
        kept = kept[:edge] + arrived[:edge]
        sums = sums + arrived[edge:]
    arrived = [swap(join(kept[m * unit:(m + 1) * unit], sums), m) for m in range(1, feat_count)]
    values, step, histograms = finish(per_dev, leaf_rows, kept[:unit], sums, arrived)
    return lambdas, values.reshape(LEAVES), step.reshape(docs), histograms.reshape(3, per_dev * BINS)


def solution(mesh):
    in_specs = (
        P(("query", "feat")),
        P("query"),
        P(("query", "feat")),
        P(("query", "feat"), None),
        P("query", None),
        P(),
    )
    out_specs = (P(None, ("query", "feat")), P(), P(("query", "feat")), P(None, ("query", "feat")))
    return jax.shard_map(local, mesh=mesh, in_specs=in_specs, out_specs=out_specs, check_vma=False)
```

```python
import functools

import jax
import jax.numpy as jnp
from jax import lax
from jax.experimental import pallas as pl
from jax.experimental.pallas import tpu as pltpu
from jax.sharding import PartitionSpec as P

BINS = 256
LEAVES = 1024
LANES = 128
GRADES = 4
LOW = 32
HIGH = BINS // LOW
GROUP = 8
CHUNK = 64
MAX_LEN = 1024

lasso_penalty = 1.0
ridge_penalty = 1.0
shrinkage = 0.1

VMEM_LIMIT = 48 * 1024 * 1024
F32 = jnp.float32
BF16 = jnp.bfloat16
NT = (((1,), (1,)), ((), ()))


def iota(shape, axis):
    return lax.broadcasted_iota(jnp.int32, shape, axis)


def vmem():
    return pl.BlockSpec(memory_space=pltpu.VMEM)


def smem():
    return pl.BlockSpec(memory_space=pltpu.SMEM)


def prepare_kernel(feat_count, masks, len_ref, pos_ref, lab_ref, owner_ref, score_ref,
                   kept_ref, qid_ref, worth_ref, inv_ref, perm_ref, bounds_ref):
    kept_ref[...] = score_ref[...]
    queries = len_ref.shape[1]
    rows = lab_ref.shape[0]
    own = rows // feat_count
    spot = iota((rows, LANES), 0) * LANES + iota((rows, LANES), 1)
    qid = jnp.zeros((rows, LANES), jnp.int32)
    begin = jnp.zeros((queries, LANES), jnp.int32)
    finish = jnp.zeros((queries, LANES), jnp.int32)
    which = iota((queries, LANES), 0)
    start = jnp.int32(0)
    for q in range(queries):
        end = start + len_ref[0, q]
        qid = qid + jnp.where(spot >= end, 1, 0)
        begin = jnp.where(which == q, start, begin)
        finish = jnp.where(which == q, end, finish)

        def set_low(r, carry, start=start, end=end):
            bounds_ref[0, r] = start
            bounds_ref[2, r] = end
            return carry

        def set_high(r, carry, end=end):
            bounds_ref[1, r] = end
            return carry

        lax.fori_loop((start + LANES - 1) // LANES, (end + LANES - 1) // LANES, set_low, 0)
        lax.fori_loop(start // LANES, end // LANES, set_high, 0)
        start = end
    qid_ref[...] = qid
    worth_ref[...] = jnp.left_shift(1, lab_ref[...]).astype(F32)

    counts = [jnp.zeros((queries, LANES), F32) for _ in range(GRADES)]
    lane = iota((queries, LANES), 1)
    for r in range(rows):
        at = lane + r * LANES
        inside = (at >= begin) & (at < finish)
        grade = jnp.where(inside, jnp.broadcast_to(lab_ref[r:r + 1, :], (queries, LANES)), 0)
        for g in range(GRADES):
            counts[g] = counts[g] + jnp.where(grade > g, 1.0, 0.0)
    position = iota((queries, MAX_LEN), 1).astype(F32)
    gain = jnp.zeros((queries, MAX_LEN), F32)
    for g in range(GRADES):
        held = jnp.sum(counts[g], axis=1, keepdims=True)
        gain = gain + jnp.where(position < held, float(2 ** g), 0.0)
    level = 1.0 / jnp.log2(2.0 + position[0:1, :])
    ideal = jnp.sum(gain * level, axis=1, keepdims=True)
    usable = ideal > 0.5
    inverse = jnp.where(usable, 1.0 / jnp.where(usable, ideal, 1.0), 0.0)
    first = pos_ref[0] % feat_count * own
    for t in range(own):
        at = lane + (first + t) * LANES
        inside = (at >= begin) & (at < finish)
        inv_ref[0:1, t * LANES:(t + 1) * LANES] = jnp.sum(jnp.where(inside, inverse, 0.0), axis=0, keepdims=True)

    features = perm_ref.shape[0]
    per_dev = features >> len(masks)
    owner = jnp.concatenate([owner_ref[k:k + 1, :] for k in range(features // LANES)], axis=1)
    square = (features, features)
    down, across = iota(square, 0), iota(square, 1)
    index = iota((features, 1), 0) // per_dev
    target = jnp.zeros((features, 1), jnp.int32)
    for b, mask in enumerate(masks):
        target = target + ((index >> b) & 1) * mask
    target = (target ^ pos_ref[0]) * per_dev + iota((features, 1), 0) % per_dev
    pick = jnp.where(target == across, 1.0, 0.0).astype(BF16)
    holds = jnp.where(jnp.broadcast_to(owner, square) == down, 1.0, 0.0).astype(BF16)
    perm_ref[...] = lax.dot_general(pick, holds, NT, preferred_element_type=F32).astype(BF16)


def prepare(feat_count, masks, lengths, pos, labels, owner, scores):
    rows = labels.shape[0]
    features = owner.shape[0] * LANES
    return pl.pallas_call(
        functools.partial(prepare_kernel, feat_count, masks),
        out_shape=(
            jax.ShapeDtypeStruct(scores.shape, F32),
            jax.ShapeDtypeStruct((rows, LANES), jnp.int32),
            jax.ShapeDtypeStruct((rows, LANES), F32),
            jax.ShapeDtypeStruct((1, rows // feat_count * LANES), F32),
            jax.ShapeDtypeStruct((features, features), BF16),
            jax.ShapeDtypeStruct((3, rows), jnp.int32),
        ),
        in_specs=[smem(), smem(), vmem(), vmem(), vmem()],
        out_specs=(vmem(),) * 5 + (smem(),),
        compiler_params=pltpu.CompilerParams(vmem_limit_bytes=VMEM_LIMIT),
        cost_estimate=pl.CostEstimate(flops=2_000_000_000, bytes_accessed=300_000, transcendentals=20_000),
        name="prepare",
    )(lengths, pos, labels, owner, scores)


def split_terms(value, terms):
    parts = []
    rest = value
    for _ in range(terms):
        part = rest.astype(BF16)
        parts.append(part)
        rest = rest - part.astype(F32)
    return parts


def pairs_kernel(feat_count, bounds_ref, pos_ref, *refs):
    scores = refs[:-20]
    (worth_ref, qid_ref, inv_ref, lam_ref, near_ref,
     s_row, a_row, d_row, s_turn, a_turn, w_turn, q_turn, d_turn, s_col, a_col, w_col, q_col, d_col, grad, curv) = refs[-20:]
    rows = worth_ref.shape[0]
    own = rows // feat_count
    docs = own * LANES
    me = pos_ref[0] % feat_count
    s_row[...] = jnp.zeros(s_row.shape, F32)
    near = [me, me ^ 1, ((me + 1) ^ 1) - 1]
    for where, ref in zip(near, scores):
        @pl.when((where >= 0) & (where < feat_count))
        def _(where=where, ref=ref):
            s_row[pl.ds(pl.multiple_of(where * own, own), own), :] = ref[...]
    a_row[...] = jnp.exp(s_row[...])
    d_row[...] = jnp.zeros(d_row.shape, F32)
    first = me * own
    window_low = bounds_ref[0, first] // (2 * LANES) * 2
    window_high = (bounds_ref[1, first + own - 1] + 2 * LANES - 1) // (2 * LANES) * 2
    stride = 4

    def widen(pairs):
        for turn, source, _ in pairs:
            turn[...] = jnp.transpose(source[...])
        for r in range(0, rows, stride):
            @pl.when((r + stride > window_low) & (r < window_high))
            def _(r=r):
                for turn, _, col in pairs:
                    for k in range(r, r + stride):
                        col[k * LANES:(k + 1) * LANES, :] = jnp.broadcast_to(turn[:, k:k + 1], (LANES, LANES))

    widen([(s_turn, s_row, s_col), (q_turn, qid_ref, q_col), (a_turn, a_row, a_col), (w_turn, worth_ref, w_col)])

    def rows_of(ref, r):
        return [jnp.broadcast_to(ref[pl.ds(r + g, 1), :], (8, LANES)) for g in range(2)]

    def spans(r):
        start, end = bounds_ref[0, r], bounds_ref[1, r + 1]
        low = jnp.maximum(start // LANES, window_low)
        high = jnp.minimum((end + LANES - 1) // LANES, window_high)
        single = bounds_ref[2, r] >= (r + 2) * LANES
        inner_low = jnp.where(single, jnp.maximum((start + LANES - 1) // LANES, window_low), r)
        inner_high = jnp.where(single, jnp.minimum(end // LANES, window_high), r)
        return low, inner_low, inner_high, high

    def rank_groups(k, carry):
        r = window_low + 2 * k
        score = rows_of(s_row, r)
        query = rows_of(qid_ref, r)

        def gather(c, acc, masked, test):
            base = pl.multiple_of(c * LANES, LANES)
            acc = list(acc)
            for u in range(LANES // 8):
                other = s_col[pl.ds(base + 8 * u, 8), :]
                for g in range(2):
                    hit = test(other, g, u)
                    if masked:
                        hit = hit & (q_col[pl.ds(base + 8 * u, 8), :] == query[g])
                    acc[2 * g + u % 2] = acc[2 * g + u % 2] + jnp.where(hit, 1.0, 0.0)
            return tuple(acc)

        def ahead(other, g, u):
            return other >= score[g]

        def behind(other, g, u):
            return other > score[g]

        def within(mine):
            def test(other, g, u):
                if g != mine:
                    return ahead(other, g, u) if mine < g else behind(other, g, u)
                earlier = iota((8, LANES), 0) + 8 * u < iota((8, LANES), 1)
                return (other > score[g]) | ((other == score[g]) & earlier)
            return test

        acc = tuple(jnp.zeros((8, LANES), F32) for _ in range(4))
        low, inner_low, inner_high, high = spans(r)
        after = jnp.maximum(inner_high, r + 2)
        acc = lax.fori_loop(low, inner_low, lambda c, acc: gather(c, acc, True, ahead), acc)
        acc = lax.fori_loop(inner_low, r, lambda c, acc: gather(c, acc, False, ahead), acc)
        acc = lax.fori_loop(r + 2, after, lambda c, acc: gather(c, acc, False, behind), acc)
        acc = lax.fori_loop(after, high, lambda c, acc: gather(c, acc, True, behind), acc)
        for mine in range(2):
            acc = gather(r + mine, acc, True, within(mine))
        for g in range(2):
            d_row[pl.ds(r + g, 1), :] = jnp.sum(acc[2 * g] + acc[2 * g + 1], axis=0, keepdims=True)
        return carry

    lax.fori_loop(0, (window_high - window_low) // 2, rank_groups, 0)
    d_row[...] = 1.0 / jnp.log2(2.0 + d_row[...])
    widen([(d_turn, d_row, d_col)])

    def pair_groups(t, carry):
        r = first + 2 * t
        a_i, w_i, d_i, query = [rows_of(ref, r) for ref in (a_row, worth_ref, d_row, qid_ref)]

        def columns(masked):
            def step(c, acc):
                base = pl.multiple_of(c * LANES, LANES)
                acc = list(acc)
                for u in range(LANES // 8):
                    at = pl.ds(base + 8 * u, 8)
                    a_j, w_j, d_j = a_col[at, :], w_col[at, :], d_col[at, :]
                    for g in range(2):
                        recip = pl.reciprocal(a_i[g] + a_j, approx=True)
                        lift = w_i[g] - w_j
                        weight = jnp.abs(d_i[g] - d_j) * recip
                        if masked:
                            weight = jnp.where(q_col[at, :] == query[g], weight, 0.0)
                        weight = weight * lift
                        k = 4 * g + u % 2
                        acc[k] = acc[k] + weight * jnp.where(lift > 0.0, a_j, a_i[g])
                        acc[k + 2] = acc[k + 2] + jnp.abs(weight) * (recip * a_j)
                return tuple(acc)
            return step

        acc = tuple(jnp.zeros((8, LANES), F32) for _ in range(8))
        low, inner_low, inner_high, high = spans(r)
        acc = lax.fori_loop(low, inner_low, columns(True), acc)
        acc = lax.fori_loop(inner_low, inner_high, columns(False), acc)
        acc = lax.fori_loop(inner_high, high, columns(True), acc)
        for g in range(2):
            at = pl.ds(2 * t + g, 1)
            grad[at, :] = -jnp.sum(acc[4 * g] + acc[4 * g + 1], axis=0, keepdims=True)
            curv[at, :] = a_i[g][0:1, :] * jnp.sum(acc[4 * g + 2] + acc[4 * g + 3], axis=0, keepdims=True)
        return carry

    lax.fori_loop(0, own // 2, pair_groups, 0)
    inverse = inv_ref[...]
    terms = [inverse * jnp.concatenate([ref[t:t + 1, :] for t in range(own)], axis=1) for ref in (grad, curv)]
    for c in range(2):
        lam_ref[c:c + 1, :] = terms[c]
        near_ref[c:c + 1, :] = terms[c]


def pair_terms(feat_count, bounds, pos, scores, worth, qid, inverse):
    rows = worth.shape[0]
    docs = inverse.shape[1]
    row = pltpu.VMEM((rows, LANES), F32)
    turn = pltpu.VMEM((LANES, rows), F32)
    col = pltpu.VMEM((rows * LANES, LANES), F32)
    mine = pltpu.VMEM((docs // LANES, LANES), F32)
    return pl.pallas_call(
        functools.partial(pairs_kernel, feat_count),
        out_shape=(jax.ShapeDtypeStruct((2, docs), F32), jax.ShapeDtypeStruct((2, docs), F32)),
        in_specs=[smem(), smem()] + [vmem()] * (len(scores) + 3),
        out_specs=(vmem(), vmem()),
        scratch_shapes=[row, row, row, turn, turn, turn, pltpu.VMEM((LANES, rows), jnp.int32), turn,
                        col, col, col, pltpu.VMEM((rows * LANES, LANES), jnp.int32), col, mine, mine],
        compiler_params=pltpu.CompilerParams(vmem_limit_bytes=VMEM_LIMIT),
        cost_estimate=pl.CostEstimate(flops=9_000_000_000, bytes_accessed=200_000, transcendentals=2_000_000),
        name="pair_terms",
    )(bounds, pos, *scores, worth, qid, inverse)


def leaf_kernel(perm_ref, bins_ref, leaf_ref, lam_ref, bins_t_ref, tile_ref, sums_ref):
    bins = bins_ref[...].astype(F32).astype(BF16)
    bins_t_ref[...] = lax.dot_general(perm_ref[...], bins, NT, preferred_element_type=F32)
    own = leaf_ref.shape[0]
    docs = own * LANES
    leaf = jnp.concatenate([leaf_ref[t:t + 1, :] for t in range(own)], axis=1)
    highs = LEAVES // LANES
    top = jnp.broadcast_to(leaf // LANES, (highs, docs)) == iota((highs, docs), 0)
    spots = jnp.where(jnp.broadcast_to(leaf % LANES, (LANES, docs)) == iota((LANES, docs), 0), 1.0, 0.0).astype(BF16)
    pieces, tiles = [], []
    for c in range(2):
        for k, part in enumerate(split_terms(lam_ref[c:c + 1, :], 3)):
            wide = jnp.broadcast_to(part.astype(F32), (highs, docs))
            pieces.append(jnp.where(top, wide, 0.0))
            if k < 2:
                tiles.append(wide)
    tile_ref[...] = jnp.concatenate(tiles, axis=0).astype(BF16)
    stacked = jnp.concatenate(pieces, axis=0).astype(BF16)
    sums = lax.dot_general(stacked, spots, NT, preferred_element_type=F32)
    for c in range(2):
        base = c * 3 * highs
        sums_ref[:, c * LANES:(c + 1) * LANES] = (
            sums[base:base + highs] + (sums[base + highs:base + 2 * highs] + sums[base + 2 * highs:base + 3 * highs])
        )


def leaf_terms(perm, bins, leaves, lambdas):
    docs, features = bins.shape
    return pl.pallas_call(
        leaf_kernel,
        out_shape=(
            jax.ShapeDtypeStruct((features, docs), F32),
            jax.ShapeDtypeStruct((4 * HIGH, docs), BF16),
            jax.ShapeDtypeStruct((LEAVES // LANES, 2 * LANES), F32),
        ),
        in_specs=[vmem()] * 4,
        out_specs=(vmem(), vmem(), vmem()),
        compiler_params=pltpu.CompilerParams(vmem_limit_bytes=VMEM_LIMIT),
        cost_estimate=pl.CostEstimate(flops=200_000_000, bytes_accessed=3_000_000, transcendentals=0),
        name="leaf_terms",
    )(perm, bins, leaves, lambdas)


def histogram_kernel(first, groups, tile_ref, bins_ref, *refs):
    out_ref = refs[-1]
    docs = tile_ref.shape[1]
    depth = 256
    rows = 16
    row = iota((rows, depth), 0)
    low_level = [(row + rows * k).astype(F32).astype(BF16) for k in range(LOW // rows)]
    high_level = (row % HIGH).astype(F32).astype(BF16)
    upper = row < HIGH
    zero = jnp.zeros((rows, depth), BF16)
    one = jnp.ones((rows, depth), BF16)
    lane_owner = iota((1, GROUP * LOW), 1) // LOW

    def one_group(g, carry):
        base = pl.multiple_of((first + g) * GROUP, GROUP)
        acc = None
        for k in range(docs // depth):
            span = slice(k * depth, (k + 1) * depth)
            code = bins_ref[pl.ds(base, GROUP), span]
            high = jnp.floor(code * (1.0 / LOW))
            low = code - high * LOW
            left, right, count = [], [], []
            wide = []
            for f in range(GROUP):
                high_f = jnp.broadcast_to(high[f:f + 1, :], (rows, depth))
                low_f = jnp.broadcast_to(low[f:f + 1, :], (rows, depth)).astype(BF16)
                wide.append(high_f)
                match = high_f.astype(BF16) == high_level
                for c in range(2):
                    left.append(jnp.where(match, tile_ref[c * rows:(c + 1) * rows, span], zero))
                for level in low_level:
                    right.append(jnp.where(low_f == level, one, zero))
            for f in range(0, GROUP, 2):
                both = jnp.where(upper, wide[f], wide[f + 1]).astype(BF16)
                count.append(jnp.where(both == high_level, one, zero))
            part = lax.dot_general(
                jnp.concatenate(left + count, axis=0), jnp.concatenate(right, axis=0), NT,
                preferred_element_type=F32,
            )
            acc = part if acc is None else acc + part
        stats = jnp.zeros((2 * rows, GROUP * LOW), F32)
        counts = jnp.zeros((HIGH, GROUP * LOW), F32)
        for f in range(GROUP):
            mine = lane_owner == f
            stats = jnp.where(mine, acc[f * 2 * rows:(f + 1) * 2 * rows], stats)
            at = GROUP * 2 * rows + f * HIGH
            counts = jnp.where(mine, acc[at:at + HIGH], counts)
        out_ref[pl.ds(pl.multiple_of(g * 3 * HIGH, 3 * HIGH), 3 * HIGH), :] = jnp.concatenate(
            [stats[0:HIGH] + stats[HIGH:2 * HIGH], stats[2 * HIGH:3 * HIGH] + stats[3 * HIGH:4 * HIGH], counts], axis=0)
        return carry

    if len(refs) > 1:
        out_ref[groups * 3 * HIGH:, :] = refs[0][...]
    lax.fori_loop(0, groups, one_group, 0, unroll=2)


def histogram_part(first, groups, tiles, bins_t, *tail):
    rows = groups * 3 * HIGH + sum(piece.shape[0] for piece in tail)
    return pl.pallas_call(
        functools.partial(histogram_kernel, first, groups),
        out_shape=jax.ShapeDtypeStruct((rows, GROUP * LOW), F32),
        in_specs=[vmem()] * (2 + len(tail)),
        out_specs=vmem(),
        compiler_params=pltpu.CompilerParams(vmem_limit_bytes=VMEM_LIMIT),
        cost_estimate=pl.CostEstimate(flops=groups * 330_000_000, bytes_accessed=groups * 60_000, transcendentals=0),
        name="histogram_part",
    )(tiles, bins_t, *tail)


def finish_kernel(per_dev, leaf_ref, kept_ref, sums_ref, *refs):
    arrived = refs[:-3]
    value_ref, step_ref, hist_ref = refs[-3:]
    unit = kept_ref.shape[0]
    totals = add_up([sums_ref[...]] + [ref[unit:, :] for ref in arrived])
    highs = LEAVES // LANES
    grad, curv = totals[:, :LANES], totals[:, LANES:]
    shrunk = jnp.maximum(jnp.abs(grad) - lasso_penalty, 0.0)
    values = jnp.where(grad > 0.0, -shrunk, shrunk) / (curv + ridge_penalty)
    value_ref[...] = values
    leaf = leaf_ref[...]
    top, spot = leaf // LANES, leaf % LANES
    step = jnp.zeros(leaf.shape, F32)
    for h in range(highs):
        row = jnp.broadcast_to(values[h:h + 1, :], leaf.shape)
        step = jnp.where(top == h, jnp.take_along_axis(row, spot, axis=1), step)
    step_ref[...] = shrinkage * step
    hist = add_up([kept_ref[...]] + [ref[:unit, :] for ref in arrived])
    if per_dev == GROUP:
        for c in range(3):
            for f in range(GROUP):
                line = [hist[c * HIGH + h:c * HIGH + h + 1, f * LOW:(f + 1) * LOW] for h in range(HIGH)]
                hist_ref[c:c + 1, f * BINS:(f + 1) * BINS] = jnp.concatenate(line, axis=1)
    else:
        hist_ref[...] = hist


def finish(per_dev, leaves, kept, sums, arrived):
    out = (3, per_dev * BINS) if per_dev == GROUP else kept.shape
    return pl.pallas_call(
        functools.partial(finish_kernel, per_dev),
        out_shape=(
            jax.ShapeDtypeStruct((LEAVES // LANES, LANES), F32),
            jax.ShapeDtypeStruct(leaves.shape, F32),
            jax.ShapeDtypeStruct(out, F32),
        ),
        in_specs=[vmem()] * (3 + len(arrived)),
        out_specs=(vmem(), vmem(), vmem()),
        compiler_params=pltpu.CompilerParams(vmem_limit_bytes=VMEM_LIMIT),
        name="finish",
    )(leaves, kept, sums, *arrived)


def add_up(parts):
    while len(parts) > 1:
        parts = [parts[k] + parts[k + 1] for k in range(0, len(parts), 2)]
    return parts[0]


def local(scores, labels, leaves, bins, lengths, owner):
    query_count = lax.axis_size("query")
    feat_count = lax.axis_size("feat")
    count = query_count * feat_count
    place = lax.axis_index("query").astype(jnp.int32) * feat_count + lax.axis_index("feat").astype(jnp.int32)
    docs = scores.shape[0]
    own = docs // LANES
    features = owner.shape[0]
    per_dev = features // count
    unit = 3 * per_dev
    axes = ("query", "feat")
    feat_masks = [1 << b for b in range(feat_count.bit_length() - 1)]
    query_masks = [feat_count << b for b in range(query_count.bit_length() - 1)]

    def swap(value, mask):
        return lax.ppermute(value, axes, [(p, p ^ mask) for p in range(count)])

    pos = place.reshape(1)
    leaf_rows = leaves.reshape(own, LANES)
    own_scores = scores.reshape(own, LANES)
    score_parts = [own_scores]
    for begin in range(2):
        links = [(z, z + 1) for z in range(begin, feat_count - 1, 2)]
        score_parts.append(lax.ppermute(own_scores, "feat", links + [(b, a) for a, b in links]))
    masks = feat_masks + query_masks[:0:-1] + query_masks[:1]
    score_parts[0], qid, worth, inverse, perm, bounds = prepare(
        feat_count, masks, lengths, pos, labels.reshape(-1, LANES), owner.reshape(-1, LANES), own_scores)
    lambdas, near_lambdas = pair_terms(feat_count, bounds, pos, score_parts, worth, qid, inverse)
    bins_t, tiles, sums = leaf_terms(perm, bins, leaf_rows, near_lambdas)

    def part(tiles, low, high, *tail):
        if per_dev == GROUP:
            return histogram_part(low, high - low, tiles, bins_t, *tail)
        groups = high - low
        wide = histogram_part(low, groups, tiles, bins_t)
        wide = wide.reshape(groups, 3, HIGH, GROUP // per_dev, per_dev, LOW).transpose(0, 3, 1, 4, 2, 5)
        return jnp.concatenate([wide.reshape(groups * GROUP // per_dev * unit, BINS), *tail], axis=0)

    def join(block, total):
        return jnp.concatenate([block, total], axis=0)

    quarter = features // GROUP // 4
    edge = count // 4 * unit
    arrived = swap(part(tiles, 3 * quarter, 4 * quarter, sums), query_masks[0])
    far = part(tiles, quarter, 2 * quarter) + arrived[:edge]
    sums = sums + arrived[edge:]
    message, tiles = lax.optimization_barrier((join(far, sums), tiles))
    crossed = swap(message, query_masks[1])
    arrived = swap(part(tiles, 2 * quarter, 3 * quarter), query_masks[0])
    kept = part(tiles, 0, quarter) + arrived + crossed[:edge]
    sums = sums + crossed[edge:]
    for mask in query_masks[2:]:
        edge = edge // 2
        arrived = swap(join(kept[edge:], sums), mask)
        kept = kept[:edge] + arrived[:edge]
        sums = sums + arrived[edge:]
    arrived = [swap(join(kept[m * unit:(m + 1) * unit], sums), m) for m in range(1, feat_count)]
    values, step, histograms = finish(per_dev, leaf_rows, kept[:unit], sums, arrived)
    return lambdas, values.reshape(LEAVES), step.reshape(docs), histograms.reshape(3, per_dev * BINS)


def solution(mesh):
    in_specs = (
        P(("query", "feat")),
        P("query"),
        P(("query", "feat")),
        P(("query", "feat"), None),
        P("query", None),
        P(),
    )
    out_specs = (P(None, ("query", "feat")), P(), P(("query", "feat")), P(None, ("query", "feat")))
    return jax.shard_map(local, mesh=mesh, in_specs=in_specs, out_specs=out_specs, check_vma=False)
```

```python
import functools

import jax
import jax.numpy as jnp
from jax import lax
from jax.experimental import pallas as pl
from jax.experimental.pallas import tpu as pltpu
from jax.sharding import PartitionSpec as P

BINS = 256
LEAVES = 1024
LANES = 128
GRADES = 4
LOW = 32
HIGH = BINS // LOW
GROUP = 8
CHUNK = 64
MAX_LEN = 1024

lasso_penalty = 1.0
ridge_penalty = 1.0
shrinkage = 0.1

VMEM_LIMIT = 48 * 1024 * 1024
F32 = jnp.float32
BF16 = jnp.bfloat16
NT = (((1,), (1,)), ((), ()))


def iota(shape, axis):
    return lax.broadcasted_iota(jnp.int32, shape, axis)


def vmem():
    return pl.BlockSpec(memory_space=pltpu.VMEM)


def smem():
    return pl.BlockSpec(memory_space=pltpu.SMEM)


def prepare_kernel(feat_count, masks, len_ref, pos_ref, lab_ref, owner_ref, score_ref,
                   kept_ref, qid_ref, worth_ref, inv_ref, perm_ref, bounds_ref):
    kept_ref[...] = score_ref[...]
    queries = len_ref.shape[1]
    rows = lab_ref.shape[0]
    own = rows // feat_count
    spot = iota((rows, LANES), 0) * LANES + iota((rows, LANES), 1)
    qid = jnp.zeros((rows, LANES), jnp.int32)
    begin = jnp.zeros((queries, LANES), jnp.int32)
    finish = jnp.zeros((queries, LANES), jnp.int32)
    which = iota((queries, LANES), 0)
    start = jnp.int32(0)
    for q in range(queries):
        end = start + len_ref[0, q]
        qid = qid + jnp.where(spot >= end, 1, 0)
        begin = jnp.where(which == q, start, begin)
        finish = jnp.where(which == q, end, finish)

        def set_low(r, carry, start=start, end=end):
            bounds_ref[0, r] = start
            bounds_ref[2, r] = end
            return carry

        def set_high(r, carry, end=end):
            bounds_ref[1, r] = end
            return carry

        lax.fori_loop((start + LANES - 1) // LANES, (end + LANES - 1) // LANES, set_low, 0)
        lax.fori_loop(start // LANES, end // LANES, set_high, 0)
        start = end
    qid_ref[...] = qid
    worth_ref[...] = jnp.left_shift(1, lab_ref[...]).astype(F32)

    counts = [jnp.zeros((queries, LANES), F32) for _ in range(GRADES)]
    lane = iota((queries, LANES), 1)
    for r in range(rows):
        at = lane + r * LANES
        inside = (at >= begin) & (at < finish)
        grade = jnp.where(inside, jnp.broadcast_to(lab_ref[r:r + 1, :], (queries, LANES)), 0)
        for g in range(GRADES):
            counts[g] = counts[g] + jnp.where(grade > g, 1.0, 0.0)
    position = iota((queries, MAX_LEN), 1).astype(F32)
    gain = jnp.zeros((queries, MAX_LEN), F32)
    for g in range(GRADES):
        held = jnp.sum(counts[g], axis=1, keepdims=True)
        gain = gain + jnp.where(position < held, float(2 ** g), 0.0)
    level = 1.0 / jnp.log2(2.0 + position[0:1, :])
    ideal = jnp.sum(gain * level, axis=1, keepdims=True)
    usable = ideal > 0.5
    inverse = jnp.where(usable, 1.0 / jnp.where(usable, ideal, 1.0), 0.0)
    first = pos_ref[0] % feat_count * own
    for t in range(own):
        at = lane + (first + t) * LANES
        inside = (at >= begin) & (at < finish)
        inv_ref[0:1, t * LANES:(t + 1) * LANES] = jnp.sum(jnp.where(inside, inverse, 0.0), axis=0, keepdims=True)

    features = perm_ref.shape[0]
    per_dev = features >> len(masks)
    owner = jnp.concatenate([owner_ref[k:k + 1, :] for k in range(features // LANES)], axis=1)
    square = (features, features)
    down, across = iota(square, 0), iota(square, 1)
    index = iota((features, 1), 0) // per_dev
    target = jnp.zeros((features, 1), jnp.int32)
    for b, mask in enumerate(masks):
        target = target + ((index >> b) & 1) * mask
    target = (target ^ pos_ref[0]) * per_dev + iota((features, 1), 0) % per_dev
    pick = jnp.where(target == across, 1.0, 0.0).astype(BF16)
    holds = jnp.where(jnp.broadcast_to(owner, square) == down, 1.0, 0.0).astype(BF16)
    perm_ref[...] = lax.dot_general(pick, holds, NT, preferred_element_type=F32).astype(BF16)


def prepare(feat_count, masks, lengths, pos, labels, owner, scores):
    rows = labels.shape[0]
    features = owner.shape[0] * LANES
    return pl.pallas_call(
        functools.partial(prepare_kernel, feat_count, masks),
        out_shape=(
            jax.ShapeDtypeStruct(scores.shape, F32),
            jax.ShapeDtypeStruct((rows, LANES), jnp.int32),
            jax.ShapeDtypeStruct((rows, LANES), F32),
            jax.ShapeDtypeStruct((1, rows // feat_count * LANES), F32),
            jax.ShapeDtypeStruct((features, features), BF16),
            jax.ShapeDtypeStruct((3, rows), jnp.int32),
        ),
        in_specs=[smem(), smem(), vmem(), vmem(), vmem()],
        out_specs=(vmem(),) * 5 + (smem(),),
        compiler_params=pltpu.CompilerParams(vmem_limit_bytes=VMEM_LIMIT),
        cost_estimate=pl.CostEstimate(flops=2_000_000_000, bytes_accessed=300_000, transcendentals=20_000),
        name="prepare",
    )(lengths, pos, labels, owner, scores)


def split_terms(value, terms):
    parts = []
    rest = value
    for _ in range(terms):
        part = rest.astype(BF16)
        parts.append(part)
        rest = rest - part.astype(F32)
    return parts


def pairs_kernel(feat_count, bounds_ref, pos_ref, *refs):
    scores = refs[:-20]
    (worth_ref, qid_ref, inv_ref, lam_ref, near_ref,
     s_row, a_row, d_row, s_turn, a_turn, w_turn, q_turn, d_turn, s_col, a_col, w_col, q_col, d_col, grad, curv) = refs[-20:]
    rows = worth_ref.shape[0]
    own = rows // feat_count
    docs = own * LANES
    me = pos_ref[0] % feat_count
    s_row[...] = jnp.zeros(s_row.shape, F32)
    near = [me, me ^ 1, ((me + 1) ^ 1) - 1]
    for where, ref in zip(near, scores):
        @pl.when((where >= 0) & (where < feat_count))
        def _(where=where, ref=ref):
            s_row[pl.ds(pl.multiple_of(where * own, own), own), :] = ref[...]
    a_row[...] = jnp.exp(s_row[...])
    d_row[...] = jnp.zeros(d_row.shape, F32)
    first = me * own
    window_low = bounds_ref[0, first] // (2 * LANES) * 2
    window_high = (bounds_ref[1, first + own - 1] + 2 * LANES - 1) // (2 * LANES) * 2
    stride = 4

    def widen(pairs):
        for turn, source, _ in pairs:
            turn[...] = jnp.transpose(source[...])
        for r in range(0, rows, stride):
            @pl.when((r + stride > window_low) & (r < window_high))
            def _(r=r):
                for turn, _, col in pairs:
                    for k in range(r, r + stride):
                        col[k * LANES:(k + 1) * LANES, :] = jnp.broadcast_to(turn[:, k:k + 1], (LANES, LANES))

    widen([(s_turn, s_row, s_col), (q_turn, qid_ref, q_col), (a_turn, a_row, a_col), (w_turn, worth_ref, w_col)])

    def rows_of(ref, r):
        return [jnp.broadcast_to(ref[pl.ds(r + g, 1), :], (8, LANES)) for g in range(2)]

    def spans(r):
        start, end = bounds_ref[0, r], bounds_ref[1, r + 1]
        low = jnp.maximum(start // LANES, window_low)
        high = jnp.minimum((end + LANES - 1) // LANES, window_high)
        single = bounds_ref[2, r] >= (r + 2) * LANES
        inner_low = jnp.where(single, jnp.maximum((start + LANES - 1) // LANES, window_low), r)
        inner_high = jnp.where(single, jnp.minimum(end // LANES, window_high), r)
        return low, inner_low, inner_high, high

    def rank_groups(k, carry):
        r = window_low + 2 * k
        score = rows_of(s_row, r)
        query = rows_of(qid_ref, r)

        def gather(c, acc, masked, test):
            base = pl.multiple_of(c * LANES, LANES)
            acc = list(acc)
            for u in range(LANES // 8):
                other = s_col[pl.ds(base + 8 * u, 8), :]
                for g in range(2):
                    hit = test(other, g, u)
                    if masked:
                        hit = hit & (q_col[pl.ds(base + 8 * u, 8), :] == query[g])
                    acc[2 * g + u % 2] = acc[2 * g + u % 2] + jnp.where(hit, 1.0, 0.0)
            return tuple(acc)

        def ahead(other, g, u):
            return other >= score[g]

        def behind(other, g, u):
            return other > score[g]

        def within(mine):
            def test(other, g, u):
                if g != mine:
                    return ahead(other, g, u) if mine < g else behind(other, g, u)
                earlier = iota((8, LANES), 0) + 8 * u < iota((8, LANES), 1)
                return (other > score[g]) | ((other == score[g]) & earlier)
            return test

        acc = tuple(jnp.zeros((8, LANES), F32) for _ in range(4))
        low, inner_low, inner_high, high = spans(r)
        after = jnp.maximum(inner_high, r + 2)
        acc = lax.fori_loop(low, inner_low, lambda c, acc: gather(c, acc, True, ahead), acc)
        acc = lax.fori_loop(inner_low, r, lambda c, acc: gather(c, acc, False, ahead), acc)
        acc = lax.fori_loop(r + 2, after, lambda c, acc: gather(c, acc, False, behind), acc)
        acc = lax.fori_loop(after, high, lambda c, acc: gather(c, acc, True, behind), acc)
        for mine in range(2):
            acc = gather(r + mine, acc, True, within(mine))
        for g in range(2):
            d_row[pl.ds(r + g, 1), :] = jnp.sum(acc[2 * g] + acc[2 * g + 1], axis=0, keepdims=True)
        return carry

    lax.fori_loop(0, (window_high - window_low) // 2, rank_groups, 0)
    d_row[...] = 1.0 / jnp.log2(2.0 + d_row[...])
    widen([(d_turn, d_row, d_col)])

    def pair_groups(t, carry):
        r = first + 2 * t
        a_i, w_i, d_i, query = [rows_of(ref, r) for ref in (a_row, worth_ref, d_row, qid_ref)]

        def columns(masked):
            def step(c, acc):
                base = pl.multiple_of(c * LANES, LANES)
                acc = list(acc)
                for u in range(LANES // 8):
                    at = pl.ds(base + 8 * u, 8)
                    a_j, w_j, d_j = a_col[at, :], w_col[at, :], d_col[at, :]
                    for g in range(2):
                        recip = pl.reciprocal(a_i[g] + a_j, approx=True)
                        lift = w_i[g] - w_j
                        weight = jnp.abs(d_i[g] - d_j) * recip
                        if masked:
                            weight = jnp.where(q_col[at, :] == query[g], weight, 0.0)
                        weight = weight * lift
                        k = 4 * g + u % 2
                        acc[k] = acc[k] + weight * jnp.where(lift > 0.0, a_j, a_i[g])
                        acc[k + 2] = acc[k + 2] + jnp.abs(weight) * (recip * a_j)
                return tuple(acc)
            return step

        acc = tuple(jnp.zeros((8, LANES), F32) for _ in range(8))
        low, inner_low, inner_high, high = spans(r)
        acc = lax.fori_loop(low, inner_low, columns(True), acc)
        acc = lax.fori_loop(inner_low, inner_high, columns(False), acc)
        acc = lax.fori_loop(inner_high, high, columns(True), acc)
        for g in range(2):
            at = pl.ds(2 * t + g, 1)
            grad[at, :] = -jnp.sum(acc[4 * g] + acc[4 * g + 1], axis=0, keepdims=True)
            curv[at, :] = a_i[g][0:1, :] * jnp.sum(acc[4 * g + 2] + acc[4 * g + 3], axis=0, keepdims=True)
        return carry

    lax.fori_loop(0, own // 2, pair_groups, 0)
    inverse = inv_ref[...]
    terms = [inverse * jnp.concatenate([ref[t:t + 1, :] for t in range(own)], axis=1) for ref in (grad, curv)]
    for c in range(2):
        lam_ref[c:c + 1, :] = terms[c]
        near_ref[c:c + 1, :] = terms[c]


def pair_terms(feat_count, bounds, pos, scores, worth, qid, inverse):
    rows = worth.shape[0]
    docs = inverse.shape[1]
    row = pltpu.VMEM((rows, LANES), F32)
    turn = pltpu.VMEM((LANES, rows), F32)
    col = pltpu.VMEM((rows * LANES, LANES), F32)
    mine = pltpu.VMEM((docs // LANES, LANES), F32)
    return pl.pallas_call(
        functools.partial(pairs_kernel, feat_count),
        out_shape=(jax.ShapeDtypeStruct((2, docs), F32), jax.ShapeDtypeStruct((2, docs), F32)),
        in_specs=[smem(), smem()] + [vmem()] * (len(scores) + 3),
        out_specs=(vmem(), vmem()),
        scratch_shapes=[row, row, row, turn, turn, turn, pltpu.VMEM((LANES, rows), jnp.int32), turn,
                        col, col, col, pltpu.VMEM((rows * LANES, LANES), jnp.int32), col, mine, mine],
        compiler_params=pltpu.CompilerParams(vmem_limit_bytes=VMEM_LIMIT),
        cost_estimate=pl.CostEstimate(flops=9_000_000_000, bytes_accessed=200_000, transcendentals=2_000_000),
        name="pair_terms",
    )(bounds, pos, *scores, worth, qid, inverse)


def leaf_kernel(perm_ref, bins_ref, leaf_ref, lam_ref, bins_t_ref, tile_ref, sums_ref):
    bins = bins_ref[...].astype(F32).astype(BF16)
    bins_t_ref[...] = lax.dot_general(perm_ref[...], bins, NT, preferred_element_type=F32)
    own = leaf_ref.shape[0]
    docs = own * LANES
    leaf = jnp.concatenate([leaf_ref[t:t + 1, :] for t in range(own)], axis=1)
    highs = LEAVES // LANES
    top = jnp.broadcast_to(leaf // LANES, (highs, docs)) == iota((highs, docs), 0)
    spots = jnp.where(jnp.broadcast_to(leaf % LANES, (LANES, docs)) == iota((LANES, docs), 0), 1.0, 0.0).astype(BF16)
    pieces, tiles = [], []
    for c in range(2):
        for k, part in enumerate(split_terms(lam_ref[c:c + 1, :], 3)):
            wide = jnp.broadcast_to(part.astype(F32), (highs, docs))
            pieces.append(jnp.where(top, wide, 0.0))
            if k < 2:
                tiles.append(wide)
    tile_ref[...] = jnp.concatenate(tiles, axis=0).astype(BF16)
    stacked = jnp.concatenate(pieces, axis=0).astype(BF16)
    sums = lax.dot_general(stacked, spots, NT, preferred_element_type=F32)
    for c in range(2):
        base = c * 3 * highs
        sums_ref[:, c * LANES:(c + 1) * LANES] = (
            sums[base:base + highs] + (sums[base + highs:base + 2 * highs] + sums[base + 2 * highs:base + 3 * highs])
        )


def leaf_terms(perm, bins, leaves, lambdas):
    docs, features = bins.shape
    return pl.pallas_call(
        leaf_kernel,
        out_shape=(
            jax.ShapeDtypeStruct((features, docs), F32),
            jax.ShapeDtypeStruct((4 * HIGH, docs), BF16),
            jax.ShapeDtypeStruct((LEAVES // LANES, 2 * LANES), F32),
        ),
        in_specs=[vmem()] * 4,
        out_specs=(vmem(), vmem(), vmem()),
        compiler_params=pltpu.CompilerParams(vmem_limit_bytes=VMEM_LIMIT),
        cost_estimate=pl.CostEstimate(flops=200_000_000, bytes_accessed=3_000_000, transcendentals=0),
        name="leaf_terms",
    )(perm, bins, leaves, lambdas)


def histogram_kernel(first, groups, tile_ref, bins_ref, *refs):
    out_ref = refs[-1]
    docs = tile_ref.shape[1]
    depth = 256
    rows = 16
    row = iota((rows, depth), 0)
    low_level = [(row + rows * k).astype(F32).astype(BF16) for k in range(LOW // rows)]
    high_level = (row % HIGH).astype(F32).astype(BF16)
    upper = row < HIGH
    zero = jnp.zeros((rows, depth), BF16)
    one = jnp.ones((rows, depth), BF16)
    lane_owner = iota((1, GROUP * LOW), 1) // LOW

    def one_group(g, carry):
        base = pl.multiple_of((first + g) * GROUP, GROUP)
        acc = None
        for k in range(docs // depth):
            span = slice(k * depth, (k + 1) * depth)
            code = bins_ref[pl.ds(base, GROUP), span]
            high = jnp.floor(code * (1.0 / LOW))
            low = code - high * LOW
            left, right, count = [], [], []
            wide = []
            for f in range(GROUP):
                high_f = jnp.broadcast_to(high[f:f + 1, :], (rows, depth))
                low_f = jnp.broadcast_to(low[f:f + 1, :], (rows, depth)).astype(BF16)
                wide.append(high_f)
                match = high_f.astype(BF16) == high_level
                for c in range(2):
                    left.append(jnp.where(match, tile_ref[c * rows:(c + 1) * rows, span], zero))
                for level in low_level:
                    right.append(jnp.where(low_f == level, one, zero))
            for f in range(0, GROUP, 2):
                both = jnp.where(upper, wide[f], wide[f + 1]).astype(BF16)
                count.append(jnp.where(both == high_level, one, zero))
            part = lax.dot_general(
                jnp.concatenate(left + count, axis=0), jnp.concatenate(right, axis=0), NT,
                preferred_element_type=F32,
            )
            acc = part if acc is None else acc + part
        stats = jnp.zeros((2 * rows, GROUP * LOW), F32)
        counts = jnp.zeros((HIGH, GROUP * LOW), F32)
        for f in range(GROUP):
            mine = lane_owner == f
            stats = jnp.where(mine, acc[f * 2 * rows:(f + 1) * 2 * rows], stats)
            at = GROUP * 2 * rows + f * HIGH
            counts = jnp.where(mine, acc[at:at + HIGH], counts)
        out_ref[pl.ds(pl.multiple_of(g * 3 * HIGH, 3 * HIGH), 3 * HIGH), :] = jnp.concatenate(
            [stats[0:HIGH] + stats[HIGH:2 * HIGH], stats[2 * HIGH:3 * HIGH] + stats[3 * HIGH:4 * HIGH], counts], axis=0)
        return carry

    if len(refs) > 1:
        out_ref[groups * 3 * HIGH:, :] = refs[0][...]
    lax.fori_loop(0, groups, one_group, 0, unroll=2)


def histogram_part(first, groups, tiles, bins_t, *tail):
    rows = groups * 3 * HIGH + sum(piece.shape[0] for piece in tail)
    return pl.pallas_call(
        functools.partial(histogram_kernel, first, groups),
        out_shape=jax.ShapeDtypeStruct((rows, GROUP * LOW), F32),
        in_specs=[vmem()] * (2 + len(tail)),
        out_specs=vmem(),
        compiler_params=pltpu.CompilerParams(vmem_limit_bytes=VMEM_LIMIT),
        cost_estimate=pl.CostEstimate(flops=groups * 330_000_000, bytes_accessed=groups * 60_000, transcendentals=0),
        name="histogram_part",
    )(tiles, bins_t, *tail)


def finish_kernel(per_dev, leaf_ref, kept_ref, sums_ref, *refs):
    arrived = refs[:-3][::-1]
    value_ref, step_ref, hist_ref = refs[-3:]
    unit = kept_ref.shape[0]
    totals = add_up([sums_ref[...]] + [ref[unit:, :] for ref in arrived])
    highs = LEAVES // LANES
    grad, curv = totals[:, :LANES], totals[:, LANES:]
    shrunk = jnp.maximum(jnp.abs(grad) - lasso_penalty, 0.0)
    values = jnp.where(grad > 0.0, -shrunk, shrunk) / (curv + ridge_penalty)
    value_ref[...] = values
    leaf = leaf_ref[...]
    top, spot = leaf // LANES, leaf % LANES
    step = jnp.zeros(leaf.shape, F32)
    for h in range(highs):
        row = jnp.broadcast_to(values[h:h + 1, :], leaf.shape)
        step = jnp.where(top == h, jnp.take_along_axis(row, spot, axis=1), step)
    step_ref[...] = shrinkage * step
    hist = add_up([kept_ref[...]] + [ref[:unit, :] for ref in arrived])
    if per_dev == GROUP:
        for c in range(3):
            for f in range(GROUP):
                line = [hist[c * HIGH + h:c * HIGH + h + 1, f * LOW:(f + 1) * LOW] for h in range(HIGH)]
                hist_ref[c:c + 1, f * BINS:(f + 1) * BINS] = jnp.concatenate(line, axis=1)
    else:
        hist_ref[...] = hist


def finish(per_dev, leaves, kept, sums, arrived):
    out = (3, per_dev * BINS) if per_dev == GROUP else kept.shape
    return pl.pallas_call(
        functools.partial(finish_kernel, per_dev),
        out_shape=(
            jax.ShapeDtypeStruct((LEAVES // LANES, LANES), F32),
            jax.ShapeDtypeStruct(leaves.shape, F32),
            jax.ShapeDtypeStruct(out, F32),
        ),
        in_specs=[vmem()] * (3 + len(arrived)),
        out_specs=(vmem(), vmem(), vmem()),
        compiler_params=pltpu.CompilerParams(vmem_limit_bytes=VMEM_LIMIT),
        name="finish",
    )(leaves, kept, sums, *arrived)


def add_up(parts):
    while len(parts) > 1:
        parts = [parts[k] + parts[k + 1] for k in range(0, len(parts), 2)]
    return parts[0]


def local(scores, labels, leaves, bins, lengths, owner):
    query_count = lax.axis_size("query")
    feat_count = lax.axis_size("feat")
    count = query_count * feat_count
    place = lax.axis_index("query").astype(jnp.int32) * feat_count + lax.axis_index("feat").astype(jnp.int32)
    docs = scores.shape[0]
    own = docs // LANES
    features = owner.shape[0]
    per_dev = features // count
    unit = 3 * per_dev
    axes = ("query", "feat")
    feat_masks = [1 << b for b in range(feat_count.bit_length() - 1)]
    query_masks = [feat_count << b for b in range(query_count.bit_length() - 1)]

    def swap(value, mask):
        return lax.ppermute(value, axes, [(p, p ^ mask) for p in range(count)])

    pos = place.reshape(1)
    leaf_rows = leaves.reshape(own, LANES)
    own_scores = scores.reshape(own, LANES)
    score_parts = [own_scores]
    for begin in range(2):
        links = [(z, z + 1) for z in range(begin, feat_count - 1, 2)]
        ends = [(z, z) for z in (0, feat_count - 1)] if begin else []
        score_parts.append(lax.ppermute(own_scores, "feat", links + [(b, a) for a, b in links] + ends))
    masks = feat_masks + query_masks[:0:-1] + query_masks[:1]
    score_parts[0], qid, worth, inverse, perm, bounds = prepare(
        feat_count, masks, lengths, pos, labels.reshape(-1, LANES), owner.reshape(-1, LANES), own_scores)
    lambdas, near_lambdas = pair_terms(feat_count, bounds, pos, score_parts, worth, qid, inverse)
    bins_t, tiles, sums = leaf_terms(perm, bins, leaf_rows, near_lambdas)

    def part(tiles, low, high, *tail):
        if per_dev == GROUP:
            return histogram_part(low, high - low, tiles, bins_t, *tail)
        groups = high - low
        wide = histogram_part(low, groups, tiles, bins_t)
        wide = wide.reshape(groups, 3, HIGH, GROUP // per_dev, per_dev, LOW).transpose(0, 3, 1, 4, 2, 5)
        return jnp.concatenate([wide.reshape(groups * GROUP // per_dev * unit, BINS), *tail], axis=0)

    def join(block, total):
        return jnp.concatenate([block, total], axis=0)

    quarter = features // GROUP // 4
    edge = count // 4 * unit
    arrived = swap(part(tiles, 3 * quarter, 4 * quarter, sums), query_masks[0])
    far = part(tiles, quarter, 2 * quarter) + arrived[:edge]
    sums = sums + arrived[edge:]
    message, tiles = lax.optimization_barrier((join(far, sums), tiles))
    crossed = swap(message, query_masks[1])
    arrived = swap(part(tiles, 2 * quarter, 3 * quarter), query_masks[0])
    kept = part(tiles, 0, quarter) + arrived + crossed[:edge]
    sums = sums + crossed[edge:]
    for mask in query_masks[2:]:
        edge = edge // 2
        arrived = swap(join(kept[edge:], sums), mask)
        kept = kept[:edge] + arrived[:edge]
        sums = sums + arrived[edge:]
    arrived = [swap(join(kept[m * unit:(m + 1) * unit], sums), m) for m in range(1, feat_count)]
    values, step, histograms = finish(per_dev, leaf_rows, kept[:unit], sums, arrived[::-1])
    return lambdas, values.reshape(LEAVES), step.reshape(docs), histograms.reshape(3, per_dev * BINS)


def solution(mesh):
    in_specs = (
        P(("query", "feat")),
        P("query"),
        P(("query", "feat")),
        P(("query", "feat"), None),
        P("query", None),
        P(),
    )
    out_specs = (P(None, ("query", "feat")), P(), P(("query", "feat")), P(None, ("query", "feat")))
    return jax.shard_map(local, mesh=mesh, in_specs=in_specs, out_specs=out_specs, check_vma=False)
```

```python
import functools

import jax
import jax.numpy as jnp
from jax import lax
from jax.experimental import pallas as pl
from jax.experimental.pallas import tpu as pltpu
from jax.sharding import PartitionSpec as P

BINS = 256
LEAVES = 1024
LANES = 128
GRADES = 4
LOW = 32
HIGH = BINS // LOW
GROUP = 8
CHUNK = 64
MAX_LEN = 1024

lasso_penalty = 1.0
ridge_penalty = 1.0
shrinkage = 0.1

VMEM_LIMIT = 48 * 1024 * 1024
F32 = jnp.float32
BF16 = jnp.bfloat16
NT = (((1,), (1,)), ((), ()))


def iota(shape, axis):
    return lax.broadcasted_iota(jnp.int32, shape, axis)


def vmem():
    return pl.BlockSpec(memory_space=pltpu.VMEM)


def smem():
    return pl.BlockSpec(memory_space=pltpu.SMEM)


def stage_kernel(score_ref, first_ref, second_ref):
    first_ref[...] = score_ref[...]
    second_ref[...] = score_ref[...]


def stage(scores):
    return pl.pallas_call(
        stage_kernel,
        out_shape=(jax.ShapeDtypeStruct(scores.shape, F32),) * 2,
        in_specs=[vmem()],
        out_specs=(vmem(), vmem()),
        cost_estimate=pl.CostEstimate(flops=10_000_000_000, bytes_accessed=10_000, transcendentals=0),
        name="stage",
    )(scores)


def prepare_kernel(feat_count, masks, len_ref, pos_ref, lab_ref, owner_ref,
                   qid_ref, worth_ref, inv_ref, perm_ref, bounds_ref):
    queries = len_ref.shape[1]
    rows = lab_ref.shape[0]
    own = rows // feat_count
    spot = iota((rows, LANES), 0) * LANES + iota((rows, LANES), 1)
    qid = jnp.zeros((rows, LANES), jnp.int32)
    begin = jnp.zeros((queries, LANES), jnp.int32)
    finish = jnp.zeros((queries, LANES), jnp.int32)
    which = iota((queries, LANES), 0)
    start = jnp.int32(0)
    for q in range(queries):
        end = start + len_ref[0, q]
        qid = qid + jnp.where(spot >= end, 1, 0)
        begin = jnp.where(which == q, start, begin)
        finish = jnp.where(which == q, end, finish)

        def set_low(r, carry, start=start, end=end):
            bounds_ref[0, r] = start
            bounds_ref[2, r] = end
            return carry

        def set_high(r, carry, end=end):
            bounds_ref[1, r] = end
            return carry

        lax.fori_loop((start + LANES - 1) // LANES, (end + LANES - 1) // LANES, set_low, 0)
        lax.fori_loop(start // LANES, end // LANES, set_high, 0)
        start = end
    qid_ref[...] = qid
    worth_ref[...] = jnp.left_shift(1, lab_ref[...]).astype(F32)

    counts = [jnp.zeros((queries, LANES), F32) for _ in range(GRADES)]
    lane = iota((queries, LANES), 1)
    for r in range(rows):
        at = lane + r * LANES
        inside = (at >= begin) & (at < finish)
        grade = jnp.where(inside, jnp.broadcast_to(lab_ref[r:r + 1, :], (queries, LANES)), 0)
        for g in range(GRADES):
            counts[g] = counts[g] + jnp.where(grade > g, 1.0, 0.0)
    position = iota((queries, MAX_LEN), 1).astype(F32)
    gain = jnp.zeros((queries, MAX_LEN), F32)
    for g in range(GRADES):
        held = jnp.sum(counts[g], axis=1, keepdims=True)
        gain = gain + jnp.where(position < held, float(2 ** g), 0.0)
    level = 1.0 / jnp.log2(2.0 + position[0:1, :])
    ideal = jnp.sum(gain * level, axis=1, keepdims=True)
    usable = ideal > 0.5
    inverse = jnp.where(usable, 1.0 / jnp.where(usable, ideal, 1.0), 0.0)
    first = pos_ref[0] % feat_count * own
    for t in range(own):
        at = lane + (first + t) * LANES
        inside = (at >= begin) & (at < finish)
        inv_ref[0:1, t * LANES:(t + 1) * LANES] = jnp.sum(jnp.where(inside, inverse, 0.0), axis=0, keepdims=True)

    features = perm_ref.shape[0]
    per_dev = features >> len(masks)
    owner = jnp.concatenate([owner_ref[k:k + 1, :] for k in range(features // LANES)], axis=1)
    square = (features, features)
    down, across = iota(square, 0), iota(square, 1)
    index = iota((features, 1), 0) // per_dev
    target = jnp.zeros((features, 1), jnp.int32)
    for b, mask in enumerate(masks):
        target = target + ((index >> b) & 1) * mask
    target = (target ^ pos_ref[0]) * per_dev + iota((features, 1), 0) % per_dev
    pick = jnp.where(target == across, 1.0, 0.0).astype(BF16)
    holds = jnp.where(jnp.broadcast_to(owner, square) == down, 1.0, 0.0).astype(BF16)
    perm_ref[...] = lax.dot_general(pick, holds, NT, preferred_element_type=F32).astype(BF16)


def prepare(feat_count, masks, lengths, pos, labels, owner):
    rows = labels.shape[0]
    features = owner.shape[0] * LANES
    return pl.pallas_call(
        functools.partial(prepare_kernel, feat_count, masks),
        out_shape=(
            jax.ShapeDtypeStruct((rows, LANES), jnp.int32),
            jax.ShapeDtypeStruct((rows, LANES), F32),
            jax.ShapeDtypeStruct((1, rows // feat_count * LANES), F32),
            jax.ShapeDtypeStruct((features, features), BF16),
            jax.ShapeDtypeStruct((3, rows), jnp.int32),
        ),
        in_specs=[smem(), smem(), vmem(), vmem()],
        out_specs=(vmem(),) * 4 + (smem(),),
        compiler_params=pltpu.CompilerParams(vmem_limit_bytes=VMEM_LIMIT),
        cost_estimate=pl.CostEstimate(flops=2_000_000_000, bytes_accessed=300_000, transcendentals=20_000),
        name="prepare",
    )(lengths, pos, labels, owner)


def split_terms(value, terms):
    parts = []
    rest = value
    for _ in range(terms):
        part = rest.astype(BF16)
        parts.append(part)
        rest = rest - part.astype(F32)
    return parts


def pairs_kernel(feat_count, bounds_ref, pos_ref, *refs):
    scores = refs[:-20]
    (worth_ref, qid_ref, inv_ref, lam_ref, near_ref,
     s_row, a_row, d_row, s_turn, a_turn, w_turn, q_turn, d_turn, s_col, a_col, w_col, q_col, d_col, grad, curv) = refs[-20:]
    rows = worth_ref.shape[0]
    own = rows // feat_count
    docs = own * LANES
    me = pos_ref[0] % feat_count
    s_row[...] = jnp.zeros(s_row.shape, F32)
    near = [me, me ^ 1, ((me + 1) ^ 1) - 1]
    for where, ref in zip(near, scores):
        @pl.when((where >= 0) & (where < feat_count))
        def _(where=where, ref=ref):
            s_row[pl.ds(pl.multiple_of(where * own, own), own), :] = ref[...]
    a_row[...] = jnp.exp(s_row[...])
    d_row[...] = jnp.zeros(d_row.shape, F32)
    first = me * own
    window_low = bounds_ref[0, first] // (2 * LANES) * 2
    window_high = (bounds_ref[1, first + own - 1] + 2 * LANES - 1) // (2 * LANES) * 2
    stride = 4

    def widen(pairs):
        for turn, source, _ in pairs:
            turn[...] = jnp.transpose(source[...])
        for r in range(0, rows, stride):
            @pl.when((r + stride > window_low) & (r < window_high))
            def _(r=r):
                for turn, _, col in pairs:
                    for k in range(r, r + stride):
                        col[k * LANES:(k + 1) * LANES, :] = jnp.broadcast_to(turn[:, k:k + 1], (LANES, LANES))

    widen([(s_turn, s_row, s_col), (q_turn, qid_ref, q_col), (a_turn, a_row, a_col), (w_turn, worth_ref, w_col)])

    def rows_of(ref, r):
        return [jnp.broadcast_to(ref[pl.ds(r + g, 1), :], (8, LANES)) for g in range(2)]

    def spans(r):
        start, end = bounds_ref[0, r], bounds_ref[1, r + 1]
        low = jnp.maximum(start // LANES, window_low)
        high = jnp.minimum((end + LANES - 1) // LANES, window_high)
        single = bounds_ref[2, r] >= (r + 2) * LANES
        inner_low = jnp.where(single, jnp.maximum((start + LANES - 1) // LANES, window_low), r)
        inner_high = jnp.where(single, jnp.minimum(end // LANES, window_high), r)
        return low, inner_low, inner_high, high

    def rank_groups(k, carry):
        r = window_low + 2 * k
        score = rows_of(s_row, r)
        query = rows_of(qid_ref, r)

        def gather(c, acc, masked, test):
            base = pl.multiple_of(c * LANES, LANES)
            acc = list(acc)
            for u in range(LANES // 8):
                other = s_col[pl.ds(base + 8 * u, 8), :]
                for g in range(2):
                    hit = test(other, g, u)
                    if masked:
                        hit = hit & (q_col[pl.ds(base + 8 * u, 8), :] == query[g])
                    acc[2 * g + u % 2] = acc[2 * g + u % 2] + jnp.where(hit, 1.0, 0.0)
            return tuple(acc)

        def ahead(other, g, u):
            return other >= score[g]

        def behind(other, g, u):
            return other > score[g]

        def within(mine):
            def test(other, g, u):
                if g != mine:
                    return ahead(other, g, u) if mine < g else behind(other, g, u)
                earlier = iota((8, LANES), 0) + 8 * u < iota((8, LANES), 1)
                return (other > score[g]) | ((other == score[g]) & earlier)
            return test

        acc = tuple(jnp.zeros((8, LANES), F32) for _ in range(4))
        low, inner_low, inner_high, high = spans(r)
        after = jnp.maximum(inner_high, r + 2)
        acc = lax.fori_loop(low, inner_low, lambda c, acc: gather(c, acc, True, ahead), acc)
        acc = lax.fori_loop(inner_low, r, lambda c, acc: gather(c, acc, False, ahead), acc)
        acc = lax.fori_loop(r + 2, after, lambda c, acc: gather(c, acc, False, behind), acc)
        acc = lax.fori_loop(after, high, lambda c, acc: gather(c, acc, True, behind), acc)
        for mine in range(2):
            acc = gather(r + mine, acc, True, within(mine))
        for g in range(2):
            d_row[pl.ds(r + g, 1), :] = jnp.sum(acc[2 * g] + acc[2 * g + 1], axis=0, keepdims=True)
        return carry

    lax.fori_loop(0, (window_high - window_low) // 2, rank_groups, 0)
    d_row[...] = 1.0 / jnp.log2(2.0 + d_row[...])
    widen([(d_turn, d_row, d_col)])

    def pair_groups(t, carry):
        r = first + 2 * t
        a_i, w_i, d_i, query = [rows_of(ref, r) for ref in (a_row, worth_ref, d_row, qid_ref)]

        def columns(masked):
            def step(c, acc):
                base = pl.multiple_of(c * LANES, LANES)
                acc = list(acc)
                for u in range(LANES // 8):
                    at = pl.ds(base + 8 * u, 8)
                    a_j, w_j, d_j = a_col[at, :], w_col[at, :], d_col[at, :]
                    for g in range(2):
                        recip = pl.reciprocal(a_i[g] + a_j, approx=True)
                        lift = w_i[g] - w_j
                        weight = jnp.abs(d_i[g] - d_j) * recip
                        if masked:
                            weight = jnp.where(q_col[at, :] == query[g], weight, 0.0)
                        weight = weight * lift
                        k = 4 * g + u % 2
                        acc[k] = acc[k] + weight * jnp.where(lift > 0.0, a_j, a_i[g])
                        acc[k + 2] = acc[k + 2] + jnp.abs(weight) * (recip * a_j)
                return tuple(acc)
            return step

        acc = tuple(jnp.zeros((8, LANES), F32) for _ in range(8))
        low, inner_low, inner_high, high = spans(r)
        acc = lax.fori_loop(low, inner_low, columns(True), acc)
        acc = lax.fori_loop(inner_low, inner_high, columns(False), acc)
        acc = lax.fori_loop(inner_high, high, columns(True), acc)
        for g in range(2):
            at = pl.ds(2 * t + g, 1)
            grad[at, :] = -jnp.sum(acc[4 * g] + acc[4 * g + 1], axis=0, keepdims=True)
            curv[at, :] = a_i[g][0:1, :] * jnp.sum(acc[4 * g + 2] + acc[4 * g + 3], axis=0, keepdims=True)
        return carry

    lax.fori_loop(0, own // 2, pair_groups, 0)
    inverse = inv_ref[...]
    terms = [inverse * jnp.concatenate([ref[t:t + 1, :] for t in range(own)], axis=1) for ref in (grad, curv)]
    for c in range(2):
        lam_ref[c:c + 1, :] = terms[c]
        near_ref[c:c + 1, :] = terms[c]


def pair_terms(feat_count, bounds, pos, scores, worth, qid, inverse):
    rows = worth.shape[0]
    docs = inverse.shape[1]
    row = pltpu.VMEM((rows, LANES), F32)
    turn = pltpu.VMEM((LANES, rows), F32)
    col = pltpu.VMEM((rows * LANES, LANES), F32)
    mine = pltpu.VMEM((docs // LANES, LANES), F32)
    return pl.pallas_call(
        functools.partial(pairs_kernel, feat_count),
        out_shape=(jax.ShapeDtypeStruct((2, docs), F32), jax.ShapeDtypeStruct((2, docs), F32)),
        in_specs=[smem(), smem()] + [vmem()] * (len(scores) + 3),
        out_specs=(vmem(), vmem()),
        scratch_shapes=[row, row, row, turn, turn, turn, pltpu.VMEM((LANES, rows), jnp.int32), turn,
                        col, col, col, pltpu.VMEM((rows * LANES, LANES), jnp.int32), col, mine, mine],
        compiler_params=pltpu.CompilerParams(vmem_limit_bytes=VMEM_LIMIT),
        cost_estimate=pl.CostEstimate(flops=9_000_000_000, bytes_accessed=200_000, transcendentals=2_000_000),
        name="pair_terms",
    )(bounds, pos, *scores, worth, qid, inverse)


def leaf_kernel(perm_ref, bins_ref, leaf_ref, lam_ref, bins_t_ref, tile_ref, sums_ref):
    bins = bins_ref[...].astype(F32).astype(BF16)
    bins_t_ref[...] = lax.dot_general(perm_ref[...], bins, NT, preferred_element_type=F32)
    own = leaf_ref.shape[0]
    docs = own * LANES
    leaf = jnp.concatenate([leaf_ref[t:t + 1, :] for t in range(own)], axis=1)
    highs = LEAVES // LANES
    top = jnp.broadcast_to(leaf // LANES, (highs, docs)) == iota((highs, docs), 0)
    spots = jnp.where(jnp.broadcast_to(leaf % LANES, (LANES, docs)) == iota((LANES, docs), 0), 1.0, 0.0).astype(BF16)
    pieces, tiles = [], []
    for c in range(2):
        for k, part in enumerate(split_terms(lam_ref[c:c + 1, :], 3)):
            wide = jnp.broadcast_to(part.astype(F32), (highs, docs))
            pieces.append(jnp.where(top, wide, 0.0))
            if k < 2:
                tiles.append(wide)
    tile_ref[...] = jnp.concatenate(tiles, axis=0).astype(BF16)
    stacked = jnp.concatenate(pieces, axis=0).astype(BF16)
    sums = lax.dot_general(stacked, spots, NT, preferred_element_type=F32)
    for c in range(2):
        base = c * 3 * highs
        sums_ref[:, c * LANES:(c + 1) * LANES] = (
            sums[base:base + highs] + (sums[base + highs:base + 2 * highs] + sums[base + 2 * highs:base + 3 * highs])
        )


def leaf_terms(perm, bins, leaves, lambdas):
    docs, features = bins.shape
    return pl.pallas_call(
        leaf_kernel,
        out_shape=(
            jax.ShapeDtypeStruct((features, docs), F32),
            jax.ShapeDtypeStruct((4 * HIGH, docs), BF16),
            jax.ShapeDtypeStruct((LEAVES // LANES, 2 * LANES), F32),
        ),
        in_specs=[vmem()] * 4,
        out_specs=(vmem(), vmem(), vmem()),
        compiler_params=pltpu.CompilerParams(vmem_limit_bytes=VMEM_LIMIT),
        cost_estimate=pl.CostEstimate(flops=200_000_000, bytes_accessed=3_000_000, transcendentals=0),
        name="leaf_terms",
    )(perm, bins, leaves, lambdas)


def histogram_kernel(first, groups, tile_ref, bins_ref, *refs):
    out_ref = refs[-1]
    docs = tile_ref.shape[1]
    depth = 256
    rows = 16
    row = iota((rows, depth), 0)
    low_level = [(row + rows * k).astype(F32).astype(BF16) for k in range(LOW // rows)]
    high_level = (row % HIGH).astype(F32).astype(BF16)
    upper = row < HIGH
    zero = jnp.zeros((rows, depth), BF16)
    one = jnp.ones((rows, depth), BF16)
    lane_owner = iota((1, GROUP * LOW), 1) // LOW

    def one_group(g, carry):
        base = pl.multiple_of((first + g) * GROUP, GROUP)
        acc = None
        for k in range(docs // depth):
            span = slice(k * depth, (k + 1) * depth)
            code = bins_ref[pl.ds(base, GROUP), span]
            high = jnp.floor(code * (1.0 / LOW))
            low = code - high * LOW
            left, right, count = [], [], []
            wide = []
            for f in range(GROUP):
                high_f = jnp.broadcast_to(high[f:f + 1, :], (rows, depth))
                low_f = jnp.broadcast_to(low[f:f + 1, :], (rows, depth)).astype(BF16)
                wide.append(high_f)
                match = high_f.astype(BF16) == high_level
                for c in range(2):
                    left.append(jnp.where(match, tile_ref[c * rows:(c + 1) * rows, span], zero))
                for level in low_level:
                    right.append(jnp.where(low_f == level, one, zero))
            for f in range(0, GROUP, 2):
                both = jnp.where(upper, wide[f], wide[f + 1]).astype(BF16)
                count.append(jnp.where(both == high_level, one, zero))
            part = lax.dot_general(
                jnp.concatenate(left + count, axis=0), jnp.concatenate(right, axis=0), NT,
                preferred_element_type=F32,
            )
            acc = part if acc is None else acc + part
        stats = jnp.zeros((2 * rows, GROUP * LOW), F32)
        counts = jnp.zeros((HIGH, GROUP * LOW), F32)
        for f in range(GROUP):
            mine = lane_owner == f
            stats = jnp.where(mine, acc[f * 2 * rows:(f + 1) * 2 * rows], stats)
            at = GROUP * 2 * rows + f * HIGH
            counts = jnp.where(mine, acc[at:at + HIGH], counts)
        out_ref[pl.ds(pl.multiple_of(g * 3 * HIGH, 3 * HIGH), 3 * HIGH), :] = jnp.concatenate(
            [stats[0:HIGH] + stats[HIGH:2 * HIGH], stats[2 * HIGH:3 * HIGH] + stats[3 * HIGH:4 * HIGH], counts], axis=0)
        return carry

    if len(refs) > 1:
        out_ref[groups * 3 * HIGH:, :] = refs[0][...]
    lax.fori_loop(0, groups, one_group, 0, unroll=2)


def histogram_part(first, groups, tiles, bins_t, *tail):
    rows = groups * 3 * HIGH + sum(piece.shape[0] for piece in tail)
    return pl.pallas_call(
        functools.partial(histogram_kernel, first, groups),
        out_shape=jax.ShapeDtypeStruct((rows, GROUP * LOW), F32),
        in_specs=[vmem()] * (2 + len(tail)),
        out_specs=vmem(),
        compiler_params=pltpu.CompilerParams(vmem_limit_bytes=VMEM_LIMIT),
        cost_estimate=pl.CostEstimate(flops=groups * 330_000_000, bytes_accessed=groups * 60_000, transcendentals=0),
        name="histogram_part",
    )(tiles, bins_t, *tail)


def finish_kernel(per_dev, leaf_ref, kept_ref, sums_ref, *refs):
    arrived = refs[:-3][::-1]
    value_ref, step_ref, hist_ref = refs[-3:]
    unit = kept_ref.shape[0]
    totals = add_up([sums_ref[...]] + [ref[unit:, :] for ref in arrived])
    highs = LEAVES // LANES
    grad, curv = totals[:, :LANES], totals[:, LANES:]
    shrunk = jnp.maximum(jnp.abs(grad) - lasso_penalty, 0.0)
    values = jnp.where(grad > 0.0, -shrunk, shrunk) / (curv + ridge_penalty)
    value_ref[...] = values
    leaf = leaf_ref[...]
    top, spot = leaf // LANES, leaf % LANES
    step = jnp.zeros(leaf.shape, F32)
    for h in range(highs):
        row = jnp.broadcast_to(values[h:h + 1, :], leaf.shape)
        step = jnp.where(top == h, jnp.take_along_axis(row, spot, axis=1), step)
    step_ref[...] = shrinkage * step
    hist = add_up([kept_ref[...]] + [ref[:unit, :] for ref in arrived])
    if per_dev == GROUP:
        for c in range(3):
            for f in range(GROUP):
                line = [hist[c * HIGH + h:c * HIGH + h + 1, f * LOW:(f + 1) * LOW] for h in range(HIGH)]
                hist_ref[c:c + 1, f * BINS:(f + 1) * BINS] = jnp.concatenate(line, axis=1)
    else:
        hist_ref[...] = hist


def finish(per_dev, leaves, kept, sums, arrived):
    out = (3, per_dev * BINS) if per_dev == GROUP else kept.shape
    return pl.pallas_call(
        functools.partial(finish_kernel, per_dev),
        out_shape=(
            jax.ShapeDtypeStruct((LEAVES // LANES, LANES), F32),
            jax.ShapeDtypeStruct(leaves.shape, F32),
            jax.ShapeDtypeStruct(out, F32),
        ),
        in_specs=[vmem()] * (3 + len(arrived)),
        out_specs=(vmem(), vmem(), vmem()),
        compiler_params=pltpu.CompilerParams(vmem_limit_bytes=VMEM_LIMIT),
        name="finish",
    )(leaves, kept, sums, *arrived)


def add_up(parts):
    while len(parts) > 1:
        parts = [parts[k] + parts[k + 1] for k in range(0, len(parts), 2)]
    return parts[0]


def local(scores, labels, leaves, bins, lengths, owner):
    query_count = lax.axis_size("query")
    feat_count = lax.axis_size("feat")
    count = query_count * feat_count
    place = lax.axis_index("query").astype(jnp.int32) * feat_count + lax.axis_index("feat").astype(jnp.int32)
    docs = scores.shape[0]
    own = docs // LANES
    features = owner.shape[0]
    per_dev = features // count
    unit = 3 * per_dev
    axes = ("query", "feat")
    feat_masks = [1 << b for b in range(feat_count.bit_length() - 1)]
    query_masks = [feat_count << b for b in range(query_count.bit_length() - 1)]

    def swap(value, mask):
        return lax.ppermute(value, axes, [(p, p ^ mask) for p in range(count)])

    pos = place.reshape(1)
    leaf_rows = leaves.reshape(own, LANES)
    first_scores, second_scores = stage(scores.reshape(own, LANES))
    score_parts = [first_scores]
    for begin, own_scores in enumerate((first_scores, second_scores)):
        links = [(z, z + 1) for z in range(begin, feat_count - 1, 2)]
        ends = [(z, z) for z in (0, feat_count - 1)] if begin else []
        score_parts.append(lax.ppermute(own_scores, "feat", links + [(b, a) for a, b in links] + ends))
    masks = feat_masks + query_masks[:0:-1] + query_masks[:1]
    qid, worth, inverse, perm, bounds = prepare(
        feat_count, masks, lengths, pos, labels.reshape(-1, LANES), owner.reshape(-1, LANES))
    lambdas, near_lambdas = pair_terms(feat_count, bounds, pos, score_parts, worth, qid, inverse)
    bins_t, tiles, sums = leaf_terms(perm, bins, leaf_rows, near_lambdas)

    def part(tiles, low, high, *tail):
        if per_dev == GROUP:
            return histogram_part(low, high - low, tiles, bins_t, *tail)
        groups = high - low
        wide = histogram_part(low, groups, tiles, bins_t)
        wide = wide.reshape(groups, 3, HIGH, GROUP // per_dev, per_dev, LOW).transpose(0, 3, 1, 4, 2, 5)
        return jnp.concatenate([wide.reshape(groups * GROUP // per_dev * unit, BINS), *tail], axis=0)

    def join(block, total):
        return jnp.concatenate([block, total], axis=0)

    quarter = features // GROUP // 4
    edge = count // 4 * unit
    arrived = swap(part(tiles, 3 * quarter, 4 * quarter, sums), query_masks[0])
    far = part(tiles, quarter, 2 * quarter) + arrived[:edge]
    sums = sums + arrived[edge:]
    message, tiles = lax.optimization_barrier((join(far, sums), tiles))
    crossed = swap(message, query_masks[1])
    arrived = swap(part(tiles, 2 * quarter, 3 * quarter), query_masks[0])
    kept = part(tiles, 0, quarter) + arrived + crossed[:edge]
    sums = sums + crossed[edge:]
    for mask in query_masks[2:]:
        edge = edge // 2
        arrived = swap(join(kept[edge:], sums), mask)
        kept = kept[:edge] + arrived[:edge]
        sums = sums + arrived[edge:]
    arrived = [swap(join(kept[m * unit:(m + 1) * unit], sums), m) for m in range(1, feat_count)]
    values, step, histograms = finish(per_dev, leaf_rows, kept[:unit], sums, arrived[::-1])
    return lambdas, values.reshape(LEAVES), step.reshape(docs), histograms.reshape(3, per_dev * BINS)


def solution(mesh):
    in_specs = (
        P(("query", "feat")),
        P("query"),
        P(("query", "feat")),
        P(("query", "feat"), None),
        P("query", None),
        P(),
    )
    out_specs = (P(None, ("query", "feat")), P(), P(("query", "feat")), P(None, ("query", "feat")))
    return jax.shard_map(local, mesh=mesh, in_specs=in_specs, out_specs=out_specs, check_vma=False)
```

```python
import functools

import jax
import jax.numpy as jnp
from jax import lax
from jax.experimental import pallas as pl
from jax.experimental.pallas import tpu as pltpu
from jax.sharding import PartitionSpec as P

BINS = 256
LEAVES = 1024
LANES = 128
GRADES = 4
LOW = 32
HIGH = BINS // LOW
GROUP = 8
CHUNK = 64
MAX_LEN = 1024

lasso_penalty = 1.0
ridge_penalty = 1.0
shrinkage = 0.1

VMEM_LIMIT = 48 * 1024 * 1024
F32 = jnp.float32
BF16 = jnp.bfloat16
NT = (((1,), (1,)), ((), ()))


def iota(shape, axis):
    return lax.broadcasted_iota(jnp.int32, shape, axis)


def vmem():
    return pl.BlockSpec(memory_space=pltpu.VMEM)


def smem():
    return pl.BlockSpec(memory_space=pltpu.SMEM)


def prepare_kernel(feat_count, masks, len_ref, pos_ref, lab_ref, owner_ref, score_ref,
                   kept_ref, qid_ref, worth_ref, inv_ref, perm_ref, bounds_ref):
    kept_ref[...] = score_ref[...]
    queries = len_ref.shape[1]
    rows = lab_ref.shape[0]
    own = rows // feat_count
    spot = iota((rows, LANES), 0) * LANES + iota((rows, LANES), 1)
    qid = jnp.zeros((rows, LANES), jnp.int32)
    begin = jnp.zeros((queries, LANES), jnp.int32)
    finish = jnp.zeros((queries, LANES), jnp.int32)
    which = iota((queries, LANES), 0)
    start = jnp.int32(0)
    for q in range(queries):
        end = start + len_ref[0, q]
        qid = qid + jnp.where(spot >= end, 1, 0)
        begin = jnp.where(which == q, start, begin)
        finish = jnp.where(which == q, end, finish)

        def set_low(r, carry, start=start, end=end):
            bounds_ref[0, r] = start
            bounds_ref[2, r] = end
            return carry

        def set_high(r, carry, end=end):
            bounds_ref[1, r] = end
            return carry

        lax.fori_loop((start + LANES - 1) // LANES, (end + LANES - 1) // LANES, set_low, 0)
        lax.fori_loop(start // LANES, end // LANES, set_high, 0)
        start = end
    qid_ref[...] = qid
    worth_ref[...] = jnp.left_shift(1, lab_ref[...]).astype(F32)

    counts = [jnp.zeros((queries, LANES), F32) for _ in range(GRADES)]
    lane = iota((queries, LANES), 1)
    for r in range(rows):
        at = lane + r * LANES
        inside = (at >= begin) & (at < finish)
        grade = jnp.where(inside, jnp.broadcast_to(lab_ref[r:r + 1, :], (queries, LANES)), 0)
        for g in range(GRADES):
            counts[g] = counts[g] + jnp.where(grade > g, 1.0, 0.0)
    position = iota((queries, MAX_LEN), 1).astype(F32)
    gain = jnp.zeros((queries, MAX_LEN), F32)
    for g in range(GRADES):
        held = jnp.sum(counts[g], axis=1, keepdims=True)
        gain = gain + jnp.where(position < held, float(2 ** g), 0.0)
    level = 1.0 / jnp.log2(2.0 + position[0:1, :])
    ideal = jnp.sum(gain * level, axis=1, keepdims=True)
    usable = ideal > 0.5
    inverse = jnp.where(usable, 1.0 / jnp.where(usable, ideal, 1.0), 0.0)
    first = pos_ref[0] % feat_count * own
    for t in range(own):
        at = lane + (first + t) * LANES
        inside = (at >= begin) & (at < finish)
        inv_ref[0:1, t * LANES:(t + 1) * LANES] = jnp.sum(jnp.where(inside, inverse, 0.0), axis=0, keepdims=True)

    features = perm_ref.shape[0]
    per_dev = features >> len(masks)
    owner = jnp.concatenate([owner_ref[k:k + 1, :] for k in range(features // LANES)], axis=1)
    square = (features, features)
    down, across = iota(square, 0), iota(square, 1)
    index = iota((features, 1), 0) // per_dev
    target = jnp.zeros((features, 1), jnp.int32)
    for b, mask in enumerate(masks):
        target = target + ((index >> b) & 1) * mask
    target = (target ^ pos_ref[0]) * per_dev + iota((features, 1), 0) % per_dev
    pick = jnp.where(target == across, 1.0, 0.0).astype(BF16)
    holds = jnp.where(jnp.broadcast_to(owner, square) == down, 1.0, 0.0).astype(BF16)
    perm_ref[...] = lax.dot_general(pick, holds, NT, preferred_element_type=F32).astype(BF16)


def prepare(feat_count, masks, lengths, pos, labels, owner, scores):
    rows = labels.shape[0]
    features = owner.shape[0] * LANES
    return pl.pallas_call(
        functools.partial(prepare_kernel, feat_count, masks),
        out_shape=(
            jax.ShapeDtypeStruct(scores.shape, F32),
            jax.ShapeDtypeStruct((rows, LANES), jnp.int32),
            jax.ShapeDtypeStruct((rows, LANES), F32),
            jax.ShapeDtypeStruct((1, rows // feat_count * LANES), F32),
            jax.ShapeDtypeStruct((features, features), BF16),
            jax.ShapeDtypeStruct((3, rows), jnp.int32),
        ),
        in_specs=[smem(), smem(), vmem(), vmem(), vmem()],
        out_specs=(vmem(),) * 5 + (smem(),),
        compiler_params=pltpu.CompilerParams(vmem_limit_bytes=VMEM_LIMIT),
        cost_estimate=pl.CostEstimate(flops=2_000_000_000, bytes_accessed=300_000, transcendentals=20_000),
        name="prepare",
    )(lengths, pos, labels, owner, scores)


def split_terms(value, terms):
    parts = []
    rest = value
    for _ in range(terms):
        part = rest.astype(BF16)
        parts.append(part)
        rest = rest - part.astype(F32)
    return parts


def pairs_kernel(feat_count, bounds_ref, pos_ref, *refs):
    scores = refs[:-20]
    (worth_ref, qid_ref, inv_ref, lam_ref, near_ref,
     s_row, a_row, d_row, s_turn, a_turn, w_turn, q_turn, d_turn, s_col, a_col, w_col, q_col, d_col, grad, curv) = refs[-20:]
    rows = worth_ref.shape[0]
    own = rows // feat_count
    docs = own * LANES
    me = pos_ref[0] % feat_count
    s_row[...] = jnp.zeros(s_row.shape, F32)
    near = [me, me ^ 1, ((me + 1) ^ 1) - 1]
    for where, ref in zip(near, scores):
        @pl.when((where >= 0) & (where < feat_count))
        def _(where=where, ref=ref):
            s_row[pl.ds(pl.multiple_of(where * own, own), own), :] = ref[...]
    a_row[...] = jnp.exp(s_row[...])
    d_row[...] = jnp.zeros(d_row.shape, F32)
    first = me * own
    window_low = bounds_ref[0, first] // (2 * LANES) * 2
    window_high = (bounds_ref[1, first + own - 1] + 2 * LANES - 1) // (2 * LANES) * 2
    stride = 4

    def widen(pairs):
        for turn, source, _ in pairs:
            turn[...] = jnp.transpose(source[...])
        for r in range(0, rows, stride):
            @pl.when((r + stride > window_low) & (r < window_high))
            def _(r=r):
                for turn, _, col in pairs:
                    for k in range(r, r + stride):
                        col[k * LANES:(k + 1) * LANES, :] = jnp.broadcast_to(turn[:, k:k + 1], (LANES, LANES))

    widen([(s_turn, s_row, s_col), (q_turn, qid_ref, q_col), (a_turn, a_row, a_col), (w_turn, worth_ref, w_col)])

    def rows_of(ref, r):
        return [jnp.broadcast_to(ref[pl.ds(r + g, 1), :], (8, LANES)) for g in range(2)]

    def spans(r):
        start, end = bounds_ref[0, r], bounds_ref[1, r + 1]
        low = jnp.maximum(start // LANES, window_low)
        high = jnp.minimum((end + LANES - 1) // LANES, window_high)
        single = bounds_ref[2, r] >= (r + 2) * LANES
        inner_low = jnp.where(single, jnp.maximum((start + LANES - 1) // LANES, window_low), r)
        inner_high = jnp.where(single, jnp.minimum(end // LANES, window_high), r)
        return low, inner_low, inner_high, high

    def rank_groups(k, carry):
        r = window_low + 2 * k
        score = rows_of(s_row, r)
        query = rows_of(qid_ref, r)

        def gather(c, acc, masked, test):
            base = pl.multiple_of(c * LANES, LANES)
            acc = list(acc)
            for u in range(LANES // 8):
                other = s_col[pl.ds(base + 8 * u, 8), :]
                for g in range(2):
                    hit = test(other, g, u)
                    if masked:
                        hit = hit & (q_col[pl.ds(base + 8 * u, 8), :] == query[g])
                    acc[2 * g + u % 2] = acc[2 * g + u % 2] + jnp.where(hit, 1.0, 0.0)
            return tuple(acc)

        def ahead(other, g, u):
            return other >= score[g]

        def behind(other, g, u):
            return other > score[g]

        def within(mine):
            def test(other, g, u):
                if g != mine:
                    return ahead(other, g, u) if mine < g else behind(other, g, u)
                earlier = iota((8, LANES), 0) + 8 * u < iota((8, LANES), 1)
                return (other > score[g]) | ((other == score[g]) & earlier)
            return test

        acc = tuple(jnp.zeros((8, LANES), F32) for _ in range(4))
        low, inner_low, inner_high, high = spans(r)
        after = jnp.maximum(inner_high, r + 2)
        acc = lax.fori_loop(low, inner_low, lambda c, acc: gather(c, acc, True, ahead), acc)
        acc = lax.fori_loop(inner_low, r, lambda c, acc: gather(c, acc, False, ahead), acc)
        acc = lax.fori_loop(r + 2, after, lambda c, acc: gather(c, acc, False, behind), acc)
        acc = lax.fori_loop(after, high, lambda c, acc: gather(c, acc, True, behind), acc)
        for mine in range(2):
            acc = gather(r + mine, acc, True, within(mine))
        for g in range(2):
            d_row[pl.ds(r + g, 1), :] = jnp.sum(acc[2 * g] + acc[2 * g + 1], axis=0, keepdims=True)
        return carry

    lax.fori_loop(0, (window_high - window_low) // 2, rank_groups, 0)
    d_row[...] = 1.0 / jnp.log2(2.0 + d_row[...])
    widen([(d_turn, d_row, d_col)])

    def pair_groups(t, carry):
        r = first + 2 * t
        a_i, w_i, d_i, query = [rows_of(ref, r) for ref in (a_row, worth_ref, d_row, qid_ref)]

        def columns(masked):
            def step(c, acc):
                base = pl.multiple_of(c * LANES, LANES)
                acc = list(acc)
                for u in range(LANES // 8):
                    at = pl.ds(base + 8 * u, 8)
                    a_j, w_j, d_j = a_col[at, :], w_col[at, :], d_col[at, :]
                    for g in range(2):
                        recip = pl.reciprocal(a_i[g] + a_j, approx=True)
                        lift = w_i[g] - w_j
                        weight = jnp.abs(d_i[g] - d_j) * recip
                        if masked:
                            weight = jnp.where(q_col[at, :] == query[g], weight, 0.0)
                        weight = weight * lift
                        k = 4 * g + u % 2
                        acc[k] = acc[k] + weight * jnp.where(lift > 0.0, a_j, a_i[g])
                        acc[k + 2] = acc[k + 2] + jnp.abs(weight) * (recip * a_j)
                return tuple(acc)
            return step

        acc = tuple(jnp.zeros((8, LANES), F32) for _ in range(8))
        low, inner_low, inner_high, high = spans(r)
        acc = lax.fori_loop(low, inner_low, columns(True), acc)
        acc = lax.fori_loop(inner_low, inner_high, columns(False), acc)
        acc = lax.fori_loop(inner_high, high, columns(True), acc)
        for g in range(2):
            at = pl.ds(2 * t + g, 1)
            grad[at, :] = -jnp.sum(acc[4 * g] + acc[4 * g + 1], axis=0, keepdims=True)
            curv[at, :] = a_i[g][0:1, :] * jnp.sum(acc[4 * g + 2] + acc[4 * g + 3], axis=0, keepdims=True)
        return carry

    lax.fori_loop(0, own // 2, pair_groups, 0)
    inverse = inv_ref[...]
    terms = [inverse * jnp.concatenate([ref[t:t + 1, :] for t in range(own)], axis=1) for ref in (grad, curv)]
    for c in range(2):
        lam_ref[c:c + 1, :] = terms[c]
        near_ref[c:c + 1, :] = terms[c]


def pair_terms(feat_count, bounds, pos, scores, worth, qid, inverse):
    rows = worth.shape[0]
    docs = inverse.shape[1]
    row = pltpu.VMEM((rows, LANES), F32)
    turn = pltpu.VMEM((LANES, rows), F32)
    col = pltpu.VMEM((rows * LANES, LANES), F32)
    mine = pltpu.VMEM((docs // LANES, LANES), F32)
    return pl.pallas_call(
        functools.partial(pairs_kernel, feat_count),
        out_shape=(jax.ShapeDtypeStruct((2, docs), F32), jax.ShapeDtypeStruct((2, docs), F32)),
        in_specs=[smem(), smem()] + [vmem()] * (len(scores) + 3),
        out_specs=(vmem(), vmem()),
        scratch_shapes=[row, row, row, turn, turn, turn, pltpu.VMEM((LANES, rows), jnp.int32), turn,
                        col, col, col, pltpu.VMEM((rows * LANES, LANES), jnp.int32), col, mine, mine],
        compiler_params=pltpu.CompilerParams(vmem_limit_bytes=VMEM_LIMIT),
        cost_estimate=pl.CostEstimate(flops=9_000_000_000, bytes_accessed=200_000, transcendentals=2_000_000),
        name="pair_terms",
    )(bounds, pos, *scores, worth, qid, inverse)


def leaf_kernel(perm_ref, bins_ref, leaf_ref, lam_ref, bins_t_ref, tile_ref, sums_ref):
    bins = bins_ref[...].astype(F32).astype(BF16)
    bins_t_ref[...] = lax.dot_general(perm_ref[...], bins, NT, preferred_element_type=F32)
    own = leaf_ref.shape[0]
    docs = own * LANES
    leaf = jnp.concatenate([leaf_ref[t:t + 1, :] for t in range(own)], axis=1)
    highs = LEAVES // LANES
    top = jnp.broadcast_to(leaf // LANES, (highs, docs)) == iota((highs, docs), 0)
    spots = jnp.where(jnp.broadcast_to(leaf % LANES, (LANES, docs)) == iota((LANES, docs), 0), 1.0, 0.0).astype(BF16)
    pieces, tiles = [], []
    for c in range(2):
        for k, part in enumerate(split_terms(lam_ref[c:c + 1, :], 3)):
            wide = jnp.broadcast_to(part.astype(F32), (highs, docs))
            pieces.append(jnp.where(top, wide, 0.0))
            if k < 2:
                tiles.append(wide)
    tile_ref[...] = jnp.concatenate(tiles, axis=0).astype(BF16)
    stacked = jnp.concatenate(pieces, axis=0).astype(BF16)
    sums = lax.dot_general(stacked, spots, NT, preferred_element_type=F32)
    for c in range(2):
        base = c * 3 * highs
        sums_ref[:, c * LANES:(c + 1) * LANES] = (
            sums[base:base + highs] + (sums[base + highs:base + 2 * highs] + sums[base + 2 * highs:base + 3 * highs])
        )


def leaf_terms(perm, bins, leaves, lambdas):
    docs, features = bins.shape
    return pl.pallas_call(
        leaf_kernel,
        out_shape=(
            jax.ShapeDtypeStruct((features, docs), F32),
            jax.ShapeDtypeStruct((4 * HIGH, docs), BF16),
            jax.ShapeDtypeStruct((LEAVES // LANES, 2 * LANES), F32),
        ),
        in_specs=[vmem()] * 4,
        out_specs=(vmem(), vmem(), vmem()),
        compiler_params=pltpu.CompilerParams(vmem_limit_bytes=VMEM_LIMIT),
        cost_estimate=pl.CostEstimate(flops=200_000_000, bytes_accessed=3_000_000, transcendentals=0),
        name="leaf_terms",
    )(perm, bins, leaves, lambdas)


def histogram_kernel(first, groups, tile_ref, bins_ref, *refs):
    out_ref = refs[-1]
    docs = tile_ref.shape[1]
    depth = 256
    rows = 16
    row = iota((rows, depth), 0)
    low_level = [(row + rows * k).astype(F32).astype(BF16) for k in range(LOW // rows)]
    high_level = (row % HIGH).astype(F32).astype(BF16)
    upper = row < HIGH
    zero = jnp.zeros((rows, depth), BF16)
    one = jnp.ones((rows, depth), BF16)
    lane_owner = iota((1, GROUP * LOW), 1) // LOW

    def one_group(g, carry):
        base = pl.multiple_of((first + g) * GROUP, GROUP)
        acc = None
        for k in range(docs // depth):
            span = slice(k * depth, (k + 1) * depth)
            code = bins_ref[pl.ds(base, GROUP), span]
            high = jnp.floor(code * (1.0 / LOW))
            low = code - high * LOW
            left, right, count = [], [], []
            wide = []
            for f in range(GROUP):
                high_f = jnp.broadcast_to(high[f:f + 1, :], (rows, depth))
                low_f = jnp.broadcast_to(low[f:f + 1, :], (rows, depth)).astype(BF16)
                wide.append(high_f)
                match = high_f.astype(BF16) == high_level
                for c in range(2):
                    left.append(jnp.where(match, tile_ref[c * rows:(c + 1) * rows, span], zero))
                for level in low_level:
                    right.append(jnp.where(low_f == level, one, zero))
            for f in range(0, GROUP, 2):
                both = jnp.where(upper, wide[f], wide[f + 1]).astype(BF16)
                count.append(jnp.where(both == high_level, one, zero))
            part = lax.dot_general(
                jnp.concatenate(left + count, axis=0), jnp.concatenate(right, axis=0), NT,
                preferred_element_type=F32,
            )
            acc = part if acc is None else acc + part
        stats = jnp.zeros((2 * rows, GROUP * LOW), F32)
        counts = jnp.zeros((HIGH, GROUP * LOW), F32)
        for f in range(GROUP):
            mine = lane_owner == f
            stats = jnp.where(mine, acc[f * 2 * rows:(f + 1) * 2 * rows], stats)
            at = GROUP * 2 * rows + f * HIGH
            counts = jnp.where(mine, acc[at:at + HIGH], counts)
        out_ref[pl.ds(pl.multiple_of(g * 3 * HIGH, 3 * HIGH), 3 * HIGH), :] = jnp.concatenate(
            [stats[0:HIGH] + stats[HIGH:2 * HIGH], stats[2 * HIGH:3 * HIGH] + stats[3 * HIGH:4 * HIGH], counts], axis=0)
        return carry

    if len(refs) > 1:
        out_ref[groups * 3 * HIGH:, :] = refs[0][...]
    lax.fori_loop(0, groups, one_group, 0, unroll=2)


def histogram_part(first, groups, tiles, bins_t, *tail):
    rows = groups * 3 * HIGH + sum(piece.shape[0] for piece in tail)
    return pl.pallas_call(
        functools.partial(histogram_kernel, first, groups),
        out_shape=jax.ShapeDtypeStruct((rows, GROUP * LOW), F32),
        in_specs=[vmem()] * (2 + len(tail)),
        out_specs=vmem(),
        compiler_params=pltpu.CompilerParams(vmem_limit_bytes=VMEM_LIMIT),
        cost_estimate=pl.CostEstimate(flops=groups * 330_000_000, bytes_accessed=groups * 60_000, transcendentals=0),
        name="histogram_part",
    )(tiles, bins_t, *tail)


def finish_kernel(per_dev, leaf_ref, kept_ref, sums_ref, *refs):
    arrived = refs[:-3][::-1]
    value_ref, step_ref, hist_ref = refs[-3:]
    unit = kept_ref.shape[0]
    totals = add_up([sums_ref[...]] + [ref[unit:, :] for ref in arrived])
    highs = LEAVES // LANES
    grad, curv = totals[:, :LANES], totals[:, LANES:]
    shrunk = jnp.maximum(jnp.abs(grad) - lasso_penalty, 0.0)
    values = jnp.where(grad > 0.0, -shrunk, shrunk) / (curv + ridge_penalty)
    value_ref[...] = values
    leaf = leaf_ref[...]
    top, spot = leaf // LANES, leaf % LANES
    step = jnp.zeros(leaf.shape, F32)
    for h in range(highs):
        row = jnp.broadcast_to(values[h:h + 1, :], leaf.shape)
        step = jnp.where(top == h, jnp.take_along_axis(row, spot, axis=1), step)
    step_ref[...] = shrinkage * step
    hist = add_up([kept_ref[...]] + [ref[:unit, :] for ref in arrived])
    if per_dev == GROUP:
        for c in range(3):
            for f in range(GROUP):
                line = [hist[c * HIGH + h:c * HIGH + h + 1, f * LOW:(f + 1) * LOW] for h in range(HIGH)]
                hist_ref[c:c + 1, f * BINS:(f + 1) * BINS] = jnp.concatenate(line, axis=1)
    else:
        hist_ref[...] = hist


def finish(per_dev, leaves, kept, sums, arrived):
    out = (3, per_dev * BINS) if per_dev == GROUP else kept.shape
    return pl.pallas_call(
        functools.partial(finish_kernel, per_dev),
        out_shape=(
            jax.ShapeDtypeStruct((LEAVES // LANES, LANES), F32),
            jax.ShapeDtypeStruct(leaves.shape, F32),
            jax.ShapeDtypeStruct(out, F32),
        ),
        in_specs=[vmem()] * (3 + len(arrived)),
        out_specs=(vmem(), vmem(), vmem()),
        compiler_params=pltpu.CompilerParams(vmem_limit_bytes=VMEM_LIMIT),
        name="finish",
    )(leaves, kept, sums, *arrived)


def add_up(parts):
    while len(parts) > 1:
        parts = [parts[k] + parts[k + 1] for k in range(0, len(parts), 2)]
    return parts[0]


def local(scores, labels, leaves, bins, lengths, owner):
    query_count = lax.axis_size("query")
    feat_count = lax.axis_size("feat")
    count = query_count * feat_count
    place = lax.axis_index("query").astype(jnp.int32) * feat_count + lax.axis_index("feat").astype(jnp.int32)
    docs = scores.shape[0]
    own = docs // LANES
    features = owner.shape[0]
    per_dev = features // count
    unit = 3 * per_dev
    axes = ("query", "feat")
    feat_masks = [1 << b for b in range(feat_count.bit_length() - 1)]
    query_masks = [feat_count << b for b in range(query_count.bit_length() - 1)]

    def swap(value, mask):
        return lax.ppermute(value, axes, [(p, p ^ mask) for p in range(count)])

    pos = place.reshape(1)
    leaf_rows = leaves.reshape(own, LANES)
    own_scores = scores.reshape(own, LANES)
    score_parts = [own_scores]
    for begin in range(2):
        links = [(z, z + 1) for z in range(begin, feat_count - 1, 2)]
        links += [(0, feat_count - 1)] if begin else []
        score_parts.append(lax.ppermute(own_scores, "feat", links + [(b, a) for a, b in links]))
    masks = feat_masks + query_masks[:0:-1] + query_masks[:1]
    score_parts[0], qid, worth, inverse, perm, bounds = prepare(
        feat_count, masks, lengths, pos, labels.reshape(-1, LANES), owner.reshape(-1, LANES), own_scores)
    lambdas, near_lambdas = pair_terms(feat_count, bounds, pos, score_parts, worth, qid, inverse)
    bins_t, tiles, sums = leaf_terms(perm, bins, leaf_rows, near_lambdas)

    def part(tiles, low, high, *tail):
        if per_dev == GROUP:
            return histogram_part(low, high - low, tiles, bins_t, *tail)
        groups = high - low
        wide = histogram_part(low, groups, tiles, bins_t)
        wide = wide.reshape(groups, 3, HIGH, GROUP // per_dev, per_dev, LOW).transpose(0, 3, 1, 4, 2, 5)
        return jnp.concatenate([wide.reshape(groups * GROUP // per_dev * unit, BINS), *tail], axis=0)

    def join(block, total):
        return jnp.concatenate([block, total], axis=0)

    quarter = features // GROUP // 4
    edge = count // 4 * unit
    arrived = swap(part(tiles, 3 * quarter, 4 * quarter, sums), query_masks[0])
    far = part(tiles, quarter, 2 * quarter) + arrived[:edge]
    sums = sums + arrived[edge:]
    message, tiles = lax.optimization_barrier((join(far, sums), tiles))
    crossed = swap(message, query_masks[1])
    arrived = swap(part(tiles, 2 * quarter, 3 * quarter), query_masks[0])
    kept = part(tiles, 0, quarter) + arrived + crossed[:edge]
    sums = sums + crossed[edge:]
    for mask in query_masks[2:]:
        edge = edge // 2
        arrived = swap(join(kept[edge:], sums), mask)
        kept = kept[:edge] + arrived[:edge]
        sums = sums + arrived[edge:]
    arrived = [swap(join(kept[m * unit:(m + 1) * unit], sums), m) for m in range(1, feat_count)]
    values, step, histograms = finish(per_dev, leaf_rows, kept[:unit], sums, arrived[::-1])
    return lambdas, values.reshape(LEAVES), step.reshape(docs), histograms.reshape(3, per_dev * BINS)


def solution(mesh):
    in_specs = (
        P(("query", "feat")),
        P("query"),
        P(("query", "feat")),
        P(("query", "feat"), None),
        P("query", None),
        P(),
    )
    out_specs = (P(None, ("query", "feat")), P(), P(("query", "feat")), P(None, ("query", "feat")))
    return jax.shard_map(local, mesh=mesh, in_specs=in_specs, out_specs=out_specs, check_vma=False)
```

```python
import functools

import jax
import jax.numpy as jnp
from jax import lax
from jax.experimental import pallas as pl
from jax.experimental.pallas import tpu as pltpu
from jax.sharding import PartitionSpec as P

BINS = 256
LEAVES = 1024
LANES = 128
GRADES = 4
LOW = 32
HIGH = BINS // LOW
GROUP = 8
CHUNK = 64
MAX_LEN = 1024

lasso_penalty = 1.0
ridge_penalty = 1.0
shrinkage = 0.1

VMEM_LIMIT = 48 * 1024 * 1024
F32 = jnp.float32
BF16 = jnp.bfloat16
NT = (((1,), (1,)), ((), ()))


def iota(shape, axis):
    return lax.broadcasted_iota(jnp.int32, shape, axis)


def vmem():
    return pl.BlockSpec(memory_space=pltpu.VMEM)


def smem():
    return pl.BlockSpec(memory_space=pltpu.SMEM)


def prepare_kernel(feat_count, masks, len_ref, pos_ref, lab_ref, owner_ref, score_ref,
                   kept_ref, qid_ref, worth_ref, inv_ref, perm_ref, bounds_ref):
    kept_ref[...] = score_ref[...]
    queries = len_ref.shape[1]
    rows = lab_ref.shape[0]
    own = rows // feat_count
    spot = iota((rows, LANES), 0) * LANES + iota((rows, LANES), 1)
    qid = jnp.zeros((rows, LANES), jnp.int32)
    begin = jnp.zeros((queries, LANES), jnp.int32)
    finish = jnp.zeros((queries, LANES), jnp.int32)
    which = iota((queries, LANES), 0)
    group = iota((1, LANES), 1) * LANES
    low = jnp.zeros((1, LANES), jnp.int32)
    high = first_end = jnp.full((1, LANES), rows * LANES, jnp.int32)
    start = jnp.int32(0)
    for q in range(queries):
        end = start + len_ref[0, q]
        qid = qid + jnp.where(spot >= end, 1, 0)
        begin = jnp.where(which == q, start, begin)
        finish = jnp.where(which == q, end, finish)

        low = low + jnp.where(end <= group, len_ref[0, q], 0)
        high = jnp.minimum(high, jnp.where(end >= group + LANES, end, rows * LANES))
        first_end = jnp.minimum(first_end, jnp.where(end > group, end, rows * LANES))
        start = end
    bounds_ref[...] = jnp.concatenate([low, high, first_end, low, low, low, low, low], axis=0)
    qid_ref[...] = qid
    worth_ref[...] = jnp.left_shift(1, lab_ref[...]).astype(F32)

    counts = [jnp.zeros((queries, LANES), F32) for _ in range(GRADES)]
    lane = iota((queries, LANES), 1)
    for r in range(rows):
        at = lane + r * LANES
        inside = (at >= begin) & (at < finish)
        grade = jnp.where(inside, jnp.broadcast_to(lab_ref[r:r + 1, :], (queries, LANES)), 0)
        for g in range(GRADES):
            counts[g] = counts[g] + jnp.where(grade > g, 1.0, 0.0)
    position = iota((queries, MAX_LEN), 1).astype(F32)
    gain = jnp.zeros((queries, MAX_LEN), F32)
    for g in range(GRADES):
        held = jnp.sum(counts[g], axis=1, keepdims=True)
        gain = gain + jnp.where(position < held, float(2 ** g), 0.0)
    level = 1.0 / jnp.log2(2.0 + position[0:1, :])
    ideal = jnp.sum(gain * level, axis=1, keepdims=True)
    usable = ideal > 0.5
    inverse = jnp.where(usable, 1.0 / jnp.where(usable, ideal, 1.0), 0.0)
    first = pos_ref[0] % feat_count * own
    for t in range(own):
        at = lane + (first + t) * LANES
        inside = (at >= begin) & (at < finish)
        inv_ref[0:1, t * LANES:(t + 1) * LANES] = jnp.sum(jnp.where(inside, inverse, 0.0), axis=0, keepdims=True)

    features = perm_ref.shape[0]
    per_dev = features >> len(masks)
    owner = jnp.concatenate([owner_ref[k:k + 1, :] for k in range(features // LANES)], axis=1)
    square = (features, features)
    down, across = iota(square, 0), iota(square, 1)
    index = iota((features, 1), 0) // per_dev
    target = jnp.zeros((features, 1), jnp.int32)
    for b, mask in enumerate(masks):
        target = target + ((index >> b) & 1) * mask
    target = (target ^ pos_ref[0]) * per_dev + iota((features, 1), 0) % per_dev
    pick = jnp.where(target == across, 1.0, 0.0).astype(BF16)
    holds = jnp.where(jnp.broadcast_to(owner, square) == down, 1.0, 0.0).astype(BF16)
    perm_ref[...] = lax.dot_general(pick, holds, NT, preferred_element_type=F32).astype(BF16)


def prepare(feat_count, masks, lengths, pos, labels, owner, scores):
    rows = labels.shape[0]
    features = owner.shape[0] * LANES
    return pl.pallas_call(
        functools.partial(prepare_kernel, feat_count, masks),
        out_shape=(
            jax.ShapeDtypeStruct(scores.shape, F32),
            jax.ShapeDtypeStruct((rows, LANES), jnp.int32),
            jax.ShapeDtypeStruct((rows, LANES), F32),
            jax.ShapeDtypeStruct((1, rows // feat_count * LANES), F32),
            jax.ShapeDtypeStruct((features, features), BF16),
            jax.ShapeDtypeStruct((8, LANES), jnp.int32),
        ),
        in_specs=[smem(), smem(), vmem(), vmem(), vmem()],
        out_specs=(vmem(),) * 6,
        compiler_params=pltpu.CompilerParams(vmem_limit_bytes=VMEM_LIMIT),
        cost_estimate=pl.CostEstimate(flops=2_000_000_000, bytes_accessed=300_000, transcendentals=20_000),
        name="prepare",
    )(lengths, pos, labels, owner, scores)


def split_terms(value, terms):
    parts = []
    rest = value
    for _ in range(terms):
        part = rest.astype(BF16)
        parts.append(part)
        rest = rest - part.astype(F32)
    return parts


def pairs_kernel(feat_count, bounds_ref, pos_ref, *refs):
    scores = refs[:-20]
    (worth_ref, qid_ref, inv_ref, lam_ref, near_ref,
     s_row, a_row, d_row, s_turn, a_turn, w_turn, q_turn, d_turn, s_col, a_col, w_col, q_col, d_col, grad, curv) = refs[-20:]
    rows = worth_ref.shape[0]
    own = rows // feat_count
    docs = own * LANES
    me = pos_ref[0] % feat_count
    s_row[...] = jnp.zeros(s_row.shape, F32)
    near = [me, ((me + 1) ^ 1) - 1, me ^ 1]
    for where, ref in zip(near, scores):
        @pl.when((where >= 0) & (where < feat_count))
        def _(where=where, ref=ref):
            s_row[pl.ds(pl.multiple_of(where * own, own), own), :] = ref[...]
    a_row[...] = jnp.exp(s_row[...])
    d_row[...] = jnp.zeros(d_row.shape, F32)
    first = me * own
    window_low = bounds_ref[0, first] // (2 * LANES) * 2
    window_high = (bounds_ref[1, first + own - 1] + 2 * LANES - 1) // (2 * LANES) * 2
    stride = 4

    def widen(pairs):
        for turn, source, _ in pairs:
            turn[...] = jnp.transpose(source[...])
        for r in range(0, rows, stride):
            @pl.when((r + stride > window_low) & (r < window_high))
            def _(r=r):
                for turn, _, col in pairs:
                    for k in range(r, r + stride):
                        col[k * LANES:(k + 1) * LANES, :] = jnp.broadcast_to(turn[:, k:k + 1], (LANES, LANES))

    widen([(s_turn, s_row, s_col), (q_turn, qid_ref, q_col), (a_turn, a_row, a_col), (w_turn, worth_ref, w_col)])

    def rows_of(ref, r):
        return [jnp.broadcast_to(ref[pl.ds(r + g, 1), :], (8, LANES)) for g in range(2)]

    def spans(r):
        start, end = bounds_ref[0, r], bounds_ref[1, r + 1]
        low = jnp.maximum(start // LANES, window_low)
        high = jnp.minimum((end + LANES - 1) // LANES, window_high)
        single = bounds_ref[2, r] >= (r + 2) * LANES
        inner_low = jnp.where(single, jnp.maximum((start + LANES - 1) // LANES, window_low), r)
        inner_high = jnp.where(single, jnp.minimum(end // LANES, window_high), r)
        return low, inner_low, inner_high, high

    def rank_groups(k, carry):
        r = window_low + 2 * k
        score = rows_of(s_row, r)
        query = rows_of(qid_ref, r)

        def gather(c, acc, masked, test):
            base = pl.multiple_of(c * LANES, LANES)
            acc = list(acc)
            for u in range(LANES // 8):
                other = s_col[pl.ds(base + 8 * u, 8), :]
                for g in range(2):
                    hit = test(other, g, u)
                    if masked:
                        hit = hit & (q_col[pl.ds(base + 8 * u, 8), :] == query[g])
                    acc[2 * g + u % 2] = acc[2 * g + u % 2] + jnp.where(hit, 1.0, 0.0)
            return tuple(acc)

        def ahead(other, g, u):
            return other >= score[g]

        def behind(other, g, u):
            return other > score[g]

        def within(mine):
            def test(other, g, u):
                if g != mine:
                    return ahead(other, g, u) if mine < g else behind(other, g, u)
                earlier = iota((8, LANES), 0) + 8 * u < iota((8, LANES), 1)
                return (other > score[g]) | ((other == score[g]) & earlier)
            return test

        acc = tuple(jnp.zeros((8, LANES), F32) for _ in range(4))
        low, inner_low, inner_high, high = spans(r)
        after = jnp.maximum(inner_high, r + 2)
        acc = lax.fori_loop(low, inner_low, lambda c, acc: gather(c, acc, True, ahead), acc)
        acc = lax.fori_loop(inner_low, r, lambda c, acc: gather(c, acc, False, ahead), acc)
        acc = lax.fori_loop(r + 2, after, lambda c, acc: gather(c, acc, False, behind), acc)
        acc = lax.fori_loop(after, high, lambda c, acc: gather(c, acc, True, behind), acc)
        for mine in range(2):
            acc = gather(r + mine, acc, True, within(mine))
        for g in range(2):
            d_row[pl.ds(r + g, 1), :] = jnp.sum(acc[2 * g] + acc[2 * g + 1], axis=0, keepdims=True)
        return carry

    lax.fori_loop(0, (window_high - window_low) // 2, rank_groups, 0)
    d_row[...] = 1.0 / jnp.log2(2.0 + d_row[...])
    widen([(d_turn, d_row, d_col)])

    def pair_groups(t, carry):
        r = first + 2 * t
        a_i, w_i, d_i, query = [rows_of(ref, r) for ref in (a_row, worth_ref, d_row, qid_ref)]

        def columns(masked):
            def step(c, acc):
                base = pl.multiple_of(c * LANES, LANES)
                acc = list(acc)
                for u in range(LANES // 8):
                    at = pl.ds(base + 8 * u, 8)
                    a_j, w_j, d_j = a_col[at, :], w_col[at, :], d_col[at, :]
                    for g in range(2):
                        recip = pl.reciprocal(a_i[g] + a_j, approx=True)
                        lift = w_i[g] - w_j
                        weight = jnp.abs(d_i[g] - d_j) * recip
                        if masked:
                            weight = jnp.where(q_col[at, :] == query[g], weight, 0.0)
                        weight = weight * lift
                        k = 4 * g + u % 2
                        acc[k] = acc[k] + weight * jnp.where(lift > 0.0, a_j, a_i[g])
                        acc[k + 2] = acc[k + 2] + jnp.abs(weight) * (recip * a_j)
                return tuple(acc)
            return step

        acc = tuple(jnp.zeros((8, LANES), F32) for _ in range(8))
        low, inner_low, inner_high, high = spans(r)
        acc = lax.fori_loop(low, inner_low, columns(True), acc)
        acc = lax.fori_loop(inner_low, inner_high, columns(False), acc)
        acc = lax.fori_loop(inner_high, high, columns(True), acc)
        for g in range(2):
            at = pl.ds(2 * t + g, 1)
            grad[at, :] = -jnp.sum(acc[4 * g] + acc[4 * g + 1], axis=0, keepdims=True)
            curv[at, :] = a_i[g][0:1, :] * jnp.sum(acc[4 * g + 2] + acc[4 * g + 3], axis=0, keepdims=True)
        return carry

    lax.fori_loop(0, own // 2, pair_groups, 0)
    inverse = inv_ref[...]
    terms = [inverse * jnp.concatenate([ref[t:t + 1, :] for t in range(own)], axis=1) for ref in (grad, curv)]
    for c in range(2):
        lam_ref[c:c + 1, :] = terms[c]
        near_ref[c:c + 1, :] = terms[c]


def pair_terms(feat_count, bounds, pos, scores, worth, qid, inverse):
    rows = worth.shape[0]
    docs = inverse.shape[1]
    row = pltpu.VMEM((rows, LANES), F32)
    turn = pltpu.VMEM((LANES, rows), F32)
    col = pltpu.VMEM((rows * LANES, LANES), F32)
    mine = pltpu.VMEM((docs // LANES, LANES), F32)
    return pl.pallas_call(
        functools.partial(pairs_kernel, feat_count),
        out_shape=(jax.ShapeDtypeStruct((2, docs), F32), jax.ShapeDtypeStruct((2, docs), F32)),
        in_specs=[smem(), smem()] + [vmem()] * (len(scores) + 3),
        out_specs=(vmem(), vmem()),
        scratch_shapes=[row, row, row, turn, turn, turn, pltpu.VMEM((LANES, rows), jnp.int32), turn,
                        col, col, col, pltpu.VMEM((rows * LANES, LANES), jnp.int32), col, mine, mine],
        compiler_params=pltpu.CompilerParams(vmem_limit_bytes=VMEM_LIMIT),
        cost_estimate=pl.CostEstimate(flops=9_000_000_000, bytes_accessed=200_000, transcendentals=2_000_000),
        name="pair_terms",
    )(bounds, pos, *scores, worth, qid, inverse)


def leaf_kernel(perm_ref, bins_ref, leaf_ref, lam_ref, bins_t_ref, tile_ref, sums_ref):
    bins = bins_ref[...].astype(F32).astype(BF16)
    bins_t_ref[...] = lax.dot_general(perm_ref[...], bins, NT, preferred_element_type=F32)
    own = leaf_ref.shape[0]
    docs = own * LANES
    leaf = jnp.concatenate([leaf_ref[t:t + 1, :] for t in range(own)], axis=1)
    highs = LEAVES // LANES
    top = jnp.broadcast_to(leaf // LANES, (highs, docs)) == iota((highs, docs), 0)
    spots = jnp.where(jnp.broadcast_to(leaf % LANES, (LANES, docs)) == iota((LANES, docs), 0), 1.0, 0.0).astype(BF16)
    pieces, tiles = [], []
    for c in range(2):
        for k, part in enumerate(split_terms(lam_ref[c:c + 1, :], 3)):
            wide = jnp.broadcast_to(part.astype(F32), (highs, docs))
            pieces.append(jnp.where(top, wide, 0.0))
            if k < 2:
                tiles.append(wide)
    tile_ref[...] = jnp.concatenate(tiles, axis=0).astype(BF16)
    stacked = jnp.concatenate(pieces, axis=0).astype(BF16)
    sums = lax.dot_general(stacked, spots, NT, preferred_element_type=F32)
    for c in range(2):
        base = c * 3 * highs
        sums_ref[:, c * LANES:(c + 1) * LANES] = (
            sums[base:base + highs] + (sums[base + highs:base + 2 * highs] + sums[base + 2 * highs:base + 3 * highs])
        )


def leaf_terms(perm, bins, leaves, lambdas):
    docs, features = bins.shape
    return pl.pallas_call(
        leaf_kernel,
        out_shape=(
            jax.ShapeDtypeStruct((features, docs), F32),
            jax.ShapeDtypeStruct((4 * HIGH, docs), BF16),
            jax.ShapeDtypeStruct((LEAVES // LANES, 2 * LANES), F32),
        ),
        in_specs=[vmem()] * 4,
        out_specs=(vmem(), vmem(), vmem()),
        compiler_params=pltpu.CompilerParams(vmem_limit_bytes=VMEM_LIMIT),
        cost_estimate=pl.CostEstimate(flops=200_000_000, bytes_accessed=3_000_000, transcendentals=0),
        name="leaf_terms",
    )(perm, bins, leaves, lambdas)


def histogram_kernel(first, groups, tile_ref, bins_ref, *refs):
    out_ref = refs[-1]
    docs = tile_ref.shape[1]
    depth = 256
    rows = 16
    row = iota((rows, depth), 0)
    low_level = [(row + rows * k).astype(F32).astype(BF16) for k in range(LOW // rows)]
    high_level = (row % HIGH).astype(F32).astype(BF16)
    upper = row < HIGH
    zero = jnp.zeros((rows, depth), BF16)
    one = jnp.ones((rows, depth), BF16)
    lane_owner = iota((1, GROUP * LOW), 1) // LOW

    def one_group(g, carry):
        base = pl.multiple_of((first + g) * GROUP, GROUP)
        acc = None
        for k in range(docs // depth):
            span = slice(k * depth, (k + 1) * depth)
            code = bins_ref[pl.ds(base, GROUP), span]
            high = jnp.floor(code * (1.0 / LOW))
            low = code - high * LOW
            left, right, count = [], [], []
            wide = []
            for f in range(GROUP):
                high_f = jnp.broadcast_to(high[f:f + 1, :], (rows, depth))
                low_f = jnp.broadcast_to(low[f:f + 1, :], (rows, depth)).astype(BF16)
                wide.append(high_f)
                match = high_f.astype(BF16) == high_level
                for c in range(2):
                    left.append(jnp.where(match, tile_ref[c * rows:(c + 1) * rows, span], zero))
                for level in low_level:
                    right.append(jnp.where(low_f == level, one, zero))
            for f in range(0, GROUP, 2):
                both = jnp.where(upper, wide[f], wide[f + 1]).astype(BF16)
                count.append(jnp.where(both == high_level, one, zero))
            part = lax.dot_general(
                jnp.concatenate(left + count, axis=0), jnp.concatenate(right, axis=0), NT,
                preferred_element_type=F32,
            )
            acc = part if acc is None else acc + part
        stats = jnp.zeros((2 * rows, GROUP * LOW), F32)
        counts = jnp.zeros((HIGH, GROUP * LOW), F32)
        for f in range(GROUP):
            mine = lane_owner == f
            stats = jnp.where(mine, acc[f * 2 * rows:(f + 1) * 2 * rows], stats)
            at = GROUP * 2 * rows + f * HIGH
            counts = jnp.where(mine, acc[at:at + HIGH], counts)
        out_ref[pl.ds(pl.multiple_of(g * 3 * HIGH, 3 * HIGH), 3 * HIGH), :] = jnp.concatenate(
            [stats[0:HIGH] + stats[HIGH:2 * HIGH], stats[2 * HIGH:3 * HIGH] + stats[3 * HIGH:4 * HIGH], counts], axis=0)
        return carry

    if len(refs) > 1:
        out_ref[groups * 3 * HIGH:, :] = refs[0][...]
    lax.fori_loop(0, groups, one_group, 0, unroll=2)


def histogram_part(first, groups, tiles, bins_t, *tail):
    rows = groups * 3 * HIGH + sum(piece.shape[0] for piece in tail)
    return pl.pallas_call(
        functools.partial(histogram_kernel, first, groups),
        out_shape=jax.ShapeDtypeStruct((rows, GROUP * LOW), F32),
        in_specs=[vmem()] * (2 + len(tail)),
        out_specs=vmem(),
        compiler_params=pltpu.CompilerParams(vmem_limit_bytes=VMEM_LIMIT),
        cost_estimate=pl.CostEstimate(flops=groups * 1_000_000, bytes_accessed=groups * 1_000, transcendentals=0),
        name="histogram_part",
    )(tiles, bins_t, *tail)


def finish_kernel(per_dev, leaf_ref, kept_ref, sums_ref, *refs):
    arrived = refs[:-3][::-1]
    value_ref, step_ref, hist_ref = refs[-3:]
    unit = kept_ref.shape[0]
    totals = add_up([sums_ref[...]] + [ref[unit:, :] for ref in arrived])
    highs = LEAVES // LANES
    grad, curv = totals[:, :LANES], totals[:, LANES:]
    shrunk = jnp.maximum(jnp.abs(grad) - lasso_penalty, 0.0)
    values = jnp.where(grad > 0.0, -shrunk, shrunk) / (curv + ridge_penalty)
    value_ref[...] = values
    leaf = leaf_ref[...]
    top, spot = leaf // LANES, leaf % LANES
    step = jnp.zeros(leaf.shape, F32)
    for h in range(highs):
        row = jnp.broadcast_to(values[h:h + 1, :], leaf.shape)
        step = jnp.where(top == h, jnp.take_along_axis(row, spot, axis=1), step)
    step_ref[...] = shrinkage * step
    hist = add_up([kept_ref[...]] + [ref[:unit, :] for ref in arrived])
    if per_dev == GROUP:
        for c in range(3):
            for f in range(GROUP):
                line = [hist[c * HIGH + h:c * HIGH + h + 1, f * LOW:(f + 1) * LOW] for h in range(HIGH)]
                hist_ref[c:c + 1, f * BINS:(f + 1) * BINS] = jnp.concatenate(line, axis=1)
    else:
        hist_ref[...] = hist


def finish(per_dev, leaves, kept, sums, arrived):
    out = (3, per_dev * BINS) if per_dev == GROUP else kept.shape
    return pl.pallas_call(
        functools.partial(finish_kernel, per_dev),
        out_shape=(
            jax.ShapeDtypeStruct((LEAVES // LANES, LANES), F32),
            jax.ShapeDtypeStruct(leaves.shape, F32),
            jax.ShapeDtypeStruct(out, F32),
        ),
        in_specs=[vmem()] * (3 + len(arrived)),
        out_specs=(vmem(), vmem(), vmem()),
        compiler_params=pltpu.CompilerParams(vmem_limit_bytes=VMEM_LIMIT),
        name="finish",
    )(leaves, kept, sums, *arrived)


def add_up(parts):
    while len(parts) > 1:
        parts = [parts[k] + parts[k + 1] for k in range(0, len(parts), 2)]
    return parts[0]


def local(scores, labels, leaves, bins, lengths, owner):
    query_count = lax.axis_size("query")
    feat_count = lax.axis_size("feat")
    count = query_count * feat_count
    place = lax.axis_index("query").astype(jnp.int32) * feat_count + lax.axis_index("feat").astype(jnp.int32)
    docs = scores.shape[0]
    own = docs // LANES
    features = owner.shape[0]
    per_dev = features // count
    unit = 3 * per_dev
    axes = ("query", "feat")
    feat_masks = [1 << b for b in range(feat_count.bit_length() - 1)]
    query_masks = [feat_count << b for b in range(query_count.bit_length() - 1)]

    def swap(value, mask):
        return lax.ppermute(value, axes, [(p, p ^ mask) for p in range(count)])

    pos = place.reshape(1)
    leaf_rows = leaves.reshape(own, LANES)
    own_scores = scores.reshape(own, LANES)
    score_parts = [own_scores]
    for begin in (1, 0):
        links = [(z, z + 1) for z in range(begin, feat_count - 1, 2)]
        links += [(0, feat_count - 1)] if begin else []
        score_parts.append(lax.ppermute(own_scores, "feat", links + [(b, a) for a, b in links]))
    masks = feat_masks + query_masks[:0:-1] + query_masks[:1]
    score_parts[0], qid, worth, inverse, perm, bounds = prepare(
        feat_count, masks, lengths, pos, labels.reshape(-1, LANES), owner.reshape(-1, LANES), own_scores)
    lambdas, near_lambdas = pair_terms(feat_count, bounds, pos, score_parts, worth, qid, inverse)
    bins_t, tiles, sums = leaf_terms(perm, bins, leaf_rows, near_lambdas)

    def part(tiles, low, high, *tail):
        if per_dev == GROUP:
            return histogram_part(low, high - low, tiles, bins_t, *tail)
        groups = high - low
        wide = histogram_part(low, groups, tiles, bins_t)
        wide = wide.reshape(groups, 3, HIGH, GROUP // per_dev, per_dev, LOW).transpose(0, 3, 1, 4, 2, 5)
        return jnp.concatenate([wide.reshape(groups * GROUP // per_dev * unit, BINS), *tail], axis=0)

    def join(block, total):
        return jnp.concatenate([block, total], axis=0)

    eighth = features // GROUP // 8
    edge = count // 8 * unit
    arrived = swap(part(tiles, 6 * eighth, 8 * eighth, sums), query_masks[0])
    block = part(tiles, 3 * eighth, 4 * eighth) + arrived[edge:2 * edge]
    sums = sums + arrived[2 * edge:]
    message, tiles = lax.optimization_barrier((join(block, sums), tiles))
    crossed_far = swap(message, query_masks[1])
    block = part(tiles, 2 * eighth, 3 * eighth) + arrived[:edge]
    message, tiles = lax.optimization_barrier((block, tiles))
    crossed_near = swap(message, query_masks[1])
    arrived = swap(part(tiles, 4 * eighth, 6 * eighth), query_masks[0])
    block = part(tiles, eighth, 2 * eighth) + arrived[edge:] + crossed_far[:edge]
    sums = sums + crossed_far[edge:]
    message, tiles = lax.optimization_barrier((join(block, sums), tiles))
    turned = swap(message, query_masks[2])
    kept = part(tiles, 0, eighth) + arrived[:edge] + crossed_near + turned[:edge]
    sums = sums + turned[edge:]
    for mask in query_masks[3:]:
        edge = edge // 2
        arrived = swap(join(kept[edge:], sums), mask)
        kept = kept[:edge] + arrived[:edge]
        sums = sums + arrived[edge:]
    arrived = [swap(join(kept[m * unit:(m + 1) * unit], sums), m) for m in range(1, feat_count)]
    values, step, histograms = finish(per_dev, leaf_rows, kept[:unit], sums, arrived[::-1])
    return lambdas, values.reshape(LEAVES), step.reshape(docs), histograms.reshape(3, per_dev * BINS)


def solution(mesh):
    in_specs = (
        P(("query", "feat")),
        P("query"),
        P(("query", "feat")),
        P(("query", "feat"), None),
        P("query", None),
        P(),
    )
    out_specs = (P(None, ("query", "feat")), P(), P(("query", "feat")), P(None, ("query", "feat")))
    return jax.shard_map(local, mesh=mesh, in_specs=in_specs, out_specs=out_specs, check_vma=False)
```

```python
import functools

import jax
import jax.numpy as jnp
from jax import lax
from jax.experimental import pallas as pl
from jax.experimental.pallas import tpu as pltpu
from jax.sharding import PartitionSpec as P

BINS = 256
LEAVES = 1024
LANES = 128
GRADES = 4
LOW = 64
HIGH = BINS // LOW
GROUP = 8
FEW = 4
CHUNK = 64
MAX_LEN = 1024

lasso_penalty = 1.0
ridge_penalty = 1.0
shrinkage = 0.1

VMEM_LIMIT = 48 * 1024 * 1024
F32 = jnp.float32
BF16 = jnp.bfloat16
NT = (((1,), (1,)), ((), ()))


def iota(shape, axis):
    return lax.broadcasted_iota(jnp.int32, shape, axis)


def vmem():
    return pl.BlockSpec(memory_space=pltpu.VMEM)


def smem():
    return pl.BlockSpec(memory_space=pltpu.SMEM)


def prepare_kernel(feat_count, masks, len_ref, pos_ref, lab_ref, owner_ref, score_ref,
                   kept_ref, qid_ref, worth_ref, inv_ref, perm_ref, bounds_ref):
    kept_ref[...] = score_ref[...]
    queries = len_ref.shape[1]
    rows = lab_ref.shape[0]
    own = rows // feat_count
    spot = iota((rows, LANES), 0) * LANES + iota((rows, LANES), 1)
    qid = jnp.zeros((rows, LANES), jnp.int32)
    begin = jnp.zeros((queries, LANES), jnp.int32)
    finish = jnp.zeros((queries, LANES), jnp.int32)
    which = iota((queries, LANES), 0)
    group = iota((1, LANES), 1) * LANES
    low = jnp.zeros((1, LANES), jnp.int32)
    high = first_end = jnp.full((1, LANES), rows * LANES, jnp.int32)
    start = jnp.int32(0)
    for q in range(queries):
        end = start + len_ref[0, q]
        qid = qid + jnp.where(spot >= end, 1, 0)
        begin = jnp.where(which == q, start, begin)
        finish = jnp.where(which == q, end, finish)

        low = low + jnp.where(end <= group, len_ref[0, q], 0)
        high = jnp.minimum(high, jnp.where(end >= group + LANES, end, rows * LANES))
        first_end = jnp.minimum(first_end, jnp.where(end > group, end, rows * LANES))
        start = end
    bounds_ref[...] = jnp.concatenate([low, high, first_end, low, low, low, low, low], axis=0)
    qid_ref[...] = qid
    worth_ref[...] = jnp.left_shift(1, lab_ref[...]).astype(F32)

    counts = [jnp.zeros((queries, LANES), F32) for _ in range(GRADES)]
    lane = iota((queries, LANES), 1)
    for r in range(rows):
        at = lane + r * LANES
        inside = (at >= begin) & (at < finish)
        grade = jnp.where(inside, jnp.broadcast_to(lab_ref[r:r + 1, :], (queries, LANES)), 0)
        for g in range(GRADES):
            counts[g] = counts[g] + jnp.where(grade > g, 1.0, 0.0)
    position = iota((queries, MAX_LEN), 1).astype(F32)
    gain = jnp.zeros((queries, MAX_LEN), F32)
    for g in range(GRADES):
        held = jnp.sum(counts[g], axis=1, keepdims=True)
        gain = gain + jnp.where(position < held, float(2 ** g), 0.0)
    level = 1.0 / jnp.log2(2.0 + position[0:1, :])
    ideal = jnp.sum(gain * level, axis=1, keepdims=True)
    usable = ideal > 0.5
    inverse = jnp.where(usable, 1.0 / jnp.where(usable, ideal, 1.0), 0.0)
    first = pos_ref[0] % feat_count * own
    for t in range(own):
        at = lane + (first + t) * LANES
        inside = (at >= begin) & (at < finish)
        inv_ref[0:1, t * LANES:(t + 1) * LANES] = jnp.sum(jnp.where(inside, inverse, 0.0), axis=0, keepdims=True)

    features = perm_ref.shape[0]
    per_dev = features >> len(masks)
    owner = jnp.concatenate([owner_ref[k:k + 1, :] for k in range(features // LANES)], axis=1)
    square = (features, features)
    down, across = iota(square, 0), iota(square, 1)
    index = iota((features, 1), 0) // per_dev
    target = jnp.zeros((features, 1), jnp.int32)
    for b, mask in enumerate(masks):
        target = target + ((index >> b) & 1) * mask
    target = (target ^ pos_ref[0]) * per_dev + iota((features, 1), 0) % per_dev
    pick = jnp.where(target == across, 1.0, 0.0).astype(BF16)
    holds = jnp.where(jnp.broadcast_to(owner, square) == down, 1.0, 0.0).astype(BF16)
    perm_ref[...] = lax.dot_general(pick, holds, NT, preferred_element_type=F32).astype(BF16)


def prepare(feat_count, masks, lengths, pos, labels, owner, scores):
    rows = labels.shape[0]
    features = owner.shape[0] * LANES
    return pl.pallas_call(
        functools.partial(prepare_kernel, feat_count, masks),
        out_shape=(
            jax.ShapeDtypeStruct(scores.shape, F32),
            jax.ShapeDtypeStruct((rows, LANES), jnp.int32),
            jax.ShapeDtypeStruct((rows, LANES), F32),
            jax.ShapeDtypeStruct((1, rows // feat_count * LANES), F32),
            jax.ShapeDtypeStruct((features, features), BF16),
            jax.ShapeDtypeStruct((8, LANES), jnp.int32),
        ),
        in_specs=[smem(), smem(), vmem(), vmem(), vmem()],
        out_specs=(vmem(),) * 6,
        compiler_params=pltpu.CompilerParams(vmem_limit_bytes=VMEM_LIMIT),
        cost_estimate=pl.CostEstimate(flops=2_000_000_000, bytes_accessed=300_000, transcendentals=20_000),
        name="prepare",
    )(lengths, pos, labels, owner, scores)


def split_terms(value, terms):
    parts = []
    rest = value
    for _ in range(terms):
        part = rest.astype(BF16)
        parts.append(part)
        rest = rest - part.astype(F32)
    return parts


def pairs_kernel(feat_count, bounds_ref, pos_ref, *refs):
    scores = refs[:-20]
    (worth_ref, qid_ref, inv_ref, lam_ref, near_ref,
     s_row, a_row, d_row, s_turn, a_turn, w_turn, q_turn, d_turn, s_col, a_col, w_col, q_col, d_col, grad, curv) = refs[-20:]
    rows = worth_ref.shape[0]
    own = rows // feat_count
    docs = own * LANES
    me = pos_ref[0] % feat_count
    s_row[...] = jnp.zeros(s_row.shape, F32)
    near = [me, ((me + 1) ^ 1) - 1, me ^ 1]
    for where, ref in zip(near, scores):
        @pl.when((where >= 0) & (where < feat_count))
        def _(where=where, ref=ref):
            s_row[pl.ds(pl.multiple_of(where * own, own), own), :] = ref[...]
    a_row[...] = jnp.exp(s_row[...])
    d_row[...] = jnp.zeros(d_row.shape, F32)
    first = me * own
    window_low = bounds_ref[0, first] // (2 * LANES) * 2
    window_high = (bounds_ref[1, first + own - 1] + 2 * LANES - 1) // (2 * LANES) * 2
    stride = 4

    def widen(pairs):
        for turn, source, _ in pairs:
            turn[...] = jnp.transpose(source[...])
        for r in range(0, rows, stride):
            @pl.when((r + stride > window_low) & (r < window_high))
            def _(r=r):
                for turn, _, col in pairs:
                    for k in range(r, r + stride):
                        col[k * LANES:(k + 1) * LANES, :] = jnp.broadcast_to(turn[:, k:k + 1], (LANES, LANES))

    widen([(s_turn, s_row, s_col), (q_turn, qid_ref, q_col), (a_turn, a_row, a_col), (w_turn, worth_ref, w_col)])

    def rows_of(ref, r):
        return [jnp.broadcast_to(ref[pl.ds(r + g, 1), :], (8, LANES)) for g in range(2)]

    def spans(r):
        start, end = bounds_ref[0, r], bounds_ref[1, r + 1]
        low = jnp.maximum(start // LANES, window_low)
        high = jnp.minimum((end + LANES - 1) // LANES, window_high)
        single = bounds_ref[2, r] >= (r + 2) * LANES
        inner_low = jnp.where(single, jnp.maximum((start + LANES - 1) // LANES, window_low), r)
        inner_high = jnp.where(single, jnp.minimum(end // LANES, window_high), r)
        return low, inner_low, inner_high, high

    def rank_groups(k, carry):
        r = window_low + 2 * k
        score = rows_of(s_row, r)
        query = rows_of(qid_ref, r)

        def gather(c, acc, masked, test):
            base = pl.multiple_of(c * LANES, LANES)
            acc = list(acc)
            for u in range(LANES // 8):
                other = s_col[pl.ds(base + 8 * u, 8), :]
                for g in range(2):
                    hit = test(other, g, u)
                    if masked:
                        hit = hit & (q_col[pl.ds(base + 8 * u, 8), :] == query[g])
                    acc[2 * g + u % 2] = acc[2 * g + u % 2] + jnp.where(hit, 1.0, 0.0)
            return tuple(acc)

        def ahead(other, g, u):
            return other >= score[g]

        def behind(other, g, u):
            return other > score[g]

        def within(mine):
            def test(other, g, u):
                if g != mine:
                    return ahead(other, g, u) if mine < g else behind(other, g, u)
                earlier = iota((8, LANES), 0) + 8 * u < iota((8, LANES), 1)
                return (other > score[g]) | ((other == score[g]) & earlier)
            return test

        acc = tuple(jnp.zeros((8, LANES), F32) for _ in range(4))
        low, inner_low, inner_high, high = spans(r)
        after = jnp.maximum(inner_high, r + 2)
        acc = lax.fori_loop(low, inner_low, lambda c, acc: gather(c, acc, True, ahead), acc)
        acc = lax.fori_loop(inner_low, r, lambda c, acc: gather(c, acc, False, ahead), acc)
        acc = lax.fori_loop(r + 2, after, lambda c, acc: gather(c, acc, False, behind), acc)
        acc = lax.fori_loop(after, high, lambda c, acc: gather(c, acc, True, behind), acc)
        for mine in range(2):
            acc = gather(r + mine, acc, True, within(mine))
        for g in range(2):
            d_row[pl.ds(r + g, 1), :] = jnp.sum(acc[2 * g] + acc[2 * g + 1], axis=0, keepdims=True)
        return carry

    lax.fori_loop(0, (window_high - window_low) // 2, rank_groups, 0)
    d_row[...] = 1.0 / jnp.log2(2.0 + d_row[...])
    widen([(d_turn, d_row, d_col)])

    def pair_groups(t, carry):
        r = first + 2 * t
        a_i, w_i, d_i, query = [rows_of(ref, r) for ref in (a_row, worth_ref, d_row, qid_ref)]

        def columns(masked):
            def step(c, acc):
                base = pl.multiple_of(c * LANES, LANES)
                acc = list(acc)
                for u in range(LANES // 8):
                    at = pl.ds(base + 8 * u, 8)
                    a_j, w_j, d_j = a_col[at, :], w_col[at, :], d_col[at, :]
                    for g in range(2):
                        recip = pl.reciprocal(a_i[g] + a_j, approx=True)
                        lift = w_i[g] - w_j
                        weight = jnp.abs(d_i[g] - d_j) * recip
                        if masked:
                            weight = jnp.where(q_col[at, :] == query[g], weight, 0.0)
                        weight = weight * lift
                        k = 4 * g + u % 2
                        acc[k] = acc[k] + weight * jnp.where(lift > 0.0, a_j, a_i[g])
                        acc[k + 2] = acc[k + 2] + jnp.abs(weight) * (recip * a_j)
                return tuple(acc)
            return step

        acc = tuple(jnp.zeros((8, LANES), F32) for _ in range(8))
        low, inner_low, inner_high, high = spans(r)
        acc = lax.fori_loop(low, inner_low, columns(True), acc)
        acc = lax.fori_loop(inner_low, inner_high, columns(False), acc)
        acc = lax.fori_loop(inner_high, high, columns(True), acc)
        for g in range(2):
            at = pl.ds(2 * t + g, 1)
            grad[at, :] = -jnp.sum(acc[4 * g] + acc[4 * g + 1], axis=0, keepdims=True)
            curv[at, :] = a_i[g][0:1, :] * jnp.sum(acc[4 * g + 2] + acc[4 * g + 3], axis=0, keepdims=True)
        return carry

    lax.fori_loop(0, own // 2, pair_groups, 0)
    inverse = inv_ref[...]
    terms = [inverse * jnp.concatenate([ref[t:t + 1, :] for t in range(own)], axis=1) for ref in (grad, curv)]
    for c in range(2):
        lam_ref[c:c + 1, :] = terms[c]
        near_ref[c:c + 1, :] = terms[c]


def pair_terms(feat_count, bounds, pos, scores, worth, qid, inverse):
    rows = worth.shape[0]
    docs = inverse.shape[1]
    row = pltpu.VMEM((rows, LANES), F32)
    turn = pltpu.VMEM((LANES, rows), F32)
    col = pltpu.VMEM((rows * LANES, LANES), F32)
    mine = pltpu.VMEM((docs // LANES, LANES), F32)
    return pl.pallas_call(
        functools.partial(pairs_kernel, feat_count),
        out_shape=(jax.ShapeDtypeStruct((2, docs), F32), jax.ShapeDtypeStruct((2, docs), F32)),
        in_specs=[smem(), smem()] + [vmem()] * (len(scores) + 3),
        out_specs=(vmem(), vmem()),
        scratch_shapes=[row, row, row, turn, turn, turn, pltpu.VMEM((LANES, rows), jnp.int32), turn,
                        col, col, col, pltpu.VMEM((rows * LANES, LANES), jnp.int32), col, mine, mine],
        compiler_params=pltpu.CompilerParams(vmem_limit_bytes=VMEM_LIMIT),
        cost_estimate=pl.CostEstimate(flops=9_000_000_000, bytes_accessed=200_000, transcendentals=2_000_000),
        name="pair_terms",
    )(bounds, pos, *scores, worth, qid, inverse)


def leaf_kernel(perm_ref, bins_ref, leaf_ref, lam_ref, bins_t_ref, tile_ref, sums_ref):
    bins = bins_ref[...].astype(F32).astype(BF16)
    bins_t_ref[...] = lax.dot_general(perm_ref[...], bins, NT, preferred_element_type=F32)
    own = leaf_ref.shape[0]
    docs = own * LANES
    leaf = jnp.concatenate([leaf_ref[t:t + 1, :] for t in range(own)], axis=1)
    highs = LEAVES // LANES
    top = jnp.broadcast_to(leaf // LANES, (highs, docs)) == iota((highs, docs), 0)
    spots = jnp.where(jnp.broadcast_to(leaf % LANES, (LANES, docs)) == iota((LANES, docs), 0), 1.0, 0.0).astype(BF16)
    pieces, tiles = [], []
    for c in range(2):
        for k, part in enumerate(split_terms(lam_ref[c:c + 1, :], 3)):
            line = part.astype(F32)
            pieces.append(jnp.where(top, jnp.broadcast_to(line, (highs, docs)), 0.0))
            if k < 2:
                tiles.append(jnp.broadcast_to(line, (HIGH, docs)))
    tile_ref[...] = jnp.concatenate(tiles, axis=0).astype(BF16)
    stacked = jnp.concatenate(pieces, axis=0).astype(BF16)
    sums = lax.dot_general(stacked, spots, NT, preferred_element_type=F32)
    for c in range(2):
        base = c * 3 * highs
        sums_ref[:, c * LANES:(c + 1) * LANES] = (
            sums[base:base + highs] + (sums[base + highs:base + 2 * highs] + sums[base + 2 * highs:base + 3 * highs])
        )


def leaf_terms(perm, bins, leaves, lambdas):
    docs, features = bins.shape
    return pl.pallas_call(
        leaf_kernel,
        out_shape=(
            jax.ShapeDtypeStruct((features, docs), F32),
            jax.ShapeDtypeStruct((4 * HIGH, docs), BF16),
            jax.ShapeDtypeStruct((LEAVES // LANES, 2 * LANES), F32),
        ),
        in_specs=[vmem()] * 4,
        out_specs=(vmem(), vmem(), vmem()),
        compiler_params=pltpu.CompilerParams(vmem_limit_bytes=VMEM_LIMIT),
        cost_estimate=pl.CostEstimate(flops=200_000_000, bytes_accessed=3_000_000, transcendentals=0),
        name="leaf_terms",
    )(perm, bins, leaves, lambdas)


def histogram_kernel(first, groups, tile_ref, bins_ref, *refs):
    out_ref = refs[-1]
    docs = tile_ref.shape[1]
    rows = 4 * HIGH
    width = FEW * LOW
    row = iota((rows, docs), 0)
    low_level = [(row + rows * k).astype(F32).astype(BF16) for k in range(LOW // rows)]
    high_level = (row % HIGH).astype(F32).astype(BF16)
    whose = [row // HIGH == f for f in range(FEW)]
    zero = jnp.zeros((rows, docs), BF16)
    one = jnp.ones((rows, docs), BF16)
    lane_owner = iota((1, width), 1) // LOW
    own_count = iota((rows, width), 0) // HIGH == iota((rows, width), 1) // LOW
    upper = iota((2 * HIGH, width), 0) < HIGH

    def fold(part):
        return part + pltpu.roll(part, HIGH, 0)

    def one_group(g, carry):
        base = pl.multiple_of((first + g) * GROUP, GROUP)
        code = bins_ref[pl.ds(base, GROUP), :]
        high = jnp.floor(code * (1.0 / LOW))
        low = code - high * LOW
        halves = []
        for half in range(GROUP // FEW):
            left, right = [], []
            both = None
            for f in range(FEW):
                at = slice(half * FEW + f, half * FEW + f + 1)
                high_f = jnp.broadcast_to(high[at, :], (rows, docs))
                low_f = jnp.broadcast_to(low[at, :], (rows, docs)).astype(BF16)
                both = high_f if both is None else jnp.where(whose[f], high_f, both)
                left.append(jnp.where(high_f.astype(BF16) == high_level, tile_ref[...], zero))
                for level in low_level:
                    right.append(jnp.where(low_f == level, one, zero))
            left.append(jnp.where(both.astype(BF16) == high_level, one, zero))
            acc = lax.dot_general(
                jnp.concatenate(left, axis=0), jnp.concatenate(right, axis=0), NT, preferred_element_type=F32)
            stats = acc[0:rows]
            for f in range(1, FEW):
                stats = jnp.where(lane_owner == f, acc[f * rows:(f + 1) * rows], stats)
            counts = jnp.where(own_count, acc[FEW * rows:], 0.0)
            halves.append([fold(stats[:2 * HIGH]), fold(stats[2 * HIGH:]), fold(counts[:2 * HIGH] + counts[2 * HIGH:])])
        out_ref[pl.ds(pl.multiple_of(g * 6 * HIGH, 6 * HIGH), 6 * HIGH), :] = jnp.concatenate(
            [jnp.where(upper, a, b) for a, b in zip(*halves)], axis=0)
        return carry

    if len(refs) > 1:
        out_ref[groups * 6 * HIGH:, :] = refs[0][...]
    lax.fori_loop(0, groups, one_group, 0, unroll=2)


def histogram_part(first, groups, tiles, bins_t, *tail):
    rows = groups * 6 * HIGH + sum(piece.shape[0] for piece in tail)
    return pl.pallas_call(
        functools.partial(histogram_kernel, first, groups),
        out_shape=jax.ShapeDtypeStruct((rows, FEW * LOW), F32),
        in_specs=[vmem()] * (2 + len(tail)),
        out_specs=vmem(),
        compiler_params=pltpu.CompilerParams(vmem_limit_bytes=VMEM_LIMIT),
        cost_estimate=pl.CostEstimate(flops=groups * 1_000_000, bytes_accessed=groups * 1_000, transcendentals=0),
        name="histogram_part",
    )(tiles, bins_t, *tail)


def finish_kernel(per_dev, leaf_ref, kept_ref, sums_ref, *refs):
    arrived = refs[:-3][::-1]
    value_ref, step_ref, hist_ref = refs[-3:]
    unit = kept_ref.shape[0]
    totals = add_up([sums_ref[...]] + [ref[unit:, :] for ref in arrived])
    highs = LEAVES // LANES
    grad, curv = totals[:, :LANES], totals[:, LANES:]
    shrunk = jnp.maximum(jnp.abs(grad) - lasso_penalty, 0.0)
    values = jnp.where(grad > 0.0, -shrunk, shrunk) / (curv + ridge_penalty)
    value_ref[...] = values
    leaf = leaf_ref[...]
    top, spot = leaf // LANES, leaf % LANES
    step = jnp.zeros(leaf.shape, F32)
    for h in range(highs):
        row = jnp.broadcast_to(values[h:h + 1, :], leaf.shape)
        step = jnp.where(top == h, jnp.take_along_axis(row, spot, axis=1), step)
    step_ref[...] = shrinkage * step
    hist = add_up([kept_ref[...]] + [ref[:unit, :] for ref in arrived])
    if per_dev == GROUP:
        for c in range(3):
            for f in range(GROUP):
                at = c * 2 * HIGH + f // FEW * HIGH
                span = slice(f % FEW * LOW, (f % FEW + 1) * LOW)
                line = [hist[at + h:at + h + 1, span] for h in range(HIGH)]
                hist_ref[c:c + 1, f * BINS:(f + 1) * BINS] = jnp.concatenate(line, axis=1)
    else:
        hist_ref[...] = hist


def finish(per_dev, leaves, kept, sums, arrived):
    out = (3, per_dev * BINS) if per_dev == GROUP else kept.shape
    return pl.pallas_call(
        functools.partial(finish_kernel, per_dev),
        out_shape=(
            jax.ShapeDtypeStruct((LEAVES // LANES, LANES), F32),
            jax.ShapeDtypeStruct(leaves.shape, F32),
            jax.ShapeDtypeStruct(out, F32),
        ),
        in_specs=[vmem()] * (3 + len(arrived)),
        out_specs=(vmem(), vmem(), vmem()),
        compiler_params=pltpu.CompilerParams(vmem_limit_bytes=VMEM_LIMIT),
        name="finish",
    )(leaves, kept, sums, *arrived)


def add_up(parts):
    while len(parts) > 1:
        parts = [parts[k] + parts[k + 1] for k in range(0, len(parts), 2)]
    return parts[0]


def local(scores, labels, leaves, bins, lengths, owner):
    query_count = lax.axis_size("query")
    feat_count = lax.axis_size("feat")
    count = query_count * feat_count
    place = lax.axis_index("query").astype(jnp.int32) * feat_count + lax.axis_index("feat").astype(jnp.int32)
    docs = scores.shape[0]
    own = docs // LANES
    features = owner.shape[0]
    per_dev = features // count
    unit = 3 * per_dev
    axes = ("query", "feat")
    feat_masks = [1 << b for b in range(feat_count.bit_length() - 1)]
    query_masks = [feat_count << b for b in range(query_count.bit_length() - 1)]

    def swap(value, mask):
        return lax.ppermute(value, axes, [(p, p ^ mask) for p in range(count)])

    pos = place.reshape(1)
    leaf_rows = leaves.reshape(own, LANES)
    own_scores = scores.reshape(own, LANES)
    score_parts = [own_scores]
    for begin in (1, 0):
        links = [(z, z + 1) for z in range(begin, feat_count - 1, 2)]
        links += [(0, feat_count - 1)] if begin else []
        score_parts.append(lax.ppermute(own_scores, "feat", links + [(b, a) for a, b in links]))
    masks = feat_masks + query_masks[:0:-1] + query_masks[:1]
    score_parts[0], qid, worth, inverse, perm, bounds = prepare(
        feat_count, masks, lengths, pos, labels.reshape(-1, LANES), owner.reshape(-1, LANES), own_scores)
    lambdas, near_lambdas = pair_terms(feat_count, bounds, pos, score_parts, worth, qid, inverse)
    bins_t, tiles, sums = leaf_terms(perm, bins, leaf_rows, near_lambdas)

    def part(tiles, low, high, *tail):
        if per_dev == GROUP:
            return histogram_part(low, high - low, tiles, bins_t, *tail)
        groups = high - low
        wide = histogram_part(low, groups, tiles, bins_t)
        wide = wide.reshape(groups, 3, GROUP // FEW, HIGH, FEW, LOW).transpose(0, 2, 4, 1, 3, 5)
        wide = wide.reshape(groups, GROUP // per_dev, per_dev, 3, BINS).transpose(0, 1, 3, 2, 4)
        return jnp.concatenate([wide.reshape(groups * GROUP // per_dev * unit, BINS), *tail], axis=0)

    def join(block, total):
        return jnp.concatenate([block, total], axis=0)

    eighth = features // GROUP // 8
    edge = count // 8 * unit
    arrived = swap(part(tiles, 6 * eighth, 8 * eighth, sums), query_masks[0])
    block = part(tiles, 3 * eighth, 4 * eighth) + arrived[edge:2 * edge]
    sums = sums + arrived[2 * edge:]
    message, tiles = lax.optimization_barrier((join(block, sums), tiles))
    crossed_far = swap(message, query_masks[1])
    block = part(tiles, 2 * eighth, 3 * eighth) + arrived[:edge]
    message, tiles = lax.optimization_barrier((block, tiles))
    crossed_near = swap(message, query_masks[1])
    arrived = swap(part(tiles, 4 * eighth, 6 * eighth), query_masks[0])
    block = part(tiles, eighth, 2 * eighth) + arrived[edge:] + crossed_far[:edge]
    sums = sums + crossed_far[edge:]
    message, tiles = lax.optimization_barrier((join(block, sums), tiles))
    turned = swap(message, query_masks[2])
    kept = part(tiles, 0, eighth) + arrived[:edge] + crossed_near + turned[:edge]
    sums = sums + turned[edge:]
    for mask in query_masks[3:]:
        edge = edge // 2
        arrived = swap(join(kept[edge:], sums), mask)
        kept = kept[:edge] + arrived[:edge]
        sums = sums + arrived[edge:]
    arrived = [swap(join(kept[m * unit:(m + 1) * unit], sums), m) for m in range(1, feat_count)]
    values, step, histograms = finish(per_dev, leaf_rows, kept[:unit], sums, arrived[::-1])
    return lambdas, values.reshape(LEAVES), step.reshape(docs), histograms.reshape(3, per_dev * BINS)


def solution(mesh):
    in_specs = (
        P(("query", "feat")),
        P("query"),
        P(("query", "feat")),
        P(("query", "feat"), None),
        P("query", None),
        P(),
    )
    out_specs = (P(None, ("query", "feat")), P(), P(("query", "feat")), P(None, ("query", "feat")))
    return jax.shard_map(local, mesh=mesh, in_specs=in_specs, out_specs=out_specs, check_vma=False)
```

```python
import functools

import jax
import jax.numpy as jnp
from jax import lax
from jax.experimental import pallas as pl
from jax.experimental.pallas import tpu as pltpu
from jax.sharding import PartitionSpec as P

BINS = 256
LEAVES = 1024
LANES = 128
GRADES = 4
LOW = 32
HIGH = BINS // LOW
GROUP = 8
CHUNK = 64
MAX_LEN = 1024

lasso_penalty = 1.0
ridge_penalty = 1.0
shrinkage = 0.1

VMEM_LIMIT = 48 * 1024 * 1024
F32 = jnp.float32
BF16 = jnp.bfloat16
NT = (((1,), (1,)), ((), ()))


def iota(shape, axis):
    return lax.broadcasted_iota(jnp.int32, shape, axis)


def vmem():
    return pl.BlockSpec(memory_space=pltpu.VMEM)


def smem():
    return pl.BlockSpec(memory_space=pltpu.SMEM)


def prepare_kernel(feat_count, masks, len_ref, pos_ref, lab_ref, owner_ref, score_ref,
                   kept_ref, qid_ref, worth_ref, inv_ref, perm_ref, bounds_ref):
    kept_ref[...] = score_ref[...]
    queries = len_ref.shape[1]
    rows = lab_ref.shape[0]
    own = rows // feat_count
    spot = iota((rows, LANES), 0) * LANES + iota((rows, LANES), 1)
    qid = jnp.zeros((rows, LANES), jnp.int32)
    begin = jnp.zeros((queries, LANES), jnp.int32)
    finish = jnp.zeros((queries, LANES), jnp.int32)
    which = iota((queries, LANES), 0)
    group = iota((1, LANES), 1) * LANES
    low = jnp.zeros((1, LANES), jnp.int32)
    high = first_end = jnp.full((1, LANES), rows * LANES, jnp.int32)
    start = jnp.int32(0)
    for q in range(queries):
        end = start + len_ref[0, q]
        qid = qid + jnp.where(spot >= end, 1, 0)
        begin = jnp.where(which == q, start, begin)
        finish = jnp.where(which == q, end, finish)

        low = low + jnp.where(end <= group, len_ref[0, q], 0)
        high = jnp.minimum(high, jnp.where(end >= group + LANES, end, rows * LANES))
        first_end = jnp.minimum(first_end, jnp.where(end > group, end, rows * LANES))
        start = end
    bounds_ref[...] = jnp.concatenate([low, high, first_end, low, low, low, low, low], axis=0)
    qid_ref[...] = qid
    worth_ref[...] = jnp.left_shift(1, lab_ref[...]).astype(F32)

    counts = [jnp.zeros((queries, LANES), F32) for _ in range(GRADES)]
    lane = iota((queries, LANES), 1)
    for r in range(rows):
        at = lane + r * LANES
        inside = (at >= begin) & (at < finish)
        grade = jnp.where(inside, jnp.broadcast_to(lab_ref[r:r + 1, :], (queries, LANES)), 0)
        for g in range(GRADES):
            counts[g] = counts[g] + jnp.where(grade > g, 1.0, 0.0)
    position = iota((queries, MAX_LEN), 1).astype(F32)
    gain = jnp.zeros((queries, MAX_LEN), F32)
    for g in range(GRADES):
        held = jnp.sum(counts[g], axis=1, keepdims=True)
        gain = gain + jnp.where(position < held, float(2 ** g), 0.0)
    level = 1.0 / jnp.log2(2.0 + position[0:1, :])
    ideal = jnp.sum(gain * level, axis=1, keepdims=True)
    usable = ideal > 0.5
    inverse = jnp.where(usable, 1.0 / jnp.where(usable, ideal, 1.0), 0.0)
    first = pos_ref[0] % feat_count * own
    for t in range(own):
        at = lane + (first + t) * LANES
        inside = (at >= begin) & (at < finish)
        inv_ref[0:1, t * LANES:(t + 1) * LANES] = jnp.sum(jnp.where(inside, inverse, 0.0), axis=0, keepdims=True)

    features = perm_ref.shape[0]
    per_dev = features >> len(masks)
    owner = jnp.concatenate([owner_ref[k:k + 1, :] for k in range(features // LANES)], axis=1)
    square = (features, features)
    down, across = iota(square, 0), iota(square, 1)
    index = iota((features, 1), 0) // per_dev
    target = jnp.zeros((features, 1), jnp.int32)
    for b, mask in enumerate(masks):
        target = target + ((index >> b) & 1) * mask
    target = (target ^ pos_ref[0]) * per_dev + iota((features, 1), 0) % per_dev
    pick = jnp.where(target == across, 1.0, 0.0).astype(BF16)
    holds = jnp.where(jnp.broadcast_to(owner, square) == down, 1.0, 0.0).astype(BF16)
    perm_ref[...] = lax.dot_general(pick, holds, NT, preferred_element_type=F32).astype(BF16)


def prepare(feat_count, masks, lengths, pos, labels, owner, scores):
    rows = labels.shape[0]
    features = owner.shape[0] * LANES
    return pl.pallas_call(
        functools.partial(prepare_kernel, feat_count, masks),
        out_shape=(
            jax.ShapeDtypeStruct(scores.shape, F32),
            jax.ShapeDtypeStruct((rows, LANES), jnp.int32),
            jax.ShapeDtypeStruct((rows, LANES), F32),
            jax.ShapeDtypeStruct((1, rows // feat_count * LANES), F32),
            jax.ShapeDtypeStruct((features, features), BF16),
            jax.ShapeDtypeStruct((8, LANES), jnp.int32),
        ),
        in_specs=[smem(), smem(), vmem(), vmem(), vmem()],
        out_specs=(vmem(),) * 6,
        compiler_params=pltpu.CompilerParams(vmem_limit_bytes=VMEM_LIMIT),
        cost_estimate=pl.CostEstimate(flops=2_000_000_000, bytes_accessed=300_000, transcendentals=20_000),
        name="prepare",
    )(lengths, pos, labels, owner, scores)


def split_terms(value, terms):
    parts = []
    rest = value
    for _ in range(terms):
        part = rest.astype(BF16)
        parts.append(part)
        rest = rest - part.astype(F32)
    return parts


def pairs_kernel(feat_count, bounds_ref, pos_ref, *refs):
    scores = refs[:-20]
    (worth_ref, qid_ref, inv_ref, lam_ref, near_ref,
     s_row, a_row, d_row, s_turn, a_turn, w_turn, q_turn, d_turn, s_col, a_col, w_col, q_col, d_col, grad, curv) = refs[-20:]
    rows = worth_ref.shape[0]
    own = rows // feat_count
    docs = own * LANES
    me = pos_ref[0] % feat_count
    s_row[...] = jnp.zeros(s_row.shape, F32)
    near = [me, ((me + 1) ^ 1) - 1, me ^ 1]
    for where, ref in zip(near, scores):
        @pl.when((where >= 0) & (where < feat_count))
        def _(where=where, ref=ref):
            s_row[pl.ds(pl.multiple_of(where * own, own), own), :] = ref[...]
    a_row[...] = jnp.exp(s_row[...])
    d_row[...] = jnp.zeros(d_row.shape, F32)
    first = me * own
    window_low = bounds_ref[0, first] // (2 * LANES) * 2
    window_high = (bounds_ref[1, first + own - 1] + 2 * LANES - 1) // (2 * LANES) * 2
    stride = 4

    def widen(pairs):
        for turn, source, _ in pairs:
            turn[...] = jnp.transpose(source[...])
        for r in range(0, rows, stride):
            @pl.when((r + stride > window_low) & (r < window_high))
            def _(r=r):
                for turn, _, col in pairs:
                    for k in range(r, r + stride):
                        col[k * LANES:(k + 1) * LANES, :] = jnp.broadcast_to(turn[:, k:k + 1], (LANES, LANES))

    widen([(s_turn, s_row, s_col), (q_turn, qid_ref, q_col), (a_turn, a_row, a_col), (w_turn, worth_ref, w_col)])

    def rows_of(ref, r):
        return [jnp.broadcast_to(ref[pl.ds(r + g, 1), :], (8, LANES)) for g in range(2)]

    def spans(r):
        start, end = bounds_ref[0, r], bounds_ref[1, r + 1]
        low = jnp.maximum(start // LANES, window_low)
        high = jnp.minimum((end + LANES - 1) // LANES, window_high)
        single = bounds_ref[2, r] >= (r + 2) * LANES
        inner_low = jnp.where(single, jnp.maximum((start + LANES - 1) // LANES, window_low), r)
        inner_high = jnp.where(single, jnp.minimum(end // LANES, window_high), r)
        return low, inner_low, inner_high, high

    def rank_groups(k, carry):
        r = window_low + 2 * k
        score = rows_of(s_row, r)
        query = rows_of(qid_ref, r)

        def gather(c, acc, masked, test):
            base = pl.multiple_of(c * LANES, LANES)
            acc = list(acc)
            for u in range(LANES // 8):
                other = s_col[pl.ds(base + 8 * u, 8), :]
                for g in range(2):
                    hit = test(other, g, u)
                    if masked:
                        hit = hit & (q_col[pl.ds(base + 8 * u, 8), :] == query[g])
                    acc[2 * g + u % 2] = acc[2 * g + u % 2] + jnp.where(hit, 1.0, 0.0)
            return tuple(acc)

        def ahead(other, g, u):
            return other >= score[g]

        def behind(other, g, u):
            return other > score[g]

        def within(mine):
            def test(other, g, u):
                if g != mine:
                    return ahead(other, g, u) if mine < g else behind(other, g, u)
                earlier = iota((8, LANES), 0) + 8 * u < iota((8, LANES), 1)
                return (other > score[g]) | ((other == score[g]) & earlier)
            return test

        acc = tuple(jnp.zeros((8, LANES), F32) for _ in range(4))
        low, inner_low, inner_high, high = spans(r)
        after = jnp.maximum(inner_high, r + 2)
        acc = lax.fori_loop(low, inner_low, lambda c, acc: gather(c, acc, True, ahead), acc)
        acc = lax.fori_loop(inner_low, r, lambda c, acc: gather(c, acc, False, ahead), acc)
        acc = lax.fori_loop(r + 2, after, lambda c, acc: gather(c, acc, False, behind), acc)
        acc = lax.fori_loop(after, high, lambda c, acc: gather(c, acc, True, behind), acc)
        for mine in range(2):
            acc = gather(r + mine, acc, True, within(mine))
        for g in range(2):
            d_row[pl.ds(r + g, 1), :] = jnp.sum(acc[2 * g] + acc[2 * g + 1], axis=0, keepdims=True)
        return carry

    lax.fori_loop(0, (window_high - window_low) // 2, rank_groups, 0)
    d_row[...] = 1.0 / jnp.log2(2.0 + d_row[...])
    widen([(d_turn, d_row, d_col)])

    def pair_groups(t, carry):
        r = first + 2 * t
        a_i, w_i, d_i, query = [rows_of(ref, r) for ref in (a_row, worth_ref, d_row, qid_ref)]

        def columns(masked):
            def step(c, acc):
                base = pl.multiple_of(c * LANES, LANES)
                acc = list(acc)
                for u in range(LANES // 8):
                    at = pl.ds(base + 8 * u, 8)
                    a_j, w_j, d_j = a_col[at, :], w_col[at, :], d_col[at, :]
                    for g in range(2):
                        recip = pl.reciprocal(a_i[g] + a_j, approx=True)
                        lift = w_i[g] - w_j
                        weight = jnp.abs(d_i[g] - d_j) * recip
                        if masked:
                            weight = jnp.where(q_col[at, :] == query[g], weight, 0.0)
                        weight = weight * lift
                        k = 4 * g + u % 2
                        acc[k] = acc[k] + weight * jnp.where(lift > 0.0, a_j, a_i[g])
                        acc[k + 2] = acc[k + 2] + jnp.abs(weight) * (recip * a_j)
                return tuple(acc)
            return step

        acc = tuple(jnp.zeros((8, LANES), F32) for _ in range(8))
        low, inner_low, inner_high, high = spans(r)
        acc = lax.fori_loop(low, inner_low, columns(True), acc)
        acc = lax.fori_loop(inner_low, inner_high, columns(False), acc)
        acc = lax.fori_loop(inner_high, high, columns(True), acc)
        for g in range(2):
            at = pl.ds(2 * t + g, 1)
            grad[at, :] = -jnp.sum(acc[4 * g] + acc[4 * g + 1], axis=0, keepdims=True)
            curv[at, :] = a_i[g][0:1, :] * jnp.sum(acc[4 * g + 2] + acc[4 * g + 3], axis=0, keepdims=True)
        return carry

    lax.fori_loop(0, own // 2, pair_groups, 0)
    inverse = inv_ref[...]
    terms = [inverse * jnp.concatenate([ref[t:t + 1, :] for t in range(own)], axis=1) for ref in (grad, curv)]
    for c in range(2):
        lam_ref[c:c + 1, :] = terms[c]
        near_ref[c:c + 1, :] = terms[c]


def pair_terms(feat_count, bounds, pos, scores, worth, qid, inverse):
    rows = worth.shape[0]
    docs = inverse.shape[1]
    row = pltpu.VMEM((rows, LANES), F32)
    turn = pltpu.VMEM((LANES, rows), F32)
    col = pltpu.VMEM((rows * LANES, LANES), F32)
    mine = pltpu.VMEM((docs // LANES, LANES), F32)
    return pl.pallas_call(
        functools.partial(pairs_kernel, feat_count),
        out_shape=(jax.ShapeDtypeStruct((2, docs), F32), jax.ShapeDtypeStruct((2, docs), F32)),
        in_specs=[smem(), smem()] + [vmem()] * (len(scores) + 3),
        out_specs=(vmem(), vmem()),
        scratch_shapes=[row, row, row, turn, turn, turn, pltpu.VMEM((LANES, rows), jnp.int32), turn,
                        col, col, col, pltpu.VMEM((rows * LANES, LANES), jnp.int32), col, mine, mine],
        compiler_params=pltpu.CompilerParams(vmem_limit_bytes=VMEM_LIMIT),
        cost_estimate=pl.CostEstimate(flops=9_000_000_000, bytes_accessed=200_000, transcendentals=2_000_000),
        name="pair_terms",
    )(bounds, pos, *scores, worth, qid, inverse)


def leaf_kernel(perm_ref, bins_ref, leaf_ref, lam_ref, bins_t_ref, tile_ref, sums_ref):
    bins = bins_ref[...].astype(F32).astype(BF16)
    bins_t_ref[...] = lax.dot_general(perm_ref[...], bins, NT, preferred_element_type=F32)
    own = leaf_ref.shape[0]
    docs = own * LANES
    leaf = jnp.concatenate([leaf_ref[t:t + 1, :] for t in range(own)], axis=1)
    highs = LEAVES // LANES
    top = jnp.broadcast_to(leaf // LANES, (highs, docs)) == iota((highs, docs), 0)
    spots = jnp.where(jnp.broadcast_to(leaf % LANES, (LANES, docs)) == iota((LANES, docs), 0), 1.0, 0.0).astype(BF16)
    pieces, tiles = [], []
    for c in range(2):
        for k, part in enumerate(split_terms(lam_ref[c:c + 1, :], 3)):
            wide = jnp.broadcast_to(part.astype(F32), (highs, docs))
            pieces.append(jnp.where(top, wide, 0.0))
            if k < 2:
                tiles.append(wide)
    tile_ref[...] = jnp.concatenate(tiles, axis=0).astype(BF16)
    stacked = jnp.concatenate(pieces, axis=0).astype(BF16)
    sums = lax.dot_general(stacked, spots, NT, preferred_element_type=F32)
    for c in range(2):
        base = c * 3 * highs
        sums_ref[:, c * LANES:(c + 1) * LANES] = (
            sums[base:base + highs] + (sums[base + highs:base + 2 * highs] + sums[base + 2 * highs:base + 3 * highs])
        )


def leaf_terms(perm, bins, leaves, lambdas):
    docs, features = bins.shape
    return pl.pallas_call(
        leaf_kernel,
        out_shape=(
            jax.ShapeDtypeStruct((features, docs), F32),
            jax.ShapeDtypeStruct((4 * HIGH, docs), BF16),
            jax.ShapeDtypeStruct((LEAVES // LANES, 2 * LANES), F32),
        ),
        in_specs=[vmem()] * 4,
        out_specs=(vmem(), vmem(), vmem()),
        compiler_params=pltpu.CompilerParams(vmem_limit_bytes=VMEM_LIMIT),
        cost_estimate=pl.CostEstimate(flops=200_000_000, bytes_accessed=3_000_000, transcendentals=0),
        name="leaf_terms",
    )(perm, bins, leaves, lambdas)


def histogram_kernel(first, groups, tile_ref, bins_ref, *refs):
    out_ref = refs[-1]
    docs = tile_ref.shape[1]
    depth = docs
    rows = 16
    row = iota((rows, depth), 0)
    low_level = [(row + rows * k).astype(F32).astype(BF16) for k in range(LOW // rows)]
    high_level = (row % HIGH).astype(F32).astype(BF16)
    upper = jnp.where(row < HIGH, 1.0, 0.0).astype(BF16) > 0
    zero = jnp.zeros((rows, depth), BF16)
    one = jnp.ones((rows, depth), BF16)
    lane_owner = iota((1, GROUP * LOW), 1) // LOW

    def one_group(g, carry):
        base = pl.multiple_of((first + g) * GROUP, GROUP)
        acc = None
        for k in range(docs // depth):
            span = slice(k * depth, (k + 1) * depth)
            code = bins_ref[pl.ds(base, GROUP), span]
            high = jnp.floor(code * (1.0 / LOW))
            low = code - high * LOW
            left, right, count = [], [], []
            wide = []
            for f in range(GROUP):
                high_f = jnp.broadcast_to(high[f:f + 1, :], (rows, depth))
                low_f = jnp.broadcast_to(low[f:f + 1, :], (rows, depth)).astype(BF16)
                high_f = high_f.astype(BF16)
                wide.append(high_f)
                match = high_f == high_level
                for c in range(2):
                    left.append(jnp.where(match, tile_ref[c * rows:(c + 1) * rows, span], zero))
                for level in low_level:
                    right.append(jnp.where(low_f == level, one, zero))
            for f in range(0, GROUP, 2):
                both = jnp.where(upper, wide[f], wide[f + 1])
                count.append(jnp.where(both == high_level, one, zero))
            part = lax.dot_general(
                jnp.concatenate(left + count, axis=0), jnp.concatenate(right, axis=0), NT,
                preferred_element_type=F32,
            )
            acc = part if acc is None else acc + part
        stats = jnp.zeros((2 * rows, GROUP * LOW), F32)
        counts = jnp.zeros((HIGH, GROUP * LOW), F32)
        for f in range(GROUP):
            mine = lane_owner == f
            stats = jnp.where(mine, acc[f * 2 * rows:(f + 1) * 2 * rows], stats)
            at = GROUP * 2 * rows + f * HIGH
            counts = jnp.where(mine, acc[at:at + HIGH], counts)
        out_ref[pl.ds(pl.multiple_of(g * 3 * HIGH, 3 * HIGH), 3 * HIGH), :] = jnp.concatenate(
            [stats[0:HIGH] + stats[HIGH:2 * HIGH], stats[2 * HIGH:3 * HIGH] + stats[3 * HIGH:4 * HIGH], counts], axis=0)
        return carry

    if len(refs) > 1:
        out_ref[groups * 3 * HIGH:, :] = refs[0][...]
    lax.fori_loop(0, groups, one_group, 0, unroll=2)


def histogram_part(first, groups, tiles, bins_t, *tail):
    rows = groups * 3 * HIGH + sum(piece.shape[0] for piece in tail)
    return pl.pallas_call(
        functools.partial(histogram_kernel, first, groups),
        out_shape=jax.ShapeDtypeStruct((rows, GROUP * LOW), F32),
        in_specs=[vmem()] * (2 + len(tail)),
        out_specs=vmem(),
        compiler_params=pltpu.CompilerParams(vmem_limit_bytes=VMEM_LIMIT),
        cost_estimate=pl.CostEstimate(flops=groups * 1_000_000, bytes_accessed=groups * 1_000, transcendentals=0),
        name="histogram_part",
    )(tiles, bins_t, *tail)


def finish_kernel(per_dev, leaf_ref, kept_ref, sums_ref, *refs):
    arrived = refs[:-3][::-1]
    value_ref, step_ref, hist_ref = refs[-3:]
    unit = kept_ref.shape[0]
    totals = add_up([sums_ref[...]] + [ref[unit:, :] for ref in arrived])
    highs = LEAVES // LANES
    grad, curv = totals[:, :LANES], totals[:, LANES:]
    shrunk = jnp.maximum(jnp.abs(grad) - lasso_penalty, 0.0)
    values = jnp.where(grad > 0.0, -shrunk, shrunk) / (curv + ridge_penalty)
    value_ref[...] = values
    leaf = leaf_ref[...]
    top, spot = leaf // LANES, leaf % LANES
    step = jnp.zeros(leaf.shape, F32)
    for h in range(highs):
        row = jnp.broadcast_to(values[h:h + 1, :], leaf.shape)
        step = jnp.where(top == h, jnp.take_along_axis(row, spot, axis=1), step)
    step_ref[...] = shrinkage * step
    hist = add_up([kept_ref[...]] + [ref[:unit, :] for ref in arrived])
    if per_dev == GROUP:
        for c in range(3):
            for f in range(GROUP):
                line = [hist[c * HIGH + h:c * HIGH + h + 1, f * LOW:(f + 1) * LOW] for h in range(HIGH)]
                hist_ref[c:c + 1, f * BINS:(f + 1) * BINS] = jnp.concatenate(line, axis=1)
    else:
        hist_ref[...] = hist


def finish(per_dev, leaves, kept, sums, arrived):
    out = (3, per_dev * BINS) if per_dev == GROUP else kept.shape
    return pl.pallas_call(
        functools.partial(finish_kernel, per_dev),
        out_shape=(
            jax.ShapeDtypeStruct((LEAVES // LANES, LANES), F32),
            jax.ShapeDtypeStruct(leaves.shape, F32),
            jax.ShapeDtypeStruct(out, F32),
        ),
        in_specs=[vmem()] * (3 + len(arrived)),
        out_specs=(vmem(), vmem(), vmem()),
        compiler_params=pltpu.CompilerParams(vmem_limit_bytes=VMEM_LIMIT),
        name="finish",
    )(leaves, kept, sums, *arrived)


def add_up(parts):
    while len(parts) > 1:
        parts = [parts[k] + parts[k + 1] for k in range(0, len(parts), 2)]
    return parts[0]


def local(scores, labels, leaves, bins, lengths, owner):
    query_count = lax.axis_size("query")
    feat_count = lax.axis_size("feat")
    count = query_count * feat_count
    place = lax.axis_index("query").astype(jnp.int32) * feat_count + lax.axis_index("feat").astype(jnp.int32)
    docs = scores.shape[0]
    own = docs // LANES
    features = owner.shape[0]
    per_dev = features // count
    unit = 3 * per_dev
    axes = ("query", "feat")
    feat_masks = [1 << b for b in range(feat_count.bit_length() - 1)]
    query_masks = [feat_count << b for b in range(query_count.bit_length() - 1)]

    def swap(value, mask):
        return lax.ppermute(value, axes, [(p, p ^ mask) for p in range(count)])

    pos = place.reshape(1)
    leaf_rows = leaves.reshape(own, LANES)
    own_scores = scores.reshape(own, LANES)
    score_parts = [own_scores]
    for begin in (1, 0):
        links = [(z, z + 1) for z in range(begin, feat_count - 1, 2)]
        links += [(0, feat_count - 1)] if begin else []
        score_parts.append(lax.ppermute(own_scores, "feat", links + [(b, a) for a, b in links]))
    masks = feat_masks + query_masks[:0:-1] + query_masks[:1]
    score_parts[0], qid, worth, inverse, perm, bounds = prepare(
        feat_count, masks, lengths, pos, labels.reshape(-1, LANES), owner.reshape(-1, LANES), own_scores)
    lambdas, near_lambdas = pair_terms(feat_count, bounds, pos, score_parts, worth, qid, inverse)
    bins_t, tiles, sums = leaf_terms(perm, bins, leaf_rows, near_lambdas)

    def part(tiles, low, high, *tail):
        if per_dev == GROUP:
            return histogram_part(low, high - low, tiles, bins_t, *tail)
        groups = high - low
        wide = histogram_part(low, groups, tiles, bins_t)
        wide = wide.reshape(groups, 3, HIGH, GROUP // per_dev, per_dev, LOW).transpose(0, 3, 1, 4, 2, 5)
        return jnp.concatenate([wide.reshape(groups * GROUP // per_dev * unit, BINS), *tail], axis=0)

    def join(block, total):
        return jnp.concatenate([block, total], axis=0)

    eighth = features // GROUP // 8
    edge = count // 8 * unit
    arrived = swap(part(tiles, 6 * eighth, 8 * eighth, sums), query_masks[0])
    block = part(tiles, 3 * eighth, 4 * eighth) + arrived[edge:2 * edge]
    sums = sums + arrived[2 * edge:]
    message, tiles = lax.optimization_barrier((join(block, sums), tiles))
    crossed_far = swap(message, query_masks[1])
    block = part(tiles, 2 * eighth, 3 * eighth) + arrived[:edge]
    message, tiles = lax.optimization_barrier((block, tiles))
    crossed_near = swap(message, query_masks[1])
    arrived = swap(part(tiles, 4 * eighth, 6 * eighth), query_masks[0])
    block = part(tiles, eighth, 2 * eighth) + arrived[edge:] + crossed_far[:edge]
    sums = sums + crossed_far[edge:]
    message, tiles = lax.optimization_barrier((join(block, sums), tiles))
    turned = swap(message, query_masks[2])
    kept = part(tiles, 0, eighth) + arrived[:edge] + crossed_near + turned[:edge]
    sums = sums + turned[edge:]
    for mask in query_masks[3:]:
        edge = edge // 2
        arrived = swap(join(kept[edge:], sums), mask)
        kept = kept[:edge] + arrived[:edge]
        sums = sums + arrived[edge:]
    arrived = [swap(join(kept[m * unit:(m + 1) * unit], sums), m) for m in range(1, feat_count)]
    values, step, histograms = finish(per_dev, leaf_rows, kept[:unit], sums, arrived[::-1])
    return lambdas, values.reshape(LEAVES), step.reshape(docs), histograms.reshape(3, per_dev * BINS)


def solution(mesh):
    in_specs = (
        P(("query", "feat")),
        P("query"),
        P(("query", "feat")),
        P(("query", "feat"), None),
        P("query", None),
        P(),
    )
    out_specs = (P(None, ("query", "feat")), P(), P(("query", "feat")), P(None, ("query", "feat")))
    return jax.shard_map(local, mesh=mesh, in_specs=in_specs, out_specs=out_specs, check_vma=False)
```

```python
import functools

import jax
import jax.numpy as jnp
from jax import lax
from jax.experimental import pallas as pl
from jax.experimental.pallas import tpu as pltpu
from jax.sharding import PartitionSpec as P

BINS = 256
LEAVES = 1024
LANES = 128
GRADES = 4
LOW = 32
HIGH = BINS // LOW
GROUP = 8
CHUNK = 64
MAX_LEN = 1024

lasso_penalty = 1.0
ridge_penalty = 1.0
shrinkage = 0.1

VMEM_LIMIT = 48 * 1024 * 1024
F32 = jnp.float32
BF16 = jnp.bfloat16
NT = (((1,), (1,)), ((), ()))


def iota(shape, axis):
    return lax.broadcasted_iota(jnp.int32, shape, axis)


def vmem():
    return pl.BlockSpec(memory_space=pltpu.VMEM)


def smem():
    return pl.BlockSpec(memory_space=pltpu.SMEM)


def prepare_kernel(feat_count, masks, len_ref, pos_ref, lab_ref, owner_ref, score_ref,
                   kept_ref, qid_ref, worth_ref, inv_ref, perm_ref, bounds_ref):
    kept_ref[...] = score_ref[...]
    queries = len_ref.shape[1]
    rows = lab_ref.shape[0]
    own = rows // feat_count
    spot = iota((rows, LANES), 0) * LANES + iota((rows, LANES), 1)
    qid = jnp.zeros((rows, LANES), jnp.int32)
    begin = jnp.zeros((queries, LANES), jnp.int32)
    finish = jnp.zeros((queries, LANES), jnp.int32)
    which = iota((queries, LANES), 0)
    group = iota((1, LANES), 1) * LANES
    low = jnp.zeros((1, LANES), jnp.int32)
    high = first_end = jnp.full((1, LANES), rows * LANES, jnp.int32)
    start = jnp.int32(0)
    for q in range(queries):
        end = start + len_ref[0, q]
        qid = qid + jnp.where(spot >= end, 1, 0)
        begin = jnp.where(which == q, start, begin)
        finish = jnp.where(which == q, end, finish)

        low = low + jnp.where(end <= group, len_ref[0, q], 0)
        high = jnp.minimum(high, jnp.where(end >= group + LANES, end, rows * LANES))
        first_end = jnp.minimum(first_end, jnp.where(end > group, end, rows * LANES))
        start = end
    bounds_ref[...] = jnp.concatenate([low, high, first_end, low, low, low, low, low], axis=0)
    qid_ref[...] = qid
    worth_ref[...] = jnp.left_shift(1, lab_ref[...]).astype(F32)

    counts = [jnp.zeros((queries, LANES), F32) for _ in range(GRADES)]
    lane = iota((queries, LANES), 1)
    for r in range(rows):
        at = lane + r * LANES
        inside = (at >= begin) & (at < finish)
        grade = jnp.where(inside, jnp.broadcast_to(lab_ref[r:r + 1, :], (queries, LANES)), 0)
        for g in range(GRADES):
            counts[g] = counts[g] + jnp.where(grade > g, 1.0, 0.0)
    position = iota((queries, MAX_LEN), 1).astype(F32)
    gain = jnp.zeros((queries, MAX_LEN), F32)
    for g in range(GRADES):
        held = jnp.sum(counts[g], axis=1, keepdims=True)
        gain = gain + jnp.where(position < held, float(2 ** g), 0.0)
    level = 1.0 / jnp.log2(2.0 + position[0:1, :])
    ideal = jnp.sum(gain * level, axis=1, keepdims=True)
    usable = ideal > 0.5
    inverse = jnp.where(usable, 1.0 / jnp.where(usable, ideal, 1.0), 0.0)
    first = pos_ref[0] % feat_count * own
    for t in range(own):
        at = lane + (first + t) * LANES
        inside = (at >= begin) & (at < finish)
        inv_ref[0:1, t * LANES:(t + 1) * LANES] = jnp.sum(jnp.where(inside, inverse, 0.0), axis=0, keepdims=True)

    features = perm_ref.shape[0]
    per_dev = features >> len(masks)
    owner = jnp.concatenate([owner_ref[k:k + 1, :] for k in range(features // LANES)], axis=1)
    square = (features, features)
    down, across = iota(square, 0), iota(square, 1)
    index = iota((features, 1), 0) // per_dev
    target = jnp.zeros((features, 1), jnp.int32)
    for b, mask in enumerate(masks):
        target = target + ((index >> b) & 1) * mask
    target = (target ^ pos_ref[0]) * per_dev + iota((features, 1), 0) % per_dev
    pick = jnp.where(target == across, 1.0, 0.0).astype(BF16)
    holds = jnp.where(jnp.broadcast_to(owner, square) == down, 1.0, 0.0).astype(BF16)
    perm_ref[...] = lax.dot_general(pick, holds, NT, preferred_element_type=F32).astype(BF16)


def prepare(feat_count, masks, lengths, pos, labels, owner, scores):
    rows = labels.shape[0]
    features = owner.shape[0] * LANES
    return pl.pallas_call(
        functools.partial(prepare_kernel, feat_count, masks),
        out_shape=(
            jax.ShapeDtypeStruct(scores.shape, F32),
            jax.ShapeDtypeStruct((rows, LANES), jnp.int32),
            jax.ShapeDtypeStruct((rows, LANES), F32),
            jax.ShapeDtypeStruct((1, rows // feat_count * LANES), F32),
            jax.ShapeDtypeStruct((features, features), BF16),
            jax.ShapeDtypeStruct((8, LANES), jnp.int32),
        ),
        in_specs=[smem(), smem(), vmem(), vmem(), vmem()],
        out_specs=(vmem(),) * 6,
        compiler_params=pltpu.CompilerParams(vmem_limit_bytes=VMEM_LIMIT),
        cost_estimate=pl.CostEstimate(flops=2_000_000_000, bytes_accessed=300_000, transcendentals=20_000),
        name="prepare",
    )(lengths, pos, labels, owner, scores)


def split_terms(value, terms):
    parts = []
    rest = value
    for _ in range(terms):
        part = rest.astype(BF16)
        parts.append(part)
        rest = rest - part.astype(F32)
    return parts


def pairs_kernel(feat_count, bounds_ref, pos_ref, *refs):
    scores = refs[:-20]
    (worth_ref, qid_ref, inv_ref, lam_ref, near_ref,
     s_row, a_row, d_row, s_turn, a_turn, w_turn, q_turn, d_turn, s_col, a_col, w_col, q_col, d_col, grad, curv) = refs[-20:]
    rows = worth_ref.shape[0]
    own = rows // feat_count
    docs = own * LANES
    me = pos_ref[0] % feat_count
    s_row[...] = jnp.zeros(s_row.shape, F32)
    near = [me, ((me + 1) ^ 1) - 1, me ^ 1]
    for where, ref in zip(near, scores):
        @pl.when((where >= 0) & (where < feat_count))
        def _(where=where, ref=ref):
            s_row[pl.ds(pl.multiple_of(where * own, own), own), :] = ref[...]
    a_row[...] = jnp.exp(s_row[...])
    d_row[...] = jnp.zeros(d_row.shape, F32)
    first = me * own
    window_low = bounds_ref[0, first] // (2 * LANES) * 2
    window_high = (bounds_ref[1, first + own - 1] + 2 * LANES - 1) // (2 * LANES) * 2
    stride = 4

    def widen(pairs):
        for turn, source, _ in pairs:
            turn[...] = jnp.transpose(source[...])
        for r in range(0, rows, stride):
            @pl.when((r + stride > window_low) & (r < window_high))
            def _(r=r):
                for turn, _, col in pairs:
                    for k in range(r, r + stride):
                        col[k * LANES:(k + 1) * LANES, :] = jnp.broadcast_to(turn[:, k:k + 1], (LANES, LANES))

    widen([(s_turn, s_row, s_col), (q_turn, qid_ref, q_col), (a_turn, a_row, a_col), (w_turn, worth_ref, w_col)])

    def rows_of(ref, r):
        return [jnp.broadcast_to(ref[pl.ds(r + g, 1), :], (8, LANES)) for g in range(2)]

    def spans(r):
        start, end = bounds_ref[0, r], bounds_ref[1, r + 1]
        low = jnp.maximum(start // LANES, window_low)
        high = jnp.minimum((end + LANES - 1) // LANES, window_high)
        single = bounds_ref[2, r] >= (r + 2) * LANES
        inner_low = jnp.where(single, jnp.maximum((start + LANES - 1) // LANES, window_low), r)
        inner_high = jnp.where(single, jnp.minimum(end // LANES, window_high), r)
        return low, inner_low, inner_high, high

    def rank_groups(k, carry):
        r = window_low + 2 * k
        score = rows_of(s_row, r)
        query = rows_of(qid_ref, r)

        def gather(c, acc, masked, test):
            base = pl.multiple_of(c * LANES, LANES)
            acc = list(acc)
            for u in range(LANES // 8):
                other = s_col[pl.ds(base + 8 * u, 8), :]
                for g in range(2):
                    hit = test(other, g, u)
                    if masked:
                        hit = hit & (q_col[pl.ds(base + 8 * u, 8), :] == query[g])
                    acc[2 * g + u % 2] = acc[2 * g + u % 2] + jnp.where(hit, 1.0, 0.0)
            return tuple(acc)

        def ahead(other, g, u):
            return other >= score[g]

        def behind(other, g, u):
            return other > score[g]

        def within(mine):
            def test(other, g, u):
                if g != mine:
                    return ahead(other, g, u) if mine < g else behind(other, g, u)
                earlier = iota((8, LANES), 0) + 8 * u < iota((8, LANES), 1)
                return (other > score[g]) | ((other == score[g]) & earlier)
            return test

        acc = tuple(jnp.zeros((8, LANES), F32) for _ in range(4))
        low, inner_low, inner_high, high = spans(r)
        after = jnp.maximum(inner_high, r + 2)
        acc = lax.fori_loop(low, inner_low, lambda c, acc: gather(c, acc, True, ahead), acc)
        acc = lax.fori_loop(inner_low, r, lambda c, acc: gather(c, acc, False, ahead), acc)
        acc = lax.fori_loop(r + 2, after, lambda c, acc: gather(c, acc, False, behind), acc)
        acc = lax.fori_loop(after, high, lambda c, acc: gather(c, acc, True, behind), acc)
        for mine in range(2):
            acc = gather(r + mine, acc, True, within(mine))
        for g in range(2):
            d_row[pl.ds(r + g, 1), :] = jnp.sum(acc[2 * g] + acc[2 * g + 1], axis=0, keepdims=True)
        return carry

    lax.fori_loop(0, (window_high - window_low) // 2, rank_groups, 0)
    d_row[...] = 1.0 / jnp.log2(2.0 + d_row[...])
    widen([(d_turn, d_row, d_col)])

    def pair_groups(t, carry):
        r = first + 2 * t
        a_i, w_i, d_i, query = [rows_of(ref, r) for ref in (a_row, worth_ref, d_row, qid_ref)]

        def columns(masked):
            def step(c, acc):
                base = pl.multiple_of(c * LANES, LANES)
                acc = list(acc)
                for u in range(LANES // 8):
                    at = pl.ds(base + 8 * u, 8)
                    a_j, w_j, d_j = a_col[at, :], w_col[at, :], d_col[at, :]
                    for g in range(2):
                        recip = pl.reciprocal(a_i[g] + a_j, approx=True)
                        lift = w_i[g] - w_j
                        weight = jnp.abs(d_i[g] - d_j) * recip
                        if masked:
                            weight = jnp.where(q_col[at, :] == query[g], weight, 0.0)
                        weight = weight * lift
                        k = 4 * g + u % 2
                        acc[k] = acc[k] + weight * jnp.where(lift > 0.0, a_j, a_i[g])
                        acc[k + 2] = acc[k + 2] + jnp.abs(weight) * (recip * a_j)
                return tuple(acc)
            return step

        acc = tuple(jnp.zeros((8, LANES), F32) for _ in range(8))
        low, inner_low, inner_high, high = spans(r)
        acc = lax.fori_loop(low, inner_low, columns(True), acc)
        acc = lax.fori_loop(inner_low, inner_high, columns(False), acc)
        acc = lax.fori_loop(inner_high, high, columns(True), acc)
        for g in range(2):
            at = pl.ds(2 * t + g, 1)
            grad[at, :] = -jnp.sum(acc[4 * g] + acc[4 * g + 1], axis=0, keepdims=True)
            curv[at, :] = a_i[g][0:1, :] * jnp.sum(acc[4 * g + 2] + acc[4 * g + 3], axis=0, keepdims=True)
        return carry

    lax.fori_loop(0, own // 2, pair_groups, 0)
    inverse = inv_ref[...]
    terms = [inverse * jnp.concatenate([ref[t:t + 1, :] for t in range(own)], axis=1) for ref in (grad, curv)]
    for c in range(2):
        lam_ref[c:c + 1, :] = terms[c]
        near_ref[c:c + 1, :] = terms[c]


def pair_terms(feat_count, bounds, pos, scores, worth, qid, inverse):
    rows = worth.shape[0]
    docs = inverse.shape[1]
    row = pltpu.VMEM((rows, LANES), F32)
    turn = pltpu.VMEM((LANES, rows), F32)
    col = pltpu.VMEM((rows * LANES, LANES), F32)
    mine = pltpu.VMEM((docs // LANES, LANES), F32)
    return pl.pallas_call(
        functools.partial(pairs_kernel, feat_count),
        out_shape=(jax.ShapeDtypeStruct((2, docs), F32), jax.ShapeDtypeStruct((2, docs), F32)),
        in_specs=[smem(), smem()] + [vmem()] * (len(scores) + 3),
        out_specs=(vmem(), vmem()),
        scratch_shapes=[row, row, row, turn, turn, turn, pltpu.VMEM((LANES, rows), jnp.int32), turn,
                        col, col, col, pltpu.VMEM((rows * LANES, LANES), jnp.int32), col, mine, mine],
        compiler_params=pltpu.CompilerParams(vmem_limit_bytes=VMEM_LIMIT),
        cost_estimate=pl.CostEstimate(flops=9_000_000_000, bytes_accessed=200_000, transcendentals=2_000_000),
        name="pair_terms",
    )(bounds, pos, *scores, worth, qid, inverse)


def leaf_kernel(perm_ref, bins_ref, leaf_ref, lam_ref, bins_t_ref, tile_ref, sums_ref):
    bins = bins_ref[...].astype(F32).astype(BF16)
    bins_t_ref[...] = lax.dot_general(perm_ref[...], bins, NT, preferred_element_type=F32)
    own = leaf_ref.shape[0]
    docs = own * LANES
    leaf = jnp.concatenate([leaf_ref[t:t + 1, :] for t in range(own)], axis=1)
    highs = LEAVES // LANES
    top = jnp.broadcast_to(leaf // LANES, (highs, docs)) == iota((highs, docs), 0)
    spots = jnp.where(jnp.broadcast_to(leaf % LANES, (LANES, docs)) == iota((LANES, docs), 0), 1.0, 0.0).astype(BF16)
    pieces, tiles = [], []
    for c in range(2):
        for k, part in enumerate(split_terms(lam_ref[c:c + 1, :], 3)):
            wide = jnp.broadcast_to(part.astype(F32), (highs, docs))
            pieces.append(jnp.where(top, wide, 0.0))
            if k < 2:
                tiles.append(wide)
    tile_ref[...] = jnp.concatenate(tiles, axis=0).astype(BF16)
    stacked = jnp.concatenate(pieces, axis=0).astype(BF16)
    sums = lax.dot_general(stacked, spots, NT, preferred_element_type=F32)
    for c in range(2):
        base = c * 3 * highs
        sums_ref[:, c * LANES:(c + 1) * LANES] = (
            sums[base:base + highs] + (sums[base + highs:base + 2 * highs] + sums[base + 2 * highs:base + 3 * highs])
        )


def leaf_terms(perm, bins, leaves, lambdas):
    docs, features = bins.shape
    return pl.pallas_call(
        leaf_kernel,
        out_shape=(
            jax.ShapeDtypeStruct((features, docs), F32),
            jax.ShapeDtypeStruct((4 * HIGH, docs), BF16),
            jax.ShapeDtypeStruct((LEAVES // LANES, 2 * LANES), F32),
        ),
        in_specs=[vmem()] * 4,
        out_specs=(vmem(), vmem(), vmem()),
        compiler_params=pltpu.CompilerParams(vmem_limit_bytes=VMEM_LIMIT),
        cost_estimate=pl.CostEstimate(flops=200_000_000, bytes_accessed=3_000_000, transcendentals=0),
        name="leaf_terms",
    )(perm, bins, leaves, lambdas)


def histogram_kernel(first, groups, tile_ref, bins_ref, *refs):
    out_ref = refs[-1]
    docs = tile_ref.shape[1]
    depth = docs
    rows = 16
    row = iota((rows, depth), 0)
    low_level = [(row + rows * k).astype(F32).astype(BF16) for k in range(LOW // rows)]
    high_level = (row % HIGH).astype(F32).astype(BF16)
    upper = jnp.where(row < HIGH, 1.0, 0.0).astype(BF16) > 0
    zero = jnp.zeros((rows, depth), BF16)
    one = jnp.ones((rows, depth), BF16)
    lane_owner = iota((1, GROUP * LOW), 1) // LOW

    def one_group(g, carry):
        base = pl.multiple_of((first + g) * GROUP, GROUP)
        acc = None
        for k in range(docs // depth):
            span = slice(k * depth, (k + 1) * depth)
            code = bins_ref[pl.ds(base, GROUP), span]
            high = jnp.floor(code * (1.0 / LOW))
            low = code - high * LOW
            left, right, count = [], [], []
            wide = []
            for f in range(GROUP):
                high_f = jnp.broadcast_to(high[f:f + 1, :], (rows, depth))
                low_f = jnp.broadcast_to(low[f:f + 1, :], (rows, depth)).astype(BF16)
                high_f = high_f.astype(BF16)
                wide.append(high_f)
                match = high_f == high_level
                for c in range(2):
                    left.append(jnp.where(match, tile_ref[c * rows:(c + 1) * rows, span], zero))
                for level in low_level:
                    right.append(jnp.where(low_f == level, one, zero))
            for f in range(0, GROUP, 2):
                both = jnp.where(upper, wide[f], wide[f + 1])
                count.append(jnp.where(both == high_level, one, zero))
            part = lax.dot_general(
                jnp.concatenate(left + count, axis=0), jnp.concatenate(right, axis=0), NT,
                preferred_element_type=F32,
            )
            acc = part if acc is None else acc + part
        stats = jnp.zeros((2 * rows, GROUP * LOW), F32)
        counts = jnp.zeros((HIGH, GROUP * LOW), F32)
        for f in range(GROUP):
            mine = lane_owner == f
            stats = jnp.where(mine, acc[f * 2 * rows:(f + 1) * 2 * rows], stats)
            at = GROUP * 2 * rows + f * HIGH
            counts = jnp.where(mine, acc[at:at + HIGH], counts)
        out_ref[pl.ds(pl.multiple_of(g * 3 * HIGH, 3 * HIGH), 3 * HIGH), :] = jnp.concatenate(
            [stats[0:HIGH] + stats[HIGH:2 * HIGH], stats[2 * HIGH:3 * HIGH] + stats[3 * HIGH:4 * HIGH], counts], axis=0)
        return carry

    if len(refs) > 1:
        out_ref[groups * 3 * HIGH:, :] = refs[0][...]
    lax.fori_loop(0, groups, one_group, 0, unroll=2)


def histogram_part(first, groups, tiles, bins_t, *tail):
    rows = groups * 3 * HIGH + sum(piece.shape[0] for piece in tail)
    return pl.pallas_call(
        functools.partial(histogram_kernel, first, groups),
        out_shape=jax.ShapeDtypeStruct((rows, GROUP * LOW), F32),
        in_specs=[vmem()] * (2 + len(tail)),
        out_specs=vmem(),
        compiler_params=pltpu.CompilerParams(vmem_limit_bytes=VMEM_LIMIT),
        cost_estimate=pl.CostEstimate(flops=groups * 1_000_000, bytes_accessed=groups * 1_000, transcendentals=0),
        name="histogram_part",
    )(tiles, bins_t, *tail)


def finish_kernel(per_dev, leaf_ref, kept_ref, sums_ref, *refs):
    arrived = refs[:-3][::-1]
    value_ref, step_ref, hist_ref = refs[-3:]
    unit = kept_ref.shape[0]
    totals = add_up([sums_ref[...]] + [ref[unit:, :] for ref in arrived])
    highs = LEAVES // LANES
    grad, curv = totals[:, :LANES], totals[:, LANES:]
    shrunk = jnp.maximum(jnp.abs(grad) - lasso_penalty, 0.0)
    values = jnp.where(grad > 0.0, -shrunk, shrunk) / (curv + ridge_penalty)
    value_ref[...] = values
    leaf = leaf_ref[...]
    top, spot = leaf // LANES, leaf % LANES
    step = jnp.zeros(leaf.shape, F32)
    for h in range(highs):
        row = jnp.broadcast_to(values[h:h + 1, :], leaf.shape)
        step = jnp.where(top == h, jnp.take_along_axis(row, spot, axis=1), step)
    step_ref[...] = shrinkage * step
    hist = add_up([kept_ref[...]] + [ref[:unit, :] for ref in arrived])
    if per_dev == GROUP:
        for c in range(3):
            for f in range(GROUP):
                line = [hist[c * HIGH + h:c * HIGH + h + 1, f * LOW:(f + 1) * LOW] for h in range(HIGH)]
                hist_ref[c:c + 1, f * BINS:(f + 1) * BINS] = jnp.concatenate(line, axis=1)
    else:
        hist_ref[...] = hist


def finish(per_dev, leaves, kept, sums, arrived):
    out = (3, per_dev * BINS) if per_dev == GROUP else kept.shape
    return pl.pallas_call(
        functools.partial(finish_kernel, per_dev),
        out_shape=(
            jax.ShapeDtypeStruct((LEAVES // LANES, LANES), F32),
            jax.ShapeDtypeStruct(leaves.shape, F32),
            jax.ShapeDtypeStruct(out, F32),
        ),
        in_specs=[vmem()] * (3 + len(arrived)),
        out_specs=(vmem(), vmem(), vmem()),
        compiler_params=pltpu.CompilerParams(vmem_limit_bytes=VMEM_LIMIT),
        name="finish",
    )(leaves, kept, sums, *arrived)


def add_up(parts):
    while len(parts) > 1:
        parts = [parts[k] + parts[k + 1] for k in range(0, len(parts), 2)]
    return parts[0]


def local(scores, labels, leaves, bins, lengths, owner):
    query_count = lax.axis_size("query")
    feat_count = lax.axis_size("feat")
    count = query_count * feat_count
    place = lax.axis_index("query").astype(jnp.int32) * feat_count + lax.axis_index("feat").astype(jnp.int32)
    docs = scores.shape[0]
    own = docs // LANES
    features = owner.shape[0]
    per_dev = features // count
    unit = 3 * per_dev
    axes = ("query", "feat")
    feat_masks = [1 << b for b in range(feat_count.bit_length() - 1)]
    query_masks = [feat_count << b for b in range(query_count.bit_length() - 1)]

    def swap(value, mask):
        return lax.ppermute(value, axes, [(p, p ^ mask) for p in range(count)])

    pos = place.reshape(1)
    leaf_rows = leaves.reshape(own, LANES)
    own_scores = scores.reshape(own, LANES)
    score_parts = [own_scores]
    def inner_partner(p):
        z = p % feat_count
        if z in (0, feat_count - 1):
            return p ^ query_masks[0]
        return p + 1 if z % 2 else p - 1

    score_parts.append(lax.ppermute(own_scores, axes, [(p, inner_partner(p)) for p in range(count)]))
    score_parts.append(swap(own_scores, 1))
    masks = feat_masks + query_masks[:0:-1] + query_masks[:1]
    score_parts[0], qid, worth, inverse, perm, bounds = prepare(
        feat_count, masks, lengths, pos, labels.reshape(-1, LANES), owner.reshape(-1, LANES), own_scores)
    lambdas, near_lambdas = pair_terms(feat_count, bounds, pos, score_parts, worth, qid, inverse)
    bins_t, tiles, sums = leaf_terms(perm, bins, leaf_rows, near_lambdas)

    def part(tiles, low, high, *tail):
        if per_dev == GROUP:
            return histogram_part(low, high - low, tiles, bins_t, *tail)
        groups = high - low
        wide = histogram_part(low, groups, tiles, bins_t)
        wide = wide.reshape(groups, 3, HIGH, GROUP // per_dev, per_dev, LOW).transpose(0, 3, 1, 4, 2, 5)
        return jnp.concatenate([wide.reshape(groups * GROUP // per_dev * unit, BINS), *tail], axis=0)

    def join(block, total):
        return jnp.concatenate([block, total], axis=0)

    eighth = features // GROUP // 8
    edge = count // 8 * unit
    arrived = swap(part(tiles, 6 * eighth, 8 * eighth, sums), query_masks[0])
    block = part(tiles, 3 * eighth, 4 * eighth) + arrived[edge:2 * edge]
    sums = sums + arrived[2 * edge:]
    message, tiles = lax.optimization_barrier((join(block, sums), tiles))
    crossed_far = swap(message, query_masks[1])
    block = part(tiles, 2 * eighth, 3 * eighth) + arrived[:edge]
    message, tiles = lax.optimization_barrier((block, tiles))
    crossed_near = swap(message, query_masks[1])
    arrived = swap(part(tiles, 4 * eighth, 6 * eighth), query_masks[0])
    block = part(tiles, eighth, 2 * eighth) + arrived[edge:] + crossed_far[:edge]
    sums = sums + crossed_far[edge:]
    message, tiles = lax.optimization_barrier((join(block, sums), tiles))
    turned = swap(message, query_masks[2])
    kept = part(tiles, 0, eighth) + arrived[:edge] + crossed_near + turned[:edge]
    sums = sums + turned[edge:]
    for mask in query_masks[3:]:
        edge = edge // 2
        arrived = swap(join(kept[edge:], sums), mask)
        kept = kept[:edge] + arrived[:edge]
        sums = sums + arrived[edge:]
    arrived = [swap(join(kept[m * unit:(m + 1) * unit], sums), m) for m in range(1, feat_count)]
    values, step, histograms = finish(per_dev, leaf_rows, kept[:unit], sums, arrived[::-1])
    return lambdas, values.reshape(LEAVES), step.reshape(docs), histograms.reshape(3, per_dev * BINS)


def solution(mesh):
    in_specs = (
        P(("query", "feat")),
        P("query"),
        P(("query", "feat")),
        P(("query", "feat"), None),
        P("query", None),
        P(),
    )
    out_specs = (P(None, ("query", "feat")), P(), P(("query", "feat")), P(None, ("query", "feat")))
    return jax.shard_map(local, mesh=mesh, in_specs=in_specs, out_specs=out_specs, check_vma=False)
```

```python
import functools

import jax
import jax.numpy as jnp
from jax import lax
from jax.experimental import pallas as pl
from jax.experimental.pallas import tpu as pltpu
from jax.sharding import PartitionSpec as P

BINS = 256
LEAVES = 1024
LANES = 128
GRADES = 4
LOW = 32
HIGH = BINS // LOW
GROUP = 8
CHUNK = 64
MAX_LEN = 1024

lasso_penalty = 1.0
ridge_penalty = 1.0
shrinkage = 0.1

VMEM_LIMIT = 48 * 1024 * 1024
F32 = jnp.float32
BF16 = jnp.bfloat16
NT = (((1,), (1,)), ((), ()))


def iota(shape, axis):
    return lax.broadcasted_iota(jnp.int32, shape, axis)


def vmem():
    return pl.BlockSpec(memory_space=pltpu.VMEM)


def smem():
    return pl.BlockSpec(memory_space=pltpu.SMEM)


def prepare_kernel(feat_count, masks, len_ref, pos_ref, lab_ref, owner_ref, score_ref, leaf_ref,
                   kept_ref, leaf_out, qid_ref, worth_ref, inv_ref, perm_ref, bounds_ref):
    kept_ref[...] = score_ref[...]
    leaf_out[...] = leaf_ref[...]
    queries = len_ref.shape[1]
    rows = lab_ref.shape[0]
    own = rows // feat_count
    spot = iota((rows, LANES), 0) * LANES + iota((rows, LANES), 1)
    qid = jnp.zeros((rows, LANES), jnp.int32)
    begin = jnp.zeros((queries, LANES), jnp.int32)
    finish = jnp.zeros((queries, LANES), jnp.int32)
    which = iota((queries, LANES), 0)
    group = iota((1, LANES), 1) * LANES
    low = jnp.zeros((1, LANES), jnp.int32)
    high = first_end = jnp.full((1, LANES), rows * LANES, jnp.int32)
    start = jnp.int32(0)
    for q in range(queries):
        end = start + len_ref[0, q]
        qid = qid + jnp.where(spot >= end, 1, 0)
        begin = jnp.where(which == q, start, begin)
        finish = jnp.where(which == q, end, finish)

        low = low + jnp.where(end <= group, len_ref[0, q], 0)
        high = jnp.minimum(high, jnp.where(end >= group + LANES, end, rows * LANES))
        first_end = jnp.minimum(first_end, jnp.where(end > group, end, rows * LANES))
        start = end
    bounds_ref[...] = jnp.concatenate([low, high, first_end, low, low, low, low, low], axis=0)
    qid_ref[...] = qid
    worth_ref[...] = jnp.left_shift(1, lab_ref[...]).astype(F32)

    counts = [jnp.zeros((queries, LANES), F32) for _ in range(GRADES)]
    lane = iota((queries, LANES), 1)
    for r in range(rows):
        at = lane + r * LANES
        inside = (at >= begin) & (at < finish)
        grade = jnp.where(inside, jnp.broadcast_to(lab_ref[r:r + 1, :], (queries, LANES)), 0)
        for g in range(GRADES):
            counts[g] = counts[g] + jnp.where(grade > g, 1.0, 0.0)
    position = iota((queries, MAX_LEN), 1).astype(F32)
    gain = jnp.zeros((queries, MAX_LEN), F32)
    for g in range(GRADES):
        held = jnp.sum(counts[g], axis=1, keepdims=True)
        gain = gain + jnp.where(position < held, float(2 ** g), 0.0)
    level = 1.0 / jnp.log2(2.0 + position[0:1, :])
    ideal = jnp.sum(gain * level, axis=1, keepdims=True)
    usable = ideal > 0.5
    inverse = jnp.where(usable, 1.0 / jnp.where(usable, ideal, 1.0), 0.0)
    first = pos_ref[0] % feat_count * own
    for t in range(own):
        at = lane + (first + t) * LANES
        inside = (at >= begin) & (at < finish)
        inv_ref[0:1, t * LANES:(t + 1) * LANES] = jnp.sum(jnp.where(inside, inverse, 0.0), axis=0, keepdims=True)

    features = perm_ref.shape[0]
    per_dev = features >> len(masks)
    owner = jnp.concatenate([owner_ref[k:k + 1, :] for k in range(features // LANES)], axis=1)
    square = (features, features)
    down, across = iota(square, 0), iota(square, 1)
    index = iota((features, 1), 0) // per_dev
    target = jnp.zeros((features, 1), jnp.int32)
    for b, mask in enumerate(masks):
        target = target + ((index >> b) & 1) * mask
    target = (target ^ pos_ref[0]) * per_dev + iota((features, 1), 0) % per_dev
    pick = jnp.where(target == across, 1.0, 0.0).astype(BF16)
    holds = jnp.where(jnp.broadcast_to(owner, square) == down, 1.0, 0.0).astype(BF16)
    perm_ref[...] = lax.dot_general(pick, holds, NT, preferred_element_type=F32).astype(BF16)


def prepare(feat_count, masks, lengths, pos, labels, owner, scores, leaves):
    rows = labels.shape[0]
    features = owner.shape[0] * LANES
    return pl.pallas_call(
        functools.partial(prepare_kernel, feat_count, masks),
        out_shape=(
            jax.ShapeDtypeStruct(scores.shape, F32),
            jax.ShapeDtypeStruct(leaves.shape, jnp.int32),
            jax.ShapeDtypeStruct((rows, LANES), jnp.int32),
            jax.ShapeDtypeStruct((rows, LANES), F32),
            jax.ShapeDtypeStruct((1, rows // feat_count * LANES), F32),
            jax.ShapeDtypeStruct((features, features), BF16),
            jax.ShapeDtypeStruct((8, LANES), jnp.int32),
        ),
        in_specs=[smem(), smem(), vmem(), vmem(), vmem(), vmem()],
        out_specs=(vmem(),) * 7,
        compiler_params=pltpu.CompilerParams(vmem_limit_bytes=VMEM_LIMIT),
        cost_estimate=pl.CostEstimate(flops=2_000_000_000, bytes_accessed=300_000, transcendentals=20_000),
        name="prepare",
    )(lengths, pos, labels, owner, scores, leaves)


def split_terms(value, terms):
    parts = []
    rest = value
    for _ in range(terms):
        part = rest.astype(BF16)
        parts.append(part)
        rest = rest - part.astype(F32)
    return parts


def pairs_kernel(feat_count, bounds_ref, pos_ref, *refs):
    scores = refs[:-20]
    (worth_ref, qid_ref, inv_ref, lam_ref, near_ref,
     s_row, a_row, d_row, s_turn, a_turn, w_turn, q_turn, d_turn, s_col, a_col, w_col, q_col, d_col, grad, curv) = refs[-20:]
    rows = worth_ref.shape[0]
    own = rows // feat_count
    docs = own * LANES
    me = pos_ref[0] % feat_count
    s_row[...] = jnp.zeros(s_row.shape, F32)
    near = [me, ((me + 1) ^ 1) - 1, me ^ 1]
    for where, ref in zip(near, scores):
        @pl.when((where >= 0) & (where < feat_count))
        def _(where=where, ref=ref):
            s_row[pl.ds(pl.multiple_of(where * own, own), own), :] = ref[...]
    a_row[...] = jnp.exp(s_row[...])
    d_row[...] = jnp.zeros(d_row.shape, F32)
    first = me * own
    window_low = bounds_ref[0, first] // (2 * LANES) * 2
    window_high = (bounds_ref[1, first + own - 1] + 2 * LANES - 1) // (2 * LANES) * 2
    stride = 4

    def widen(pairs):
        for turn, source, _ in pairs:
            turn[...] = jnp.transpose(source[...])
        for r in range(0, rows, stride):
            @pl.when((r + stride > window_low) & (r < window_high))
            def _(r=r):
                for turn, _, col in pairs:
                    for k in range(r, r + stride):
                        col[k * LANES:(k + 1) * LANES, :] = jnp.broadcast_to(turn[:, k:k + 1], (LANES, LANES))

    widen([(s_turn, s_row, s_col), (q_turn, qid_ref, q_col), (a_turn, a_row, a_col), (w_turn, worth_ref, w_col)])

    def rows_of(ref, r):
        return [jnp.broadcast_to(ref[pl.ds(r + g, 1), :], (8, LANES)) for g in range(2)]

    def spans(r):
        start, end = bounds_ref[0, r], bounds_ref[1, r + 1]
        low = jnp.maximum(start // LANES, window_low)
        high = jnp.minimum((end + LANES - 1) // LANES, window_high)
        single = bounds_ref[2, r] >= (r + 2) * LANES
        inner_low = jnp.where(single, jnp.maximum((start + LANES - 1) // LANES, window_low), r)
        inner_high = jnp.where(single, jnp.minimum(end // LANES, window_high), r)
        return low, inner_low, inner_high, high

    def rank_groups(k, carry):
        r = window_low + 2 * k
        score = rows_of(s_row, r)
        query = rows_of(qid_ref, r)

        def gather(c, acc, masked, test):
            base = pl.multiple_of(c * LANES, LANES)
            acc = list(acc)
            for u in range(LANES // 8):
                other = s_col[pl.ds(base + 8 * u, 8), :]
                for g in range(2):
                    hit = test(other, g, u)
                    if masked:
                        hit = hit & (q_col[pl.ds(base + 8 * u, 8), :] == query[g])
                    acc[2 * g + u % 2] = acc[2 * g + u % 2] + jnp.where(hit, 1.0, 0.0)
            return tuple(acc)

        def ahead(other, g, u):
            return other >= score[g]

        def behind(other, g, u):
            return other > score[g]

        def within(mine):
            def test(other, g, u):
                if g != mine:
                    return ahead(other, g, u) if mine < g else behind(other, g, u)
                earlier = iota((8, LANES), 0) + 8 * u < iota((8, LANES), 1)
                return (other > score[g]) | ((other == score[g]) & earlier)
            return test

        acc = tuple(jnp.zeros((8, LANES), F32) for _ in range(4))
        low, inner_low, inner_high, high = spans(r)
        after = jnp.maximum(inner_high, r + 2)
        acc = lax.fori_loop(low, inner_low, lambda c, acc: gather(c, acc, True, ahead), acc)
        acc = lax.fori_loop(inner_low, r, lambda c, acc: gather(c, acc, False, ahead), acc)
        acc = lax.fori_loop(r + 2, after, lambda c, acc: gather(c, acc, False, behind), acc)
        acc = lax.fori_loop(after, high, lambda c, acc: gather(c, acc, True, behind), acc)
        for mine in range(2):
            acc = gather(r + mine, acc, True, within(mine))
        for g in range(2):
            d_row[pl.ds(r + g, 1), :] = jnp.sum(acc[2 * g] + acc[2 * g + 1], axis=0, keepdims=True)
        return carry

    lax.fori_loop(0, (window_high - window_low) // 2, rank_groups, 0)
    d_row[...] = 1.0 / jnp.log2(2.0 + d_row[...])
    widen([(d_turn, d_row, d_col)])

    def pair_groups(t, carry):
        r = first + 2 * t
        a_i, w_i, d_i, query = [rows_of(ref, r) for ref in (a_row, worth_ref, d_row, qid_ref)]

        def columns(masked):
            def step(c, acc):
                base = pl.multiple_of(c * LANES, LANES)
                acc = list(acc)
                for u in range(LANES // 8):
                    at = pl.ds(base + 8 * u, 8)
                    a_j, w_j, d_j = a_col[at, :], w_col[at, :], d_col[at, :]
                    for g in range(2):
                        recip = pl.reciprocal(a_i[g] + a_j, approx=True)
                        lift = w_i[g] - w_j
                        weight = jnp.abs(d_i[g] - d_j) * recip
                        if masked:
                            weight = jnp.where(q_col[at, :] == query[g], weight, 0.0)
                        weight = weight * lift
                        k = 4 * g + u % 2
                        acc[k] = acc[k] + weight * jnp.where(lift > 0.0, a_j, a_i[g])
                        acc[k + 2] = acc[k + 2] + jnp.abs(weight) * (recip * a_j)
                return tuple(acc)
            return step

        acc = tuple(jnp.zeros((8, LANES), F32) for _ in range(8))
        low, inner_low, inner_high, high = spans(r)
        acc = lax.fori_loop(low, inner_low, columns(True), acc)
        acc = lax.fori_loop(inner_low, inner_high, columns(False), acc)
        acc = lax.fori_loop(inner_high, high, columns(True), acc)
        for g in range(2):
            at = pl.ds(2 * t + g, 1)
            grad[at, :] = -jnp.sum(acc[4 * g] + acc[4 * g + 1], axis=0, keepdims=True)
            curv[at, :] = a_i[g][0:1, :] * jnp.sum(acc[4 * g + 2] + acc[4 * g + 3], axis=0, keepdims=True)
        return carry

    lax.fori_loop(0, own // 2, pair_groups, 0)
    inverse = inv_ref[...]
    terms = [inverse * jnp.concatenate([ref[t:t + 1, :] for t in range(own)], axis=1) for ref in (grad, curv)]
    for c in range(2):
        lam_ref[c:c + 1, :] = terms[c]
        near_ref[c:c + 1, :] = terms[c]


def pair_terms(feat_count, bounds, pos, scores, worth, qid, inverse):
    rows = worth.shape[0]
    docs = inverse.shape[1]
    row = pltpu.VMEM((rows, LANES), F32)
    turn = pltpu.VMEM((LANES, rows), F32)
    col = pltpu.VMEM((rows * LANES, LANES), F32)
    mine = pltpu.VMEM((docs // LANES, LANES), F32)
    return pl.pallas_call(
        functools.partial(pairs_kernel, feat_count),
        out_shape=(jax.ShapeDtypeStruct((2, docs), F32), jax.ShapeDtypeStruct((2, docs), F32)),
        in_specs=[smem(), smem()] + [vmem()] * (len(scores) + 3),
        out_specs=(vmem(), vmem()),
        scratch_shapes=[row, row, row, turn, turn, turn, pltpu.VMEM((LANES, rows), jnp.int32), turn,
                        col, col, col, pltpu.VMEM((rows * LANES, LANES), jnp.int32), col, mine, mine],
        compiler_params=pltpu.CompilerParams(vmem_limit_bytes=VMEM_LIMIT),
        cost_estimate=pl.CostEstimate(flops=9_000_000_000, bytes_accessed=200_000, transcendentals=2_000_000),
        name="pair_terms",
    )(bounds, pos, *scores, worth, qid, inverse)


def leaf_kernel(perm_ref, bins_ref, leaf_ref, lam_ref, bins_t_ref, tile_ref, sums_ref):
    bins = bins_ref[...].astype(F32).astype(BF16)
    bins_t_ref[...] = lax.dot_general(perm_ref[...], bins, NT, preferred_element_type=F32)
    own = leaf_ref.shape[0]
    docs = own * LANES
    leaf = jnp.concatenate([leaf_ref[t:t + 1, :] for t in range(own)], axis=1)
    highs = LEAVES // LANES
    top = jnp.broadcast_to(leaf // LANES, (highs, docs)) == iota((highs, docs), 0)
    spots = jnp.where(jnp.broadcast_to(leaf % LANES, (LANES, docs)) == iota((LANES, docs), 0), 1.0, 0.0).astype(BF16)
    pieces, tiles = [], []
    for c in range(2):
        for k, part in enumerate(split_terms(lam_ref[c:c + 1, :], 3)):
            wide = jnp.broadcast_to(part.astype(F32), (highs, docs))
            pieces.append(jnp.where(top, wide, 0.0))
            if k < 2:
                tiles.append(wide)
    tile_ref[...] = jnp.concatenate(tiles, axis=0).astype(BF16)
    stacked = jnp.concatenate(pieces, axis=0).astype(BF16)
    sums = lax.dot_general(stacked, spots, NT, preferred_element_type=F32)
    for c in range(2):
        base = c * 3 * highs
        sums_ref[:, c * LANES:(c + 1) * LANES] = (
            sums[base:base + highs] + (sums[base + highs:base + 2 * highs] + sums[base + 2 * highs:base + 3 * highs])
        )


def leaf_terms(perm, bins, leaves, lambdas):
    docs, features = bins.shape
    return pl.pallas_call(
        leaf_kernel,
        out_shape=(
            jax.ShapeDtypeStruct((features, docs), F32),
            jax.ShapeDtypeStruct((4 * HIGH, docs), BF16),
            jax.ShapeDtypeStruct((LEAVES // LANES, 2 * LANES), F32),
        ),
        in_specs=[vmem()] * 4,
        out_specs=(vmem(), vmem(), vmem()),
        compiler_params=pltpu.CompilerParams(vmem_limit_bytes=VMEM_LIMIT),
        cost_estimate=pl.CostEstimate(flops=200_000_000, bytes_accessed=3_000_000, transcendentals=0),
        name="leaf_terms",
    )(perm, bins, leaves, lambdas)


def histogram_kernel(first, groups, tile_ref, bins_ref, *refs):
    out_ref = refs[-1]
    docs = tile_ref.shape[1]
    depth = docs
    rows = 16
    row = iota((rows, depth), 0)
    low_level = [(row + rows * k).astype(F32).astype(BF16) for k in range(LOW // rows)]
    high_level = (row % HIGH).astype(F32).astype(BF16)
    upper = jnp.where(row < HIGH, 1.0, 0.0).astype(BF16) > 0
    zero = jnp.zeros((rows, depth), BF16)
    one = jnp.ones((rows, depth), BF16)
    lane_owner = iota((1, GROUP * LOW), 1) // LOW

    def one_group(g, carry):
        base = pl.multiple_of((first + g) * GROUP, GROUP)
        acc = None
        for k in range(docs // depth):
            span = slice(k * depth, (k + 1) * depth)
            code = bins_ref[pl.ds(base, GROUP), span]
            high = jnp.floor(code * (1.0 / LOW))
            low = code - high * LOW
            left, right, count = [], [], []
            wide = []
            for f in range(GROUP):
                high_f = jnp.broadcast_to(high[f:f + 1, :], (rows, depth))
                low_f = jnp.broadcast_to(low[f:f + 1, :], (rows, depth)).astype(BF16)
                high_f = high_f.astype(BF16)
                wide.append(high_f)
                match = high_f == high_level
                for c in range(2):
                    left.append(jnp.where(match, tile_ref[c * rows:(c + 1) * rows, span], zero))
                for level in low_level:
                    right.append(jnp.where(low_f == level, one, zero))
            for f in range(0, GROUP, 2):
                both = jnp.where(upper, wide[f], wide[f + 1])
                count.append(jnp.where(both == high_level, one, zero))
            part = lax.dot_general(
                jnp.concatenate(left + count, axis=0), jnp.concatenate(right, axis=0), NT,
                preferred_element_type=F32,
            )
            acc = part if acc is None else acc + part
        stats = jnp.zeros((2 * rows, GROUP * LOW), F32)
        counts = jnp.zeros((HIGH, GROUP * LOW), F32)
        for f in range(GROUP):
            mine = lane_owner == f
            stats = jnp.where(mine, acc[f * 2 * rows:(f + 1) * 2 * rows], stats)
            at = GROUP * 2 * rows + f * HIGH
            counts = jnp.where(mine, acc[at:at + HIGH], counts)
        out_ref[pl.ds(pl.multiple_of(g * 3 * HIGH, 3 * HIGH), 3 * HIGH), :] = jnp.concatenate(
            [stats[0:HIGH] + stats[HIGH:2 * HIGH], stats[2 * HIGH:3 * HIGH] + stats[3 * HIGH:4 * HIGH], counts], axis=0)
        return carry

    if len(refs) > 1:
        out_ref[groups * 3 * HIGH:, :] = refs[0][...]
    lax.fori_loop(0, groups, one_group, 0, unroll=2)


def histogram_part(first, groups, tiles, bins_t, *tail):
    rows = groups * 3 * HIGH + sum(piece.shape[0] for piece in tail)
    return pl.pallas_call(
        functools.partial(histogram_kernel, first, groups),
        out_shape=jax.ShapeDtypeStruct((rows, GROUP * LOW), F32),
        in_specs=[vmem()] * (2 + len(tail)),
        out_specs=vmem(),
        compiler_params=pltpu.CompilerParams(vmem_limit_bytes=VMEM_LIMIT),
        cost_estimate=pl.CostEstimate(flops=groups * 1_000_000, bytes_accessed=groups * 1_000, transcendentals=0),
        name="histogram_part",
    )(tiles, bins_t, *tail)


def finish_kernel(per_dev, leaf_ref, kept_ref, sums_ref, *refs):
    arrived = refs[:-3][::-1]
    value_ref, step_ref, hist_ref = refs[-3:]
    unit = kept_ref.shape[0]
    totals = add_up([sums_ref[...]] + [ref[unit:, :] for ref in arrived])
    highs = LEAVES // LANES
    grad, curv = totals[:, :LANES], totals[:, LANES:]
    shrunk = jnp.maximum(jnp.abs(grad) - lasso_penalty, 0.0)
    values = jnp.where(grad > 0.0, -shrunk, shrunk) / (curv + ridge_penalty)
    value_ref[...] = values
    leaf = leaf_ref[...]
    top, spot = leaf // LANES, leaf % LANES
    step = jnp.zeros(leaf.shape, F32)
    for h in range(highs):
        row = jnp.broadcast_to(values[h:h + 1, :], leaf.shape)
        step = jnp.where(top == h, jnp.take_along_axis(row, spot, axis=1), step)
    step_ref[...] = shrinkage * step
    hist = add_up([kept_ref[...]] + [ref[:unit, :] for ref in arrived])
    if per_dev == GROUP:
        shape = hist.shape
        line, place = iota(shape, 0), iota(shape, 1) // LOW
        step = 1
        while step < GROUP:
            down, across = (line // step) % 2, (place // step) % 2
            shift = step * LOW
            ahead = pltpu.roll(pltpu.roll(hist, shape[0] - step, 0), shift, 1)
            behind = pltpu.roll(pltpu.roll(hist, step, 0), shape[1] - shift, 1)
            hist = jnp.where(down == across, hist, jnp.where(across == 1, ahead, behind))
            step *= 2
        for c in range(3):
            for f in range(GROUP):
                hist_ref[c:c + 1, f * BINS:(f + 1) * BINS] = hist[c * HIGH + f:c * HIGH + f + 1, :]
    else:
        hist_ref[...] = hist


def finish(per_dev, leaves, kept, sums, arrived):
    out = (3, per_dev * BINS) if per_dev == GROUP else kept.shape
    return pl.pallas_call(
        functools.partial(finish_kernel, per_dev),
        out_shape=(
            jax.ShapeDtypeStruct((LEAVES // LANES, LANES), F32),
            jax.ShapeDtypeStruct(leaves.shape, F32),
            jax.ShapeDtypeStruct(out, F32),
        ),
        in_specs=[vmem()] * (3 + len(arrived)),
        out_specs=(vmem(), vmem(), vmem()),
        compiler_params=pltpu.CompilerParams(vmem_limit_bytes=VMEM_LIMIT),
        name="finish",
    )(leaves, kept, sums, *arrived)


def add_up(parts):
    while len(parts) > 1:
        parts = [parts[k] + parts[k + 1] for k in range(0, len(parts), 2)]
    return parts[0]


def local(scores, labels, leaves, bins, lengths, owner):
    query_count = lax.axis_size("query")
    feat_count = lax.axis_size("feat")
    count = query_count * feat_count
    place = lax.axis_index("query").astype(jnp.int32) * feat_count + lax.axis_index("feat").astype(jnp.int32)
    docs = scores.shape[0]
    own = docs // LANES
    features = owner.shape[0]
    per_dev = features // count
    unit = 3 * per_dev
    axes = ("query", "feat")
    feat_masks = [1 << b for b in range(feat_count.bit_length() - 1)]
    query_masks = [feat_count << b for b in range(query_count.bit_length() - 1)]

    def swap(value, mask):
        return lax.ppermute(value, axes, [(p, p ^ mask) for p in range(count)])

    pos = place.reshape(1)
    leaf_rows = leaves.reshape(own, LANES)
    own_scores = scores.reshape(own, LANES)
    score_parts = [own_scores]
    def inner_partner(p):
        z = p % feat_count
        if z in (0, feat_count - 1):
            return p ^ query_masks[0]
        return p + 1 if z % 2 else p - 1

    score_parts.append(lax.ppermute(own_scores, axes, [(p, inner_partner(p)) for p in range(count)]))
    score_parts.append(swap(own_scores, 1))
    masks = feat_masks + query_masks[:0:-1] + query_masks[:1]
    score_parts[0], leaf_rows, qid, worth, inverse, perm, bounds = prepare(
        feat_count, masks, lengths, pos, labels.reshape(-1, LANES), owner.reshape(-1, LANES), own_scores, leaf_rows)
    lambdas, near_lambdas = pair_terms(feat_count, bounds, pos, score_parts, worth, qid, inverse)
    bins_t, tiles, sums = leaf_terms(perm, bins, leaf_rows, near_lambdas)

    def part(tiles, low, high, *tail):
        if per_dev == GROUP:
            return histogram_part(low, high - low, tiles, bins_t, *tail)
        groups = high - low
        wide = histogram_part(low, groups, tiles, bins_t)
        wide = wide.reshape(groups, 3, HIGH, GROUP // per_dev, per_dev, LOW).transpose(0, 3, 1, 4, 2, 5)
        return jnp.concatenate([wide.reshape(groups * GROUP // per_dev * unit, BINS), *tail], axis=0)

    def join(block, total):
        return jnp.concatenate([block, total], axis=0)

    eighth = features // GROUP // 8
    edge = count // 8 * unit
    arrived = swap(part(tiles, 7 * eighth, 8 * eighth, sums), query_masks[0])
    block = part(tiles, 3 * eighth, 4 * eighth) + arrived[:edge]
    sums = sums + arrived[edge:]
    message, tiles = lax.optimization_barrier((join(block, sums), tiles))
    crossed_far = swap(message, query_masks[1])
    arrived = swap(part(tiles, 4 * eighth, 7 * eighth), query_masks[0])
    block = part(tiles, eighth, 2 * eighth) + arrived[edge:2 * edge] + crossed_far[:edge]
    sums = sums + crossed_far[edge:]
    message, tiles = lax.optimization_barrier((join(block, sums), tiles))
    turned = swap(message, query_masks[2])
    block = part(tiles, 2 * eighth, 3 * eighth) + arrived[2 * edge:]
    message, tiles = lax.optimization_barrier((block, tiles))
    crossed_near = swap(message, query_masks[1])
    kept = part(tiles, 0, eighth) + arrived[:edge] + crossed_near + turned[:edge]
    sums = sums + turned[edge:]
    for mask in query_masks[3:]:
        edge = edge // 2
        arrived = swap(join(kept[edge:], sums), mask)
        kept = kept[:edge] + arrived[:edge]
        sums = sums + arrived[edge:]
    arrived = [swap(join(kept[m * unit:(m + 1) * unit], sums), m) for m in range(1, feat_count)]
    values, step, histograms = finish(per_dev, leaf_rows, kept[:unit], sums, arrived[::-1])
    return lambdas, values.reshape(LEAVES), step.reshape(docs), histograms.reshape(3, per_dev * BINS)


def solution(mesh):
    in_specs = (
        P(("query", "feat")),
        P("query"),
        P(("query", "feat")),
        P(("query", "feat"), None),
        P("query", None),
        P(),
    )
    out_specs = (P(None, ("query", "feat")), P(), P(("query", "feat")), P(None, ("query", "feat")))
    return jax.shard_map(local, mesh=mesh, in_specs=in_specs, out_specs=out_specs, check_vma=False)
```

```python
import functools

import jax
import jax.numpy as jnp
from jax import lax
from jax.experimental import pallas as pl
from jax.experimental.pallas import tpu as pltpu
from jax.sharding import PartitionSpec as P

BINS = 256
LEAVES = 1024
LANES = 128
GRADES = 4
LOW = 32
HIGH = BINS // LOW
GROUP = 8
CHUNK = 64
MAX_LEN = 1024

lasso_penalty = 1.0
ridge_penalty = 1.0
shrinkage = 0.1

VMEM_LIMIT = 48 * 1024 * 1024
F32 = jnp.float32
BF16 = jnp.bfloat16
NT = (((1,), (1,)), ((), ()))


def iota(shape, axis):
    return lax.broadcasted_iota(jnp.int32, shape, axis)


def vmem():
    return pl.BlockSpec(memory_space=pltpu.VMEM)


def smem():
    return pl.BlockSpec(memory_space=pltpu.SMEM)


def prepare_kernel(feat_count, masks, len_ref, pos_ref, lab_ref, owner_ref, score_ref, leaf_ref,
                   kept_ref, leaf_out, qid_ref, worth_ref, inv_ref, perm_ref, bounds_ref):
    kept_ref[...] = score_ref[...]
    leaf_out[...] = leaf_ref[...]
    queries = len_ref.shape[1]
    rows = lab_ref.shape[0]
    own = rows // feat_count
    spot = iota((rows, LANES), 0) * LANES + iota((rows, LANES), 1)
    qid = jnp.zeros((rows, LANES), jnp.int32)
    begin = jnp.zeros((queries, LANES), jnp.int32)
    finish = jnp.zeros((queries, LANES), jnp.int32)
    which = iota((queries, LANES), 0)
    group = iota((1, LANES), 1) * LANES
    low = jnp.zeros((1, LANES), jnp.int32)
    high = first_end = jnp.full((1, LANES), rows * LANES, jnp.int32)
    start = jnp.int32(0)
    for q in range(queries):
        end = start + len_ref[0, q]
        qid = qid + jnp.where(spot >= end, 1, 0)
        begin = jnp.where(which == q, start, begin)
        finish = jnp.where(which == q, end, finish)

        low = low + jnp.where(end <= group, len_ref[0, q], 0)
        high = jnp.minimum(high, jnp.where(end >= group + LANES, end, rows * LANES))
        first_end = jnp.minimum(first_end, jnp.where(end > group, end, rows * LANES))
        start = end
    bounds_ref[...] = jnp.concatenate([low, high, first_end, low, low, low, low, low], axis=0)
    qid_ref[...] = qid
    worth_ref[...] = jnp.left_shift(1, lab_ref[...]).astype(F32)

    counts = [jnp.zeros((queries, LANES), F32) for _ in range(GRADES)]
    lane = iota((queries, LANES), 1)
    for r in range(rows):
        at = lane + r * LANES
        inside = (at >= begin) & (at < finish)
        grade = jnp.where(inside, jnp.broadcast_to(lab_ref[r:r + 1, :], (queries, LANES)), 0)
        for g in range(GRADES):
            counts[g] = counts[g] + jnp.where(grade > g, 1.0, 0.0)
    position = iota((queries, MAX_LEN), 1).astype(F32)
    gain = jnp.zeros((queries, MAX_LEN), F32)
    for g in range(GRADES):
        held = jnp.sum(counts[g], axis=1, keepdims=True)
        gain = gain + jnp.where(position < held, float(2 ** g), 0.0)
    level = 1.0 / jnp.log2(2.0 + position[0:1, :])
    ideal = jnp.sum(gain * level, axis=1, keepdims=True)
    usable = ideal > 0.5
    inverse = jnp.where(usable, 1.0 / jnp.where(usable, ideal, 1.0), 0.0)
    first = pos_ref[0] % feat_count * own
    for t in range(own):
        at = lane + (first + t) * LANES
        inside = (at >= begin) & (at < finish)
        inv_ref[0:1, t * LANES:(t + 1) * LANES] = jnp.sum(jnp.where(inside, inverse, 0.0), axis=0, keepdims=True)

    features = perm_ref.shape[0]
    per_dev = features >> len(masks)
    owner = jnp.concatenate([owner_ref[k:k + 1, :] for k in range(features // LANES)], axis=1)
    square = (features, features)
    down, across = iota(square, 0), iota(square, 1)
    index = iota((features, 1), 0) // per_dev
    target = jnp.zeros((features, 1), jnp.int32)
    for b, mask in enumerate(masks):
        target = target + ((index >> b) & 1) * mask
    target = (target ^ pos_ref[0]) * per_dev + iota((features, 1), 0) % per_dev
    pick = jnp.where(target == across, 1.0, 0.0).astype(BF16)
    holds = jnp.where(jnp.broadcast_to(owner, square) == down, 1.0, 0.0).astype(BF16)
    perm_ref[...] = lax.dot_general(pick, holds, NT, preferred_element_type=F32).astype(BF16)


def prepare(feat_count, masks, lengths, pos, labels, owner, scores, leaves):
    rows = labels.shape[0]
    features = owner.shape[0] * LANES
    return pl.pallas_call(
        functools.partial(prepare_kernel, feat_count, masks),
        out_shape=(
            jax.ShapeDtypeStruct(scores.shape, F32),
            jax.ShapeDtypeStruct(leaves.shape, jnp.int32),
            jax.ShapeDtypeStruct((rows, LANES), jnp.int32),
            jax.ShapeDtypeStruct((rows, LANES), F32),
            jax.ShapeDtypeStruct((1, rows // feat_count * LANES), F32),
            jax.ShapeDtypeStruct((features, features), BF16),
            jax.ShapeDtypeStruct((8, LANES), jnp.int32),
        ),
        in_specs=[smem(), smem(), vmem(), vmem(), vmem(), vmem()],
        out_specs=(vmem(),) * 7,
        compiler_params=pltpu.CompilerParams(vmem_limit_bytes=VMEM_LIMIT),
        cost_estimate=pl.CostEstimate(flops=2_000_000_000, bytes_accessed=300_000, transcendentals=20_000),
        name="prepare",
    )(lengths, pos, labels, owner, scores, leaves)


def split_terms(value, terms):
    parts = []
    rest = value
    for _ in range(terms):
        part = rest.astype(BF16)
        parts.append(part)
        rest = rest - part.astype(F32)
    return parts


def pairs_kernel(feat_count, bounds_ref, pos_ref, *refs):
    scores = refs[:-20]
    (worth_ref, qid_ref, inv_ref, lam_ref, near_ref,
     s_row, a_row, d_row, s_turn, a_turn, w_turn, q_turn, d_turn, s_col, a_col, w_col, q_col, d_col, grad, curv) = refs[-20:]
    rows = worth_ref.shape[0]
    own = rows // feat_count
    docs = own * LANES
    me = pos_ref[0] % feat_count
    s_row[...] = jnp.zeros(s_row.shape, F32)
    near = [me, ((me + 1) ^ 1) - 1, me ^ 1]
    for where, ref in zip(near, scores):
        @pl.when((where >= 0) & (where < feat_count))
        def _(where=where, ref=ref):
            s_row[pl.ds(pl.multiple_of(where * own, own), own), :] = ref[...]
    a_row[...] = jnp.exp(s_row[...])
    d_row[...] = jnp.zeros(d_row.shape, F32)
    first = me * own
    window_low = bounds_ref[0, first] // (2 * LANES) * 2
    window_high = (bounds_ref[1, first + own - 1] + 2 * LANES - 1) // (2 * LANES) * 2
    stride = 4

    def widen(pairs):
        for turn, source, _ in pairs:
            turn[...] = jnp.transpose(source[...])
        for r in range(0, rows, stride):
            @pl.when((r + stride > window_low) & (r < window_high))
            def _(r=r):
                for turn, _, col in pairs:
                    for k in range(r, r + stride):
                        col[k * LANES:(k + 1) * LANES, :] = jnp.broadcast_to(turn[:, k:k + 1], (LANES, LANES))

    widen([(s_turn, s_row, s_col), (q_turn, qid_ref, q_col), (a_turn, a_row, a_col), (w_turn, worth_ref, w_col)])

    def rows_of(ref, r):
        return [jnp.broadcast_to(ref[pl.ds(r + g, 1), :], (8, LANES)) for g in range(2)]

    def spans(r):
        start, end = bounds_ref[0, r], bounds_ref[1, r + 1]
        low = jnp.maximum(start // LANES, window_low)
        high = jnp.minimum((end + LANES - 1) // LANES, window_high)
        single = bounds_ref[2, r] >= (r + 2) * LANES
        inner_low = jnp.where(single, jnp.maximum((start + LANES - 1) // LANES, window_low), r)
        inner_high = jnp.where(single, jnp.minimum(end // LANES, window_high), r)
        return low, inner_low, inner_high, high

    def rank_groups(k, carry):
        r = window_low + 2 * k
        score = rows_of(s_row, r)
        query = rows_of(qid_ref, r)

        def gather(c, acc, masked, test):
            base = pl.multiple_of(c * LANES, LANES)
            acc = list(acc)
            for u in range(LANES // 8):
                other = s_col[pl.ds(base + 8 * u, 8), :]
                for g in range(2):
                    hit = test(other, g, u)
                    if masked:
                        hit = hit & (q_col[pl.ds(base + 8 * u, 8), :] == query[g])
                    acc[2 * g + u % 2] = acc[2 * g + u % 2] + jnp.where(hit, 1.0, 0.0)
            return tuple(acc)

        def ahead(other, g, u):
            return other >= score[g]

        def behind(other, g, u):
            return other > score[g]

        def within(mine):
            def test(other, g, u):
                if g != mine:
                    return ahead(other, g, u) if mine < g else behind(other, g, u)
                earlier = iota((8, LANES), 0) + 8 * u < iota((8, LANES), 1)
                return (other > score[g]) | ((other == score[g]) & earlier)
            return test

        acc = tuple(jnp.zeros((8, LANES), F32) for _ in range(4))
        low, inner_low, inner_high, high = spans(r)
        after = jnp.maximum(inner_high, r + 2)
        acc = lax.fori_loop(low, inner_low, lambda c, acc: gather(c, acc, True, ahead), acc)
        acc = lax.fori_loop(inner_low, r, lambda c, acc: gather(c, acc, False, ahead), acc)
        acc = lax.fori_loop(r + 2, after, lambda c, acc: gather(c, acc, False, behind), acc)
        acc = lax.fori_loop(after, high, lambda c, acc: gather(c, acc, True, behind), acc)
        for mine in range(2):
            acc = gather(r + mine, acc, True, within(mine))
        for g in range(2):
            d_row[pl.ds(r + g, 1), :] = jnp.sum(acc[2 * g] + acc[2 * g + 1], axis=0, keepdims=True)
        return carry

    lax.fori_loop(0, (window_high - window_low) // 2, rank_groups, 0)
    d_row[...] = 1.0 / jnp.log2(2.0 + d_row[...])
    widen([(d_turn, d_row, d_col)])

    def pair_groups(t, carry):
        r = first + 2 * t
        a_i, w_i, d_i, query = [rows_of(ref, r) for ref in (a_row, worth_ref, d_row, qid_ref)]

        def columns(masked):
            def step(c, acc):
                base = pl.multiple_of(c * LANES, LANES)
                acc = list(acc)
                for u in range(LANES // 8):
                    at = pl.ds(base + 8 * u, 8)
                    a_j, w_j, d_j = a_col[at, :], w_col[at, :], d_col[at, :]
                    for g in range(2):
                        recip = pl.reciprocal(a_i[g] + a_j, approx=True)
                        lift = w_i[g] - w_j
                        weight = jnp.abs(d_i[g] - d_j) * recip
                        if masked:
                            weight = jnp.where(q_col[at, :] == query[g], weight, 0.0)
                        weight = weight * lift
                        k = 4 * g + u % 2
                        acc[k] = acc[k] + weight * jnp.where(lift > 0.0, a_j, a_i[g])
                        acc[k + 2] = acc[k + 2] + jnp.abs(weight) * (recip * a_j)
                return tuple(acc)
            return step

        acc = tuple(jnp.zeros((8, LANES), F32) for _ in range(8))
        low, inner_low, inner_high, high = spans(r)
        acc = lax.fori_loop(low, inner_low, columns(True), acc)
        acc = lax.fori_loop(inner_low, inner_high, columns(False), acc)
        acc = lax.fori_loop(inner_high, high, columns(True), acc)
        for g in range(2):
            at = pl.ds(2 * t + g, 1)
            grad[at, :] = -jnp.sum(acc[4 * g] + acc[4 * g + 1], axis=0, keepdims=True)
            curv[at, :] = a_i[g][0:1, :] * jnp.sum(acc[4 * g + 2] + acc[4 * g + 3], axis=0, keepdims=True)
        return carry

    lax.fori_loop(0, own // 2, pair_groups, 0)
    inverse = inv_ref[...]
    terms = [inverse * jnp.concatenate([ref[t:t + 1, :] for t in range(own)], axis=1) for ref in (grad, curv)]
    for c in range(2):
        lam_ref[c:c + 1, :] = terms[c]
        near_ref[c:c + 1, :] = terms[c]


def pair_terms(feat_count, bounds, pos, scores, worth, qid, inverse):
    rows = worth.shape[0]
    docs = inverse.shape[1]
    row = pltpu.VMEM((rows, LANES), F32)
    turn = pltpu.VMEM((LANES, rows), F32)
    col = pltpu.VMEM((rows * LANES, LANES), F32)
    mine = pltpu.VMEM((docs // LANES, LANES), F32)
    return pl.pallas_call(
        functools.partial(pairs_kernel, feat_count),
        out_shape=(jax.ShapeDtypeStruct((2, docs), F32), jax.ShapeDtypeStruct((2, docs), F32)),
        in_specs=[smem(), smem()] + [vmem()] * (len(scores) + 3),
        out_specs=(vmem(), vmem()),
        scratch_shapes=[row, row, row, turn, turn, turn, pltpu.VMEM((LANES, rows), jnp.int32), turn,
                        col, col, col, pltpu.VMEM((rows * LANES, LANES), jnp.int32), col, mine, mine],
        compiler_params=pltpu.CompilerParams(vmem_limit_bytes=VMEM_LIMIT),
        cost_estimate=pl.CostEstimate(flops=9_000_000_000, bytes_accessed=200_000, transcendentals=2_000_000),
        name="pair_terms",
    )(bounds, pos, *scores, worth, qid, inverse)


def leaf_kernel(perm_ref, bins_ref, leaf_ref, lam_ref, bins_t_ref, tile_ref, sums_ref):
    bins = bins_ref[...].astype(F32).astype(BF16)
    bins_t_ref[...] = lax.dot_general(perm_ref[...], bins, NT, preferred_element_type=F32)
    own = leaf_ref.shape[0]
    docs = own * LANES
    leaf = jnp.concatenate([leaf_ref[t:t + 1, :] for t in range(own)], axis=1)
    highs = LEAVES // LANES
    top = jnp.broadcast_to(leaf // LANES, (highs, docs)) == iota((highs, docs), 0)
    spots = jnp.where(jnp.broadcast_to(leaf % LANES, (LANES, docs)) == iota((LANES, docs), 0), 1.0, 0.0).astype(BF16)
    pieces, tiles = [], []
    for c in range(2):
        for k, part in enumerate(split_terms(lam_ref[c:c + 1, :], 3)):
            wide = jnp.broadcast_to(part.astype(F32), (highs, docs))
            pieces.append(jnp.where(top, wide, 0.0))
            if k < 2:
                tiles.append(wide)
    tile_ref[...] = jnp.concatenate(tiles, axis=0).astype(BF16)
    stacked = jnp.concatenate(pieces, axis=0).astype(BF16)
    sums = lax.dot_general(stacked, spots, NT, preferred_element_type=F32)
    for c in range(2):
        base = c * 3 * highs
        sums_ref[:, c * LANES:(c + 1) * LANES] = (
            sums[base:base + highs] + (sums[base + highs:base + 2 * highs] + sums[base + 2 * highs:base + 3 * highs])
        )


def leaf_terms(perm, bins, leaves, lambdas):
    docs, features = bins.shape
    return pl.pallas_call(
        leaf_kernel,
        out_shape=(
            jax.ShapeDtypeStruct((features, docs), F32),
            jax.ShapeDtypeStruct((4 * HIGH, docs), BF16),
            jax.ShapeDtypeStruct((LEAVES // LANES, 2 * LANES), F32),
        ),
        in_specs=[vmem()] * 4,
        out_specs=(vmem(), vmem(), vmem()),
        compiler_params=pltpu.CompilerParams(vmem_limit_bytes=VMEM_LIMIT),
        cost_estimate=pl.CostEstimate(flops=200_000_000, bytes_accessed=3_000_000, transcendentals=0),
        name="leaf_terms",
    )(perm, bins, leaves, lambdas)


def histogram_kernel(first, groups, tile_ref, bins_ref, *refs):
    out_ref = refs[-1]
    docs = tile_ref.shape[1]
    depth = docs
    rows = 16
    row = iota((rows, depth), 0)
    low_level = [(row + rows * k).astype(F32).astype(BF16) for k in range(LOW // rows)]
    high_level = (row % HIGH).astype(F32).astype(BF16)
    upper = jnp.where(row < HIGH, 1.0, 0.0).astype(BF16) > 0
    zero = jnp.zeros((rows, depth), BF16)
    one = jnp.ones((rows, depth), BF16)
    lane_owner = iota((1, GROUP * LOW), 1) // LOW

    def one_group(g, carry):
        base = pl.multiple_of((first + g) * GROUP, GROUP)
        acc = None
        for k in range(docs // depth):
            span = slice(k * depth, (k + 1) * depth)
            code = bins_ref[pl.ds(base, GROUP), span]
            high = jnp.floor(code * (1.0 / LOW))
            low = code - high * LOW
            left, right, count = [], [], []
            wide = []
            for f in range(GROUP):
                high_f = jnp.broadcast_to(high[f:f + 1, :], (rows, depth))
                low_f = jnp.broadcast_to(low[f:f + 1, :], (rows, depth)).astype(BF16)
                high_f = high_f.astype(BF16)
                wide.append(high_f)
                match = high_f == high_level
                for c in range(2):
                    left.append(jnp.where(match, tile_ref[c * rows:(c + 1) * rows, span], zero))
                for level in low_level:
                    right.append(jnp.where(low_f == level, one, zero))
            for f in range(0, GROUP, 2):
                both = jnp.where(upper, wide[f], wide[f + 1])
                count.append(jnp.where(both == high_level, one, zero))
            part = lax.dot_general(
                jnp.concatenate(left + count, axis=0), jnp.concatenate(right, axis=0), NT,
                preferred_element_type=F32,
            )
            acc = part if acc is None else acc + part
        stats = jnp.zeros((2 * rows, GROUP * LOW), F32)
        counts = jnp.zeros((HIGH, GROUP * LOW), F32)
        for f in range(GROUP):
            mine = lane_owner == f
            stats = jnp.where(mine, acc[f * 2 * rows:(f + 1) * 2 * rows], stats)
            at = GROUP * 2 * rows + f * HIGH
            counts = jnp.where(mine, acc[at:at + HIGH], counts)
        out_ref[pl.ds(pl.multiple_of(g * 3 * HIGH, 3 * HIGH), 3 * HIGH), :] = jnp.concatenate(
            [stats[0:HIGH] + stats[HIGH:2 * HIGH], stats[2 * HIGH:3 * HIGH] + stats[3 * HIGH:4 * HIGH], counts], axis=0)
        return carry

    if len(refs) > 1:
        out_ref[groups * 3 * HIGH:, :] = refs[0][...]
    lax.fori_loop(0, groups, one_group, 0, unroll=2)


def histogram_part(first, groups, tiles, bins_t, *tail):
    rows = groups * 3 * HIGH + sum(piece.shape[0] for piece in tail)
    return pl.pallas_call(
        functools.partial(histogram_kernel, first, groups),
        out_shape=jax.ShapeDtypeStruct((rows, GROUP * LOW), F32),
        in_specs=[vmem()] * (2 + len(tail)),
        out_specs=vmem(),
        compiler_params=pltpu.CompilerParams(vmem_limit_bytes=VMEM_LIMIT),
        cost_estimate=pl.CostEstimate(flops=groups * 1_000_000, bytes_accessed=groups * 1_000, transcendentals=0),
        name="histogram_part",
    )(tiles, bins_t, *tail)


def finish_kernel(per_dev, leaf_ref, kept_ref, sums_ref, *refs):
    arrived = refs[:-3][::-1]
    value_ref, step_ref, hist_ref = refs[-3:]
    unit = kept_ref.shape[0]
    totals = add_up([sums_ref[...]] + [ref[unit:, :] for ref in arrived])
    highs = LEAVES // LANES
    grad, curv = totals[:, :LANES], totals[:, LANES:]
    shrunk = jnp.maximum(jnp.abs(grad) - lasso_penalty, 0.0)
    values = jnp.where(grad > 0.0, -shrunk, shrunk) / (curv + ridge_penalty)
    value_ref[...] = values
    leaf = leaf_ref[...]
    top, spot = leaf // LANES, leaf % LANES
    step = jnp.zeros(leaf.shape, F32)
    for h in range(highs):
        row = jnp.broadcast_to(values[h:h + 1, :], leaf.shape)
        step = jnp.where(top == h, jnp.take_along_axis(row, spot, axis=1), step)
    step_ref[...] = shrinkage * step
    hist = add_up([kept_ref[...]] + [ref[:unit, :] for ref in arrived])
    if per_dev == GROUP:
        shape = hist.shape
        line, place = iota(shape, 0), iota(shape, 1) // LOW
        step = 1
        while step < GROUP:
            down, across = (line // step) % 2, (place // step) % 2
            shift = step * LOW
            ahead = pltpu.roll(pltpu.roll(hist, shape[0] - step, 0), shift, 1)
            behind = pltpu.roll(pltpu.roll(hist, step, 0), shape[1] - shift, 1)
            hist = jnp.where(down == across, hist, jnp.where(across == 1, ahead, behind))
            step *= 2
        for c in range(3):
            for f in range(GROUP):
                hist_ref[c:c + 1, f * BINS:(f + 1) * BINS] = hist[c * HIGH + f:c * HIGH + f + 1, :]
    else:
        hist_ref[...] = hist


def finish(per_dev, leaves, kept, sums, arrived):
    out = (3, per_dev * BINS) if per_dev == GROUP else kept.shape
    return pl.pallas_call(
        functools.partial(finish_kernel, per_dev),
        out_shape=(
            jax.ShapeDtypeStruct((LEAVES // LANES, LANES), F32),
            jax.ShapeDtypeStruct(leaves.shape, F32),
            jax.ShapeDtypeStruct(out, F32),
        ),
        in_specs=[vmem()] * (3 + len(arrived)),
        out_specs=(vmem(), vmem(), vmem()),
        compiler_params=pltpu.CompilerParams(vmem_limit_bytes=VMEM_LIMIT),
        name="finish",
    )(leaves, kept, sums, *arrived)


def add_up(parts):
    while len(parts) > 1:
        parts = [parts[k] + parts[k + 1] for k in range(0, len(parts), 2)]
    return parts[0]


def local(scores, labels, leaves, bins, lengths, owner):
    query_count = lax.axis_size("query")
    feat_count = lax.axis_size("feat")
    count = query_count * feat_count
    place = lax.axis_index("query").astype(jnp.int32) * feat_count + lax.axis_index("feat").astype(jnp.int32)
    docs = scores.shape[0]
    own = docs // LANES
    features = owner.shape[0]
    per_dev = features // count
    unit = 3 * per_dev
    axes = ("query", "feat")
    feat_masks = [1 << b for b in range(feat_count.bit_length() - 1)]
    query_masks = [feat_count << b for b in range(query_count.bit_length() - 1)]

    def swap(value, mask):
        return lax.ppermute(value, axes, [(p, p ^ mask) for p in range(count)])

    pos = place.reshape(1)
    leaf_rows = leaves.reshape(own, LANES)
    own_scores = scores.reshape(own, LANES)
    score_parts = [own_scores]
    def inner_partner(p):
        z = p % feat_count
        if z in (0, feat_count - 1):
            return p ^ query_masks[0]
        return p + 1 if z % 2 else p - 1

    score_parts.append(lax.ppermute(own_scores, axes, [(p, inner_partner(p)) for p in range(count)]))
    score_parts.append(swap(own_scores, 1))
    masks = feat_masks + query_masks[:0:-1] + query_masks[:1]
    score_parts[0], leaf_rows, qid, worth, inverse, perm, bounds = prepare(
        feat_count, masks, lengths, pos, labels.reshape(-1, LANES), owner.reshape(-1, LANES), own_scores, leaf_rows)
    lambdas, near_lambdas = pair_terms(feat_count, bounds, pos, score_parts, worth, qid, inverse)
    bins_t, tiles, sums = leaf_terms(perm, bins, leaf_rows, near_lambdas)

    def part(tiles, low, high, *tail):
        if per_dev == GROUP:
            return histogram_part(low, high - low, tiles, bins_t, *tail)
        groups = high - low
        wide = histogram_part(low, groups, tiles, bins_t)
        wide = wide.reshape(groups, 3, HIGH, GROUP // per_dev, per_dev, LOW).transpose(0, 3, 1, 4, 2, 5)
        return jnp.concatenate([wide.reshape(groups * GROUP // per_dev * unit, BINS), *tail], axis=0)

    def join(block, total):
        return jnp.concatenate([block, total], axis=0)

    eighth = features // GROUP // 8
    edge = count // 8 * unit
    arrived = swap(part(tiles, 7 * eighth, 8 * eighth, sums), query_masks[0])
    block = part(tiles, 3 * eighth, 4 * eighth) + arrived[:edge]
    sums = sums + arrived[edge:]
    message, tiles = lax.optimization_barrier((join(block, sums), tiles))
    crossed_far = swap(message, query_masks[1])
    arrived = swap(part(tiles, 5 * eighth, 7 * eighth), query_masks[0])
    both = part(tiles, eighth, 3 * eighth) + arrived
    sums = sums + crossed_far[edge:]
    message, rest, tiles = lax.optimization_barrier(
        (join(both[:edge] + crossed_far[:edge], sums), join(both[edge:], sums), tiles))
    turned = swap(message, query_masks[2])
    crossed_near = swap(rest, query_masks[1])
    arrived = swap(part(tiles, 4 * eighth, 5 * eighth), query_masks[0])
    kept = part(tiles, 0, eighth) + arrived + crossed_near[:edge] + turned[:edge]
    sums = sums + turned[edge:]
    for mask in query_masks[3:]:
        edge = edge // 2
        arrived = swap(join(kept[edge:], sums), mask)
        kept = kept[:edge] + arrived[:edge]
        sums = sums + arrived[edge:]
    arrived = [swap(join(kept[m * unit:(m + 1) * unit], sums), m) for m in range(1, feat_count)]
    values, step, histograms = finish(per_dev, leaf_rows, kept[:unit], sums, arrived[::-1])
    return lambdas, values.reshape(LEAVES), step.reshape(docs), histograms.reshape(3, per_dev * BINS)


def solution(mesh):
    in_specs = (
        P(("query", "feat")),
        P("query"),
        P(("query", "feat")),
        P(("query", "feat"), None),
        P("query", None),
        P(),
    )
    out_specs = (P(None, ("query", "feat")), P(), P(("query", "feat")), P(None, ("query", "feat")))
    return jax.shard_map(local, mesh=mesh, in_specs=in_specs, out_specs=out_specs, check_vma=False)
```

```python
import functools

import jax
import jax.numpy as jnp
from jax import lax
from jax.experimental import pallas as pl
from jax.experimental.pallas import tpu as pltpu
from jax.sharding import PartitionSpec as P

BINS = 256
LEAVES = 1024
LANES = 128
GRADES = 4
LOW = 32
HIGH = BINS // LOW
GROUP = 8
CHUNK = 64
MAX_LEN = 1024

lasso_penalty = 1.0
ridge_penalty = 1.0
shrinkage = 0.1

VMEM_LIMIT = 48 * 1024 * 1024
F32 = jnp.float32
BF16 = jnp.bfloat16
NT = (((1,), (1,)), ((), ()))


def iota(shape, axis):
    return lax.broadcasted_iota(jnp.int32, shape, axis)


def vmem():
    return pl.BlockSpec(memory_space=pltpu.VMEM)


def smem():
    return pl.BlockSpec(memory_space=pltpu.SMEM)


def prepare_kernel(feat_count, masks, len_ref, pos_ref, lab_ref, owner_ref, score_ref, leaf_ref,
                   kept_ref, leaf_out, qid_ref, worth_ref, inv_ref, perm_ref, bounds_ref):
    kept_ref[...] = score_ref[...]
    leaf_out[...] = leaf_ref[...]
    queries = len_ref.shape[1]
    rows = lab_ref.shape[0]
    own = rows // feat_count
    spot = iota((rows, LANES), 0) * LANES + iota((rows, LANES), 1)
    qid = jnp.zeros((rows, LANES), jnp.int32)
    begin = jnp.zeros((queries, LANES), jnp.int32)
    finish = jnp.zeros((queries, LANES), jnp.int32)
    which = iota((queries, LANES), 0)
    group = iota((1, LANES), 1) * LANES
    low = jnp.zeros((1, LANES), jnp.int32)
    high = first_end = jnp.full((1, LANES), rows * LANES, jnp.int32)
    start = jnp.int32(0)
    for q in range(queries):
        end = start + len_ref[0, q]
        qid = qid + jnp.where(spot >= end, 1, 0)
        begin = jnp.where(which == q, start, begin)
        finish = jnp.where(which == q, end, finish)

        low = low + jnp.where(end <= group, len_ref[0, q], 0)
        high = jnp.minimum(high, jnp.where(end >= group + LANES, end, rows * LANES))
        first_end = jnp.minimum(first_end, jnp.where(end > group, end, rows * LANES))
        start = end
    bounds_ref[...] = jnp.concatenate([low, high, first_end, low, low, low, low, low], axis=0)
    qid_ref[...] = qid
    worth_ref[...] = jnp.left_shift(1, lab_ref[...]).astype(F32)

    counts = [jnp.zeros((queries, LANES), F32) for _ in range(GRADES)]
    lane = iota((queries, LANES), 1)
    for r in range(rows):
        at = lane + r * LANES
        inside = (at >= begin) & (at < finish)
        grade = jnp.where(inside, jnp.broadcast_to(lab_ref[r:r + 1, :], (queries, LANES)), 0)
        for g in range(GRADES):
            counts[g] = counts[g] + jnp.where(grade > g, 1.0, 0.0)
    position = iota((queries, MAX_LEN), 1).astype(F32)
    gain = jnp.zeros((queries, MAX_LEN), F32)
    for g in range(GRADES):
        held = jnp.sum(counts[g], axis=1, keepdims=True)
        gain = gain + jnp.where(position < held, float(2 ** g), 0.0)
    level = 1.0 / jnp.log2(2.0 + position[0:1, :])
    ideal = jnp.sum(gain * level, axis=1, keepdims=True)
    usable = ideal > 0.5
    inverse = jnp.where(usable, 1.0 / jnp.where(usable, ideal, 1.0), 0.0)
    first = pos_ref[0] % feat_count * own
    for t in range(own):
        at = lane + (first + t) * LANES
        inside = (at >= begin) & (at < finish)
        inv_ref[0:1, t * LANES:(t + 1) * LANES] = jnp.sum(jnp.where(inside, inverse, 0.0), axis=0, keepdims=True)

    features = perm_ref.shape[0]
    per_dev = features >> len(masks)
    owner = jnp.concatenate([owner_ref[k:k + 1, :] for k in range(features // LANES)], axis=1)
    square = (features, features)
    down, across = iota(square, 0), iota(square, 1)
    index = iota((features, 1), 0) // per_dev
    target = jnp.zeros((features, 1), jnp.int32)
    for b, mask in enumerate(masks):
        target = target + ((index >> b) & 1) * mask
    target = (target ^ pos_ref[0]) * per_dev + iota((features, 1), 0) % per_dev
    pick = jnp.where(target == across, 1.0, 0.0).astype(BF16)
    holds = jnp.where(jnp.broadcast_to(owner, square) == down, 1.0, 0.0).astype(BF16)
    perm_ref[...] = lax.dot_general(pick, holds, NT, preferred_element_type=F32).astype(BF16)


def prepare(feat_count, masks, lengths, pos, labels, owner, scores, leaves):
    rows = labels.shape[0]
    features = owner.shape[0] * LANES
    return pl.pallas_call(
        functools.partial(prepare_kernel, feat_count, masks),
        out_shape=(
            jax.ShapeDtypeStruct(scores.shape, F32),
            jax.ShapeDtypeStruct(leaves.shape, jnp.int32),
            jax.ShapeDtypeStruct((rows, LANES), jnp.int32),
            jax.ShapeDtypeStruct((rows, LANES), F32),
            jax.ShapeDtypeStruct((1, rows // feat_count * LANES), F32),
            jax.ShapeDtypeStruct((features, features), BF16),
            jax.ShapeDtypeStruct((8, LANES), jnp.int32),
        ),
        in_specs=[smem(), smem(), vmem(), vmem(), vmem(), vmem()],
        out_specs=(vmem(),) * 7,
        compiler_params=pltpu.CompilerParams(vmem_limit_bytes=VMEM_LIMIT),
        cost_estimate=pl.CostEstimate(flops=2_000_000_000, bytes_accessed=300_000, transcendentals=20_000),
        name="prepare",
    )(lengths, pos, labels, owner, scores, leaves)


def split_terms(value, terms):
    parts = []
    rest = value
    for _ in range(terms):
        part = rest.astype(BF16)
        parts.append(part)
        rest = rest - part.astype(F32)
    return parts


def pairs_kernel(feat_count, bounds_ref, pos_ref, *refs):
    scores = refs[:-20]
    (worth_ref, qid_ref, inv_ref, lam_ref, near_ref,
     s_row, a_row, d_row, s_turn, a_turn, w_turn, q_turn, d_turn, s_col, a_col, w_col, q_col, d_col, grad, curv) = refs[-20:]
    rows = worth_ref.shape[0]
    own = rows // feat_count
    docs = own * LANES
    me = pos_ref[0] % feat_count
    s_row[...] = jnp.zeros(s_row.shape, F32)
    near = [me, ((me + 1) ^ 1) - 1, me ^ 1]
    for where, ref in zip(near, scores):
        @pl.when((where >= 0) & (where < feat_count))
        def _(where=where, ref=ref):
            s_row[pl.ds(pl.multiple_of(where * own, own), own), :] = ref[...]
    a_row[...] = jnp.exp(s_row[...])
    d_row[...] = jnp.zeros(d_row.shape, F32)
    first = me * own
    window_low = bounds_ref[0, first] // (2 * LANES) * 2
    window_high = (bounds_ref[1, first + own - 1] + 2 * LANES - 1) // (2 * LANES) * 2
    stride = 4

    def widen(pairs):
        for turn, source, _ in pairs:
            turn[...] = jnp.transpose(source[...])
        for r in range(0, rows, stride):
            @pl.when((r + stride > window_low) & (r < window_high))
            def _(r=r):
                for turn, _, col in pairs:
                    for k in range(r, r + stride):
                        col[k * LANES:(k + 1) * LANES, :] = jnp.broadcast_to(turn[:, k:k + 1], (LANES, LANES))

    widen([(s_turn, s_row, s_col), (q_turn, qid_ref, q_col), (a_turn, a_row, a_col), (w_turn, worth_ref, w_col)])

    def rows_of(ref, r):
        return [jnp.broadcast_to(ref[pl.ds(r + g, 1), :], (8, LANES)) for g in range(2)]

    def spans(r):
        start, end = bounds_ref[0, r], bounds_ref[1, r + 1]
        low = jnp.maximum(start // LANES, window_low)
        high = jnp.minimum((end + LANES - 1) // LANES, window_high)
        single = bounds_ref[2, r] >= (r + 2) * LANES
        inner_low = jnp.where(single, jnp.maximum((start + LANES - 1) // LANES, window_low), r)
        inner_high = jnp.where(single, jnp.minimum(end // LANES, window_high), r)
        return low, inner_low, inner_high, high

    def rank_groups(k, carry):
        r = window_low + 2 * k
        score = rows_of(s_row, r)
        query = rows_of(qid_ref, r)

        def gather(c, acc, masked, test):
            base = pl.multiple_of(c * LANES, LANES)
            acc = list(acc)
            for u in range(LANES // 8):
                other = s_col[pl.ds(base + 8 * u, 8), :]
                for g in range(2):
                    hit = test(other, g, u)
                    if masked:
                        hit = hit & (q_col[pl.ds(base + 8 * u, 8), :] == query[g])
                    k = 4 * g + u % 4
                    acc[k] = acc[k] + jnp.where(hit, 1.0, 0.0)
            return tuple(acc)

        def ahead(other, g, u):
            return other >= score[g]

        def behind(other, g, u):
            return other > score[g]

        def within(mine):
            def test(other, g, u):
                if g != mine:
                    return ahead(other, g, u) if mine < g else behind(other, g, u)
                earlier = iota((8, LANES), 0) + 8 * u < iota((8, LANES), 1)
                return (other > score[g]) | ((other == score[g]) & earlier)
            return test

        def twice(low, high, test, acc):
            twos = (high - low) // 2
            acc = lax.fori_loop(0, twos, lambda k, acc: gather(
                low + 2 * k + 1, gather(low + 2 * k, acc, False, test), False, test), acc)
            return lax.fori_loop(low + 2 * twos, high, lambda c, acc: gather(c, acc, False, test), acc)

        acc = tuple(jnp.zeros((8, LANES), F32) for _ in range(8))
        low, inner_low, inner_high, high = spans(r)
        after = jnp.maximum(inner_high, r + 2)
        acc = lax.fori_loop(low, inner_low, lambda c, acc: gather(c, acc, True, ahead), acc)
        acc = twice(inner_low, r, ahead, acc)
        acc = twice(r + 2, after, behind, acc)
        acc = lax.fori_loop(after, high, lambda c, acc: gather(c, acc, True, behind), acc)
        for mine in range(2):
            acc = gather(r + mine, acc, True, within(mine))
        for g in range(2):
            total = (acc[4 * g] + acc[4 * g + 1]) + (acc[4 * g + 2] + acc[4 * g + 3])
            d_row[pl.ds(r + g, 1), :] = jnp.sum(total, axis=0, keepdims=True)
        return carry

    lax.fori_loop(0, (window_high - window_low) // 2, rank_groups, 0)
    d_row[...] = 1.0 / jnp.log2(2.0 + d_row[...])
    widen([(d_turn, d_row, d_col)])

    def pair_groups(t, carry):
        r = first + 2 * t
        a_i, w_i, d_i, query = [rows_of(ref, r) for ref in (a_row, worth_ref, d_row, qid_ref)]

        def columns(masked):
            def step(c, acc):
                base = pl.multiple_of(c * LANES, LANES)
                acc = list(acc)
                for u in range(LANES // 8):
                    at = pl.ds(base + 8 * u, 8)
                    a_j, w_j, d_j = a_col[at, :], w_col[at, :], d_col[at, :]
                    for g in range(2):
                        recip = pl.reciprocal(a_i[g] + a_j, approx=True)
                        lift = w_i[g] - w_j
                        weight = jnp.abs(d_i[g] - d_j) * recip
                        if masked:
                            weight = jnp.where(q_col[at, :] == query[g], weight, 0.0)
                        weight = weight * lift
                        k = 4 * g + u % 2
                        acc[k] = acc[k] + weight * jnp.where(lift > 0.0, a_j, a_i[g])
                        acc[k + 2] = acc[k + 2] + jnp.abs(weight) * (recip * a_j)
                return tuple(acc)
            return step

        acc = tuple(jnp.zeros((8, LANES), F32) for _ in range(8))
        low, inner_low, inner_high, high = spans(r)
        acc = lax.fori_loop(low, inner_low, columns(True), acc)
        acc = lax.fori_loop(inner_low, inner_high, columns(False), acc)
        acc = lax.fori_loop(inner_high, high, columns(True), acc)
        for g in range(2):
            at = pl.ds(2 * t + g, 1)
            grad[at, :] = -jnp.sum(acc[4 * g] + acc[4 * g + 1], axis=0, keepdims=True)
            curv[at, :] = a_i[g][0:1, :] * jnp.sum(acc[4 * g + 2] + acc[4 * g + 3], axis=0, keepdims=True)
        return carry

    lax.fori_loop(0, own // 2, pair_groups, 0)
    inverse = inv_ref[...]
    terms = [inverse * jnp.concatenate([ref[t:t + 1, :] for t in range(own)], axis=1) for ref in (grad, curv)]
    for c in range(2):
        lam_ref[c:c + 1, :] = terms[c]
        near_ref[c:c + 1, :] = terms[c]


def pair_terms(feat_count, bounds, pos, scores, worth, qid, inverse):
    rows = worth.shape[0]
    docs = inverse.shape[1]
    row = pltpu.VMEM((rows, LANES), F32)
    turn = pltpu.VMEM((LANES, rows), F32)
    col = pltpu.VMEM((rows * LANES, LANES), F32)
    mine = pltpu.VMEM((docs // LANES, LANES), F32)
    return pl.pallas_call(
        functools.partial(pairs_kernel, feat_count),
        out_shape=(jax.ShapeDtypeStruct((2, docs), F32), jax.ShapeDtypeStruct((2, docs), F32)),
        in_specs=[smem(), smem()] + [vmem()] * (len(scores) + 3),
        out_specs=(vmem(), vmem()),
        scratch_shapes=[row, row, row, turn, turn, turn, pltpu.VMEM((LANES, rows), jnp.int32), turn,
                        col, col, col, pltpu.VMEM((rows * LANES, LANES), jnp.int32), col, mine, mine],
        compiler_params=pltpu.CompilerParams(vmem_limit_bytes=VMEM_LIMIT),
        cost_estimate=pl.CostEstimate(flops=9_000_000_000, bytes_accessed=200_000, transcendentals=2_000_000),
        name="pair_terms",
    )(bounds, pos, *scores, worth, qid, inverse)


def leaf_kernel(perm_ref, bins_ref, leaf_ref, lam_ref, bins_t_ref, tile_ref, sums_ref):
    bins = bins_ref[...].astype(F32).astype(BF16)
    bins_t_ref[...] = lax.dot_general(perm_ref[...], bins, NT, preferred_element_type=F32)
    own = leaf_ref.shape[0]
    docs = own * LANES
    leaf = jnp.concatenate([leaf_ref[t:t + 1, :] for t in range(own)], axis=1)
    highs = LEAVES // LANES
    top = jnp.broadcast_to(leaf // LANES, (highs, docs)) == iota((highs, docs), 0)
    spots = jnp.where(jnp.broadcast_to(leaf % LANES, (LANES, docs)) == iota((LANES, docs), 0), 1.0, 0.0).astype(BF16)
    pieces, tiles = [], []
    for c in range(2):
        for k, part in enumerate(split_terms(lam_ref[c:c + 1, :], 3)):
            wide = jnp.broadcast_to(part.astype(F32), (highs, docs))
            pieces.append(jnp.where(top, wide, 0.0))
            if k < 2:
                tiles.append(wide)
    tile_ref[...] = jnp.concatenate(tiles, axis=0).astype(BF16)
    stacked = jnp.concatenate(pieces, axis=0).astype(BF16)
    sums = lax.dot_general(stacked, spots, NT, preferred_element_type=F32)
    for c in range(2):
        base = c * 3 * highs
        sums_ref[:, c * LANES:(c + 1) * LANES] = (
            sums[base:base + highs] + (sums[base + highs:base + 2 * highs] + sums[base + 2 * highs:base + 3 * highs])
        )


def leaf_terms(perm, bins, leaves, lambdas):
    docs, features = bins.shape
    return pl.pallas_call(
        leaf_kernel,
        out_shape=(
            jax.ShapeDtypeStruct((features, docs), F32),
            jax.ShapeDtypeStruct((4 * HIGH, docs), BF16),
            jax.ShapeDtypeStruct((LEAVES // LANES, 2 * LANES), F32),
        ),
        in_specs=[vmem()] * 4,
        out_specs=(vmem(), vmem(), vmem()),
        compiler_params=pltpu.CompilerParams(vmem_limit_bytes=VMEM_LIMIT),
        cost_estimate=pl.CostEstimate(flops=200_000_000, bytes_accessed=3_000_000, transcendentals=0),
        name="leaf_terms",
    )(perm, bins, leaves, lambdas)


def histogram_kernel(first, groups, tile_ref, bins_ref, *refs):
    out_ref = refs[-1]
    docs = tile_ref.shape[1]
    depth = docs
    rows = 16
    row = iota((rows, depth), 0)
    low_level = [(row + rows * k).astype(F32).astype(BF16) for k in range(LOW // rows)]
    high_level = (row % HIGH).astype(F32).astype(BF16)
    upper = jnp.where(row < HIGH, 1.0, 0.0).astype(BF16) > 0
    zero = jnp.zeros((rows, depth), BF16)
    one = jnp.ones((rows, depth), BF16)
    lane_owner = iota((1, GROUP * LOW), 1) // LOW

    def one_group(g, carry):
        base = pl.multiple_of((first + g) * GROUP, GROUP)
        acc = None
        for k in range(docs // depth):
            span = slice(k * depth, (k + 1) * depth)
            code = bins_ref[pl.ds(base, GROUP), span]
            high = jnp.floor(code * (1.0 / LOW))
            low = code - high * LOW
            left, right, count = [], [], []
            wide = []
            for f in range(GROUP):
                high_f = jnp.broadcast_to(high[f:f + 1, :], (rows, depth))
                low_f = jnp.broadcast_to(low[f:f + 1, :], (rows, depth)).astype(BF16)
                high_f = high_f.astype(BF16)
                wide.append(high_f)
                match = high_f == high_level
                for c in range(2):
                    left.append(jnp.where(match, tile_ref[c * rows:(c + 1) * rows, span], zero))
                for level in low_level:
                    right.append(jnp.where(low_f == level, one, zero))
            for f in range(0, GROUP, 2):
                both = jnp.where(upper, wide[f], wide[f + 1])
                count.append(jnp.where(both == high_level, one, zero))
            part = lax.dot_general(
                jnp.concatenate(left + count, axis=0), jnp.concatenate(right, axis=0), NT,
                preferred_element_type=F32,
            )
            acc = part if acc is None else acc + part
        stats = jnp.zeros((2 * rows, GROUP * LOW), F32)
        counts = jnp.zeros((HIGH, GROUP * LOW), F32)
        for f in range(GROUP):
            mine = lane_owner == f
            stats = jnp.where(mine, acc[f * 2 * rows:(f + 1) * 2 * rows], stats)
            at = GROUP * 2 * rows + f * HIGH
            counts = jnp.where(mine, acc[at:at + HIGH], counts)
        out_ref[pl.ds(pl.multiple_of(g * 3 * HIGH, 3 * HIGH), 3 * HIGH), :] = jnp.concatenate(
            [stats[0:HIGH] + stats[HIGH:2 * HIGH], stats[2 * HIGH:3 * HIGH] + stats[3 * HIGH:4 * HIGH], counts], axis=0)
        return carry

    if len(refs) > 1:
        out_ref[groups * 3 * HIGH:, :] = refs[0][...]
    lax.fori_loop(0, groups, one_group, 0, unroll=2)


def histogram_part(first, groups, tiles, bins_t, *tail):
    rows = groups * 3 * HIGH + sum(piece.shape[0] for piece in tail)
    return pl.pallas_call(
        functools.partial(histogram_kernel, first, groups),
        out_shape=jax.ShapeDtypeStruct((rows, GROUP * LOW), F32),
        in_specs=[vmem()] * (2 + len(tail)),
        out_specs=vmem(),
        compiler_params=pltpu.CompilerParams(vmem_limit_bytes=VMEM_LIMIT),
        cost_estimate=pl.CostEstimate(flops=groups * 1_000_000, bytes_accessed=groups * 1_000, transcendentals=0),
        name="histogram_part",
    )(tiles, bins_t, *tail)


def finish_kernel(per_dev, leaf_ref, kept_ref, sums_ref, *refs):
    arrived = list(refs[1::-1]) + list(refs[2:-3])
    value_ref, step_ref, hist_ref = refs[-3:]
    unit = kept_ref.shape[0]
    totals = add_up([sums_ref[...]] + [ref[unit:, :] for ref in arrived])
    highs = LEAVES // LANES
    grad, curv = totals[:, :LANES], totals[:, LANES:]
    shrunk = jnp.maximum(jnp.abs(grad) - lasso_penalty, 0.0)
    values = jnp.where(grad > 0.0, -shrunk, shrunk) / (curv + ridge_penalty)
    value_ref[...] = values
    leaf = leaf_ref[...]
    top, spot = leaf // LANES, leaf % LANES
    step = jnp.zeros(leaf.shape, F32)
    for h in range(highs):
        row = jnp.broadcast_to(values[h:h + 1, :], leaf.shape)
        step = jnp.where(top == h, jnp.take_along_axis(row, spot, axis=1), step)
    step_ref[...] = shrinkage * step
    hist = add_up([kept_ref[...]] + [ref[:unit, :] for ref in arrived])
    if per_dev == GROUP:
        shape = hist.shape
        line, place = iota(shape, 0), iota(shape, 1) // LOW
        step = 1
        while step < GROUP:
            down, across = (line // step) % 2, (place // step) % 2
            shift = step * LOW
            ahead = pltpu.roll(pltpu.roll(hist, shape[0] - step, 0), shift, 1)
            behind = pltpu.roll(pltpu.roll(hist, step, 0), shape[1] - shift, 1)
            hist = jnp.where(down == across, hist, jnp.where(across == 1, ahead, behind))
            step *= 2
        for c in range(3):
            for f in range(GROUP):
                hist_ref[c:c + 1, f * BINS:(f + 1) * BINS] = hist[c * HIGH + f:c * HIGH + f + 1, :]
    else:
        hist_ref[...] = hist


def finish(per_dev, leaves, kept, sums, arrived):
    out = (3, per_dev * BINS) if per_dev == GROUP else kept.shape
    return pl.pallas_call(
        functools.partial(finish_kernel, per_dev),
        out_shape=(
            jax.ShapeDtypeStruct((LEAVES // LANES, LANES), F32),
            jax.ShapeDtypeStruct(leaves.shape, F32),
            jax.ShapeDtypeStruct(out, F32),
        ),
        in_specs=[vmem()] * (3 + len(arrived)),
        out_specs=(vmem(), vmem(), vmem()),
        compiler_params=pltpu.CompilerParams(vmem_limit_bytes=VMEM_LIMIT),
        name="finish",
    )(leaves, kept, sums, *arrived)


def add_up(parts):
    while len(parts) > 1:
        parts = [parts[k] + parts[k + 1] for k in range(0, len(parts), 2)]
    return parts[0]


def local(scores, labels, leaves, bins, lengths, owner):
    query_count = lax.axis_size("query")
    feat_count = lax.axis_size("feat")
    count = query_count * feat_count
    place = lax.axis_index("query").astype(jnp.int32) * feat_count + lax.axis_index("feat").astype(jnp.int32)
    docs = scores.shape[0]
    own = docs // LANES
    features = owner.shape[0]
    per_dev = features // count
    unit = 3 * per_dev
    axes = ("query", "feat")
    feat_masks = [1 << b for b in range(feat_count.bit_length() - 1)]
    query_masks = [feat_count << b for b in range(query_count.bit_length() - 1)]

    def swap(value, mask):
        return lax.ppermute(value, axes, [(p, p ^ mask) for p in range(count)])

    pos = place.reshape(1)
    leaf_rows = leaves.reshape(own, LANES)
    own_scores = scores.reshape(own, LANES)
    score_parts = [own_scores]
    def inner_partner(p):
        z = p % feat_count
        if z in (0, feat_count - 1):
            return p ^ query_masks[0]
        return p + 1 if z % 2 else p - 1

    score_parts.append(lax.ppermute(own_scores, axes, [(p, inner_partner(p)) for p in range(count)]))
    score_parts.append(swap(own_scores, 1))
    masks = feat_masks + query_masks[:0:-1] + query_masks[:1]
    score_parts[0], leaf_rows, qid, worth, inverse, perm, bounds = prepare(
        feat_count, masks, lengths, pos, labels.reshape(-1, LANES), owner.reshape(-1, LANES), own_scores, leaf_rows)
    lambdas, near_lambdas = pair_terms(feat_count, bounds, pos, score_parts, worth, qid, inverse)
    bins_t, tiles, sums = leaf_terms(perm, bins, leaf_rows, near_lambdas)

    def part(tiles, low, high, *tail):
        if per_dev == GROUP:
            return histogram_part(low, high - low, tiles, bins_t, *tail)
        groups = high - low
        wide = histogram_part(low, groups, tiles, bins_t)
        wide = wide.reshape(groups, 3, HIGH, GROUP // per_dev, per_dev, LOW).transpose(0, 3, 1, 4, 2, 5)
        return jnp.concatenate([wide.reshape(groups * GROUP // per_dev * unit, BINS), *tail], axis=0)

    def join(block, total):
        return jnp.concatenate([block, total], axis=0)

    eighth = features // GROUP // 8
    edge = count // 8 * unit
    arrived = swap(part(tiles, 7 * eighth, 8 * eighth, sums), query_masks[0])
    block = part(tiles, 3 * eighth, 4 * eighth) + arrived[:edge]
    sums = sums + arrived[edge:]
    message, tiles = lax.optimization_barrier((join(block, sums), tiles))
    crossed_far = swap(message, query_masks[1])
    arrived = swap(part(tiles, 5 * eighth, 7 * eighth), query_masks[0])
    both = part(tiles, eighth, 3 * eighth) + arrived
    sums = sums + crossed_far[edge:]
    message, rest, tiles = lax.optimization_barrier(
        (join(both[:edge] + crossed_far[:edge], sums), join(both[edge:], sums), tiles))
    turned = swap(message, query_masks[2])
    crossed_near = swap(rest, query_masks[1])
    arrived = swap(part(tiles, 4 * eighth, 5 * eighth), query_masks[0])
    kept = part(tiles, 0, eighth) + arrived + crossed_near[:edge] + turned[:edge]
    sums = sums + turned[edge:]
    for mask in query_masks[3:]:
        edge = edge // 2
        arrived = swap(join(kept[edge:], sums), mask)
        kept = kept[:edge] + arrived[:edge]
        sums = sums + arrived[edge:]
    arrived = [swap(join(kept[m * unit:(m + 1) * unit], sums), m) for m in range(1, feat_count)]
    arrived[:2] = arrived[1::-1]
    values, step, histograms = finish(per_dev, leaf_rows, kept[:unit], sums, arrived)
    return lambdas, values.reshape(LEAVES), step.reshape(docs), histograms.reshape(3, per_dev * BINS)


def solution(mesh):
    in_specs = (
        P(("query", "feat")),
        P("query"),
        P(("query", "feat")),
        P(("query", "feat"), None),
        P("query", None),
        P(),
    )
    out_specs = (P(None, ("query", "feat")), P(), P(("query", "feat")), P(None, ("query", "feat")))
    return jax.shard_map(local, mesh=mesh, in_specs=in_specs, out_specs=out_specs, check_vma=False)
```

```python
import functools

import jax
import jax.numpy as jnp
from jax import lax
from jax.experimental import pallas as pl
from jax.experimental.pallas import tpu as pltpu
from jax.sharding import PartitionSpec as P

BINS = 256
LEAVES = 1024
LANES = 128
GRADES = 4
LOW = 32
HIGH = BINS // LOW
GROUP = 8
CHUNK = 64
MAX_LEN = 1024

lasso_penalty = 1.0
ridge_penalty = 1.0
shrinkage = 0.1

VMEM_LIMIT = 48 * 1024 * 1024
F32 = jnp.float32
BF16 = jnp.bfloat16
NT = (((1,), (1,)), ((), ()))


def iota(shape, axis):
    return lax.broadcasted_iota(jnp.int32, shape, axis)


def vmem():
    return pl.BlockSpec(memory_space=pltpu.VMEM)


def smem():
    return pl.BlockSpec(memory_space=pltpu.SMEM)


def prepare_kernel(feat_count, masks, len_ref, pos_ref, lab_ref, owner_ref, score_ref, leaf_ref,
                   kept_ref, leaf_out, qid_ref, worth_ref, inv_ref, perm_ref, bounds_ref):
    kept_ref[...] = score_ref[...]
    leaf_out[...] = leaf_ref[...]
    queries = len_ref.shape[1]
    rows = lab_ref.shape[0]
    own = rows // feat_count
    spot = iota((rows, LANES), 0) * LANES + iota((rows, LANES), 1)
    qid = jnp.zeros((rows, LANES), F32)
    begin = jnp.zeros((queries, LANES), jnp.int32)
    finish = jnp.zeros((queries, LANES), jnp.int32)
    which = iota((queries, LANES), 0)
    group = iota((1, LANES), 1) * LANES
    low = jnp.zeros((1, LANES), jnp.int32)
    high = first_end = jnp.full((1, LANES), rows * LANES, jnp.int32)
    start = jnp.int32(0)
    for q in range(queries):
        end = start + len_ref[0, q]
        qid = qid + jnp.where(spot >= end, 1.0, 0.0)
        begin = jnp.where(which == q, start, begin)
        finish = jnp.where(which == q, end, finish)

        low = low + jnp.where(end <= group, len_ref[0, q], 0)
        high = jnp.minimum(high, jnp.where(end >= group + LANES, end, rows * LANES))
        first_end = jnp.minimum(first_end, jnp.where(end > group, end, rows * LANES))
        start = end
    bounds_ref[...] = jnp.concatenate([low, high, first_end, low, low, low, low, low], axis=0)
    qid_ref[...] = qid
    worth_ref[...] = jnp.left_shift(1, lab_ref[...]).astype(F32)

    counts = [jnp.zeros((queries, LANES), F32) for _ in range(GRADES)]
    lane = iota((queries, LANES), 1)
    for r in range(rows):
        at = lane + r * LANES
        inside = (at >= begin) & (at < finish)
        grade = jnp.where(inside, jnp.broadcast_to(lab_ref[r:r + 1, :], (queries, LANES)), 0)
        for g in range(GRADES):
            counts[g] = counts[g] + jnp.where(grade > g, 1.0, 0.0)
    position = iota((queries, MAX_LEN), 1).astype(F32)
    gain = jnp.zeros((queries, MAX_LEN), F32)
    for g in range(GRADES):
        held = jnp.sum(counts[g], axis=1, keepdims=True)
        gain = gain + jnp.where(position < held, float(2 ** g), 0.0)
    level = 1.0 / jnp.log2(2.0 + position[0:1, :])
    ideal = jnp.sum(gain * level, axis=1, keepdims=True)
    usable = ideal > 0.5
    inverse = jnp.where(usable, 1.0 / jnp.where(usable, ideal, 1.0), 0.0)
    first = pos_ref[0] % feat_count * own
    for t in range(own):
        at = lane + (first + t) * LANES
        inside = (at >= begin) & (at < finish)
        inv_ref[0:1, t * LANES:(t + 1) * LANES] = jnp.sum(jnp.where(inside, inverse, 0.0), axis=0, keepdims=True)

    features = perm_ref.shape[0]
    per_dev = features >> len(masks)
    owner = jnp.concatenate([owner_ref[k:k + 1, :] for k in range(features // LANES)], axis=1)
    square = (features, features)
    down, across = iota(square, 0), iota(square, 1)
    index = iota((features, 1), 0) // per_dev
    target = jnp.zeros((features, 1), jnp.int32)
    for b, mask in enumerate(masks):
        target = target + ((index >> b) & 1) * mask
    target = (target ^ pos_ref[0]) * per_dev + iota((features, 1), 0) % per_dev
    pick = jnp.where(target == across, 1.0, 0.0).astype(BF16)
    holds = jnp.where(jnp.broadcast_to(owner, square) == down, 1.0, 0.0).astype(BF16)
    perm_ref[...] = lax.dot_general(pick, holds, NT, preferred_element_type=F32).astype(BF16)


def prepare(feat_count, masks, lengths, pos, labels, owner, scores, leaves):
    rows = labels.shape[0]
    features = owner.shape[0] * LANES
    return pl.pallas_call(
        functools.partial(prepare_kernel, feat_count, masks),
        out_shape=(
            jax.ShapeDtypeStruct(scores.shape, F32),
            jax.ShapeDtypeStruct(leaves.shape, jnp.int32),
            jax.ShapeDtypeStruct((rows, LANES), F32),
            jax.ShapeDtypeStruct((rows, LANES), F32),
            jax.ShapeDtypeStruct((1, rows // feat_count * LANES), F32),
            jax.ShapeDtypeStruct((features, features), BF16),
            jax.ShapeDtypeStruct((8, LANES), jnp.int32),
        ),
        in_specs=[smem(), smem(), vmem(), vmem(), vmem(), vmem()],
        out_specs=(vmem(),) * 7,
        compiler_params=pltpu.CompilerParams(vmem_limit_bytes=VMEM_LIMIT),
        cost_estimate=pl.CostEstimate(flops=2_000_000_000, bytes_accessed=300_000, transcendentals=20_000),
        name="prepare",
    )(lengths, pos, labels, owner, scores, leaves)


def split_terms(value, terms):
    parts = []
    rest = value
    for _ in range(terms):
        part = rest.astype(BF16)
        parts.append(part)
        rest = rest - part.astype(F32)
    return parts


def pairs_kernel(feat_count, bounds_ref, pos_ref, *refs):
    scores = refs[:-16]
    (worth_ref, qid_ref, inv_ref, lam_ref, near_ref,
     s_row, a_row, d_row, turn, s_col, a_col, w_col, q_col, d_col, grad, curv) = refs[-16:]
    rows = worth_ref.shape[0]
    own = rows // feat_count
    docs = own * LANES
    me = pos_ref[0] % feat_count
    s_row[...] = jnp.zeros(s_row.shape, F32)
    near = [me, ((me + 1) ^ 1) - 1, me ^ 1]
    for where, ref in zip(near, scores):
        @pl.when((where >= 0) & (where < feat_count))
        def _(where=where, ref=ref):
            s_row[pl.ds(pl.multiple_of(where * own, own), own), :] = ref[...]
    a_row[...] = jnp.exp(s_row[...])
    d_row[...] = jnp.zeros(d_row.shape, F32)
    first = me * own
    window_low = bounds_ref[0, first] // (2 * LANES) * 2
    window_high = (bounds_ref[1, first + own - 1] + 2 * LANES - 1) // (2 * LANES) * 2
    stride = 4

    def widen(pairs):
        lines = jnp.concatenate([source[...] for source, _ in pairs], axis=0)
        if lines.shape[0] % LANES:
            lines = jnp.concatenate([lines, jnp.zeros((LANES - lines.shape[0] % LANES, LANES), F32)], axis=0)
        for k in range(lines.shape[0] // LANES):
            turn[:, k * LANES:(k + 1) * LANES] = jnp.transpose(lines[k * LANES:(k + 1) * LANES])
        for r in range(0, rows, stride):
            @pl.when((r + stride > window_low) & (r < window_high))
            def _(r=r):
                for k, (_, col) in enumerate(pairs):
                    for m in range(r, r + stride):
                        at = k * rows + m
                        col[m * LANES:(m + 1) * LANES, :] = jnp.broadcast_to(turn[:, at:at + 1], (LANES, LANES))

    widen([(s_row, s_col), (qid_ref, q_col), (a_row, a_col), (worth_ref, w_col)])

    def rows_of(ref, r):
        return [jnp.broadcast_to(ref[pl.ds(r + g, 1), :], (8, LANES)) for g in range(2)]

    def spans(r):
        start, end = bounds_ref[0, r], bounds_ref[1, r + 1]
        low = jnp.maximum(start // LANES, window_low)
        high = jnp.minimum((end + LANES - 1) // LANES, window_high)
        single = bounds_ref[2, r] >= (r + 2) * LANES
        inner_low = jnp.where(single, jnp.maximum((start + LANES - 1) // LANES, window_low), r)
        inner_high = jnp.where(single, jnp.minimum(end // LANES, window_high), r)
        return low, inner_low, inner_high, high

    def rank_groups(k, carry):
        r = window_low + 2 * k
        score = rows_of(s_row, r)
        query = rows_of(qid_ref, r)

        def gather(c, acc, masked, test):
            base = pl.multiple_of(c * LANES, LANES)
            acc = list(acc)
            for u in range(LANES // 8):
                other = s_col[pl.ds(base + 8 * u, 8), :]
                for g in range(2):
                    hit = test(other, g, u)
                    if masked:
                        hit = hit & (q_col[pl.ds(base + 8 * u, 8), :] == query[g])
                    k = 4 * g + u % 4
                    acc[k] = acc[k] + jnp.where(hit, 1.0, 0.0)
            return tuple(acc)

        def ahead(other, g, u):
            return other >= score[g]

        def behind(other, g, u):
            return other > score[g]

        def within(mine):
            def test(other, g, u):
                if g != mine:
                    return ahead(other, g, u) if mine < g else behind(other, g, u)
                earlier = iota((8, LANES), 0) + 8 * u < iota((8, LANES), 1)
                return (other > score[g]) | ((other == score[g]) & earlier)
            return test

        def twice(low, high, test, acc):
            twos = (high - low) // 2
            acc = lax.fori_loop(0, twos, lambda k, acc: gather(
                low + 2 * k + 1, gather(low + 2 * k, acc, False, test), False, test), acc)
            return lax.fori_loop(low + 2 * twos, high, lambda c, acc: gather(c, acc, False, test), acc)

        acc = tuple(jnp.zeros((8, LANES), F32) for _ in range(8))
        low, inner_low, inner_high, high = spans(r)
        after = jnp.maximum(inner_high, r + 2)
        acc = lax.fori_loop(low, inner_low, lambda c, acc: gather(c, acc, True, ahead), acc)
        acc = twice(inner_low, r, ahead, acc)
        acc = twice(r + 2, after, behind, acc)
        acc = lax.fori_loop(after, high, lambda c, acc: gather(c, acc, True, behind), acc)
        for mine in range(2):
            acc = gather(r + mine, acc, True, within(mine))
        for g in range(2):
            total = (acc[4 * g] + acc[4 * g + 1]) + (acc[4 * g + 2] + acc[4 * g + 3])
            d_row[pl.ds(r + g, 1), :] = jnp.sum(total, axis=0, keepdims=True)
        return carry

    lax.fori_loop(0, (window_high - window_low) // 2, rank_groups, 0)
    d_row[...] = 1.0 / jnp.log2(2.0 + d_row[...])
    widen([(d_row, d_col)])

    def pair_groups(t, carry):
        r = first + 2 * t
        a_i, w_i, d_i, query = [rows_of(ref, r) for ref in (a_row, worth_ref, d_row, qid_ref)]

        def columns(masked):
            def step(c, acc):
                base = pl.multiple_of(c * LANES, LANES)
                acc = list(acc)
                for u in range(LANES // 8):
                    at = pl.ds(base + 8 * u, 8)
                    a_j, w_j, d_j = a_col[at, :], w_col[at, :], d_col[at, :]
                    for g in range(2):
                        recip = pl.reciprocal(a_i[g] + a_j, approx=True)
                        lift = w_i[g] - w_j
                        weight = jnp.abs(d_i[g] - d_j) * recip
                        if masked:
                            weight = jnp.where(q_col[at, :] == query[g], weight, 0.0)
                        weight = weight * lift
                        k = 4 * g + u % 2
                        acc[k] = acc[k] + weight * jnp.where(lift > 0.0, a_j, a_i[g])
                        acc[k + 2] = acc[k + 2] + jnp.abs(weight) * (recip * a_j)
                return tuple(acc)
            return step

        acc = tuple(jnp.zeros((8, LANES), F32) for _ in range(8))
        low, inner_low, inner_high, high = spans(r)
        acc = lax.fori_loop(low, inner_low, columns(True), acc)
        acc = lax.fori_loop(inner_low, inner_high, columns(False), acc)
        acc = lax.fori_loop(inner_high, high, columns(True), acc)
        for g in range(2):
            at = pl.ds(2 * t + g, 1)
            grad[at, :] = -jnp.sum(acc[4 * g] + acc[4 * g + 1], axis=0, keepdims=True)
            curv[at, :] = a_i[g][0:1, :] * jnp.sum(acc[4 * g + 2] + acc[4 * g + 3], axis=0, keepdims=True)
        return carry

    lax.fori_loop(0, own // 2, pair_groups, 0)
    inverse = inv_ref[...]
    terms = [inverse * jnp.concatenate([ref[t:t + 1, :] for t in range(own)], axis=1) for ref in (grad, curv)]
    for c in range(2):
        lam_ref[c:c + 1, :] = terms[c]
        near_ref[c:c + 1, :] = terms[c]


def pair_terms(feat_count, bounds, pos, scores, worth, qid, inverse):
    rows = worth.shape[0]
    docs = inverse.shape[1]
    row = pltpu.VMEM((rows, LANES), F32)
    turn = pltpu.VMEM((LANES, 4 * rows), F32)
    col = pltpu.VMEM((rows * LANES, LANES), F32)
    mine = pltpu.VMEM((docs // LANES, LANES), F32)
    return pl.pallas_call(
        functools.partial(pairs_kernel, feat_count),
        out_shape=(jax.ShapeDtypeStruct((2, docs), F32), jax.ShapeDtypeStruct((2, docs), F32)),
        in_specs=[smem(), smem()] + [vmem()] * (len(scores) + 3),
        out_specs=(vmem(), vmem()),
        scratch_shapes=[row, row, row, turn, col, col, col, col, col, mine, mine],
        compiler_params=pltpu.CompilerParams(vmem_limit_bytes=VMEM_LIMIT),
        cost_estimate=pl.CostEstimate(flops=9_000_000_000, bytes_accessed=200_000, transcendentals=2_000_000),
        name="pair_terms",
    )(bounds, pos, *scores, worth, qid, inverse)


def leaf_kernel(perm_ref, bins_ref, leaf_ref, lam_ref, bins_t_ref, tile_ref, sums_ref):
    bins = bins_ref[...].astype(F32).astype(BF16)
    bins_t_ref[...] = lax.dot_general(perm_ref[...], bins, NT, preferred_element_type=F32)
    own = leaf_ref.shape[0]
    docs = own * LANES
    leaf = jnp.concatenate([leaf_ref[t:t + 1, :] for t in range(own)], axis=1)
    highs = LEAVES // LANES
    top = jnp.broadcast_to(leaf // LANES, (highs, docs)) == iota((highs, docs), 0)
    spots = jnp.where(jnp.broadcast_to(leaf % LANES, (LANES, docs)) == iota((LANES, docs), 0), 1.0, 0.0).astype(BF16)
    pieces, tiles = [], []
    for c in range(2):
        for k, part in enumerate(split_terms(lam_ref[c:c + 1, :], 3)):
            wide = jnp.broadcast_to(part.astype(F32), (highs, docs))
            pieces.append(jnp.where(top, wide, 0.0))
            if k < 2:
                tiles.append(wide)
    tile_ref[...] = jnp.concatenate(tiles, axis=0).astype(BF16)
    stacked = jnp.concatenate(pieces, axis=0).astype(BF16)
    sums = lax.dot_general(stacked, spots, NT, preferred_element_type=F32)
    for c in range(2):
        base = c * 3 * highs
        sums_ref[:, c * LANES:(c + 1) * LANES] = (
            sums[base:base + highs] + (sums[base + highs:base + 2 * highs] + sums[base + 2 * highs:base + 3 * highs])
        )


def leaf_terms(perm, bins, leaves, lambdas):
    docs, features = bins.shape
    return pl.pallas_call(
        leaf_kernel,
        out_shape=(
            jax.ShapeDtypeStruct((features, docs), F32),
            jax.ShapeDtypeStruct((4 * HIGH, docs), BF16),
            jax.ShapeDtypeStruct((LEAVES // LANES, 2 * LANES), F32),
        ),
        in_specs=[vmem()] * 4,
        out_specs=(vmem(), vmem(), vmem()),
        compiler_params=pltpu.CompilerParams(vmem_limit_bytes=VMEM_LIMIT),
        cost_estimate=pl.CostEstimate(flops=200_000_000, bytes_accessed=3_000_000, transcendentals=0),
        name="leaf_terms",
    )(perm, bins, leaves, lambdas)


def histogram_kernel(first, groups, tile_ref, bins_ref, *refs):
    out_ref = refs[-1]
    docs = tile_ref.shape[1]
    depth = docs
    rows = 16
    row = iota((rows, depth), 0)
    low_level = [(row + rows * k).astype(F32).astype(BF16) for k in range(LOW // rows)]
    high_level = (row % HIGH).astype(F32).astype(BF16)
    upper = jnp.where(row < HIGH, 1.0, 0.0).astype(BF16) > 0
    zero = jnp.zeros((rows, depth), BF16)
    one = jnp.ones((rows, depth), BF16)
    lane_owner = iota((1, GROUP * LOW), 1) // LOW

    def one_group(g, carry):
        base = pl.multiple_of((first + g) * GROUP, GROUP)
        acc = None
        for k in range(docs // depth):
            span = slice(k * depth, (k + 1) * depth)
            code = bins_ref[pl.ds(base, GROUP), span]
            high = jnp.floor(code * (1.0 / LOW))
            low = code - high * LOW
            left, right, count = [], [], []
            wide = []
            for f in range(GROUP):
                high_f = jnp.broadcast_to(high[f:f + 1, :], (rows, depth))
                low_f = jnp.broadcast_to(low[f:f + 1, :], (rows, depth)).astype(BF16)
                high_f = high_f.astype(BF16)
                wide.append(high_f)
                match = high_f == high_level
                for c in range(2):
                    left.append(jnp.where(match, tile_ref[c * rows:(c + 1) * rows, span], zero))
                for level in low_level:
                    right.append(jnp.where(low_f == level, one, zero))
            for f in range(0, GROUP, 2):
                both = jnp.where(upper, wide[f], wide[f + 1])
                count.append(jnp.where(both == high_level, one, zero))
            part = lax.dot_general(
                jnp.concatenate(left + count, axis=0), jnp.concatenate(right, axis=0), NT,
                preferred_element_type=F32,
            )
            acc = part if acc is None else acc + part
        stats = jnp.zeros((2 * rows, GROUP * LOW), F32)
        counts = jnp.zeros((HIGH, GROUP * LOW), F32)
        for f in range(GROUP):
            mine = lane_owner == f
            stats = jnp.where(mine, acc[f * 2 * rows:(f + 1) * 2 * rows], stats)
            at = GROUP * 2 * rows + f * HIGH
            counts = jnp.where(mine, acc[at:at + HIGH], counts)
        out_ref[pl.ds(pl.multiple_of(g * 3 * HIGH, 3 * HIGH), 3 * HIGH), :] = jnp.concatenate(
            [stats[0:HIGH] + stats[HIGH:2 * HIGH], stats[2 * HIGH:3 * HIGH] + stats[3 * HIGH:4 * HIGH], counts], axis=0)
        return carry

    if len(refs) > 1:
        out_ref[groups * 3 * HIGH:, :] = refs[0][...]
    lax.fori_loop(0, groups, one_group, 0, unroll=4)


def histogram_part(first, groups, tiles, bins_t, *tail):
    rows = groups * 3 * HIGH + sum(piece.shape[0] for piece in tail)
    return pl.pallas_call(
        functools.partial(histogram_kernel, first, groups),
        out_shape=jax.ShapeDtypeStruct((rows, GROUP * LOW), F32),
        in_specs=[vmem()] * (2 + len(tail)),
        out_specs=vmem(),
        compiler_params=pltpu.CompilerParams(vmem_limit_bytes=VMEM_LIMIT),
        cost_estimate=pl.CostEstimate(flops=groups * 1_000_000, bytes_accessed=groups * 1_000, transcendentals=0),
        name="histogram_part",
    )(tiles, bins_t, *tail)


def finish_kernel(per_dev, leaf_ref, kept_ref, sums_ref, *refs):
    arrived = list(refs[1::-1]) + list(refs[2:-3])
    value_ref, step_ref, hist_ref = refs[-3:]
    unit = kept_ref.shape[0]
    totals = add_up([sums_ref[...]] + [ref[unit:, :] for ref in arrived])
    highs = LEAVES // LANES
    grad, curv = totals[:, :LANES], totals[:, LANES:]
    shrunk = jnp.maximum(jnp.abs(grad) - lasso_penalty, 0.0)
    values = jnp.where(grad > 0.0, -shrunk, shrunk) / (curv + ridge_penalty)
    value_ref[...] = values
    leaf = leaf_ref[...]
    top, spot = leaf // LANES, leaf % LANES
    step = jnp.zeros(leaf.shape, F32)
    for h in range(highs):
        row = jnp.broadcast_to(values[h:h + 1, :], leaf.shape)
        step = jnp.where(top == h, jnp.take_along_axis(row, spot, axis=1), step)
    step_ref[...] = shrinkage * step
    hist = add_up([kept_ref[...]] + [ref[:unit, :] for ref in arrived])
    if per_dev == GROUP:
        shape = hist.shape
        line, place = iota(shape, 0), iota(shape, 1) // LOW
        step = 1
        while step < GROUP:
            down, across = (line // step) % 2, (place // step) % 2
            shift = step * LOW
            ahead = pltpu.roll(pltpu.roll(hist, shape[0] - step, 0), shift, 1)
            behind = pltpu.roll(pltpu.roll(hist, step, 0), shape[1] - shift, 1)
            hist = jnp.where(down == across, hist, jnp.where(across == 1, ahead, behind))
            step *= 2
        for c in range(3):
            for f in range(GROUP):
                hist_ref[c:c + 1, f * BINS:(f + 1) * BINS] = hist[c * HIGH + f:c * HIGH + f + 1, :]
    else:
        hist_ref[...] = hist


def finish(per_dev, leaves, kept, sums, arrived):
    out = (3, per_dev * BINS) if per_dev == GROUP else kept.shape
    return pl.pallas_call(
        functools.partial(finish_kernel, per_dev),
        out_shape=(
            jax.ShapeDtypeStruct((LEAVES // LANES, LANES), F32),
            jax.ShapeDtypeStruct(leaves.shape, F32),
            jax.ShapeDtypeStruct(out, F32),
        ),
        in_specs=[vmem()] * (3 + len(arrived)),
        out_specs=(vmem(), vmem(), vmem()),
        compiler_params=pltpu.CompilerParams(vmem_limit_bytes=VMEM_LIMIT),
        name="finish",
    )(leaves, kept, sums, *arrived)


def add_up(parts):
    while len(parts) > 1:
        parts = [parts[k] + parts[k + 1] for k in range(0, len(parts), 2)]
    return parts[0]


def local(scores, labels, leaves, bins, lengths, owner):
    query_count = lax.axis_size("query")
    feat_count = lax.axis_size("feat")
    count = query_count * feat_count
    place = lax.axis_index("query").astype(jnp.int32) * feat_count + lax.axis_index("feat").astype(jnp.int32)
    docs = scores.shape[0]
    own = docs // LANES
    features = owner.shape[0]
    per_dev = features // count
    unit = 3 * per_dev
    axes = ("query", "feat")
    feat_masks = [1 << b for b in range(feat_count.bit_length() - 1)]
    query_masks = [feat_count << b for b in range(query_count.bit_length() - 1)]

    def swap(value, mask):
        return lax.ppermute(value, axes, [(p, p ^ mask) for p in range(count)])

    pos = place.reshape(1)
    leaf_rows = leaves.reshape(own, LANES)
    own_scores = scores.reshape(own, LANES)
    score_parts = [own_scores]
    def inner_partner(p):
        z = p % feat_count
        if z in (0, feat_count - 1):
            return p ^ query_masks[0]
        return p + 1 if z % 2 else p - 1

    score_parts.append(lax.ppermute(own_scores, axes, [(p, inner_partner(p)) for p in range(count)]))
    score_parts.append(swap(own_scores, 1))
    masks = feat_masks + query_masks[:0:-1] + query_masks[:1]
    score_parts[0], leaf_rows, qid, worth, inverse, perm, bounds = prepare(
        feat_count, masks, lengths, pos, labels.reshape(-1, LANES), owner.reshape(-1, LANES), own_scores, leaf_rows)
    lambdas, near_lambdas = pair_terms(feat_count, bounds, pos, score_parts, worth, qid, inverse)
    bins_t, tiles, sums = leaf_terms(perm, bins, leaf_rows, near_lambdas)

    def part(tiles, low, high, *tail):
        if per_dev == GROUP:
            return histogram_part(low, high - low, tiles, bins_t, *tail)
        groups = high - low
        wide = histogram_part(low, groups, tiles, bins_t)
        wide = wide.reshape(groups, 3, HIGH, GROUP // per_dev, per_dev, LOW).transpose(0, 3, 1, 4, 2, 5)
        return jnp.concatenate([wide.reshape(groups * GROUP // per_dev * unit, BINS), *tail], axis=0)

    def join(block, total):
        return jnp.concatenate([block, total], axis=0)

    eighth = features // GROUP // 8
    edge = count // 8 * unit
    arrived = swap(part(tiles, 7 * eighth, 8 * eighth, sums), query_masks[0])
    block = part(tiles, 3 * eighth, 4 * eighth) + arrived[:edge]
    sums = sums + arrived[edge:]
    message, tiles = lax.optimization_barrier((join(block, sums), tiles))
    crossed_far = swap(message, query_masks[1])
    arrived = swap(part(tiles, 5 * eighth, 7 * eighth), query_masks[0])
    both = part(tiles, eighth, 3 * eighth) + arrived
    sums = sums + crossed_far[edge:]
    message, rest, tiles = lax.optimization_barrier(
        (join(both[:edge] + crossed_far[:edge], sums), join(both[edge:], sums), tiles))
    turned = swap(message, query_masks[2])
    crossed_near = swap(rest, query_masks[1])
    arrived = swap(part(tiles, 4 * eighth, 5 * eighth), query_masks[0])
    kept = part(tiles, 0, eighth) + arrived + crossed_near[:edge] + turned[:edge]
    sums = sums + turned[edge:]
    for mask in query_masks[3:]:
        edge = edge // 2
        arrived = swap(join(kept[edge:], sums), mask)
        kept = kept[:edge] + arrived[:edge]
        sums = sums + arrived[edge:]
    arrived = [swap(join(kept[m * unit:(m + 1) * unit], sums), m) for m in range(1, feat_count)]
    arrived[:2] = arrived[1::-1]
    values, step, histograms = finish(per_dev, leaf_rows, kept[:unit], sums, arrived)
    return lambdas, values.reshape(LEAVES), step.reshape(docs), histograms.reshape(3, per_dev * BINS)


def solution(mesh):
    in_specs = (
        P(("query", "feat")),
        P("query"),
        P(("query", "feat")),
        P(("query", "feat"), None),
        P("query", None),
        P(),
    )
    out_specs = (P(None, ("query", "feat")), P(), P(("query", "feat")), P(None, ("query", "feat")))
    return jax.shard_map(local, mesh=mesh, in_specs=in_specs, out_specs=out_specs, check_vma=False)
```

```python
import functools

import jax
import jax.numpy as jnp
from jax import lax
from jax.experimental import pallas as pl
from jax.experimental.pallas import tpu as pltpu
from jax.sharding import PartitionSpec as P

BINS = 256
LEAVES = 1024
LANES = 128
GRADES = 4
LOW = 32
HIGH = BINS // LOW
GROUP = 8
CHUNK = 64
MAX_LEN = 1024

lasso_penalty = 1.0
ridge_penalty = 1.0
shrinkage = 0.1

VMEM_LIMIT = 48 * 1024 * 1024
F32 = jnp.float32
BF16 = jnp.bfloat16
NT = (((1,), (1,)), ((), ()))


def iota(shape, axis):
    return lax.broadcasted_iota(jnp.int32, shape, axis)


def vmem():
    return pl.BlockSpec(memory_space=pltpu.VMEM)


def smem():
    return pl.BlockSpec(memory_space=pltpu.SMEM)


def prepare_kernel(feat_count, masks, len_ref, pos_ref, lab_ref, owner_ref, score_ref, leaf_ref,
                   kept_ref, leaf_out, qid_ref, worth_ref, inv_ref, perm_ref, bounds_ref):
    kept_ref[...] = score_ref[...]
    leaf_out[...] = leaf_ref[...]
    queries = len_ref.shape[1]
    rows = lab_ref.shape[0]
    own = rows // feat_count
    spot = iota((rows, LANES), 0) * LANES + iota((rows, LANES), 1)
    qid = jnp.zeros((rows, LANES), F32)
    begin = jnp.zeros((queries, LANES), jnp.int32)
    finish = jnp.zeros((queries, LANES), jnp.int32)
    which = iota((queries, LANES), 0)
    group = iota((1, LANES), 1) * LANES
    low = jnp.zeros((1, LANES), jnp.int32)
    high = first_end = jnp.full((1, LANES), rows * LANES, jnp.int32)
    start = jnp.int32(0)
    for q in range(queries):
        end = start + len_ref[0, q]
        qid = qid + jnp.where(spot >= end, 1.0, 0.0)
        begin = jnp.where(which == q, start, begin)
        finish = jnp.where(which == q, end, finish)

        low = low + jnp.where(end <= group, len_ref[0, q], 0)
        high = jnp.minimum(high, jnp.where(end >= group + LANES, end, rows * LANES))
        first_end = jnp.minimum(first_end, jnp.where(end > group, end, rows * LANES))
        start = end
    bounds_ref[...] = jnp.concatenate([low, high, first_end, low, low, low, low, low], axis=0)
    qid_ref[...] = qid
    worth_ref[...] = jnp.left_shift(1, lab_ref[...]).astype(F32)

    counts = [jnp.zeros((queries, LANES), F32) for _ in range(GRADES)]
    lane = iota((queries, LANES), 1)
    for r in range(rows):
        at = lane + r * LANES
        inside = (at >= begin) & (at < finish)
        grade = jnp.where(inside, jnp.broadcast_to(lab_ref[r:r + 1, :], (queries, LANES)), 0)
        for g in range(GRADES):
            counts[g] = counts[g] + jnp.where(grade > g, 1.0, 0.0)
    position = iota((queries, MAX_LEN), 1).astype(F32)
    gain = jnp.zeros((queries, MAX_LEN), F32)
    for g in range(GRADES):
        held = jnp.sum(counts[g], axis=1, keepdims=True)
        gain = gain + jnp.where(position < held, float(2 ** g), 0.0)
    level = 1.0 / jnp.log2(2.0 + position[0:1, :])
    ideal = jnp.sum(gain * level, axis=1, keepdims=True)
    usable = ideal > 0.5
    inverse = jnp.where(usable, 1.0 / jnp.where(usable, ideal, 1.0), 0.0)
    first = pos_ref[0] % feat_count * own
    for t in range(own):
        at = lane + (first + t) * LANES
        inside = (at >= begin) & (at < finish)
        inv_ref[0:1, t * LANES:(t + 1) * LANES] = jnp.sum(jnp.where(inside, inverse, 0.0), axis=0, keepdims=True)

    features = perm_ref.shape[0]
    per_dev = features >> len(masks)
    owner = jnp.concatenate([owner_ref[k:k + 1, :] for k in range(features // LANES)], axis=1)
    square = (features, features)
    down, across = iota(square, 0), iota(square, 1)
    index = iota((features, 1), 0) // per_dev
    target = jnp.zeros((features, 1), jnp.int32)
    for b, mask in enumerate(masks):
        target = target + ((index >> b) & 1) * mask
    target = (target ^ pos_ref[0]) * per_dev + iota((features, 1), 0) % per_dev
    pick = jnp.where(target == across, 1.0, 0.0).astype(BF16)
    holds = jnp.where(jnp.broadcast_to(owner, square) == down, 1.0, 0.0).astype(BF16)
    perm_ref[...] = lax.dot_general(pick, holds, NT, preferred_element_type=F32).astype(BF16)


def prepare(feat_count, masks, lengths, pos, labels, owner, scores, leaves):
    rows = labels.shape[0]
    features = owner.shape[0] * LANES
    return pl.pallas_call(
        functools.partial(prepare_kernel, feat_count, masks),
        out_shape=(
            jax.ShapeDtypeStruct(scores.shape, F32),
            jax.ShapeDtypeStruct(leaves.shape, jnp.int32),
            jax.ShapeDtypeStruct((rows, LANES), F32),
            jax.ShapeDtypeStruct((rows, LANES), F32),
            jax.ShapeDtypeStruct((1, rows // feat_count * LANES), F32),
            jax.ShapeDtypeStruct((features, features), BF16),
            jax.ShapeDtypeStruct((8, LANES), jnp.int32),
        ),
        in_specs=[smem(), smem(), vmem(), vmem(), vmem(), vmem()],
        out_specs=(vmem(),) * 7,
        compiler_params=pltpu.CompilerParams(vmem_limit_bytes=VMEM_LIMIT),
        cost_estimate=pl.CostEstimate(flops=2_000_000_000, bytes_accessed=300_000, transcendentals=20_000),
        name="prepare",
    )(lengths, pos, labels, owner, scores, leaves)


def split_terms(value, terms):
    parts = []
    rest = value
    for _ in range(terms):
        part = rest.astype(BF16)
        parts.append(part)
        rest = rest - part.astype(F32)
    return parts


def pairs_kernel(feat_count, bounds_ref, pos_ref, *refs):
    scores = refs[:-16]
    (worth_ref, qid_ref, inv_ref, lam_ref, near_ref,
     s_row, a_row, d_row, turn, s_col, a_col, w_col, q_col, d_col, grad, curv) = refs[-16:]
    rows = worth_ref.shape[0]
    own = rows // feat_count
    docs = own * LANES
    me = pos_ref[0] % feat_count
    s_row[...] = jnp.zeros(s_row.shape, F32)
    near = [me, ((me + 1) ^ 1) - 1, me ^ 1]
    for where, ref in zip(near, scores):
        @pl.when((where >= 0) & (where < feat_count))
        def _(where=where, ref=ref):
            s_row[pl.ds(pl.multiple_of(where * own, own), own), :] = ref[...]
    a_row[...] = jnp.exp(s_row[...])
    d_row[...] = jnp.zeros(d_row.shape, F32)
    first = me * own
    window_low = bounds_ref[0, first] // (2 * LANES) * 2
    window_high = (bounds_ref[1, first + own - 1] + 2 * LANES - 1) // (2 * LANES) * 2
    stride = 4

    def widen(pairs):
        lines = jnp.concatenate([source[...] for source, _ in pairs], axis=0)
        if lines.shape[0] % LANES:
            lines = jnp.concatenate([lines, jnp.zeros((LANES - lines.shape[0] % LANES, LANES), F32)], axis=0)
        for k in range(lines.shape[0] // LANES):
            turn[:, k * LANES:(k + 1) * LANES] = jnp.transpose(lines[k * LANES:(k + 1) * LANES])
        for r in range(0, rows, stride):
            @pl.when((r + stride > window_low) & (r < window_high))
            def _(r=r):
                for k, (_, col) in enumerate(pairs):
                    for m in range(r, r + stride):
                        at = k * rows + m
                        col[m * LANES:(m + 1) * LANES, :] = jnp.broadcast_to(turn[:, at:at + 1], (LANES, LANES))

    widen([(s_row, s_col), (qid_ref, q_col), (a_row, a_col), (worth_ref, w_col)])

    def rows_of(ref, r):
        return [jnp.broadcast_to(ref[pl.ds(r + g, 1), :], (8, LANES)) for g in range(2)]

    def spans(r):
        start, end = bounds_ref[0, r], bounds_ref[1, r + 1]
        low = jnp.maximum(start // LANES, window_low)
        high = jnp.minimum((end + LANES - 1) // LANES, window_high)
        single = bounds_ref[2, r] >= (r + 2) * LANES
        inner_low = jnp.where(single, jnp.maximum((start + LANES - 1) // LANES, window_low), r)
        inner_high = jnp.where(single, jnp.minimum(end // LANES, window_high), r)
        return low, inner_low, inner_high, high

    def rank_groups(k, carry):
        r = window_low + 2 * k
        score = rows_of(s_row, r)
        query = rows_of(qid_ref, r)

        def gather(c, acc, masked, test):
            base = pl.multiple_of(c * LANES, LANES)
            acc = list(acc)
            for u in range(LANES // 8):
                other = s_col[pl.ds(base + 8 * u, 8), :]
                for g in range(2):
                    hit = test(other, g, u)
                    if masked:
                        hit = hit & (q_col[pl.ds(base + 8 * u, 8), :] == query[g])
                    k = 4 * g + u % 4
                    acc[k] = acc[k] + jnp.where(hit, 1.0, 0.0)
            return tuple(acc)

        def ahead(other, g, u):
            return other >= score[g]

        def behind(other, g, u):
            return other > score[g]

        def within(mine):
            def test(other, g, u):
                if g != mine:
                    return ahead(other, g, u) if mine < g else behind(other, g, u)
                earlier = iota((8, LANES), 0) + 8 * u < iota((8, LANES), 1)
                return (other > score[g]) | ((other == score[g]) & earlier)
            return test

        def twice(low, high, test, acc):
            twos = (high - low) // 2
            acc = lax.fori_loop(0, twos, lambda k, acc: gather(
                low + 2 * k + 1, gather(low + 2 * k, acc, False, test), False, test), acc)
            return lax.fori_loop(low + 2 * twos, high, lambda c, acc: gather(c, acc, False, test), acc)

        acc = tuple(jnp.zeros((8, LANES), F32) for _ in range(8))
        low, inner_low, inner_high, high = spans(r)
        after = jnp.maximum(inner_high, r + 2)
        acc = lax.fori_loop(low, inner_low, lambda c, acc: gather(c, acc, True, ahead), acc)
        acc = twice(inner_low, r, ahead, acc)
        acc = twice(r + 2, after, behind, acc)
        acc = lax.fori_loop(after, high, lambda c, acc: gather(c, acc, True, behind), acc)
        for mine in range(2):
            acc = gather(r + mine, acc, True, within(mine))
        for g in range(2):
            total = (acc[4 * g] + acc[4 * g + 1]) + (acc[4 * g + 2] + acc[4 * g + 3])
            d_row[pl.ds(r + g, 1), :] = jnp.sum(total, axis=0, keepdims=True)
        return carry

    lax.fori_loop(0, (window_high - window_low) // 2, rank_groups, 0)
    d_row[...] = 1.0 / jnp.log2(2.0 + d_row[...])
    widen([(d_row, d_col)])

    def pair_groups(t, carry):
        r = first + 2 * t
        a_i, w_i, d_i, query = [rows_of(ref, r) for ref in (a_row, worth_ref, d_row, qid_ref)]

        def columns(masked):
            def step(c, acc):
                base = pl.multiple_of(c * LANES, LANES)
                acc = list(acc)
                for u in range(LANES // 8):
                    at = pl.ds(base + 8 * u, 8)
                    a_j, w_j, d_j = a_col[at, :], w_col[at, :], d_col[at, :]
                    for g in range(2):
                        recip = pl.reciprocal(a_i[g] + a_j, approx=True)
                        lift = w_i[g] - w_j
                        weight = jnp.abs(d_i[g] - d_j) * recip
                        if masked:
                            weight = jnp.where(q_col[at, :] == query[g], weight, 0.0)
                        weight = weight * lift
                        k = 4 * g + u % 2
                        acc[k] = acc[k] + weight * jnp.where(lift > 0.0, a_j, a_i[g])
                        acc[k + 2] = acc[k + 2] + jnp.abs(weight) * (recip * a_j)
                return tuple(acc)
            return step

        def twice(low, high, step, acc):
            twos = (high - low) // 2
            acc = lax.fori_loop(0, twos, lambda k, acc: step(low + 2 * k + 1, step(low + 2 * k, acc)), acc)
            return lax.fori_loop(low + 2 * twos, high, step, acc)

        acc = tuple(jnp.zeros((8, LANES), F32) for _ in range(8))
        low, inner_low, inner_high, high = spans(r)
        whole = inner_low < inner_high
        inner_low = jnp.where(whole, inner_low, low)
        inner_high = jnp.where(whole, inner_high, low)
        acc = lax.fori_loop(low, inner_low, columns(True), acc)
        acc = twice(inner_low, inner_high, columns(False), acc)
        acc = twice(inner_high, high, columns(True), acc)
        for g in range(2):
            at = pl.ds(2 * t + g, 1)
            grad[at, :] = -jnp.sum(acc[4 * g] + acc[4 * g + 1], axis=0, keepdims=True)
            curv[at, :] = a_i[g][0:1, :] * jnp.sum(acc[4 * g + 2] + acc[4 * g + 3], axis=0, keepdims=True)
        return carry

    lax.fori_loop(0, own // 2, pair_groups, 0)
    inverse = inv_ref[...]
    terms = [inverse * jnp.concatenate([ref[t:t + 1, :] for t in range(own)], axis=1) for ref in (grad, curv)]
    for c in range(2):
        lam_ref[c:c + 1, :] = terms[c]
        near_ref[c:c + 1, :] = terms[c]


def pair_terms(feat_count, bounds, pos, scores, worth, qid, inverse):
    rows = worth.shape[0]
    docs = inverse.shape[1]
    row = pltpu.VMEM((rows, LANES), F32)
    turn = pltpu.VMEM((LANES, 4 * rows), F32)
    col = pltpu.VMEM((rows * LANES, LANES), F32)
    mine = pltpu.VMEM((docs // LANES, LANES), F32)
    return pl.pallas_call(
        functools.partial(pairs_kernel, feat_count),
        out_shape=(jax.ShapeDtypeStruct((2, docs), F32), jax.ShapeDtypeStruct((2, docs), F32)),
        in_specs=[smem(), smem()] + [vmem()] * (len(scores) + 3),
        out_specs=(vmem(), vmem()),
        scratch_shapes=[row, row, row, turn, col, col, col, col, col, mine, mine],
        compiler_params=pltpu.CompilerParams(vmem_limit_bytes=VMEM_LIMIT),
        cost_estimate=pl.CostEstimate(flops=9_000_000_000, bytes_accessed=200_000, transcendentals=2_000_000),
        name="pair_terms",
    )(bounds, pos, *scores, worth, qid, inverse)


def leaf_kernel(perm_ref, bins_ref, leaf_ref, lam_ref, bins_t_ref, tile_ref, sums_ref):
    bins = bins_ref[...].astype(F32).astype(BF16)
    bins_t_ref[...] = lax.dot_general(perm_ref[...], bins, NT, preferred_element_type=F32)
    own = leaf_ref.shape[0]
    docs = own * LANES
    leaf = jnp.concatenate([leaf_ref[t:t + 1, :] for t in range(own)], axis=1)
    highs = LEAVES // LANES
    top = jnp.broadcast_to(leaf // LANES, (highs, docs)) == iota((highs, docs), 0)
    spots = jnp.where(jnp.broadcast_to(leaf % LANES, (LANES, docs)) == iota((LANES, docs), 0), 1.0, 0.0).astype(BF16)
    pieces, tiles = [], []
    for c in range(2):
        for k, part in enumerate(split_terms(lam_ref[c:c + 1, :], 3)):
            wide = jnp.broadcast_to(part.astype(F32), (highs, docs))
            pieces.append(jnp.where(top, wide, 0.0))
            if k < 2:
                tiles.append(wide)
    tile_ref[...] = jnp.concatenate(tiles, axis=0).astype(BF16)
    stacked = jnp.concatenate(pieces, axis=0).astype(BF16)
    sums = lax.dot_general(stacked, spots, NT, preferred_element_type=F32)
    for c in range(2):
        base = c * 3 * highs
        sums_ref[:, c * LANES:(c + 1) * LANES] = (
            sums[base:base + highs] + (sums[base + highs:base + 2 * highs] + sums[base + 2 * highs:base + 3 * highs])
        )


def leaf_terms(perm, bins, leaves, lambdas):
    docs, features = bins.shape
    return pl.pallas_call(
        leaf_kernel,
        out_shape=(
            jax.ShapeDtypeStruct((features, docs), F32),
            jax.ShapeDtypeStruct((4 * HIGH, docs), BF16),
            jax.ShapeDtypeStruct((LEAVES // LANES, 2 * LANES), F32),
        ),
        in_specs=[vmem()] * 4,
        out_specs=(vmem(), vmem(), vmem()),
        compiler_params=pltpu.CompilerParams(vmem_limit_bytes=VMEM_LIMIT),
        cost_estimate=pl.CostEstimate(flops=200_000_000, bytes_accessed=3_000_000, transcendentals=0),
        name="leaf_terms",
    )(perm, bins, leaves, lambdas)


def histogram_kernel(first, groups, tile_ref, bins_ref, *refs):
    out_ref = refs[-1]
    docs = tile_ref.shape[1]
    depth = docs
    rows = 16
    row = iota((rows, depth), 0)
    low_level = [(row + rows * k).astype(F32).astype(BF16) for k in range(LOW // rows)]
    high_level = (row % HIGH).astype(F32).astype(BF16)
    upper = jnp.where(row < HIGH, 1.0, 0.0).astype(BF16) > 0
    zero = jnp.zeros((rows, depth), BF16)
    one = jnp.ones((rows, depth), BF16)
    lane_owner = iota((1, GROUP * LOW), 1) // LOW

    def one_group(g, carry):
        base = pl.multiple_of((first + g) * GROUP, GROUP)
        acc = None
        for k in range(docs // depth):
            span = slice(k * depth, (k + 1) * depth)
            code = bins_ref[pl.ds(base, GROUP), span]
            high = jnp.floor(code * (1.0 / LOW))
            low = code - high * LOW
            left, right, count = [], [], []
            wide = []
            for f in range(GROUP):
                high_f = jnp.broadcast_to(high[f:f + 1, :], (rows, depth))
                low_f = jnp.broadcast_to(low[f:f + 1, :], (rows, depth)).astype(BF16)
                high_f = high_f.astype(BF16)
                wide.append(high_f)
                match = high_f == high_level
                for c in range(2):
                    left.append(jnp.where(match, tile_ref[c * rows:(c + 1) * rows, span], zero))
                for level in low_level:
                    right.append(jnp.where(low_f == level, one, zero))
            for f in range(0, GROUP, 2):
                both = jnp.where(upper, wide[f], wide[f + 1])
                count.append(jnp.where(both == high_level, one, zero))
            part = lax.dot_general(
                jnp.concatenate(left + count, axis=0), jnp.concatenate(right, axis=0), NT,
                preferred_element_type=F32,
            )
            acc = part if acc is None else acc + part
        stats = jnp.zeros((2 * rows, GROUP * LOW), F32)
        counts = jnp.zeros((HIGH, GROUP * LOW), F32)
        for f in range(GROUP):
            mine = lane_owner == f
            stats = jnp.where(mine, acc[f * 2 * rows:(f + 1) * 2 * rows], stats)
            at = GROUP * 2 * rows + f * HIGH
            counts = jnp.where(mine, acc[at:at + HIGH], counts)
        out_ref[pl.ds(pl.multiple_of(g * 3 * HIGH, 3 * HIGH), 3 * HIGH), :] = jnp.concatenate(
            [stats[0:HIGH] + stats[HIGH:2 * HIGH], stats[2 * HIGH:3 * HIGH] + stats[3 * HIGH:4 * HIGH], counts], axis=0)
        return carry

    if len(refs) > 1:
        out_ref[groups * 3 * HIGH:, :] = refs[0][...]
    lax.fori_loop(0, groups, one_group, 0, unroll=min(groups, 8))


def histogram_part(first, groups, tiles, bins_t, *tail):
    rows = groups * 3 * HIGH + sum(piece.shape[0] for piece in tail)
    return pl.pallas_call(
        functools.partial(histogram_kernel, first, groups),
        out_shape=jax.ShapeDtypeStruct((rows, GROUP * LOW), F32),
        in_specs=[vmem()] * (2 + len(tail)),
        out_specs=vmem(),
        compiler_params=pltpu.CompilerParams(vmem_limit_bytes=VMEM_LIMIT),
        cost_estimate=pl.CostEstimate(flops=groups * 1_000_000, bytes_accessed=groups * 1_000, transcendentals=0),
        name="histogram_part",
    )(tiles, bins_t, *tail)


def finish_kernel(per_dev, leaf_ref, kept_ref, sums_ref, *refs):
    arrived = list(refs[1::-1]) + list(refs[2:-3])
    value_ref, step_ref, hist_ref = refs[-3:]
    unit = kept_ref.shape[0]
    totals = add_up([sums_ref[...]] + [ref[unit:, :] for ref in arrived])
    highs = LEAVES // LANES
    grad, curv = totals[:, :LANES], totals[:, LANES:]
    shrunk = jnp.maximum(jnp.abs(grad) - lasso_penalty, 0.0)
    values = jnp.where(grad > 0.0, -shrunk, shrunk) / (curv + ridge_penalty)
    value_ref[...] = values
    leaf = leaf_ref[...]
    top, spot = leaf // LANES, leaf % LANES
    step = jnp.zeros(leaf.shape, F32)
    for h in range(highs):
        row = jnp.broadcast_to(values[h:h + 1, :], leaf.shape)
        step = jnp.where(top == h, jnp.take_along_axis(row, spot, axis=1), step)
    step_ref[...] = shrinkage * step
    hist = add_up([kept_ref[...]] + [ref[:unit, :] for ref in arrived])
    if per_dev == GROUP:
        shape = hist.shape
        line, place = iota(shape, 0), iota(shape, 1) // LOW
        step = 1
        while step < GROUP:
            down, across = (line // step) % 2, (place // step) % 2
            shift = step * LOW
            ahead = pltpu.roll(pltpu.roll(hist, shape[0] - step, 0), shift, 1)
            behind = pltpu.roll(pltpu.roll(hist, step, 0), shape[1] - shift, 1)
            hist = jnp.where(down == across, hist, jnp.where(across == 1, ahead, behind))
            step *= 2
        for c in range(3):
            for f in range(GROUP):
                hist_ref[c:c + 1, f * BINS:(f + 1) * BINS] = hist[c * HIGH + f:c * HIGH + f + 1, :]
    else:
        hist_ref[...] = hist


def finish(per_dev, leaves, kept, sums, arrived):
    out = (3, per_dev * BINS) if per_dev == GROUP else kept.shape
    return pl.pallas_call(
        functools.partial(finish_kernel, per_dev),
        out_shape=(
            jax.ShapeDtypeStruct((LEAVES // LANES, LANES), F32),
            jax.ShapeDtypeStruct(leaves.shape, F32),
            jax.ShapeDtypeStruct(out, F32),
        ),
        in_specs=[vmem()] * (3 + len(arrived)),
        out_specs=(vmem(), vmem(), vmem()),
        compiler_params=pltpu.CompilerParams(vmem_limit_bytes=VMEM_LIMIT),
        name="finish",
    )(leaves, kept, sums, *arrived)


def add_up(parts):
    while len(parts) > 1:
        parts = [parts[k] + parts[k + 1] for k in range(0, len(parts), 2)]
    return parts[0]


def local(scores, labels, leaves, bins, lengths, owner):
    query_count = lax.axis_size("query")
    feat_count = lax.axis_size("feat")
    count = query_count * feat_count
    place = lax.axis_index("query").astype(jnp.int32) * feat_count + lax.axis_index("feat").astype(jnp.int32)
    docs = scores.shape[0]
    own = docs // LANES
    features = owner.shape[0]
    per_dev = features // count
    unit = 3 * per_dev
    axes = ("query", "feat")
    feat_masks = [1 << b for b in range(feat_count.bit_length() - 1)]
    query_masks = [feat_count << b for b in range(query_count.bit_length() - 1)]

    def swap(value, mask):
        return lax.ppermute(value, axes, [(p, p ^ mask) for p in range(count)])

    pos = place.reshape(1)
    leaf_rows = leaves.reshape(own, LANES)
    own_scores = scores.reshape(own, LANES)
    score_parts = [own_scores]
    def inner_partner(p):
        z = p % feat_count
        if z in (0, feat_count - 1):
            return p ^ query_masks[0]
        return p + 1 if z % 2 else p - 1

    score_parts.append(lax.ppermute(own_scores, axes, [(p, inner_partner(p)) for p in range(count)]))
    score_parts.append(swap(own_scores, 1))
    masks = feat_masks + query_masks[:0:-1] + query_masks[:1]
    score_parts[0], leaf_rows, qid, worth, inverse, perm, bounds = prepare(
        feat_count, masks, lengths, pos, labels.reshape(-1, LANES), owner.reshape(-1, LANES), own_scores, leaf_rows)
    lambdas, near_lambdas = pair_terms(feat_count, bounds, pos, score_parts, worth, qid, inverse)
    bins_t, tiles, sums = leaf_terms(perm, bins, leaf_rows, near_lambdas)

    def part(tiles, low, high, *tail):
        if per_dev == GROUP:
            return histogram_part(low, high - low, tiles, bins_t, *tail)
        groups = high - low
        wide = histogram_part(low, groups, tiles, bins_t)
        wide = wide.reshape(groups, 3, HIGH, GROUP // per_dev, per_dev, LOW).transpose(0, 3, 1, 4, 2, 5)
        return jnp.concatenate([wide.reshape(groups * GROUP // per_dev * unit, BINS), *tail], axis=0)

    def join(block, total):
        return jnp.concatenate([block, total], axis=0)

    eighth = features // GROUP // 8
    edge = count // 8 * unit
    arrived = swap(part(tiles, 7 * eighth, 8 * eighth, sums), query_masks[0])
    block = part(tiles, 3 * eighth, 4 * eighth) + arrived[:edge]
    sums = sums + arrived[edge:]
    message, tiles = lax.optimization_barrier((join(block, sums), tiles))
    crossed_far = swap(message, query_masks[1])
    arrived = swap(part(tiles, 5 * eighth, 7 * eighth), query_masks[0])
    both = part(tiles, eighth, 3 * eighth) + arrived
    sums = sums + crossed_far[edge:]
    message, rest, tiles = lax.optimization_barrier(
        (join(both[:edge] + crossed_far[:edge], sums), join(both[edge:], sums), tiles))
    turned = swap(message, query_masks[2])
    crossed_near = swap(rest, query_masks[1])
    arrived = swap(part(tiles, 4 * eighth, 5 * eighth), query_masks[0])
    kept = part(tiles, 0, eighth) + arrived + crossed_near[:edge] + turned[:edge]
    sums = sums + turned[edge:]
    for mask in query_masks[3:]:
        edge = edge // 2
        arrived = swap(join(kept[edge:], sums), mask)
        kept = kept[:edge] + arrived[:edge]
        sums = sums + arrived[edge:]
    arrived = [swap(join(kept[m * unit:(m + 1) * unit], sums), m) for m in range(1, feat_count)]
    arrived[:2] = arrived[1::-1]
    values, step, histograms = finish(per_dev, leaf_rows, kept[:unit], sums, arrived)
    return lambdas, values.reshape(LEAVES), step.reshape(docs), histograms.reshape(3, per_dev * BINS)


def solution(mesh):
    in_specs = (
        P(("query", "feat")),
        P("query"),
        P(("query", "feat")),
        P(("query", "feat"), None),
        P("query", None),
        P(),
    )
    out_specs = (P(None, ("query", "feat")), P(), P(("query", "feat")), P(None, ("query", "feat")))
    return jax.shard_map(local, mesh=mesh, in_specs=in_specs, out_specs=out_specs, check_vma=False)
```

```python
import functools

import jax
import jax.numpy as jnp
from jax import lax
from jax.experimental import pallas as pl
from jax.experimental.pallas import tpu as pltpu
from jax.sharding import PartitionSpec as P

BINS = 256
LEAVES = 1024
LANES = 128
GRADES = 4
LOW = 32
HIGH = BINS // LOW
GROUP = 8
CHUNK = 64
MAX_LEN = 1024

lasso_penalty = 1.0
ridge_penalty = 1.0
shrinkage = 0.1

VMEM_LIMIT = 48 * 1024 * 1024
F32 = jnp.float32
BF16 = jnp.bfloat16
NT = (((1,), (1,)), ((), ()))


def iota(shape, axis):
    return lax.broadcasted_iota(jnp.int32, shape, axis)


def vmem():
    return pl.BlockSpec(memory_space=pltpu.VMEM)


def smem():
    return pl.BlockSpec(memory_space=pltpu.SMEM)


def prepare_kernel(feat_count, masks, len_ref, pos_ref, lab_ref, owner_ref, score_ref, leaf_ref,
                   kept_ref, leaf_out, qid_ref, worth_ref, inv_ref, perm_ref, bounds_ref):
    kept_ref[...] = score_ref[...]
    leaf_out[...] = leaf_ref[...]
    queries = len_ref.shape[1]
    rows = lab_ref.shape[0]
    own = rows // feat_count
    spot = iota((rows, LANES), 0) * LANES + iota((rows, LANES), 1)
    qid = jnp.zeros((rows, LANES), F32)
    begin = jnp.zeros((queries, LANES), jnp.int32)
    finish = jnp.zeros((queries, LANES), jnp.int32)
    which = iota((queries, LANES), 0)
    group = iota((1, LANES), 1) * LANES
    low = jnp.zeros((1, LANES), jnp.int32)
    high = first_end = jnp.full((1, LANES), rows * LANES, jnp.int32)
    start = jnp.int32(0)
    for q in range(queries):
        end = start + len_ref[0, q]
        qid = qid + jnp.where(spot >= end, 1.0, 0.0)
        begin = jnp.where(which == q, start, begin)
        finish = jnp.where(which == q, end, finish)

        low = low + jnp.where(end <= group, len_ref[0, q], 0)
        high = jnp.minimum(high, jnp.where(end >= group + LANES, end, rows * LANES))
        first_end = jnp.minimum(first_end, jnp.where(end > group, end, rows * LANES))
        start = end
    bounds_ref[...] = jnp.concatenate([low, high, first_end, low, low, low, low, low], axis=0)
    qid_ref[...] = qid
    worth_ref[...] = jnp.left_shift(1, lab_ref[...]).astype(F32)

    counts = [jnp.zeros((queries, LANES), F32) for _ in range(GRADES)]
    lane = iota((queries, LANES), 1)
    for r in range(rows):
        at = lane + r * LANES
        inside = (at >= begin) & (at < finish)
        grade = jnp.where(inside, jnp.broadcast_to(lab_ref[r:r + 1, :], (queries, LANES)), 0)
        for g in range(GRADES):
            counts[g] = counts[g] + jnp.where(grade > g, 1.0, 0.0)
    position = iota((queries, MAX_LEN), 1).astype(F32)
    gain = jnp.zeros((queries, MAX_LEN), F32)
    for g in range(GRADES):
        held = jnp.sum(counts[g], axis=1, keepdims=True)
        gain = gain + jnp.where(position < held, float(2 ** g), 0.0)
    level = 1.0 / jnp.log2(2.0 + position[0:1, :])
    ideal = jnp.sum(gain * level, axis=1, keepdims=True)
    usable = ideal > 0.5
    inverse = jnp.where(usable, 1.0 / jnp.where(usable, ideal, 1.0), 0.0)
    first = pos_ref[0] % feat_count * own
    for t in range(own):
        at = lane + (first + t) * LANES
        inside = (at >= begin) & (at < finish)
        inv_ref[0:1, t * LANES:(t + 1) * LANES] = jnp.sum(jnp.where(inside, inverse, 0.0), axis=0, keepdims=True)

    features = perm_ref.shape[0]
    per_dev = features >> len(masks)
    owner = jnp.concatenate([owner_ref[k:k + 1, :] for k in range(features // LANES)], axis=1)
    square = (features, features)
    down, across = iota(square, 0), iota(square, 1)
    index = iota((features, 1), 0) // per_dev
    target = jnp.zeros((features, 1), jnp.int32)
    for b, mask in enumerate(masks):
        target = target + ((index >> b) & 1) * mask
    target = (target ^ pos_ref[0]) * per_dev + iota((features, 1), 0) % per_dev
    pick = jnp.where(target == across, 1.0, 0.0).astype(BF16)
    holds = jnp.where(jnp.broadcast_to(owner, square) == down, 1.0, 0.0).astype(BF16)
    perm_ref[...] = lax.dot_general(pick, holds, NT, preferred_element_type=F32).astype(BF16)


def prepare(feat_count, masks, lengths, pos, labels, owner, scores, leaves):
    rows = labels.shape[0]
    features = owner.shape[0] * LANES
    return pl.pallas_call(
        functools.partial(prepare_kernel, feat_count, masks),
        out_shape=(
            jax.ShapeDtypeStruct(scores.shape, F32),
            jax.ShapeDtypeStruct(leaves.shape, jnp.int32),
            jax.ShapeDtypeStruct((rows, LANES), F32),
            jax.ShapeDtypeStruct((rows, LANES), F32),
            jax.ShapeDtypeStruct((1, rows // feat_count * LANES), F32),
            jax.ShapeDtypeStruct((features, features), BF16),
            jax.ShapeDtypeStruct((8, LANES), jnp.int32),
        ),
        in_specs=[smem(), smem(), vmem(), vmem(), vmem(), vmem()],
        out_specs=(vmem(),) * 7,
        compiler_params=pltpu.CompilerParams(vmem_limit_bytes=VMEM_LIMIT),
        cost_estimate=pl.CostEstimate(flops=2_000_000_000, bytes_accessed=300_000, transcendentals=20_000),
        name="prepare",
    )(lengths, pos, labels, owner, scores, leaves)


def split_terms(value, terms):
    parts = []
    rest = value
    for _ in range(terms):
        part = rest.astype(BF16)
        parts.append(part)
        rest = rest - part.astype(F32)
    return parts


def pairs_kernel(feat_count, bounds_ref, pos_ref, *refs):
    scores = refs[:-16]
    (worth_ref, qid_ref, inv_ref, lam_ref, near_ref,
     s_row, a_row, d_row, turn, s_col, a_col, w_col, q_col, d_col, grad, curv) = refs[-16:]
    rows = worth_ref.shape[0]
    own = rows // feat_count
    docs = own * LANES
    me = pos_ref[0] % feat_count
    s_row[...] = jnp.zeros(s_row.shape, F32)
    near = [me, ((me + 1) ^ 1) - 1, me ^ 1]
    for where, ref in zip(near, scores):
        @pl.when((where >= 0) & (where < feat_count))
        def _(where=where, ref=ref):
            s_row[pl.ds(pl.multiple_of(where * own, own), own), :] = ref[...]
    a_row[...] = jnp.exp(s_row[...])
    d_row[...] = jnp.zeros(d_row.shape, F32)
    first = me * own
    window_low = bounds_ref[0, first] // (2 * LANES) * 2
    window_high = (bounds_ref[1, first + own - 1] + 2 * LANES - 1) // (2 * LANES) * 2
    stride = 4

    def widen(pairs):
        lines = jnp.concatenate([source[...] for source, _ in pairs], axis=0)
        if lines.shape[0] % LANES:
            lines = jnp.concatenate([lines, jnp.zeros((LANES - lines.shape[0] % LANES, LANES), F32)], axis=0)
        for k in range(lines.shape[0] // LANES):
            turn[:, k * LANES:(k + 1) * LANES] = jnp.transpose(lines[k * LANES:(k + 1) * LANES])
        for r in range(0, rows, stride):
            @pl.when((r + stride > window_low) & (r < window_high))
            def _(r=r):
                for k, (_, col) in enumerate(pairs):
                    for m in range(r, r + stride):
                        at = k * rows + m
                        col[m * LANES:(m + 1) * LANES, :] = jnp.broadcast_to(turn[:, at:at + 1], (LANES, LANES))

    widen([(s_row, s_col), (qid_ref, q_col), (a_row, a_col), (worth_ref, w_col)])

    def rows_of(ref, r):
        return [jnp.broadcast_to(ref[pl.ds(r + g, 1), :], (8, LANES)) for g in range(2)]

    per = LANES // CHUNK

    def spans(r):
        start, end = bounds_ref[0, r], bounds_ref[1, r + 1]
        low = jnp.maximum(start // CHUNK, per * window_low)
        high = jnp.minimum((end + CHUNK - 1) // CHUNK, per * window_high)
        single = bounds_ref[2, r] >= (r + 2) * LANES
        inner_low = jnp.maximum((start + LANES - 1) // LANES, window_low)
        inner_high = jnp.minimum(end // LANES, window_high)
        return low, high, single, inner_low, inner_high

    def rank_groups(k, carry):
        r = window_low + 2 * k
        score = rows_of(s_row, r)
        query = rows_of(qid_ref, r)

        def gather(c, acc, masked, test):
            size = CHUNK if masked else LANES
            base = pl.multiple_of(c * size, size)
            acc = list(acc)
            for u in range(size // 8):
                other = s_col[pl.ds(base + 8 * u, 8), :]
                for g in range(2):
                    hit = test(other, g, u)
                    if masked:
                        hit = hit & (q_col[pl.ds(base + 8 * u, 8), :] == query[g])
                    k = 4 * g + u % 4
                    acc[k] = acc[k] + jnp.where(hit, 1.0, 0.0)
            return tuple(acc)

        def ahead(other, g, u):
            return other >= score[g]

        def behind(other, g, u):
            return other > score[g]

        def within(mine, offset):
            def test(other, g, u):
                if g != mine:
                    return ahead(other, g, u) if mine < g else behind(other, g, u)
                earlier = iota((8, LANES), 0) + (offset + 8 * u) < iota((8, LANES), 1)
                return (other > score[g]) | ((other == score[g]) & earlier)
            return test

        def twice(low, high, test, acc):
            twos = (high - low) // 2
            acc = lax.fori_loop(0, twos, lambda k, acc: gather(
                low + 2 * k + 1, gather(low + 2 * k, acc, False, test), False, test), acc)
            return lax.fori_loop(low + 2 * twos, high, lambda c, acc: gather(c, acc, False, test), acc)

        acc = tuple(jnp.zeros((8, LANES), F32) for _ in range(8))
        low, high, single, inner_low, inner_high = spans(r)
        inner_low = jnp.where(single, inner_low, r)
        after = jnp.where(single, inner_high, r + 2)
        acc = lax.fori_loop(low, per * inner_low, lambda c, acc: gather(c, acc, True, ahead), acc)
        acc = twice(inner_low, r, ahead, acc)
        acc = twice(r + 2, after, behind, acc)
        acc = lax.fori_loop(per * after, high, lambda c, acc: gather(c, acc, True, behind), acc)
        for c in range(2 * per):
            acc = gather(per * r + c, acc, True, within(c // per, c % per * CHUNK))
        for g in range(2):
            total = (acc[4 * g] + acc[4 * g + 1]) + (acc[4 * g + 2] + acc[4 * g + 3])
            d_row[pl.ds(r + g, 1), :] = jnp.sum(total, axis=0, keepdims=True)
        return carry

    lax.fori_loop(0, (window_high - window_low) // 2, rank_groups, 0)
    d_row[...] = 1.0 / jnp.log2(2.0 + d_row[...])
    widen([(d_row, d_col)])

    def pair_groups(t, carry):
        r = first + 2 * t
        a_i, w_i, d_i, query = [rows_of(ref, r) for ref in (a_row, worth_ref, d_row, qid_ref)]

        def columns(masked):
            def step(c, acc):
                size = CHUNK if masked else LANES
                base = pl.multiple_of(c * size, size)
                acc = list(acc)
                for u in range(size // 8):
                    at = pl.ds(base + 8 * u, 8)
                    a_j, w_j, d_j = a_col[at, :], w_col[at, :], d_col[at, :]
                    for g in range(2):
                        recip = pl.reciprocal(a_i[g] + a_j, approx=True)
                        lift = w_i[g] - w_j
                        weight = jnp.abs(d_i[g] - d_j) * recip
                        if masked:
                            weight = jnp.where(q_col[at, :] == query[g], weight, 0.0)
                        weight = weight * lift
                        k = 4 * g + u % 2
                        acc[k] = acc[k] + weight * jnp.where(lift > 0.0, a_j, a_i[g])
                        acc[k + 2] = acc[k + 2] + jnp.abs(weight) * (recip * a_j)
                return tuple(acc)
            return step

        def twice(low, high, step, acc):
            twos = (high - low) // 2
            acc = lax.fori_loop(0, twos, lambda k, acc: step(low + 2 * k + 1, step(low + 2 * k, acc)), acc)
            return lax.fori_loop(low + 2 * twos, high, step, acc)

        acc = tuple(jnp.zeros((8, LANES), F32) for _ in range(8))
        low, high, single, inner_low, inner_high = spans(r)
        acc = lax.fori_loop(low, jnp.where(single, per * inner_low, low), columns(True), acc)
        acc = twice(inner_low, jnp.where(single, inner_high, inner_low), columns(False), acc)
        acc = twice(jnp.where(single, per * inner_high, low), high, columns(True), acc)
        for g in range(2):
            at = pl.ds(2 * t + g, 1)
            grad[at, :] = -jnp.sum(acc[4 * g] + acc[4 * g + 1], axis=0, keepdims=True)
            curv[at, :] = a_i[g][0:1, :] * jnp.sum(acc[4 * g + 2] + acc[4 * g + 3], axis=0, keepdims=True)
        return carry

    lax.fori_loop(0, own // 2, pair_groups, 0)
    inverse = inv_ref[...]
    terms = [inverse * jnp.concatenate([ref[t:t + 1, :] for t in range(own)], axis=1) for ref in (grad, curv)]
    for c in range(2):
        lam_ref[c:c + 1, :] = terms[c]
        near_ref[c:c + 1, :] = terms[c]


def pair_terms(feat_count, bounds, pos, scores, worth, qid, inverse):
    rows = worth.shape[0]
    docs = inverse.shape[1]
    row = pltpu.VMEM((rows, LANES), F32)
    turn = pltpu.VMEM((LANES, 4 * rows), F32)
    col = pltpu.VMEM((rows * LANES, LANES), F32)
    mine = pltpu.VMEM((docs // LANES, LANES), F32)
    return pl.pallas_call(
        functools.partial(pairs_kernel, feat_count),
        out_shape=(jax.ShapeDtypeStruct((2, docs), F32), jax.ShapeDtypeStruct((2, docs), F32)),
        in_specs=[smem(), smem()] + [vmem()] * (len(scores) + 3),
        out_specs=(vmem(), vmem()),
        scratch_shapes=[row, row, row, turn, col, col, col, col, col, mine, mine],
        compiler_params=pltpu.CompilerParams(vmem_limit_bytes=VMEM_LIMIT),
        cost_estimate=pl.CostEstimate(flops=9_000_000_000, bytes_accessed=200_000, transcendentals=2_000_000),
        name="pair_terms",
    )(bounds, pos, *scores, worth, qid, inverse)


def leaf_kernel(perm_ref, bins_ref, leaf_ref, lam_ref, bins_t_ref, tile_ref, sums_ref):
    bins = bins_ref[...].astype(F32).astype(BF16)
    bins_t_ref[...] = lax.dot_general(perm_ref[...], bins, NT, preferred_element_type=F32)
    own = leaf_ref.shape[0]
    docs = own * LANES
    leaf = jnp.concatenate([leaf_ref[t:t + 1, :] for t in range(own)], axis=1)
    highs = LEAVES // LANES
    top = jnp.broadcast_to(leaf // LANES, (highs, docs)) == iota((highs, docs), 0)
    spots = jnp.where(jnp.broadcast_to(leaf % LANES, (LANES, docs)) == iota((LANES, docs), 0), 1.0, 0.0).astype(BF16)
    pieces, tiles = [], []
    for c in range(2):
        for k, part in enumerate(split_terms(lam_ref[c:c + 1, :], 3)):
            wide = jnp.broadcast_to(part.astype(F32), (highs, docs))
            pieces.append(jnp.where(top, wide, 0.0))
            if k < 2:
                tiles.append(wide)
    tile_ref[...] = jnp.concatenate(tiles, axis=0).astype(BF16)
    stacked = jnp.concatenate(pieces, axis=0).astype(BF16)
    sums = lax.dot_general(stacked, spots, NT, preferred_element_type=F32)
    for c in range(2):
        base = c * 3 * highs
        sums_ref[:, c * LANES:(c + 1) * LANES] = (
            sums[base:base + highs] + (sums[base + highs:base + 2 * highs] + sums[base + 2 * highs:base + 3 * highs])
        )


def leaf_terms(perm, bins, leaves, lambdas):
    docs, features = bins.shape
    return pl.pallas_call(
        leaf_kernel,
        out_shape=(
            jax.ShapeDtypeStruct((features, docs), F32),
            jax.ShapeDtypeStruct((4 * HIGH, docs), BF16),
            jax.ShapeDtypeStruct((LEAVES // LANES, 2 * LANES), F32),
        ),
        in_specs=[vmem()] * 4,
        out_specs=(vmem(), vmem(), vmem()),
        compiler_params=pltpu.CompilerParams(vmem_limit_bytes=VMEM_LIMIT),
        cost_estimate=pl.CostEstimate(flops=200_000_000, bytes_accessed=3_000_000, transcendentals=0),
        name="leaf_terms",
    )(perm, bins, leaves, lambdas)


def histogram_kernel(first, groups, tile_ref, bins_ref, *refs):
    out_ref = refs[-1]
    docs = tile_ref.shape[1]
    depth = docs
    rows = 16
    row = iota((rows, depth), 0)
    low_level = [(row + rows * k).astype(F32).astype(BF16) for k in range(LOW // rows)]
    high_level = (row % HIGH).astype(F32).astype(BF16)
    upper = jnp.where(row < HIGH, 1.0, 0.0).astype(BF16) > 0
    zero = jnp.zeros((rows, depth), BF16)
    one = jnp.ones((rows, depth), BF16)
    lane_owner = iota((1, GROUP * LOW), 1) // LOW

    def one_group(g, carry):
        base = pl.multiple_of((first + g) * GROUP, GROUP)
        acc = None
        for k in range(docs // depth):
            span = slice(k * depth, (k + 1) * depth)
            code = bins_ref[pl.ds(base, GROUP), span]
            high = jnp.floor(code * (1.0 / LOW))
            low = code - high * LOW
            left, right, count = [], [], []
            wide = []
            for f in range(GROUP):
                high_f = jnp.broadcast_to(high[f:f + 1, :], (rows, depth))
                low_f = jnp.broadcast_to(low[f:f + 1, :], (rows, depth)).astype(BF16)
                high_f = high_f.astype(BF16)
                wide.append(high_f)
                match = high_f == high_level
                for c in range(2):
                    left.append(jnp.where(match, tile_ref[c * rows:(c + 1) * rows, span], zero))
                for level in low_level:
                    right.append(jnp.where(low_f == level, one, zero))
            for f in range(0, GROUP, 2):
                both = jnp.where(upper, wide[f], wide[f + 1])
                count.append(jnp.where(both == high_level, one, zero))
            part = lax.dot_general(
                jnp.concatenate(left + count, axis=0), jnp.concatenate(right, axis=0), NT,
                preferred_element_type=F32,
            )
            acc = part if acc is None else acc + part
        stats = jnp.zeros((2 * rows, GROUP * LOW), F32)
        counts = jnp.zeros((HIGH, GROUP * LOW), F32)
        for f in range(GROUP):
            mine = lane_owner == f
            stats = jnp.where(mine, acc[f * 2 * rows:(f + 1) * 2 * rows], stats)
            at = GROUP * 2 * rows + f * HIGH
            counts = jnp.where(mine, acc[at:at + HIGH], counts)
        out_ref[pl.ds(pl.multiple_of(g * 3 * HIGH, 3 * HIGH), 3 * HIGH), :] = jnp.concatenate(
            [stats[0:HIGH] + stats[HIGH:2 * HIGH], stats[2 * HIGH:3 * HIGH] + stats[3 * HIGH:4 * HIGH], counts], axis=0)
        return carry

    if len(refs) > 1:
        out_ref[groups * 3 * HIGH:, :] = refs[0][...]
    lax.fori_loop(0, groups, one_group, 0, unroll=min(groups, 8))


def histogram_part(first, groups, tiles, bins_t, *tail):
    rows = groups * 3 * HIGH + sum(piece.shape[0] for piece in tail)
    return pl.pallas_call(
        functools.partial(histogram_kernel, first, groups),
        out_shape=jax.ShapeDtypeStruct((rows, GROUP * LOW), F32),
        in_specs=[vmem()] * (2 + len(tail)),
        out_specs=vmem(),
        compiler_params=pltpu.CompilerParams(vmem_limit_bytes=VMEM_LIMIT),
        cost_estimate=pl.CostEstimate(flops=groups * 1_000_000, bytes_accessed=groups * 1_000, transcendentals=0),
        name="histogram_part",
    )(tiles, bins_t, *tail)


def finish_kernel(per_dev, leaf_ref, kept_ref, sums_ref, *refs):
    arrived = list(refs[1::-1]) + list(refs[2:-3])
    value_ref, step_ref, hist_ref = refs[-3:]
    unit = kept_ref.shape[0]
    totals = add_up([sums_ref[...]] + [ref[unit:, :] for ref in arrived])
    highs = LEAVES // LANES
    grad, curv = totals[:, :LANES], totals[:, LANES:]
    shrunk = jnp.maximum(jnp.abs(grad) - lasso_penalty, 0.0)
    values = jnp.where(grad > 0.0, -shrunk, shrunk) / (curv + ridge_penalty)
    value_ref[...] = values
    leaf = leaf_ref[...]
    top, spot = leaf // LANES, leaf % LANES
    step = jnp.zeros(leaf.shape, F32)
    for h in range(highs):
        row = jnp.broadcast_to(values[h:h + 1, :], leaf.shape)
        step = jnp.where(top == h, jnp.take_along_axis(row, spot, axis=1), step)
    step_ref[...] = shrinkage * step
    hist = add_up([kept_ref[...]] + [ref[:unit, :] for ref in arrived])
    if per_dev == GROUP:
        shape = hist.shape
        line, place = iota(shape, 0), iota(shape, 1) // LOW
        step = 1
        while step < GROUP:
            down, across = (line // step) % 2, (place // step) % 2
            shift = step * LOW
            ahead = pltpu.roll(pltpu.roll(hist, shape[0] - step, 0), shift, 1)
            behind = pltpu.roll(pltpu.roll(hist, step, 0), shape[1] - shift, 1)
            hist = jnp.where(down == across, hist, jnp.where(across == 1, ahead, behind))
            step *= 2
        for c in range(3):
            for f in range(GROUP):
                hist_ref[c:c + 1, f * BINS:(f + 1) * BINS] = hist[c * HIGH + f:c * HIGH + f + 1, :]
    else:
        hist_ref[...] = hist


def finish(per_dev, leaves, kept, sums, arrived):
    out = (3, per_dev * BINS) if per_dev == GROUP else kept.shape
    return pl.pallas_call(
        functools.partial(finish_kernel, per_dev),
        out_shape=(
            jax.ShapeDtypeStruct((LEAVES // LANES, LANES), F32),
            jax.ShapeDtypeStruct(leaves.shape, F32),
            jax.ShapeDtypeStruct(out, F32),
        ),
        in_specs=[vmem()] * (3 + len(arrived)),
        out_specs=(vmem(), vmem(), vmem()),
        compiler_params=pltpu.CompilerParams(vmem_limit_bytes=VMEM_LIMIT),
        name="finish",
    )(leaves, kept, sums, *arrived)


def add_up(parts):
    while len(parts) > 1:
        parts = [parts[k] + parts[k + 1] for k in range(0, len(parts), 2)]
    return parts[0]


def local(scores, labels, leaves, bins, lengths, owner):
    query_count = lax.axis_size("query")
    feat_count = lax.axis_size("feat")
    count = query_count * feat_count
    place = lax.axis_index("query").astype(jnp.int32) * feat_count + lax.axis_index("feat").astype(jnp.int32)
    docs = scores.shape[0]
    own = docs // LANES
    features = owner.shape[0]
    per_dev = features // count
    unit = 3 * per_dev
    axes = ("query", "feat")
    feat_masks = [1 << b for b in range(feat_count.bit_length() - 1)]
    query_masks = [feat_count << b for b in range(query_count.bit_length() - 1)]

    def swap(value, mask):
        return lax.ppermute(value, axes, [(p, p ^ mask) for p in range(count)])

    pos = place.reshape(1)
    leaf_rows = leaves.reshape(own, LANES)
    own_scores = scores.reshape(own, LANES)
    score_parts = [own_scores]
    def inner_partner(p):
        z = p % feat_count
        if z in (0, feat_count - 1):
            return p ^ query_masks[0]
        return p + 1 if z % 2 else p - 1

    score_parts.append(lax.ppermute(own_scores, axes, [(p, inner_partner(p)) for p in range(count)]))
    score_parts.append(swap(own_scores, 1))
    masks = feat_masks + query_masks[:0:-1] + query_masks[:1]
    score_parts[0], leaf_rows, qid, worth, inverse, perm, bounds = prepare(
        feat_count, masks, lengths, pos, labels.reshape(-1, LANES), owner.reshape(-1, LANES), own_scores, leaf_rows)
    lambdas, near_lambdas = pair_terms(feat_count, bounds, pos, score_parts, worth, qid, inverse)
    bins_t, tiles, sums = leaf_terms(perm, bins, leaf_rows, near_lambdas)

    def part(tiles, low, high, *tail):
        if per_dev == GROUP:
            return histogram_part(low, high - low, tiles, bins_t, *tail)
        groups = high - low
        wide = histogram_part(low, groups, tiles, bins_t)
        wide = wide.reshape(groups, 3, HIGH, GROUP // per_dev, per_dev, LOW).transpose(0, 3, 1, 4, 2, 5)
        return jnp.concatenate([wide.reshape(groups * GROUP // per_dev * unit, BINS), *tail], axis=0)

    def join(block, total):
        return jnp.concatenate([block, total], axis=0)

    eighth = features // GROUP // 8
    edge = count // 8 * unit
    arrived = swap(part(tiles, 7 * eighth, 8 * eighth, sums), query_masks[0])
    block = part(tiles, 3 * eighth, 4 * eighth) + arrived[:edge]
    sums = sums + arrived[edge:]
    message, tiles = lax.optimization_barrier((join(block, sums), tiles))
    crossed_far = swap(message, query_masks[1])
    arrived = swap(part(tiles, 5 * eighth, 7 * eighth), query_masks[0])
    both = part(tiles, eighth, 3 * eighth) + arrived
    sums = sums + crossed_far[edge:]
    message, rest, tiles = lax.optimization_barrier(
        (join(both[:edge] + crossed_far[:edge], sums), join(both[edge:], sums), tiles))
    turned = swap(message, query_masks[2])
    crossed_near = swap(rest, query_masks[1])
    arrived = swap(part(tiles, 4 * eighth, 5 * eighth), query_masks[0])
    kept = part(tiles, 0, eighth) + arrived + crossed_near[:edge] + turned[:edge]
    sums = sums + turned[edge:]
    for mask in query_masks[3:]:
        edge = edge // 2
        arrived = swap(join(kept[edge:], sums), mask)
        kept = kept[:edge] + arrived[:edge]
        sums = sums + arrived[edge:]
    arrived = [swap(join(kept[m * unit:(m + 1) * unit], sums), m) for m in range(1, feat_count)]
    arrived[:2] = arrived[1::-1]
    values, step, histograms = finish(per_dev, leaf_rows, kept[:unit], sums, arrived)
    return lambdas, values.reshape(LEAVES), step.reshape(docs), histograms.reshape(3, per_dev * BINS)


def solution(mesh):
    in_specs = (
        P(("query", "feat")),
        P("query"),
        P(("query", "feat")),
        P(("query", "feat"), None),
        P("query", None),
        P(),
    )
    out_specs = (P(None, ("query", "feat")), P(), P(("query", "feat")), P(None, ("query", "feat")))
    return jax.shard_map(local, mesh=mesh, in_specs=in_specs, out_specs=out_specs, check_vma=False)
```

```python
import functools

import jax
import jax.numpy as jnp
from jax import lax
from jax.experimental import pallas as pl
from jax.experimental.pallas import tpu as pltpu
from jax.sharding import PartitionSpec as P

BINS = 256
LEAVES = 1024
LANES = 128
GRADES = 4
LOW = 32
HIGH = BINS // LOW
GROUP = 8
CHUNK = 64
MAX_LEN = 1024

lasso_penalty = 1.0
ridge_penalty = 1.0
shrinkage = 0.1

VMEM_LIMIT = 48 * 1024 * 1024
F32 = jnp.float32
BF16 = jnp.bfloat16
NT = (((1,), (1,)), ((), ()))


def iota(shape, axis):
    return lax.broadcasted_iota(jnp.int32, shape, axis)


def vmem():
    return pl.BlockSpec(memory_space=pltpu.VMEM)


def smem():
    return pl.BlockSpec(memory_space=pltpu.SMEM)


def prepare_kernel(feat_count, masks, len_ref, pos_ref, lab_ref, owner_ref, score_ref, leaf_ref,
                   kept_ref, leaf_out, qid_ref, worth_ref, inv_ref, perm_ref, bounds_ref):
    kept_ref[...] = score_ref[...]
    leaf_out[...] = leaf_ref[...]
    queries = len_ref.shape[1]
    rows = lab_ref.shape[0]
    own = rows // feat_count
    spot = iota((rows, LANES), 0) * LANES + iota((rows, LANES), 1)
    qid = jnp.zeros((rows, LANES), F32)
    begin = jnp.zeros((queries, LANES), jnp.int32)
    finish = jnp.zeros((queries, LANES), jnp.int32)
    which = iota((queries, LANES), 0)
    group = iota((1, LANES), 1) * LANES
    low = jnp.zeros((1, LANES), jnp.int32)
    high = first_end = jnp.full((1, LANES), rows * LANES, jnp.int32)
    start = jnp.int32(0)
    for q in range(queries):
        end = start + len_ref[0, q]
        qid = qid + jnp.where(spot >= end, 1.0, 0.0)
        begin = jnp.where(which == q, start, begin)
        finish = jnp.where(which == q, end, finish)

        low = low + jnp.where(end <= group, len_ref[0, q], 0)
        high = jnp.minimum(high, jnp.where(end >= group + LANES, end, rows * LANES))
        first_end = jnp.minimum(first_end, jnp.where(end > group, end, rows * LANES))
        start = end
    bounds_ref[...] = jnp.concatenate([low, high, first_end, low, low, low, low, low], axis=0)
    qid_ref[...] = qid
    worth_ref[...] = jnp.left_shift(1, lab_ref[...]).astype(F32)

    counts = [jnp.zeros((queries, LANES), F32) for _ in range(GRADES)]
    lane = iota((queries, LANES), 1)
    for r in range(rows):
        at = lane + r * LANES
        inside = (at >= begin) & (at < finish)
        grade = jnp.where(inside, jnp.broadcast_to(lab_ref[r:r + 1, :], (queries, LANES)), 0)
        for g in range(GRADES):
            counts[g] = counts[g] + jnp.where(grade > g, 1.0, 0.0)
    position = iota((queries, MAX_LEN), 1).astype(F32)
    gain = jnp.zeros((queries, MAX_LEN), F32)
    for g in range(GRADES):
        held = jnp.sum(counts[g], axis=1, keepdims=True)
        gain = gain + jnp.where(position < held, float(2 ** g), 0.0)
    level = 1.0 / jnp.log2(2.0 + position[0:1, :])
    ideal = jnp.sum(gain * level, axis=1, keepdims=True)
    usable = ideal > 0.5
    inverse = jnp.where(usable, 1.0 / jnp.where(usable, ideal, 1.0), 0.0)
    first = pos_ref[0] % feat_count * own
    for t in range(own):
        at = lane + (first + t) * LANES
        inside = (at >= begin) & (at < finish)
        inv_ref[0:1, t * LANES:(t + 1) * LANES] = jnp.sum(jnp.where(inside, inverse, 0.0), axis=0, keepdims=True)

    features = perm_ref.shape[0]
    per_dev = features >> len(masks)
    owner = jnp.concatenate([owner_ref[k:k + 1, :] for k in range(features // LANES)], axis=1)
    square = (features, features)
    down, across = iota(square, 0), iota(square, 1)
    index = iota((features, 1), 0) // per_dev
    target = jnp.zeros((features, 1), jnp.int32)
    for b, mask in enumerate(masks):
        target = target + ((index >> b) & 1) * mask
    target = (target ^ pos_ref[0]) * per_dev + iota((features, 1), 0) % per_dev
    pick = jnp.where(target == across, 1.0, 0.0).astype(BF16)
    holds = jnp.where(jnp.broadcast_to(owner, square) == down, 1.0, 0.0).astype(BF16)
    perm_ref[...] = lax.dot_general(pick, holds, NT, preferred_element_type=F32).astype(BF16)


def prepare(feat_count, masks, lengths, pos, labels, owner, scores, leaves):
    rows = labels.shape[0]
    features = owner.shape[0] * LANES
    return pl.pallas_call(
        functools.partial(prepare_kernel, feat_count, masks),
        out_shape=(
            jax.ShapeDtypeStruct(scores.shape, F32),
            jax.ShapeDtypeStruct(leaves.shape, jnp.int32),
            jax.ShapeDtypeStruct((rows, LANES), F32),
            jax.ShapeDtypeStruct((rows, LANES), F32),
            jax.ShapeDtypeStruct((1, rows // feat_count * LANES), F32),
            jax.ShapeDtypeStruct((features, features), BF16),
            jax.ShapeDtypeStruct((8, LANES), jnp.int32),
        ),
        in_specs=[smem(), smem(), vmem(), vmem(), vmem(), vmem()],
        out_specs=(vmem(),) * 7,
        compiler_params=pltpu.CompilerParams(vmem_limit_bytes=VMEM_LIMIT),
        cost_estimate=pl.CostEstimate(flops=2_000_000_000, bytes_accessed=300_000, transcendentals=20_000),
        name="prepare",
    )(lengths, pos, labels, owner, scores, leaves)


def split_terms(value, terms):
    parts = []
    rest = value
    for _ in range(terms):
        part = rest.astype(BF16)
        parts.append(part)
        rest = rest - part.astype(F32)
    return parts


def pairs_kernel(feat_count, bounds_ref, pos_ref, *refs):
    scores = refs[:-16]
    (worth_ref, qid_ref, inv_ref, lam_ref, near_ref,
     s_row, a_row, d_row, turn, s_col, a_col, w_col, q_col, d_col, grad, curv) = refs[-16:]
    rows = worth_ref.shape[0]
    own = rows // feat_count
    docs = own * LANES
    me = pos_ref[0] % feat_count
    s_row[...] = jnp.zeros(s_row.shape, F32)
    near = [me, ((me + 1) ^ 1) - 1, me ^ 1]
    for where, ref in zip(near, scores):
        @pl.when((where >= 0) & (where < feat_count))
        def _(where=where, ref=ref):
            s_row[pl.ds(pl.multiple_of(where * own, own), own), :] = ref[...]
    a_row[...] = jnp.exp(s_row[...])
    d_row[...] = jnp.zeros(d_row.shape, F32)
    first = me * own
    window_low = bounds_ref[0, first] // (2 * LANES) * 2
    window_high = (bounds_ref[1, first + own - 1] + 2 * LANES - 1) // (2 * LANES) * 2
    stride = 4

    def widen(pairs):
        lines = jnp.concatenate([source[...] for source, _ in pairs], axis=0)
        if lines.shape[0] % LANES:
            lines = jnp.concatenate([lines, jnp.zeros((LANES - lines.shape[0] % LANES, LANES), F32)], axis=0)
        for k in range(lines.shape[0] // LANES):
            turn[:, k * LANES:(k + 1) * LANES] = jnp.transpose(lines[k * LANES:(k + 1) * LANES])
        for r in range(0, rows, stride):
            @pl.when((r + stride > window_low) & (r < window_high))
            def _(r=r):
                for k, (_, col) in enumerate(pairs):
                    for m in range(r, r + stride):
                        at = k * rows + m
                        col[m * LANES:(m + 1) * LANES, :] = jnp.broadcast_to(turn[:, at:at + 1], (LANES, LANES))

    widen([(s_row, s_col), (qid_ref, q_col), (a_row, a_col), (worth_ref, w_col)])

    def rows_of(ref, r):
        return [jnp.broadcast_to(ref[pl.ds(r + g, 1), :], (8, LANES)) for g in range(2)]

    per = LANES // CHUNK

    def spans(r):
        start, end = bounds_ref[0, r], bounds_ref[1, r + 1]
        low = jnp.maximum(start // CHUNK, per * window_low)
        high = jnp.minimum((end + CHUNK - 1) // CHUNK, per * window_high)
        single = bounds_ref[2, r] >= (r + 2) * LANES
        inner_low = jnp.maximum((start + LANES - 1) // LANES, window_low)
        inner_high = jnp.minimum(end // LANES, window_high)
        return low, high, single, inner_low, inner_high

    def rank_groups(k, carry):
        r = window_low + 2 * k
        score = rows_of(s_row, r)
        query = rows_of(qid_ref, r)

        def gather(c, acc, masked, test):
            size = CHUNK if masked else LANES
            base = pl.multiple_of(c * size, size)
            acc = list(acc)
            for u in range(size // 8):
                other = s_col[pl.ds(base + 8 * u, 8), :]
                for g in range(2):
                    hit = test(other, g, u)
                    if masked:
                        hit = hit & (q_col[pl.ds(base + 8 * u, 8), :] == query[g])
                    k = 4 * g + u % 4
                    acc[k] = acc[k] + jnp.where(hit, 1.0, 0.0)
            return tuple(acc)

        def ahead(other, g, u):
            return other >= score[g]

        def behind(other, g, u):
            return other > score[g]

        def within(mine, offset):
            def test(other, g, u):
                if g != mine:
                    return ahead(other, g, u) if mine < g else behind(other, g, u)
                earlier = iota((8, LANES), 0) + (offset + 8 * u) < iota((8, LANES), 1)
                return (other > score[g]) | ((other == score[g]) & earlier)
            return test

        def twice(low, high, test, acc):
            twos = (high - low) // 2
            acc = lax.fori_loop(0, twos, lambda k, acc: gather(
                low + 2 * k + 1, gather(low + 2 * k, acc, False, test), False, test), acc)
            return lax.fori_loop(low + 2 * twos, high, lambda c, acc: gather(c, acc, False, test), acc)

        acc = tuple(jnp.zeros((8, LANES), F32) for _ in range(8))
        low, high, single, inner_low, inner_high = spans(r)
        inner_low = jnp.where(single, inner_low, r)
        after = jnp.where(single, inner_high, r + 2)
        acc = lax.fori_loop(low, per * inner_low, lambda c, acc: gather(c, acc, True, ahead), acc)
        acc = twice(inner_low, r, ahead, acc)
        acc = twice(r + 2, after, behind, acc)
        acc = lax.fori_loop(per * after, high, lambda c, acc: gather(c, acc, True, behind), acc)
        for c in range(2 * per):
            acc = gather(per * r + c, acc, True, within(c // per, c % per * CHUNK))
        for g in range(2):
            total = (acc[4 * g] + acc[4 * g + 1]) + (acc[4 * g + 2] + acc[4 * g + 3])
            d_row[pl.ds(r + g, 1), :] = jnp.sum(total, axis=0, keepdims=True)
        return carry

    lax.fori_loop(0, (window_high - window_low) // 2, rank_groups, 0)
    d_row[...] = 1.0 / jnp.log2(2.0 + d_row[...])
    widen([(d_row, d_col)])

    def pair_groups(t, carry):
        r = first + 2 * t
        a_i, w_i, d_i, query = [rows_of(ref, r) for ref in (a_row, worth_ref, d_row, qid_ref)]

        def columns(masked):
            def step(c, acc):
                size = CHUNK if masked else LANES
                base = pl.multiple_of(c * size, size)
                acc = list(acc)
                for u in range(size // 8):
                    at = pl.ds(base + 8 * u, 8)
                    a_j, w_j, d_j = a_col[at, :], w_col[at, :], d_col[at, :]
                    for g in range(2):
                        recip = pl.reciprocal(a_i[g] + a_j, approx=True)
                        lift = w_i[g] - w_j
                        weight = jnp.abs(d_i[g] - d_j) * recip
                        if masked:
                            weight = jnp.where(q_col[at, :] == query[g], weight, 0.0)
                        weight = weight * lift
                        k = 4 * g + u % 2
                        acc[k] = acc[k] + weight * jnp.where(lift > 0.0, a_j, a_i[g])
                        acc[k + 2] = acc[k + 2] + jnp.abs(weight) * (recip * a_j)
                return tuple(acc)
            return step

        def twice(low, high, step, acc):
            twos = (high - low) // 2
            acc = lax.fori_loop(0, twos, lambda k, acc: step(low + 2 * k + 1, step(low + 2 * k, acc)), acc)
            return lax.fori_loop(low + 2 * twos, high, step, acc)

        acc = tuple(jnp.zeros((8, LANES), F32) for _ in range(8))
        low, high, single, inner_low, inner_high = spans(r)
        acc = lax.fori_loop(low, jnp.where(single, per * inner_low, low), columns(True), acc)
        acc = twice(inner_low, jnp.where(single, inner_high, inner_low), columns(False), acc)
        acc = twice(jnp.where(single, per * inner_high, low), high, columns(True), acc)
        for g in range(2):
            at = pl.ds(2 * t + g, 1)
            grad[at, :] = -jnp.sum(acc[4 * g] + acc[4 * g + 1], axis=0, keepdims=True)
            curv[at, :] = a_i[g][0:1, :] * jnp.sum(acc[4 * g + 2] + acc[4 * g + 3], axis=0, keepdims=True)
        return carry

    lax.fori_loop(0, own // 2, pair_groups, 0)
    inverse = inv_ref[...]
    terms = [inverse * jnp.concatenate([ref[t:t + 1, :] for t in range(own)], axis=1) for ref in (grad, curv)]
    for c in range(2):
        lam_ref[c:c + 1, :] = terms[c]
        near_ref[c:c + 1, :] = terms[c]


def pair_terms(feat_count, bounds, pos, scores, worth, qid, inverse):
    rows = worth.shape[0]
    docs = inverse.shape[1]
    row = pltpu.VMEM((rows, LANES), F32)
    turn = pltpu.VMEM((LANES, 4 * rows), F32)
    col = pltpu.VMEM((rows * LANES, LANES), F32)
    mine = pltpu.VMEM((docs // LANES, LANES), F32)
    return pl.pallas_call(
        functools.partial(pairs_kernel, feat_count),
        out_shape=(jax.ShapeDtypeStruct((2, docs), F32), jax.ShapeDtypeStruct((2, docs), F32)),
        in_specs=[smem(), smem()] + [vmem()] * (len(scores) + 3),
        out_specs=(vmem(), vmem()),
        scratch_shapes=[row, row, row, turn, col, col, col, col, col, mine, mine],
        compiler_params=pltpu.CompilerParams(vmem_limit_bytes=VMEM_LIMIT),
        cost_estimate=pl.CostEstimate(flops=9_000_000_000, bytes_accessed=200_000, transcendentals=2_000_000),
        name="pair_terms",
    )(bounds, pos, *scores, worth, qid, inverse)


def leaf_kernel(perm_ref, bins_ref, leaf_ref, lam_ref, bins_t_ref, tile_ref, sums_ref):
    bins = bins_ref[...].astype(F32).astype(BF16)
    bins_t_ref[...] = lax.dot_general(perm_ref[...], bins, NT, preferred_element_type=F32)
    own = leaf_ref.shape[0]
    docs = own * LANES
    leaf = jnp.concatenate([leaf_ref[t:t + 1, :] for t in range(own)], axis=1)
    highs = LEAVES // LANES
    top = jnp.broadcast_to(leaf // LANES, (highs, docs)) == iota((highs, docs), 0)
    spots = jnp.where(jnp.broadcast_to(leaf % LANES, (LANES, docs)) == iota((LANES, docs), 0), 1.0, 0.0).astype(BF16)
    pieces, tiles = [], []
    for c in range(2):
        for k, part in enumerate(split_terms(lam_ref[c:c + 1, :], 3)):
            wide = jnp.broadcast_to(part.astype(F32), (highs, docs))
            pieces.append(jnp.where(top, wide, 0.0))
            if k < 2:
                tiles.append(wide)
    tile_ref[...] = jnp.concatenate(tiles, axis=0).astype(BF16)
    stacked = jnp.concatenate(pieces, axis=0).astype(BF16)
    sums = lax.dot_general(stacked, spots, NT, preferred_element_type=F32)
    for c in range(2):
        base = c * 3 * highs
        sums_ref[:, c * LANES:(c + 1) * LANES] = (
            sums[base:base + highs] + (sums[base + highs:base + 2 * highs] + sums[base + 2 * highs:base + 3 * highs])
        )


def leaf_terms(perm, bins, leaves, lambdas):
    docs, features = bins.shape
    return pl.pallas_call(
        leaf_kernel,
        out_shape=(
            jax.ShapeDtypeStruct((features, docs), F32),
            jax.ShapeDtypeStruct((4 * HIGH, docs), BF16),
            jax.ShapeDtypeStruct((LEAVES // LANES, 2 * LANES), F32),
        ),
        in_specs=[vmem()] * 4,
        out_specs=(vmem(), vmem(), vmem()),
        compiler_params=pltpu.CompilerParams(vmem_limit_bytes=VMEM_LIMIT),
        cost_estimate=pl.CostEstimate(flops=200_000_000, bytes_accessed=3_000_000, transcendentals=0),
        name="leaf_terms",
    )(perm, bins, leaves, lambdas)


def histogram_kernel(first, groups, tile_ref, bins_ref, *refs):
    out_ref = refs[-1]
    docs = tile_ref.shape[1]
    depth = docs
    rows = 16
    row = iota((rows, depth), 0)
    low_level = [(row + rows * k).astype(F32).astype(BF16) for k in range(LOW // rows)]
    high_level = (row % HIGH).astype(F32).astype(BF16)
    upper = jnp.where(row < HIGH, 1.0, 0.0).astype(BF16) > 0
    zero = jnp.zeros((rows, depth), BF16)
    one = jnp.ones((rows, depth), BF16)
    lane_owner = iota((1, GROUP * LOW), 1) // LOW

    def one_group(g, carry):
        base = pl.multiple_of((first + g) * GROUP, GROUP)
        acc = None
        for k in range(docs // depth):
            span = slice(k * depth, (k + 1) * depth)
            code = bins_ref[pl.ds(base, GROUP), span]
            high = jnp.floor(code * (1.0 / LOW))
            low = code - high * LOW
            left, right, count = [], [], []
            wide = []
            for f in range(GROUP):
                high_f = jnp.broadcast_to(high[f:f + 1, :], (rows, depth))
                low_f = jnp.broadcast_to(low[f:f + 1, :], (rows, depth)).astype(BF16)
                high_f = high_f.astype(BF16)
                wide.append(high_f)
                match = high_f == high_level
                for c in range(2):
                    left.append(jnp.where(match, tile_ref[c * rows:(c + 1) * rows, span], zero))
                for level in low_level:
                    right.append(jnp.where(low_f == level, one, zero))
            for f in range(0, GROUP, 2):
                both = jnp.where(upper, wide[f], wide[f + 1])
                count.append(jnp.where(both == high_level, one, zero))
            part = lax.dot_general(
                jnp.concatenate(left + count, axis=0), jnp.concatenate(right, axis=0), NT,
                preferred_element_type=F32,
            )
            acc = part if acc is None else acc + part
        stats = jnp.zeros((2 * rows, GROUP * LOW), F32)
        counts = jnp.zeros((HIGH, GROUP * LOW), F32)
        for f in range(GROUP):
            mine = lane_owner == f
            stats = jnp.where(mine, acc[f * 2 * rows:(f + 1) * 2 * rows], stats)
            at = GROUP * 2 * rows + f * HIGH
            counts = jnp.where(mine, acc[at:at + HIGH], counts)
        out_ref[pl.ds(pl.multiple_of(g * 3 * HIGH, 3 * HIGH), 3 * HIGH), :] = jnp.concatenate(
            [stats[0:HIGH] + stats[HIGH:2 * HIGH], stats[2 * HIGH:3 * HIGH] + stats[3 * HIGH:4 * HIGH], counts], axis=0)
        return carry

    if len(refs) > 1:
        out_ref[groups * 3 * HIGH:, :] = refs[0][...]
    lax.fori_loop(0, groups, one_group, 0, unroll=min(groups, 8))


def histogram_part(first, groups, tiles, bins_t, *tail):
    rows = groups * 3 * HIGH + sum(piece.shape[0] for piece in tail)
    return pl.pallas_call(
        functools.partial(histogram_kernel, first, groups),
        out_shape=jax.ShapeDtypeStruct((rows, GROUP * LOW), F32),
        in_specs=[vmem()] * (2 + len(tail)),
        out_specs=vmem(),
        compiler_params=pltpu.CompilerParams(vmem_limit_bytes=VMEM_LIMIT),
        cost_estimate=pl.CostEstimate(flops=groups * 1_000_000, bytes_accessed=groups * 1_000, transcendentals=0),
        name="histogram_part",
    )(tiles, bins_t, *tail)


def finish_kernel(per_dev, leaf_ref, kept_ref, sums_ref, *refs):
    arrived = list(refs[1::-1]) + list(refs[2:-3])
    value_ref, step_ref, hist_ref = refs[-3:]
    unit = kept_ref.shape[0]
    totals = add_up([sums_ref[...]] + [ref[unit:, :] for ref in arrived])
    highs = LEAVES // LANES
    grad, curv = totals[:, :LANES], totals[:, LANES:]
    shrunk = jnp.maximum(jnp.abs(grad) - lasso_penalty, 0.0)
    values = jnp.where(grad > 0.0, -shrunk, shrunk) / (curv + ridge_penalty)
    value_ref[...] = values
    leaf = leaf_ref[...]
    top, spot = leaf // LANES, leaf % LANES
    step = jnp.zeros(leaf.shape, F32)
    for h in range(highs):
        row = jnp.broadcast_to(values[h:h + 1, :], leaf.shape)
        step = jnp.where(top == h, jnp.take_along_axis(row, spot, axis=1), step)
    step_ref[...] = shrinkage * step
    hist = add_up([kept_ref[...]] + [ref[:unit, :] for ref in arrived])
    if per_dev == GROUP:
        shape = hist.shape
        line, place = iota(shape, 0), iota(shape, 1) // LOW
        step = 1
        while step < GROUP:
            down, across = (line // step) % 2, (place // step) % 2
            shift = step * LOW
            ahead = pltpu.roll(pltpu.roll(hist, shape[0] - step, 0), shift, 1)
            behind = pltpu.roll(pltpu.roll(hist, step, 0), shape[1] - shift, 1)
            hist = jnp.where(down == across, hist, jnp.where(across == 1, ahead, behind))
            step *= 2
        for c in range(3):
            for f in range(GROUP):
                hist_ref[c:c + 1, f * BINS:(f + 1) * BINS] = hist[c * HIGH + f:c * HIGH + f + 1, :]
    else:
        hist_ref[...] = hist


def finish(per_dev, leaves, kept, sums, arrived):
    out = (3, per_dev * BINS) if per_dev == GROUP else kept.shape
    return pl.pallas_call(
        functools.partial(finish_kernel, per_dev),
        out_shape=(
            jax.ShapeDtypeStruct((LEAVES // LANES, LANES), F32),
            jax.ShapeDtypeStruct(leaves.shape, F32),
            jax.ShapeDtypeStruct(out, F32),
        ),
        in_specs=[vmem()] * (3 + len(arrived)),
        out_specs=(vmem(), vmem(), vmem()),
        compiler_params=pltpu.CompilerParams(vmem_limit_bytes=VMEM_LIMIT),
        name="finish",
    )(leaves, kept, sums, *arrived)


def add_up(parts):
    while len(parts) > 1:
        parts = [parts[k] + parts[k + 1] for k in range(0, len(parts), 2)]
    return parts[0]


def local(scores, labels, leaves, bins, lengths, owner):
    query_count = lax.axis_size("query")
    feat_count = lax.axis_size("feat")
    count = query_count * feat_count
    place = lax.axis_index("query").astype(jnp.int32) * feat_count + lax.axis_index("feat").astype(jnp.int32)
    docs = scores.shape[0]
    own = docs // LANES
    features = owner.shape[0]
    per_dev = features // count
    unit = 3 * per_dev
    axes = ("query", "feat")
    feat_masks = [1 << b for b in range(feat_count.bit_length() - 1)]
    query_masks = [feat_count << b for b in range(query_count.bit_length() - 1)]

    def swap(value, mask):
        return lax.ppermute(value, axes, [(p, p ^ mask) for p in range(count)])

    pos = place.reshape(1)
    leaf_rows = leaves.reshape(own, LANES)
    own_scores = scores.reshape(own, LANES)
    score_parts = [own_scores]
    def inner_partner(p):
        z = p % feat_count
        if z in (0, feat_count - 1):
            return p ^ query_masks[0]
        return p + 1 if z % 2 else p - 1

    score_parts.append(lax.ppermute(own_scores, axes, [(p, inner_partner(p)) for p in range(count)]))
    score_parts.append(swap(own_scores, 1))
    masks = feat_masks + query_masks[:0:-1] + query_masks[:1]
    score_parts[0], leaf_rows, qid, worth, inverse, perm, bounds = prepare(
        feat_count, masks, lengths, pos, labels.reshape(-1, LANES), owner.reshape(-1, LANES), own_scores, leaf_rows)
    lambdas, near_lambdas = pair_terms(feat_count, bounds, pos, score_parts, worth, qid, inverse)
    bins_t, tiles, sums = leaf_terms(perm, bins, leaf_rows, near_lambdas)

    def part(tiles, low, high, *tail):
        if per_dev == GROUP:
            return histogram_part(low, high - low, tiles, bins_t, *tail)
        groups = high - low
        wide = histogram_part(low, groups, tiles, bins_t)
        wide = wide.reshape(groups, 3, HIGH, GROUP // per_dev, per_dev, LOW).transpose(0, 3, 1, 4, 2, 5)
        return jnp.concatenate([wide.reshape(groups * GROUP // per_dev * unit, BINS), *tail], axis=0)

    def join(block, total):
        return jnp.concatenate([block, total], axis=0)

    eighth = features // GROUP // 8
    edge = count // 8 * unit
    arrived = swap(part(tiles, 7 * eighth, 8 * eighth, sums), query_masks[0])
    block = part(tiles, 3 * eighth, 4 * eighth) + arrived[:edge]
    sums = sums + arrived[edge:]
    message, tiles = lax.optimization_barrier((join(block, sums), tiles))
    crossed_far = swap(message, query_masks[1])
    arrived = swap(part(tiles, 6 * eighth, 7 * eighth), query_masks[0])
    rest = part(tiles, 2 * eighth, 3 * eighth) + arrived
    rest, tiles = lax.optimization_barrier((join(rest, sums), tiles))
    crossed_near = swap(rest, query_masks[1])
    arrived = swap(part(tiles, 4 * eighth, 6 * eighth), query_masks[0])
    block = part(tiles, eighth, 2 * eighth) + arrived[edge:] + crossed_far[:edge]
    sums = sums + crossed_far[edge:]
    message, tiles = lax.optimization_barrier((join(block, sums), tiles))
    turned = swap(message, query_masks[2])
    kept = part(tiles, 0, eighth) + arrived[:edge] + crossed_near[:edge] + turned[:edge]
    sums = sums + turned[edge:]
    for mask in query_masks[3:]:
        edge = edge // 2
        arrived = swap(join(kept[edge:], sums), mask)
        kept = kept[:edge] + arrived[:edge]
        sums = sums + arrived[edge:]
    arrived = [swap(join(kept[m * unit:(m + 1) * unit], sums), m) for m in range(1, feat_count)]
    arrived[:2] = arrived[1::-1]
    values, step, histograms = finish(per_dev, leaf_rows, kept[:unit], sums, arrived)
    return lambdas, values.reshape(LEAVES), step.reshape(docs), histograms.reshape(3, per_dev * BINS)


def solution(mesh):
    in_specs = (
        P(("query", "feat")),
        P("query"),
        P(("query", "feat")),
        P(("query", "feat"), None),
        P("query", None),
        P(),
    )
    out_specs = (P(None, ("query", "feat")), P(), P(("query", "feat")), P(None, ("query", "feat")))
    return jax.shard_map(local, mesh=mesh, in_specs=in_specs, out_specs=out_specs, check_vma=False)
```

```python
import functools

import jax
import jax.numpy as jnp
from jax import lax
from jax.experimental import pallas as pl
from jax.experimental.pallas import tpu as pltpu
from jax.sharding import PartitionSpec as P

BINS = 256
LEAVES = 1024
LANES = 128
GRADES = 4
LOW = 32
HIGH = BINS // LOW
GROUP = 8
CHUNK = 64
MAX_LEN = 1024

lasso_penalty = 1.0
ridge_penalty = 1.0
shrinkage = 0.1

VMEM_LIMIT = 48 * 1024 * 1024
F32 = jnp.float32
BF16 = jnp.bfloat16
NT = (((1,), (1,)), ((), ()))


def iota(shape, axis):
    return lax.broadcasted_iota(jnp.int32, shape, axis)


def vmem():
    return pl.BlockSpec(memory_space=pltpu.VMEM)


def smem():
    return pl.BlockSpec(memory_space=pltpu.SMEM)


def prepare_kernel(feat_count, masks, len_ref, pos_ref, lab_ref, owner_ref, score_ref, leaf_ref,
                   kept_ref, leaf_out, qid_ref, worth_ref, inv_ref, perm_ref, bounds_ref):
    kept_ref[...] = score_ref[...]
    leaf_out[...] = leaf_ref[...]
    queries = len_ref.shape[1]
    rows = lab_ref.shape[0]
    own = rows // feat_count
    spot = iota((rows, LANES), 0) * LANES + iota((rows, LANES), 1)
    qid = jnp.zeros((rows, LANES), F32)
    begin = jnp.zeros((queries, LANES), jnp.int32)
    finish = jnp.zeros((queries, LANES), jnp.int32)
    which = iota((queries, LANES), 0)
    group = iota((1, LANES), 1) * LANES
    low = jnp.zeros((1, LANES), jnp.int32)
    high = first_end = jnp.full((1, LANES), rows * LANES, jnp.int32)
    start = jnp.int32(0)
    for q in range(queries):
        end = start + len_ref[0, q]
        qid = qid + jnp.where(spot >= end, 1.0, 0.0)
        begin = jnp.where(which == q, start, begin)
        finish = jnp.where(which == q, end, finish)

        low = low + jnp.where(end <= group, len_ref[0, q], 0)
        high = jnp.minimum(high, jnp.where(end >= group + LANES, end, rows * LANES))
        first_end = jnp.minimum(first_end, jnp.where(end > group, end, rows * LANES))
        start = end
    bounds_ref[...] = jnp.concatenate([low, high, first_end, low, low, low, low, low], axis=0)
    qid_ref[...] = qid
    worth_ref[...] = jnp.left_shift(1, lab_ref[...]).astype(F32)

    counts = [jnp.zeros((queries, LANES), F32) for _ in range(GRADES)]
    lane = iota((queries, LANES), 1)
    for r in range(rows):
        at = lane + r * LANES
        inside = (at >= begin) & (at < finish)
        grade = jnp.where(inside, jnp.broadcast_to(lab_ref[r:r + 1, :], (queries, LANES)), 0)
        for g in range(GRADES):
            counts[g] = counts[g] + jnp.where(grade > g, 1.0, 0.0)
    position = iota((queries, MAX_LEN), 1).astype(F32)
    gain = jnp.zeros((queries, MAX_LEN), F32)
    for g in range(GRADES):
        held = jnp.sum(counts[g], axis=1, keepdims=True)
        gain = gain + jnp.where(position < held, float(2 ** g), 0.0)
    level = 1.0 / jnp.log2(2.0 + position[0:1, :])
    ideal = jnp.sum(gain * level, axis=1, keepdims=True)
    usable = ideal > 0.5
    inverse = jnp.where(usable, 1.0 / jnp.where(usable, ideal, 1.0), 0.0)
    first = pos_ref[0] % feat_count * own
    for t in range(own):
        at = lane + (first + t) * LANES
        inside = (at >= begin) & (at < finish)
        inv_ref[0:1, t * LANES:(t + 1) * LANES] = jnp.sum(jnp.where(inside, inverse, 0.0), axis=0, keepdims=True)

    features = perm_ref.shape[0]
    per_dev = features >> len(masks)
    owner = jnp.concatenate([owner_ref[k:k + 1, :] for k in range(features // LANES)], axis=1)
    square = (features, features)
    down, across = iota(square, 0), iota(square, 1)
    index = iota((features, 1), 0) // per_dev
    target = jnp.zeros((features, 1), jnp.int32)
    for b, mask in enumerate(masks):
        target = target + ((index >> b) & 1) * mask
    target = (target ^ pos_ref[0]) * per_dev + iota((features, 1), 0) % per_dev
    pick = jnp.where(target == across, 1.0, 0.0).astype(BF16)
    holds = jnp.where(jnp.broadcast_to(owner, square) == down, 1.0, 0.0).astype(BF16)
    perm_ref[...] = lax.dot_general(pick, holds, NT, preferred_element_type=F32).astype(BF16)


def prepare(feat_count, masks, lengths, pos, labels, owner, scores, leaves):
    rows = labels.shape[0]
    features = owner.shape[0] * LANES
    return pl.pallas_call(
        functools.partial(prepare_kernel, feat_count, masks),
        out_shape=(
            jax.ShapeDtypeStruct(scores.shape, F32),
            jax.ShapeDtypeStruct(leaves.shape, jnp.int32),
            jax.ShapeDtypeStruct((rows, LANES), F32),
            jax.ShapeDtypeStruct((rows, LANES), F32),
            jax.ShapeDtypeStruct((1, rows // feat_count * LANES), F32),
            jax.ShapeDtypeStruct((features, features), BF16),
            jax.ShapeDtypeStruct((8, LANES), jnp.int32),
        ),
        in_specs=[smem(), smem(), vmem(), vmem(), vmem(), vmem()],
        out_specs=(vmem(),) * 7,
        compiler_params=pltpu.CompilerParams(vmem_limit_bytes=VMEM_LIMIT),
        cost_estimate=pl.CostEstimate(flops=2_000_000_000, bytes_accessed=300_000, transcendentals=20_000),
        name="prepare",
    )(lengths, pos, labels, owner, scores, leaves)


def split_terms(value, terms):
    parts = []
    rest = value
    for _ in range(terms):
        part = rest.astype(BF16)
        parts.append(part)
        rest = rest - part.astype(F32)
    return parts


def pairs_kernel(feat_count, bounds_ref, pos_ref, *refs):
    scores = refs[:-16]
    (worth_ref, qid_ref, inv_ref, lam_ref, near_ref,
     s_row, a_row, d_row, turn, s_col, a_col, w_col, q_col, d_col, grad, curv) = refs[-16:]
    rows = worth_ref.shape[0]
    own = rows // feat_count
    docs = own * LANES
    me = pos_ref[0] % feat_count
    s_row[...] = jnp.zeros(s_row.shape, F32)
    near = [me, ((me + 1) ^ 1) - 1, me ^ 1]
    for where, ref in zip(near, scores):
        @pl.when((where >= 0) & (where < feat_count))
        def _(where=where, ref=ref):
            s_row[pl.ds(pl.multiple_of(where * own, own), own), :] = ref[...]
    a_row[...] = jnp.exp(s_row[...])
    d_row[...] = jnp.zeros(d_row.shape, F32)
    first = me * own
    window_low = bounds_ref[0, first] // (2 * LANES) * 2
    window_high = (bounds_ref[1, first + own - 1] + 2 * LANES - 1) // (2 * LANES) * 2
    stride = 4

    def widen(pairs):
        lines = jnp.concatenate([source[...] for source, _ in pairs], axis=0)
        if lines.shape[0] % LANES:
            lines = jnp.concatenate([lines, jnp.zeros((LANES - lines.shape[0] % LANES, LANES), F32)], axis=0)
        for k in range(lines.shape[0] // LANES):
            turn[:, k * LANES:(k + 1) * LANES] = jnp.transpose(lines[k * LANES:(k + 1) * LANES])
        for r in range(0, rows, stride):
            @pl.when((r + stride > window_low) & (r < window_high))
            def _(r=r):
                for k, (_, col) in enumerate(pairs):
                    for m in range(r, r + stride):
                        at = k * rows + m
                        col[m * LANES:(m + 1) * LANES, :] = jnp.broadcast_to(turn[:, at:at + 1], (LANES, LANES))

    widen([(s_row, s_col), (qid_ref, q_col), (a_row, a_col), (worth_ref, w_col)])

    def rows_of(ref, r):
        return [jnp.broadcast_to(ref[pl.ds(r + g, 1), :], (8, LANES)) for g in range(2)]

    per = LANES // CHUNK

    def spans(r):
        start, end = bounds_ref[0, r], bounds_ref[1, r + 1]
        low = jnp.maximum(start // CHUNK, per * window_low)
        high = jnp.minimum((end + CHUNK - 1) // CHUNK, per * window_high)
        single = bounds_ref[2, r] >= (r + 2) * LANES
        inner_low = jnp.maximum((start + LANES - 1) // LANES, window_low)
        inner_high = jnp.minimum(end // LANES, window_high)
        return low, high, single, inner_low, inner_high

    def rank_groups(k, carry):
        r = window_low + 2 * k
        score = rows_of(s_row, r)
        query = rows_of(qid_ref, r)

        def gather(c, acc, masked, test):
            size = CHUNK if masked else LANES
            base = pl.multiple_of(c * size, size)
            acc = list(acc)
            for u in range(size // 8):
                other = s_col[pl.ds(base + 8 * u, 8), :]
                for g in range(2):
                    hit = test(other, g, u)
                    if masked:
                        hit = hit & (q_col[pl.ds(base + 8 * u, 8), :] == query[g])
                    k = 4 * g + u % 4
                    acc[k] = acc[k] + jnp.where(hit, 1.0, 0.0)
            return tuple(acc)

        def ahead(other, g, u):
            return other >= score[g]

        def behind(other, g, u):
            return other > score[g]

        def within(mine, offset):
            def test(other, g, u):
                if g != mine:
                    return ahead(other, g, u) if mine < g else behind(other, g, u)
                earlier = iota((8, LANES), 0) + (offset + 8 * u) < iota((8, LANES), 1)
                return (other > score[g]) | ((other == score[g]) & earlier)
            return test

        def twice(low, high, test, acc):
            twos = (high - low) // 2
            acc = lax.fori_loop(0, twos, lambda k, acc: gather(
                low + 2 * k + 1, gather(low + 2 * k, acc, False, test), False, test), acc)
            return lax.fori_loop(low + 2 * twos, high, lambda c, acc: gather(c, acc, False, test), acc)

        acc = tuple(jnp.zeros((8, LANES), F32) for _ in range(8))
        low, high, single, inner_low, inner_high = spans(r)
        inner_low = jnp.where(single, inner_low, r)
        after = jnp.where(single, inner_high, r + 2)
        acc = lax.fori_loop(low, per * inner_low, lambda c, acc: gather(c, acc, True, ahead), acc)
        acc = twice(inner_low, r, ahead, acc)
        acc = twice(r + 2, after, behind, acc)
        acc = lax.fori_loop(per * after, high, lambda c, acc: gather(c, acc, True, behind), acc)
        for c in range(2 * per):
            acc = gather(per * r + c, acc, True, within(c // per, c % per * CHUNK))
        for g in range(2):
            total = (acc[4 * g] + acc[4 * g + 1]) + (acc[4 * g + 2] + acc[4 * g + 3])
            d_row[pl.ds(r + g, 1), :] = jnp.sum(total, axis=0, keepdims=True)
        return carry

    lax.fori_loop(0, (window_high - window_low) // 2, rank_groups, 0)
    d_row[...] = 1.0 / jnp.log2(2.0 + d_row[...])
    widen([(d_row, d_col)])

    def pair_groups(t, carry):
        r = first + 2 * t
        a_i, w_i, d_i, query = [rows_of(ref, r) for ref in (a_row, worth_ref, d_row, qid_ref)]

        def columns(masked):
            def step(c, acc):
                size = CHUNK if masked else LANES
                base = pl.multiple_of(c * size, size)
                acc = list(acc)
                for u in range(size // 8):
                    at = pl.ds(base + 8 * u, 8)
                    a_j, w_j, d_j = a_col[at, :], w_col[at, :], d_col[at, :]
                    totals = [a_i[g] + a_j for g in range(2)]
                    product = pl.reciprocal(totals[0] * totals[1], approx=True)
                    for g in range(2):
                        recip = product * totals[1 - g]
                        lift = w_i[g] - w_j
                        weight = jnp.abs(d_i[g] - d_j) * recip
                        if masked:
                            weight = jnp.where(q_col[at, :] == query[g], weight, 0.0)
                        weight = weight * lift
                        k = 4 * g + u % 2
                        acc[k] = acc[k] + weight * jnp.where(lift > 0.0, a_j, a_i[g])
                        acc[k + 2] = acc[k + 2] + jnp.abs(weight) * (recip * a_j)
                return tuple(acc)
            return step

        def twice(low, high, step, acc):
            twos = (high - low) // 2
            acc = lax.fori_loop(0, twos, lambda k, acc: step(low + 2 * k + 1, step(low + 2 * k, acc)), acc)
            return lax.fori_loop(low + 2 * twos, high, step, acc)

        acc = tuple(jnp.zeros((8, LANES), F32) for _ in range(8))
        low, high, single, inner_low, inner_high = spans(r)
        acc = lax.fori_loop(low, jnp.where(single, per * inner_low, low), columns(True), acc)
        acc = twice(inner_low, jnp.where(single, inner_high, inner_low), columns(False), acc)
        acc = twice(jnp.where(single, per * inner_high, low), high, columns(True), acc)
        for g in range(2):
            at = pl.ds(2 * t + g, 1)
            grad[at, :] = -jnp.sum(acc[4 * g] + acc[4 * g + 1], axis=0, keepdims=True)
            curv[at, :] = a_i[g][0:1, :] * jnp.sum(acc[4 * g + 2] + acc[4 * g + 3], axis=0, keepdims=True)
        return carry

    lax.fori_loop(0, own // 2, pair_groups, 0)
    inverse = inv_ref[...]
    terms = [inverse * jnp.concatenate([ref[t:t + 1, :] for t in range(own)], axis=1) for ref in (grad, curv)]
    for c in range(2):
        lam_ref[c:c + 1, :] = terms[c]
        near_ref[c:c + 1, :] = terms[c]


def pair_terms(feat_count, bounds, pos, scores, worth, qid, inverse):
    rows = worth.shape[0]
    docs = inverse.shape[1]
    row = pltpu.VMEM((rows, LANES), F32)
    turn = pltpu.VMEM((LANES, 4 * rows), F32)
    col = pltpu.VMEM((rows * LANES, LANES), F32)
    mine = pltpu.VMEM((docs // LANES, LANES), F32)
    return pl.pallas_call(
        functools.partial(pairs_kernel, feat_count),
        out_shape=(jax.ShapeDtypeStruct((2, docs), F32), jax.ShapeDtypeStruct((2, docs), F32)),
        in_specs=[smem(), smem()] + [vmem()] * (len(scores) + 3),
        out_specs=(vmem(), vmem()),
        scratch_shapes=[row, row, row, turn, col, col, col, col, col, mine, mine],
        compiler_params=pltpu.CompilerParams(vmem_limit_bytes=VMEM_LIMIT),
        cost_estimate=pl.CostEstimate(flops=9_000_000_000, bytes_accessed=200_000, transcendentals=2_000_000),
        name="pair_terms",
    )(bounds, pos, *scores, worth, qid, inverse)


def leaf_kernel(perm_ref, bins_ref, leaf_ref, lam_ref, bins_t_ref, tile_ref, sums_ref):
    bins = bins_ref[...].astype(F32).astype(BF16)
    bins_t_ref[...] = lax.dot_general(perm_ref[...], bins, NT, preferred_element_type=F32)
    own = leaf_ref.shape[0]
    docs = own * LANES
    leaf = jnp.concatenate([leaf_ref[t:t + 1, :] for t in range(own)], axis=1)
    highs = LEAVES // LANES
    top = jnp.broadcast_to(leaf // LANES, (highs, docs)) == iota((highs, docs), 0)
    spots = jnp.where(jnp.broadcast_to(leaf % LANES, (LANES, docs)) == iota((LANES, docs), 0), 1.0, 0.0).astype(BF16)
    pieces, tiles = [], []
    for c in range(2):
        for k, part in enumerate(split_terms(lam_ref[c:c + 1, :], 3)):
            wide = jnp.broadcast_to(part.astype(F32), (highs, docs))
            pieces.append(jnp.where(top, wide, 0.0))
            if k < 2:
                tiles.append(wide)
    tile_ref[...] = jnp.concatenate(tiles, axis=0).astype(BF16)
    stacked = jnp.concatenate(pieces, axis=0).astype(BF16)
    sums = lax.dot_general(stacked, spots, NT, preferred_element_type=F32)
    for c in range(2):
        base = c * 3 * highs
        sums_ref[:, c * LANES:(c + 1) * LANES] = (
            sums[base:base + highs] + (sums[base + highs:base + 2 * highs] + sums[base + 2 * highs:base + 3 * highs])
        )


def leaf_terms(perm, bins, leaves, lambdas):
    docs, features = bins.shape
    return pl.pallas_call(
        leaf_kernel,
        out_shape=(
            jax.ShapeDtypeStruct((features, docs), F32),
            jax.ShapeDtypeStruct((4 * HIGH, docs), BF16),
            jax.ShapeDtypeStruct((LEAVES // LANES, 2 * LANES), F32),
        ),
        in_specs=[vmem()] * 4,
        out_specs=(vmem(), vmem(), vmem()),
        compiler_params=pltpu.CompilerParams(vmem_limit_bytes=VMEM_LIMIT),
        cost_estimate=pl.CostEstimate(flops=200_000_000, bytes_accessed=3_000_000, transcendentals=0),
        name="leaf_terms",
    )(perm, bins, leaves, lambdas)


def histogram_kernel(first, groups, tile_ref, bins_ref, *refs):
    out_ref = refs[-1]
    docs = tile_ref.shape[1]
    depth = docs
    rows = 16
    row = iota((rows, depth), 0)
    low_level = [(row + rows * k).astype(F32).astype(BF16) for k in range(LOW // rows)]
    high_level = (row % HIGH).astype(F32).astype(BF16)
    upper = jnp.where(row < HIGH, 1.0, 0.0).astype(BF16) > 0
    zero = jnp.zeros((rows, depth), BF16)
    one = jnp.ones((rows, depth), BF16)
    lane_owner = iota((1, GROUP * LOW), 1) // LOW

    def one_group(g, carry):
        base = pl.multiple_of((first + g) * GROUP, GROUP)
        acc = None
        for k in range(docs // depth):
            span = slice(k * depth, (k + 1) * depth)
            code = bins_ref[pl.ds(base, GROUP), span]
            high = jnp.floor(code * (1.0 / LOW))
            low = code - high * LOW
            left, right, count = [], [], []
            wide = []
            for f in range(GROUP):
                high_f = jnp.broadcast_to(high[f:f + 1, :], (rows, depth))
                low_f = jnp.broadcast_to(low[f:f + 1, :], (rows, depth)).astype(BF16)
                high_f = high_f.astype(BF16)
                wide.append(high_f)
                match = high_f == high_level
                for c in range(2):
                    left.append(jnp.where(match, tile_ref[c * rows:(c + 1) * rows, span], zero))
                for level in low_level:
                    right.append(jnp.where(low_f == level, one, zero))
            for f in range(0, GROUP, 2):
                both = jnp.where(upper, wide[f], wide[f + 1])
                count.append(jnp.where(both == high_level, one, zero))
            part = lax.dot_general(
                jnp.concatenate(left + count, axis=0), jnp.concatenate(right, axis=0), NT,
                preferred_element_type=F32,
            )
            acc = part if acc is None else acc + part
        stats = jnp.zeros((2 * rows, GROUP * LOW), F32)
        counts = jnp.zeros((HIGH, GROUP * LOW), F32)
        for f in range(GROUP):
            mine = lane_owner == f
            stats = jnp.where(mine, acc[f * 2 * rows:(f + 1) * 2 * rows], stats)
            at = GROUP * 2 * rows + f * HIGH
            counts = jnp.where(mine, acc[at:at + HIGH], counts)
        out_ref[pl.ds(pl.multiple_of(g * 3 * HIGH, 3 * HIGH), 3 * HIGH), :] = jnp.concatenate(
            [stats[0:HIGH] + stats[HIGH:2 * HIGH], stats[2 * HIGH:3 * HIGH] + stats[3 * HIGH:4 * HIGH], counts], axis=0)
        return carry

    if len(refs) > 1:
        out_ref[groups * 3 * HIGH:, :] = refs[0][...]
    lax.fori_loop(0, groups, one_group, 0, unroll=min(groups, 8))


def histogram_part(first, groups, tiles, bins_t, *tail):
    rows = groups * 3 * HIGH + sum(piece.shape[0] for piece in tail)
    return pl.pallas_call(
        functools.partial(histogram_kernel, first, groups),
        out_shape=jax.ShapeDtypeStruct((rows, GROUP * LOW), F32),
        in_specs=[vmem()] * (2 + len(tail)),
        out_specs=vmem(),
        compiler_params=pltpu.CompilerParams(vmem_limit_bytes=VMEM_LIMIT),
        cost_estimate=pl.CostEstimate(flops=groups * 1_000_000, bytes_accessed=groups * 1_000, transcendentals=0),
        name="histogram_part",
    )(tiles, bins_t, *tail)


def finish_kernel(per_dev, leaf_ref, kept_ref, sums_ref, *refs):
    arrived = list(refs[1::-1]) + list(refs[2:-3])
    value_ref, step_ref, hist_ref = refs[-3:]
    unit = kept_ref.shape[0]
    totals = add_up([sums_ref[...]] + [ref[unit:, :] for ref in arrived])
    highs = LEAVES // LANES
    grad, curv = totals[:, :LANES], totals[:, LANES:]
    shrunk = jnp.maximum(jnp.abs(grad) - lasso_penalty, 0.0)
    values = jnp.where(grad > 0.0, -shrunk, shrunk) / (curv + ridge_penalty)
    value_ref[...] = values
    leaf = leaf_ref[...]
    top, spot = leaf // LANES, leaf % LANES
    step = jnp.zeros(leaf.shape, F32)
    for h in range(highs):
        row = jnp.broadcast_to(values[h:h + 1, :], leaf.shape)
        step = jnp.where(top == h, jnp.take_along_axis(row, spot, axis=1), step)
    step_ref[...] = shrinkage * step
    hist = add_up([kept_ref[...]] + [ref[:unit, :] for ref in arrived])
    if per_dev == GROUP:
        shape = hist.shape
        line, place = iota(shape, 0), iota(shape, 1) // LOW
        step = 1
        while step < GROUP:
            down, across = (line // step) % 2, (place // step) % 2
            shift = step * LOW
            ahead = pltpu.roll(pltpu.roll(hist, shape[0] - step, 0), shift, 1)
            behind = pltpu.roll(pltpu.roll(hist, step, 0), shape[1] - shift, 1)
            hist = jnp.where(down == across, hist, jnp.where(across == 1, ahead, behind))
            step *= 2
        for c in range(3):
            for f in range(GROUP):
                hist_ref[c:c + 1, f * BINS:(f + 1) * BINS] = hist[c * HIGH + f:c * HIGH + f + 1, :]
    else:
        hist_ref[...] = hist


def finish(per_dev, leaves, kept, sums, arrived):
    out = (3, per_dev * BINS) if per_dev == GROUP else kept.shape
    return pl.pallas_call(
        functools.partial(finish_kernel, per_dev),
        out_shape=(
            jax.ShapeDtypeStruct((LEAVES // LANES, LANES), F32),
            jax.ShapeDtypeStruct(leaves.shape, F32),
            jax.ShapeDtypeStruct(out, F32),
        ),
        in_specs=[vmem()] * (3 + len(arrived)),
        out_specs=(vmem(), vmem(), vmem()),
        compiler_params=pltpu.CompilerParams(vmem_limit_bytes=VMEM_LIMIT),
        name="finish",
    )(leaves, kept, sums, *arrived)


def add_up(parts):
    while len(parts) > 1:
        parts = [parts[k] + parts[k + 1] for k in range(0, len(parts), 2)]
    return parts[0]


def local(scores, labels, leaves, bins, lengths, owner):
    query_count = lax.axis_size("query")
    feat_count = lax.axis_size("feat")
    count = query_count * feat_count
    place = lax.axis_index("query").astype(jnp.int32) * feat_count + lax.axis_index("feat").astype(jnp.int32)
    docs = scores.shape[0]
    own = docs // LANES
    features = owner.shape[0]
    per_dev = features // count
    unit = 3 * per_dev
    axes = ("query", "feat")
    feat_masks = [1 << b for b in range(feat_count.bit_length() - 1)]
    query_masks = [feat_count << b for b in range(query_count.bit_length() - 1)]

    def swap(value, mask):
        return lax.ppermute(value, axes, [(p, p ^ mask) for p in range(count)])

    pos = place.reshape(1)
    leaf_rows = leaves.reshape(own, LANES)
    own_scores = scores.reshape(own, LANES)
    score_parts = [own_scores]
    def inner_partner(p):
        z = p % feat_count
        if z in (0, feat_count - 1):
            return p ^ query_masks[0]
        return p + 1 if z % 2 else p - 1

    score_parts.append(lax.ppermute(own_scores, axes, [(p, inner_partner(p)) for p in range(count)]))
    score_parts.append(swap(own_scores, 1))
    masks = feat_masks + query_masks[:0:-1] + query_masks[:1]
    score_parts[0], leaf_rows, qid, worth, inverse, perm, bounds = prepare(
        feat_count, masks, lengths, pos, labels.reshape(-1, LANES), owner.reshape(-1, LANES), own_scores, leaf_rows)
    lambdas, near_lambdas = pair_terms(feat_count, bounds, pos, score_parts, worth, qid, inverse)
    bins_t, tiles, sums = leaf_terms(perm, bins, leaf_rows, near_lambdas)

    def part(tiles, low, high, *tail):
        if per_dev == GROUP:
            return histogram_part(low, high - low, tiles, bins_t, *tail)
        groups = high - low
        wide = histogram_part(low, groups, tiles, bins_t)
        wide = wide.reshape(groups, 3, HIGH, GROUP // per_dev, per_dev, LOW).transpose(0, 3, 1, 4, 2, 5)
        return jnp.concatenate([wide.reshape(groups * GROUP // per_dev * unit, BINS), *tail], axis=0)

    def join(block, total):
        return jnp.concatenate([block, total], axis=0)

    eighth = features // GROUP // 8
    edge = count // 8 * unit
    arrived = swap(part(tiles, 7 * eighth, 8 * eighth, sums), query_masks[0])
    block = part(tiles, 3 * eighth, 4 * eighth) + arrived[:edge]
    sums = sums + arrived[edge:]
    message, tiles = lax.optimization_barrier((join(block, sums), tiles))
    crossed_far = swap(message, query_masks[1])
    arrived = swap(part(tiles, 5 * eighth, 7 * eighth), query_masks[0])
    both = part(tiles, eighth, 3 * eighth) + arrived
    sums = sums + crossed_far[edge:]
    message, rest, tiles = lax.optimization_barrier(
        (join(both[:edge] + crossed_far[:edge], sums), join(both[edge:], sums), tiles))
    turned = swap(message, query_masks[2])
    crossed_near = swap(rest, query_masks[1])
    arrived = swap(part(tiles, 4 * eighth, 5 * eighth), query_masks[0])
    kept = part(tiles, 0, eighth) + arrived + crossed_near[:edge] + turned[:edge]
    sums = sums + turned[edge:]
    for mask in query_masks[3:]:
        edge = edge // 2
        arrived = swap(join(kept[edge:], sums), mask)
        kept = kept[:edge] + arrived[:edge]
        sums = sums + arrived[edge:]
    arrived = [swap(join(kept[m * unit:(m + 1) * unit], sums), m) for m in range(1, feat_count)]
    arrived[:2] = arrived[1::-1]
    values, step, histograms = finish(per_dev, leaf_rows, kept[:unit], sums, arrived)
    return lambdas, values.reshape(LEAVES), step.reshape(docs), histograms.reshape(3, per_dev * BINS)


def solution(mesh):
    in_specs = (
        P(("query", "feat")),
        P("query"),
        P(("query", "feat")),
        P(("query", "feat"), None),
        P("query", None),
        P(),
    )
    out_specs = (P(None, ("query", "feat")), P(), P(("query", "feat")), P(None, ("query", "feat")))
    return jax.shard_map(local, mesh=mesh, in_specs=in_specs, out_specs=out_specs, check_vma=False)
```

```python
import functools

import jax
import jax.numpy as jnp
from jax import lax
from jax.experimental import pallas as pl
from jax.experimental.pallas import tpu as pltpu
from jax.sharding import PartitionSpec as P

BINS = 256
LEAVES = 1024
LANES = 128
GRADES = 4
LOW = 32
HIGH = BINS // LOW
GROUP = 8
CHUNK = 64
MAX_LEN = 1024

lasso_penalty = 1.0
ridge_penalty = 1.0
shrinkage = 0.1

VMEM_LIMIT = 48 * 1024 * 1024
F32 = jnp.float32
BF16 = jnp.bfloat16
NT = (((1,), (1,)), ((), ()))


def iota(shape, axis):
    return lax.broadcasted_iota(jnp.int32, shape, axis)


def vmem():
    return pl.BlockSpec(memory_space=pltpu.VMEM)


def smem():
    return pl.BlockSpec(memory_space=pltpu.SMEM)


def prepare_kernel(feat_count, masks, len_ref, pos_ref, lab_ref, owner_ref, score_ref, leaf_ref,
                   kept_ref, leaf_out, qid_ref, worth_ref, inv_ref, perm_ref, bounds_ref):
    kept_ref[...] = score_ref[...]
    leaf_out[...] = leaf_ref[...]
    queries = len_ref.shape[1]
    rows = lab_ref.shape[0]
    own = rows // feat_count
    spot = iota((rows, LANES), 0) * LANES + iota((rows, LANES), 1)
    qid = jnp.zeros((rows, LANES), F32)
    begin = jnp.zeros((queries, LANES), jnp.int32)
    finish = jnp.zeros((queries, LANES), jnp.int32)
    which = iota((queries, LANES), 0)
    group = iota((1, LANES), 1) * LANES
    low = jnp.zeros((1, LANES), jnp.int32)
    high = first_end = jnp.full((1, LANES), rows * LANES, jnp.int32)
    start = jnp.int32(0)
    for q in range(queries):
        end = start + len_ref[0, q]
        qid = qid + jnp.where(spot >= end, 1.0, 0.0)
        begin = jnp.where(which == q, start, begin)
        finish = jnp.where(which == q, end, finish)

        low = low + jnp.where(end <= group, len_ref[0, q], 0)
        high = jnp.minimum(high, jnp.where(end >= group + LANES, end, rows * LANES))
        first_end = jnp.minimum(first_end, jnp.where(end > group, end, rows * LANES))
        start = end
    bounds_ref[...] = jnp.concatenate([low, high, first_end, low, low, low, low, low], axis=0)
    qid_ref[...] = qid
    worth_ref[...] = jnp.left_shift(1, lab_ref[...]).astype(F32)

    counts = [jnp.zeros((queries, LANES), F32) for _ in range(GRADES)]
    lane = iota((queries, LANES), 1)
    for r in range(rows):
        at = lane + r * LANES
        inside = (at >= begin) & (at < finish)
        grade = jnp.where(inside, jnp.broadcast_to(lab_ref[r:r + 1, :], (queries, LANES)), 0)
        for g in range(GRADES):
            counts[g] = counts[g] + jnp.where(grade > g, 1.0, 0.0)
    position = iota((queries, MAX_LEN), 1).astype(F32)
    gain = jnp.zeros((queries, MAX_LEN), F32)
    for g in range(GRADES):
        held = jnp.sum(counts[g], axis=1, keepdims=True)
        gain = gain + jnp.where(position < held, float(2 ** g), 0.0)
    level = 1.0 / jnp.log2(2.0 + position[0:1, :])
    ideal = jnp.sum(gain * level, axis=1, keepdims=True)
    usable = ideal > 0.5
    inverse = jnp.where(usable, 1.0 / jnp.where(usable, ideal, 1.0), 0.0)
    first = pos_ref[0] % feat_count * own
    for t in range(own):
        at = lane + (first + t) * LANES
        inside = (at >= begin) & (at < finish)
        inv_ref[0:1, t * LANES:(t + 1) * LANES] = jnp.sum(jnp.where(inside, inverse, 0.0), axis=0, keepdims=True)

    features = perm_ref.shape[0]
    per_dev = features >> len(masks)
    owner = jnp.concatenate([owner_ref[k:k + 1, :] for k in range(features // LANES)], axis=1)
    square = (features, features)
    down, across = iota(square, 0), iota(square, 1)
    index = iota((features, 1), 0) // per_dev
    target = jnp.zeros((features, 1), jnp.int32)
    for b, mask in enumerate(masks):
        target = target + ((index >> b) & 1) * mask
    target = (target ^ pos_ref[0]) * per_dev + iota((features, 1), 0) % per_dev
    pick = jnp.where(target == across, 1.0, 0.0).astype(BF16)
    holds = jnp.where(jnp.broadcast_to(owner, square) == down, 1.0, 0.0).astype(BF16)
    perm_ref[...] = lax.dot_general(pick, holds, NT, preferred_element_type=F32).astype(BF16)


def prepare(feat_count, masks, lengths, pos, labels, owner, scores, leaves):
    rows = labels.shape[0]
    features = owner.shape[0] * LANES
    return pl.pallas_call(
        functools.partial(prepare_kernel, feat_count, masks),
        out_shape=(
            jax.ShapeDtypeStruct(scores.shape, F32),
            jax.ShapeDtypeStruct(leaves.shape, jnp.int32),
            jax.ShapeDtypeStruct((rows, LANES), F32),
            jax.ShapeDtypeStruct((rows, LANES), F32),
            jax.ShapeDtypeStruct((1, rows // feat_count * LANES), F32),
            jax.ShapeDtypeStruct((features, features), BF16),
            jax.ShapeDtypeStruct((8, LANES), jnp.int32),
        ),
        in_specs=[smem(), smem(), vmem(), vmem(), vmem(), vmem()],
        out_specs=(vmem(),) * 7,
        compiler_params=pltpu.CompilerParams(vmem_limit_bytes=VMEM_LIMIT),
        cost_estimate=pl.CostEstimate(flops=2_000_000_000, bytes_accessed=300_000, transcendentals=20_000),
        name="prepare",
    )(lengths, pos, labels, owner, scores, leaves)


def split_terms(value, terms):
    parts = []
    rest = value
    for _ in range(terms):
        part = rest.astype(BF16)
        parts.append(part)
        rest = rest - part.astype(F32)
    return parts


def pairs_kernel(feat_count, bounds_ref, pos_ref, *refs):
    scores = refs[:-15]
    (worth_ref, qid_ref, inv_ref, lam_ref,
     s_row, a_row, d_row, turn, s_col, a_col, w_col, q_col, d_col, grad, curv) = refs[-15:]
    rows = worth_ref.shape[0]
    own = rows // feat_count
    docs = own * LANES
    me = pos_ref[0] % feat_count
    s_row[...] = jnp.zeros(s_row.shape, F32)
    near = [me, ((me + 1) ^ 1) - 1, me ^ 1]
    for where, ref in zip(near, scores):
        @pl.when((where >= 0) & (where < feat_count))
        def _(where=where, ref=ref):
            s_row[pl.ds(pl.multiple_of(where * own, own), own), :] = ref[...]
    a_row[...] = jnp.exp(s_row[...])
    d_row[...] = jnp.zeros(d_row.shape, F32)
    first = me * own
    window_low = bounds_ref[0, first] // (2 * LANES) * 2
    window_high = (bounds_ref[1, first + own - 1] + 2 * LANES - 1) // (2 * LANES) * 2
    stride = 4

    def widen(pairs):
        lines = jnp.concatenate([source[...] for source, _ in pairs], axis=0)
        if lines.shape[0] % LANES:
            lines = jnp.concatenate([lines, jnp.zeros((LANES - lines.shape[0] % LANES, LANES), F32)], axis=0)
        for k in range(lines.shape[0] // LANES):
            turn[:, k * LANES:(k + 1) * LANES] = jnp.transpose(lines[k * LANES:(k + 1) * LANES])
        for r in range(0, rows, stride):
            @pl.when((r + stride > window_low) & (r < window_high))
            def _(r=r):
                for k, (_, col) in enumerate(pairs):
                    for m in range(r, r + stride):
                        at = k * rows + m
                        col[m * LANES:(m + 1) * LANES, :] = jnp.broadcast_to(turn[:, at:at + 1], (LANES, LANES))

    widen([(s_row, s_col), (qid_ref, q_col), (a_row, a_col), (worth_ref, w_col)])

    def rows_of(ref, r):
        return [jnp.broadcast_to(ref[pl.ds(r + g, 1), :], (8, LANES)) for g in range(2)]

    per = LANES // CHUNK

    def spans(r):
        start, end = bounds_ref[0, r], bounds_ref[1, r + 1]
        low = jnp.maximum(start // CHUNK, per * window_low)
        high = jnp.minimum((end + CHUNK - 1) // CHUNK, per * window_high)
        single = bounds_ref[2, r] >= (r + 2) * LANES
        inner_low = jnp.maximum((start + LANES - 1) // LANES, window_low)
        inner_high = jnp.minimum(end // LANES, window_high)
        return low, high, single, inner_low, inner_high

    def rank_groups(k, carry):
        r = window_low + 2 * k
        score = rows_of(s_row, r)
        query = rows_of(qid_ref, r)

        def gather(c, acc, masked, test):
            size = CHUNK if masked else LANES
            base = pl.multiple_of(c * size, size)
            acc = list(acc)
            for u in range(size // 8):
                other = s_col[pl.ds(base + 8 * u, 8), :]
                for g in range(2):
                    hit = test(other, g, u)
                    if masked:
                        hit = hit & (q_col[pl.ds(base + 8 * u, 8), :] == query[g])
                    k = 4 * g + u % 4
                    acc[k] = acc[k] + jnp.where(hit, 1.0, 0.0)
            return tuple(acc)

        def ahead(other, g, u):
            return other >= score[g]

        def behind(other, g, u):
            return other > score[g]

        def within(mine, offset):
            def test(other, g, u):
                if g != mine:
                    return ahead(other, g, u) if mine < g else behind(other, g, u)
                earlier = iota((8, LANES), 0) + (offset + 8 * u) < iota((8, LANES), 1)
                return (other > score[g]) | ((other == score[g]) & earlier)
            return test

        def twice(low, high, test, acc):
            twos = (high - low) // 2
            acc = lax.fori_loop(0, twos, lambda k, acc: gather(
                low + 2 * k + 1, gather(low + 2 * k, acc, False, test), False, test), acc)
            return lax.fori_loop(low + 2 * twos, high, lambda c, acc: gather(c, acc, False, test), acc)

        acc = tuple(jnp.zeros((8, LANES), F32) for _ in range(8))
        low, high, single, inner_low, inner_high = spans(r)
        inner_low = jnp.where(single, inner_low, r)
        after = jnp.where(single, inner_high, r + 2)
        acc = lax.fori_loop(low, per * inner_low, lambda c, acc: gather(c, acc, True, ahead), acc)
        acc = twice(inner_low, r, ahead, acc)
        acc = twice(r + 2, after, behind, acc)
        acc = lax.fori_loop(per * after, high, lambda c, acc: gather(c, acc, True, behind), acc)
        for c in range(2 * per):
            acc = gather(per * r + c, acc, True, within(c // per, c % per * CHUNK))
        for g in range(2):
            total = (acc[4 * g] + acc[4 * g + 1]) + (acc[4 * g + 2] + acc[4 * g + 3])
            d_row[pl.ds(r + g, 1), :] = jnp.sum(total, axis=0, keepdims=True)
        return carry

    lax.fori_loop(0, (window_high - window_low) // 2, rank_groups, 0)
    d_row[...] = 1.0 / jnp.log2(2.0 + d_row[...])
    widen([(d_row, d_col)])

    def pair_groups(t, carry):
        r = first + 2 * t
        a_i, w_i, d_i, query = [rows_of(ref, r) for ref in (a_row, worth_ref, d_row, qid_ref)]

        def columns(masked):
            def step(c, acc):
                size = CHUNK if masked else LANES
                base = pl.multiple_of(c * size, size)
                acc = list(acc)
                for u in range(size // 8):
                    at = pl.ds(base + 8 * u, 8)
                    a_j, w_j, d_j = a_col[at, :], w_col[at, :], d_col[at, :]
                    for g in range(2):
                        recip = pl.reciprocal(a_i[g] + a_j, approx=True)
                        lift = w_i[g] - w_j
                        weight = jnp.abs(d_i[g] - d_j) * recip
                        if masked:
                            weight = jnp.where(q_col[at, :] == query[g], weight, 0.0)
                        weight = weight * lift
                        k = 4 * g + u % 2
                        acc[k] = acc[k] + weight * jnp.where(lift > 0.0, a_j, a_i[g])
                        acc[k + 2] = acc[k + 2] + jnp.abs(weight) * (recip * a_j)
                return tuple(acc)
            return step

        def twice(low, high, step, acc):
            twos = (high - low) // 2
            acc = lax.fori_loop(0, twos, lambda k, acc: step(low + 2 * k + 1, step(low + 2 * k, acc)), acc)
            return lax.fori_loop(low + 2 * twos, high, step, acc)

        acc = tuple(jnp.zeros((8, LANES), F32) for _ in range(8))
        low, high, single, inner_low, inner_high = spans(r)
        acc = lax.fori_loop(low, jnp.where(single, per * inner_low, low), columns(True), acc)
        acc = twice(inner_low, jnp.where(single, inner_high, inner_low), columns(False), acc)
        acc = twice(jnp.where(single, per * inner_high, low), high, columns(True), acc)
        for g in range(2):
            at = pl.ds(2 * t + g, 1)
            grad[at, :] = -jnp.sum(acc[4 * g] + acc[4 * g + 1], axis=0, keepdims=True)
            curv[at, :] = a_i[g][0:1, :] * jnp.sum(acc[4 * g + 2] + acc[4 * g + 3], axis=0, keepdims=True)
        return carry

    lax.fori_loop(0, own // 2, pair_groups, 0)
    inverse = inv_ref[...]
    terms = [inverse * jnp.concatenate([ref[t:t + 1, :] for t in range(own)], axis=1) for ref in (grad, curv)]
    for c in range(2):
        lam_ref[c:c + 1, :] = terms[c]


def pair_terms(feat_count, bounds, pos, scores, worth, qid, inverse):
    rows = worth.shape[0]
    docs = inverse.shape[1]
    row = pltpu.VMEM((rows, LANES), F32)
    turn = pltpu.VMEM((LANES, 4 * rows), F32)
    col = pltpu.VMEM((rows * LANES, LANES), F32)
    mine = pltpu.VMEM((docs // LANES, LANES), F32)
    return pl.pallas_call(
        functools.partial(pairs_kernel, feat_count),
        out_shape=jax.ShapeDtypeStruct((2, docs), F32),
        in_specs=[smem(), smem()] + [vmem()] * (len(scores) + 3),
        out_specs=vmem(),
        scratch_shapes=[row, row, row, turn, col, col, col, col, col, mine, mine],
        compiler_params=pltpu.CompilerParams(vmem_limit_bytes=VMEM_LIMIT),
        cost_estimate=pl.CostEstimate(flops=9_000_000_000, bytes_accessed=200_000, transcendentals=2_000_000),
        name="pair_terms",
    )(bounds, pos, *scores, worth, qid, inverse)


def leaf_kernel(perm_ref, bins_ref, leaf_ref, lam_ref, bins_t_ref, tile_ref, sums_ref):
    bins = bins_ref[...].astype(F32).astype(BF16)
    bins_t_ref[...] = lax.dot_general(perm_ref[...], bins, NT, preferred_element_type=F32)
    own = leaf_ref.shape[0]
    docs = own * LANES
    leaf = jnp.concatenate([leaf_ref[t:t + 1, :] for t in range(own)], axis=1)
    highs = LEAVES // LANES
    top = jnp.broadcast_to(leaf // LANES, (highs, docs)) == iota((highs, docs), 0)
    spots = jnp.where(jnp.broadcast_to(leaf % LANES, (LANES, docs)) == iota((LANES, docs), 0), 1.0, 0.0).astype(BF16)
    pieces, tiles = [], []
    for c in range(2):
        for k, part in enumerate(split_terms(lam_ref[c:c + 1, :], 3)):
            wide = jnp.broadcast_to(part.astype(F32), (highs, docs))
            pieces.append(jnp.where(top, wide, 0.0))
            if k < 2:
                tiles.append(wide)
    tile_ref[...] = jnp.concatenate(tiles, axis=0).astype(BF16)
    stacked = jnp.concatenate(pieces, axis=0).astype(BF16)
    sums = lax.dot_general(stacked, spots, NT, preferred_element_type=F32)
    for c in range(2):
        base = c * 3 * highs
        sums_ref[:, c * LANES:(c + 1) * LANES] = (
            sums[base:base + highs] + (sums[base + highs:base + 2 * highs] + sums[base + 2 * highs:base + 3 * highs])
        )


def leaf_terms(perm, bins, leaves, lambdas):
    docs, features = bins.shape
    return pl.pallas_call(
        leaf_kernel,
        out_shape=(
            jax.ShapeDtypeStruct((features, docs), F32),
            jax.ShapeDtypeStruct((4 * HIGH, docs), BF16),
            jax.ShapeDtypeStruct((LEAVES // LANES, 2 * LANES), F32),
        ),
        in_specs=[vmem()] * 4,
        out_specs=(vmem(), vmem(), vmem()),
        compiler_params=pltpu.CompilerParams(vmem_limit_bytes=VMEM_LIMIT),
        cost_estimate=pl.CostEstimate(flops=200_000_000, bytes_accessed=3_000_000, transcendentals=0),
        name="leaf_terms",
    )(perm, bins, leaves, lambdas)


def histogram_kernel(first, groups, tile_ref, bins_ref, *refs):
    out_ref = refs[-1]
    docs = tile_ref.shape[1]
    depth = docs
    rows = 16
    row = iota((rows, depth), 0)
    low_level = [(row + rows * k).astype(F32).astype(BF16) for k in range(LOW // rows)]
    high_level = (row % HIGH).astype(F32).astype(BF16)
    upper = jnp.where(row < HIGH, 1.0, 0.0).astype(BF16) > 0
    zero = jnp.zeros((rows, depth), BF16)
    one = jnp.ones((rows, depth), BF16)
    lane_owner = iota((1, GROUP * LOW), 1) // LOW

    def one_group(g, carry):
        base = pl.multiple_of((first + g) * GROUP, GROUP)
        acc = None
        for k in range(docs // depth):
            span = slice(k * depth, (k + 1) * depth)
            code = bins_ref[pl.ds(base, GROUP), span]
            high = jnp.floor(code * (1.0 / LOW))
            low = code - high * LOW
            left, right, count = [], [], []
            wide = []
            for f in range(GROUP):
                high_f = jnp.broadcast_to(high[f:f + 1, :], (rows, depth))
                low_f = jnp.broadcast_to(low[f:f + 1, :], (rows, depth)).astype(BF16)
                high_f = high_f.astype(BF16)
                wide.append(high_f)
                match = high_f == high_level
                for c in range(2):
                    left.append(jnp.where(match, tile_ref[c * rows:(c + 1) * rows, span], zero))
                for level in low_level:
                    right.append(jnp.where(low_f == level, one, zero))
            for f in range(0, GROUP, 2):
                both = jnp.where(upper, wide[f], wide[f + 1])
                count.append(jnp.where(both == high_level, one, zero))
            part = lax.dot_general(
                jnp.concatenate(left + count, axis=0), jnp.concatenate(right, axis=0), NT,
                preferred_element_type=F32,
            )
            acc = part if acc is None else acc + part
        stats = jnp.zeros((2 * rows, GROUP * LOW), F32)
        counts = jnp.zeros((HIGH, GROUP * LOW), F32)
        for f in range(GROUP):
            mine = lane_owner == f
            stats = jnp.where(mine, acc[f * 2 * rows:(f + 1) * 2 * rows], stats)
            at = GROUP * 2 * rows + f * HIGH
            counts = jnp.where(mine, acc[at:at + HIGH], counts)
        out_ref[pl.ds(pl.multiple_of(g * 3 * HIGH, 3 * HIGH), 3 * HIGH), :] = jnp.concatenate(
            [stats[0:HIGH] + stats[HIGH:2 * HIGH], stats[2 * HIGH:3 * HIGH] + stats[3 * HIGH:4 * HIGH], counts], axis=0)
        return carry

    if len(refs) > 1:
        out_ref[groups * 3 * HIGH:, :] = refs[0][...]
    lax.fori_loop(0, groups, one_group, 0, unroll=min(groups, 8))


def histogram_part(first, groups, tiles, bins_t, *tail):
    rows = groups * 3 * HIGH + sum(piece.shape[0] for piece in tail)
    return pl.pallas_call(
        functools.partial(histogram_kernel, first, groups),
        out_shape=jax.ShapeDtypeStruct((rows, GROUP * LOW), F32),
        in_specs=[vmem()] * (2 + len(tail)),
        out_specs=vmem(),
        compiler_params=pltpu.CompilerParams(vmem_limit_bytes=VMEM_LIMIT),
        cost_estimate=pl.CostEstimate(flops=groups * 1_000_000, bytes_accessed=groups * 1_000, transcendentals=0),
        name="histogram_part",
    )(tiles, bins_t, *tail)


def finish_kernel(per_dev, lam_ref, leaf_ref, kept_ref, sums_ref, *refs):
    arrived = list(refs[1::-1]) + list(refs[2:-4])
    lam_out, value_ref, step_ref, hist_ref = refs[-4:]
    lam_out[...] = lam_ref[...]
    unit = kept_ref.shape[0]
    totals = add_up([sums_ref[...]] + [ref[unit:, :] for ref in arrived])
    highs = LEAVES // LANES
    grad, curv = totals[:, :LANES], totals[:, LANES:]
    shrunk = jnp.maximum(jnp.abs(grad) - lasso_penalty, 0.0)
    values = jnp.where(grad > 0.0, -shrunk, shrunk) / (curv + ridge_penalty)
    value_ref[...] = values
    leaf = leaf_ref[...]
    top, spot = leaf // LANES, leaf % LANES
    step = jnp.zeros(leaf.shape, F32)
    for h in range(highs):
        row = jnp.broadcast_to(values[h:h + 1, :], leaf.shape)
        step = jnp.where(top == h, jnp.take_along_axis(row, spot, axis=1), step)
    step_ref[...] = shrinkage * step
    hist = add_up([kept_ref[...]] + [ref[:unit, :] for ref in arrived])
    if per_dev == GROUP:
        shape = hist.shape
        line, place = iota(shape, 0), iota(shape, 1) // LOW
        step = 1
        while step < GROUP:
            down, across = (line // step) % 2, (place // step) % 2
            shift = step * LOW
            ahead = pltpu.roll(pltpu.roll(hist, shape[0] - step, 0), shift, 1)
            behind = pltpu.roll(pltpu.roll(hist, step, 0), shape[1] - shift, 1)
            hist = jnp.where(down == across, hist, jnp.where(across == 1, ahead, behind))
            step *= 2
        for c in range(3):
            for f in range(GROUP):
                hist_ref[c:c + 1, f * BINS:(f + 1) * BINS] = hist[c * HIGH + f:c * HIGH + f + 1, :]
    else:
        hist_ref[...] = hist


def finish(per_dev, lambdas, leaves, kept, sums, arrived):
    out = (3, per_dev * BINS) if per_dev == GROUP else kept.shape
    return pl.pallas_call(
        functools.partial(finish_kernel, per_dev),
        out_shape=(
            jax.ShapeDtypeStruct(lambdas.shape, F32),
            jax.ShapeDtypeStruct((LEAVES // LANES, LANES), F32),
            jax.ShapeDtypeStruct(leaves.shape, F32),
            jax.ShapeDtypeStruct(out, F32),
        ),
        in_specs=[vmem()] * (4 + len(arrived)),
        out_specs=(vmem(),) * 4,
        compiler_params=pltpu.CompilerParams(vmem_limit_bytes=VMEM_LIMIT),
        name="finish",
    )(lambdas, leaves, kept, sums, *arrived)


def add_up(parts):
    while len(parts) > 1:
        parts = [parts[k] + parts[k + 1] for k in range(0, len(parts), 2)]
    return parts[0]


def local(scores, labels, leaves, bins, lengths, owner):
    query_count = lax.axis_size("query")
    feat_count = lax.axis_size("feat")
    count = query_count * feat_count
    place = lax.axis_index("query").astype(jnp.int32) * feat_count + lax.axis_index("feat").astype(jnp.int32)
    docs = scores.shape[0]
    own = docs // LANES
    features = owner.shape[0]
    per_dev = features // count
    unit = 3 * per_dev
    axes = ("query", "feat")
    feat_masks = [1 << b for b in range(feat_count.bit_length() - 1)]
    query_masks = [feat_count << b for b in range(query_count.bit_length() - 1)]

    def swap(value, mask):
        return lax.ppermute(value, axes, [(p, p ^ mask) for p in range(count)])

    pos = place.reshape(1)
    leaf_rows = leaves.reshape(own, LANES)
    own_scores = scores.reshape(own, LANES)
    score_parts = [own_scores]
    def inner_partner(p):
        z = p % feat_count
        if z in (0, feat_count - 1):
            return p ^ query_masks[0]
        return p + 1 if z % 2 else p - 1

    score_parts.append(lax.ppermute(own_scores, axes, [(p, inner_partner(p)) for p in range(count)]))
    score_parts.append(swap(own_scores, 1))
    masks = feat_masks + query_masks[:0:-1] + query_masks[:1]
    score_parts[0], leaf_rows, qid, worth, inverse, perm, bounds = prepare(
        feat_count, masks, lengths, pos, labels.reshape(-1, LANES), owner.reshape(-1, LANES), own_scores, leaf_rows)
    lambdas = pair_terms(feat_count, bounds, pos, score_parts, worth, qid, inverse)
    bins_t, tiles, sums = leaf_terms(perm, bins, leaf_rows, lambdas)

    def part(tiles, low, high, *tail):
        if per_dev == GROUP:
            return histogram_part(low, high - low, tiles, bins_t, *tail)
        groups = high - low
        wide = histogram_part(low, groups, tiles, bins_t)
        wide = wide.reshape(groups, 3, HIGH, GROUP // per_dev, per_dev, LOW).transpose(0, 3, 1, 4, 2, 5)
        return jnp.concatenate([wide.reshape(groups * GROUP // per_dev * unit, BINS), *tail], axis=0)

    def join(block, total):
        return jnp.concatenate([block, total], axis=0)

    eighth = features // GROUP // 8
    edge = count // 8 * unit
    arrived = swap(part(tiles, 7 * eighth, 8 * eighth, sums), query_masks[0])
    block = part(tiles, 3 * eighth, 4 * eighth) + arrived[:edge]
    sums = sums + arrived[edge:]
    message, tiles = lax.optimization_barrier((join(block, sums), tiles))
    crossed_far = swap(message, query_masks[1])
    arrived = swap(part(tiles, 5 * eighth, 7 * eighth), query_masks[0])
    both = part(tiles, eighth, 3 * eighth) + arrived
    sums = sums + crossed_far[edge:]
    message, rest, tiles = lax.optimization_barrier(
        (join(both[:edge] + crossed_far[:edge], sums), join(both[edge:], sums), tiles))
    turned = swap(message, query_masks[2])
    crossed_near = swap(rest, query_masks[1])
    arrived = swap(part(tiles, 4 * eighth, 5 * eighth), query_masks[0])
    kept = part(tiles, 0, eighth) + arrived + crossed_near[:edge] + turned[:edge]
    sums = sums + turned[edge:]
    for mask in query_masks[3:]:
        edge = edge // 2
        arrived = swap(join(kept[edge:], sums), mask)
        kept = kept[:edge] + arrived[:edge]
        sums = sums + arrived[edge:]
    arrived = [swap(join(kept[m * unit:(m + 1) * unit], sums), m) for m in range(1, feat_count)]
    arrived[:2] = arrived[1::-1]
    lambdas, values, step, histograms = finish(per_dev, lambdas, leaf_rows, kept[:unit], sums, arrived)
    return lambdas, values.reshape(LEAVES), step.reshape(docs), histograms.reshape(3, per_dev * BINS)


def solution(mesh):
    in_specs = (
        P(("query", "feat")),
        P("query"),
        P(("query", "feat")),
        P(("query", "feat"), None),
        P("query", None),
        P(),
    )
    out_specs = (P(None, ("query", "feat")), P(), P(("query", "feat")), P(None, ("query", "feat")))
    return jax.shard_map(local, mesh=mesh, in_specs=in_specs, out_specs=out_specs, check_vma=False)
```

```python
import functools

import jax
import jax.numpy as jnp
from jax import lax
from jax.experimental import pallas as pl
from jax.experimental.pallas import tpu as pltpu
from jax.sharding import PartitionSpec as P

BINS = 256
LEAVES = 1024
LANES = 128
GRADES = 4
LOW = 32
HIGH = BINS // LOW
GROUP = 8
CHUNK = 64
MAX_LEN = 1024

lasso_penalty = 1.0
ridge_penalty = 1.0
shrinkage = 0.1

VMEM_LIMIT = 48 * 1024 * 1024
F32 = jnp.float32
BF16 = jnp.bfloat16
NT = (((1,), (1,)), ((), ()))


def iota(shape, axis):
    return lax.broadcasted_iota(jnp.int32, shape, axis)


def vmem():
    return pl.BlockSpec(memory_space=pltpu.VMEM)


def smem():
    return pl.BlockSpec(memory_space=pltpu.SMEM)


def prepare_kernel(feat_count, masks, len_ref, pos_ref, lab_ref, owner_ref, score_ref, leaf_ref,
                   kept_ref, leaf_out, qid_ref, worth_ref, inv_ref, perm_ref, bounds_ref):
    kept_ref[...] = score_ref[...]
    leaf_out[...] = leaf_ref[...]
    queries = len_ref.shape[1]
    rows = lab_ref.shape[0]
    own = rows // feat_count
    spot = iota((rows, LANES), 0) * LANES + iota((rows, LANES), 1)
    qid = jnp.zeros((rows, LANES), F32)
    begin = jnp.zeros((queries, LANES), jnp.int32)
    finish = jnp.zeros((queries, LANES), jnp.int32)
    which = iota((queries, LANES), 0)
    group = iota((1, LANES), 1) * LANES
    low = jnp.zeros((1, LANES), jnp.int32)
    high = first_end = jnp.full((1, LANES), rows * LANES, jnp.int32)
    start = jnp.int32(0)
    for q in range(queries):
        end = start + len_ref[0, q]
        qid = qid + jnp.where(spot >= end, 1.0, 0.0)
        begin = jnp.where(which == q, start, begin)
        finish = jnp.where(which == q, end, finish)

        low = low + jnp.where(end <= group, len_ref[0, q], 0)
        high = jnp.minimum(high, jnp.where(end >= group + LANES, end, rows * LANES))
        first_end = jnp.minimum(first_end, jnp.where(end > group, end, rows * LANES))
        start = end
    bounds_ref[...] = jnp.concatenate([low, high, first_end, low, low, low, low, low], axis=0)
    qid_ref[...] = qid
    worth_ref[...] = jnp.left_shift(1, lab_ref[...]).astype(F32)

    counts = [jnp.zeros((queries, LANES), F32) for _ in range(GRADES)]
    lane = iota((queries, LANES), 1)
    for r in range(rows):
        at = lane + r * LANES
        inside = (at >= begin) & (at < finish)
        grade = jnp.where(inside, jnp.broadcast_to(lab_ref[r:r + 1, :], (queries, LANES)), 0)
        for g in range(GRADES):
            counts[g] = counts[g] + jnp.where(grade > g, 1.0, 0.0)
    position = iota((queries, MAX_LEN), 1).astype(F32)
    gain = jnp.zeros((queries, MAX_LEN), F32)
    for g in range(GRADES):
        held = jnp.sum(counts[g], axis=1, keepdims=True)
        gain = gain + jnp.where(position < held, float(2 ** g), 0.0)
    level = 1.0 / jnp.log2(2.0 + position[0:1, :])
    ideal = jnp.sum(gain * level, axis=1, keepdims=True)
    usable = ideal > 0.5
    inverse = jnp.where(usable, 1.0 / jnp.where(usable, ideal, 1.0), 0.0)
    first = pos_ref[0] % feat_count * own
    for t in range(own):
        at = lane + (first + t) * LANES
        inside = (at >= begin) & (at < finish)
        inv_ref[0:1, t * LANES:(t + 1) * LANES] = jnp.sum(jnp.where(inside, inverse, 0.0), axis=0, keepdims=True)

    features = perm_ref.shape[0]
    per_dev = features >> len(masks)
    owner = jnp.concatenate([owner_ref[k:k + 1, :] for k in range(features // LANES)], axis=1)
    square = (features, features)
    down, across = iota(square, 0), iota(square, 1)
    index = iota((features, 1), 0) // per_dev
    target = jnp.zeros((features, 1), jnp.int32)
    for b, mask in enumerate(masks):
        target = target + ((index >> b) & 1) * mask
    target = (target ^ pos_ref[0]) * per_dev + iota((features, 1), 0) % per_dev
    pick = jnp.where(target == across, 1.0, 0.0).astype(BF16)
    holds = jnp.where(jnp.broadcast_to(owner, square) == down, 1.0, 0.0).astype(BF16)
    perm_ref[...] = lax.dot_general(pick, holds, NT, preferred_element_type=F32).astype(BF16)


def prepare(feat_count, masks, lengths, pos, labels, owner, scores, leaves):
    rows = labels.shape[0]
    features = owner.shape[0] * LANES
    return pl.pallas_call(
        functools.partial(prepare_kernel, feat_count, masks),
        out_shape=(
            jax.ShapeDtypeStruct(scores.shape, F32),
            jax.ShapeDtypeStruct(leaves.shape, jnp.int32),
            jax.ShapeDtypeStruct((rows, LANES), F32),
            jax.ShapeDtypeStruct((rows, LANES), F32),
            jax.ShapeDtypeStruct((1, rows // feat_count * LANES), F32),
            jax.ShapeDtypeStruct((features, features), BF16),
            jax.ShapeDtypeStruct((8, LANES), jnp.int32),
        ),
        in_specs=[smem(), smem(), vmem(), vmem(), vmem(), vmem()],
        out_specs=(vmem(),) * 7,
        compiler_params=pltpu.CompilerParams(vmem_limit_bytes=VMEM_LIMIT),
        cost_estimate=pl.CostEstimate(flops=2_000_000_000, bytes_accessed=300_000, transcendentals=20_000),
        name="prepare",
    )(lengths, pos, labels, owner, scores, leaves)


def split_terms(value, terms):
    parts = []
    rest = value
    for _ in range(terms):
        part = rest.astype(BF16)
        parts.append(part)
        rest = rest - part.astype(F32)
    return parts


def pairs_kernel(feat_count, bounds_ref, pos_ref, *refs):
    scores = refs[:-15]
    (worth_ref, qid_ref, inv_ref, lam_ref,
     s_row, a_row, d_row, turn, s_col, a_col, w_col, q_col, d_col, grad, curv) = refs[-15:]
    rows = worth_ref.shape[0]
    own = rows // feat_count
    docs = own * LANES
    me = pos_ref[0] % feat_count
    s_row[...] = jnp.zeros(s_row.shape, F32)
    near = [me, ((me + 1) ^ 1) - 1, me ^ 1]
    for where, ref in zip(near, scores):
        @pl.when((where >= 0) & (where < feat_count))
        def _(where=where, ref=ref):
            s_row[pl.ds(pl.multiple_of(where * own, own), own), :] = ref[...]
    a_row[...] = jnp.exp(s_row[...])
    d_row[...] = jnp.zeros(d_row.shape, F32)
    first = me * own
    window_low = bounds_ref[0, first] // (2 * LANES) * 2
    window_high = (bounds_ref[1, first + own - 1] + 2 * LANES - 1) // (2 * LANES) * 2
    stride = 2

    def widen(pairs):
        lines = jnp.concatenate([source[...] for source, _ in pairs], axis=0)
        if lines.shape[0] % LANES:
            lines = jnp.concatenate([lines, jnp.zeros((LANES - lines.shape[0] % LANES, LANES), F32)], axis=0)
        for k in range(lines.shape[0] // LANES):
            turn[:, k * LANES:(k + 1) * LANES] = jnp.transpose(lines[k * LANES:(k + 1) * LANES])
        for r in range(0, rows, stride):
            @pl.when((r + stride > window_low) & (r < window_high))
            def _(r=r):
                for k, (_, col) in enumerate(pairs):
                    for m in range(r, r + stride):
                        at = k * rows + m
                        col[m * LANES:(m + 1) * LANES, :] = jnp.broadcast_to(turn[:, at:at + 1], (LANES, LANES))

    widen([(s_row, s_col), (qid_ref, q_col), (a_row, a_col), (worth_ref, w_col)])

    def rows_of(ref, r):
        return [jnp.broadcast_to(ref[pl.ds(r + g, 1), :], (8, LANES)) for g in range(2)]

    per = LANES // CHUNK

    def spans(r):
        start, end = bounds_ref[0, r], bounds_ref[1, r + 1]
        low = jnp.maximum(start // CHUNK, per * window_low)
        high = jnp.minimum((end + CHUNK - 1) // CHUNK, per * window_high)
        single = bounds_ref[2, r] >= (r + 2) * LANES
        inner_low = jnp.maximum((start + LANES - 1) // LANES, window_low)
        inner_high = jnp.minimum(end // LANES, window_high)
        return low, high, single, inner_low, inner_high

    def rank_groups(k, carry):
        r = window_low + 2 * k
        score = rows_of(s_row, r)
        query = rows_of(qid_ref, r)

        def gather(c, acc, masked, test):
            size = CHUNK if masked else LANES
            base = pl.multiple_of(c * size, size)
            acc = list(acc)
            for u in range(size // 8):
                other = s_col[pl.ds(base + 8 * u, 8), :]
                for g in range(2):
                    hit = test(other, g, u)
                    if masked:
                        hit = hit & (q_col[pl.ds(base + 8 * u, 8), :] == query[g])
                    k = 4 * g + u % 4
                    acc[k] = acc[k] + jnp.where(hit, 1.0, 0.0)
            return tuple(acc)

        def ahead(other, g, u):
            return other >= score[g]

        def behind(other, g, u):
            return other > score[g]

        def within(mine, offset):
            def test(other, g, u):
                if g != mine:
                    return ahead(other, g, u) if mine < g else behind(other, g, u)
                earlier = iota((8, LANES), 0) + (offset + 8 * u) < iota((8, LANES), 1)
                return (other > score[g]) | ((other == score[g]) & earlier)
            return test

        def twice(low, high, test, acc):
            twos = (high - low) // 2
            acc = lax.fori_loop(0, twos, lambda k, acc: gather(
                low + 2 * k + 1, gather(low + 2 * k, acc, False, test), False, test), acc)
            return lax.fori_loop(low + 2 * twos, high, lambda c, acc: gather(c, acc, False, test), acc)

        acc = tuple(jnp.zeros((8, LANES), F32) for _ in range(8))
        low, high, single, inner_low, inner_high = spans(r)
        inner_low = jnp.where(single, inner_low, r)
        after = jnp.where(single, inner_high, r + 2)
        acc = lax.fori_loop(low, per * inner_low, lambda c, acc: gather(c, acc, True, ahead), acc)
        acc = twice(inner_low, r, ahead, acc)
        acc = twice(r + 2, after, behind, acc)
        acc = lax.fori_loop(per * after, high, lambda c, acc: gather(c, acc, True, behind), acc)
        for c in range(2 * per):
            acc = gather(per * r + c, acc, True, within(c // per, c % per * CHUNK))
        for g in range(2):
            total = (acc[4 * g] + acc[4 * g + 1]) + (acc[4 * g + 2] + acc[4 * g + 3])
            d_row[pl.ds(r + g, 1), :] = jnp.sum(total, axis=0, keepdims=True)
        return carry

    lax.fori_loop(0, (window_high - window_low) // 2, rank_groups, 0)
    d_row[...] = 1.0 / jnp.log2(2.0 + d_row[...])
    widen([(d_row, d_col)])

    def pair_groups(t, carry):
        r = first + 2 * t
        a_i, w_i, d_i, query = [rows_of(ref, r) for ref in (a_row, worth_ref, d_row, qid_ref)]

        def columns(masked):
            def step(c, acc):
                size = CHUNK if masked else LANES
                base = pl.multiple_of(c * size, size)
                acc = list(acc)
                for u in range(size // 8):
                    at = pl.ds(base + 8 * u, 8)
                    a_j, w_j, d_j = a_col[at, :], w_col[at, :], d_col[at, :]
                    for g in range(2):
                        recip = pl.reciprocal(a_i[g] + a_j, approx=True)
                        lift = w_i[g] - w_j
                        weight = jnp.abs(d_i[g] - d_j) * recip
                        if masked:
                            weight = jnp.where(q_col[at, :] == query[g], weight, 0.0)
                        weight = weight * lift
                        k = 4 * g + u % 2
                        acc[k] = acc[k] + weight * jnp.where(lift > 0.0, a_j, a_i[g])
                        acc[k + 2] = acc[k + 2] + jnp.abs(weight) * (recip * a_j)
                return tuple(acc)
            return step

        def twice(low, high, step, acc):
            twos = (high - low) // 2
            acc = lax.fori_loop(0, twos, lambda k, acc: step(low + 2 * k + 1, step(low + 2 * k, acc)), acc)
            return lax.fori_loop(low + 2 * twos, high, step, acc)

        acc = tuple(jnp.zeros((8, LANES), F32) for _ in range(8))
        low, high, single, inner_low, inner_high = spans(r)
        acc = lax.fori_loop(low, jnp.where(single, per * inner_low, low), columns(True), acc)
        acc = twice(inner_low, jnp.where(single, inner_high, inner_low), columns(False), acc)
        acc = twice(jnp.where(single, per * inner_high, low), high, columns(True), acc)
        for g in range(2):
            at = pl.ds(2 * t + g, 1)
            grad[at, :] = -jnp.sum(acc[4 * g] + acc[4 * g + 1], axis=0, keepdims=True)
            curv[at, :] = a_i[g][0:1, :] * jnp.sum(acc[4 * g + 2] + acc[4 * g + 3], axis=0, keepdims=True)
        return carry

    lax.fori_loop(0, own // 2, pair_groups, 0)
    inverse = inv_ref[...]
    terms = [inverse * jnp.concatenate([ref[t:t + 1, :] for t in range(own)], axis=1) for ref in (grad, curv)]
    for c in range(2):
        lam_ref[c:c + 1, :] = terms[c]


def pair_terms(feat_count, bounds, pos, scores, worth, qid, inverse):
    rows = worth.shape[0]
    docs = inverse.shape[1]
    row = pltpu.VMEM((rows, LANES), F32)
    turn = pltpu.VMEM((LANES, 4 * rows), F32)
    col = pltpu.VMEM((rows * LANES, LANES), F32)
    mine = pltpu.VMEM((docs // LANES, LANES), F32)
    return pl.pallas_call(
        functools.partial(pairs_kernel, feat_count),
        out_shape=jax.ShapeDtypeStruct((2, docs), F32),
        in_specs=[smem(), smem()] + [vmem()] * (len(scores) + 3),
        out_specs=vmem(),
        scratch_shapes=[row, row, row, turn, col, col, col, col, col, mine, mine],
        compiler_params=pltpu.CompilerParams(vmem_limit_bytes=VMEM_LIMIT),
        cost_estimate=pl.CostEstimate(flops=9_000_000_000, bytes_accessed=200_000, transcendentals=2_000_000),
        name="pair_terms",
    )(bounds, pos, *scores, worth, qid, inverse)


def leaf_kernel(perm_ref, bins_ref, leaf_ref, lam_ref, bins_t_ref, tile_ref, sums_ref):
    bins = bins_ref[...].astype(F32).astype(BF16)
    bins_t_ref[...] = lax.dot_general(perm_ref[...], bins, NT, preferred_element_type=F32)
    own = leaf_ref.shape[0]
    docs = own * LANES
    leaf = jnp.concatenate([leaf_ref[t:t + 1, :] for t in range(own)], axis=1)
    highs = LEAVES // LANES
    top = jnp.broadcast_to(leaf // LANES, (highs, docs)) == iota((highs, docs), 0)
    spots = jnp.where(jnp.broadcast_to(leaf % LANES, (LANES, docs)) == iota((LANES, docs), 0), 1.0, 0.0).astype(BF16)
    pieces, tiles = [], []
    for c in range(2):
        for k, part in enumerate(split_terms(lam_ref[c:c + 1, :], 3)):
            wide = jnp.broadcast_to(part.astype(F32), (highs, docs))
            pieces.append(jnp.where(top, wide, 0.0))
            if k < 2:
                tiles.append(wide)
    tile_ref[...] = jnp.concatenate(tiles, axis=0).astype(BF16)
    stacked = jnp.concatenate(pieces, axis=0).astype(BF16)
    sums = lax.dot_general(stacked, spots, NT, preferred_element_type=F32)
    for c in range(2):
        base = c * 3 * highs
        sums_ref[:, c * LANES:(c + 1) * LANES] = (
            sums[base:base + highs] + (sums[base + highs:base + 2 * highs] + sums[base + 2 * highs:base + 3 * highs])
        )


def leaf_terms(perm, bins, leaves, lambdas):
    docs, features = bins.shape
    return pl.pallas_call(
        leaf_kernel,
        out_shape=(
            jax.ShapeDtypeStruct((features, docs), F32),
            jax.ShapeDtypeStruct((4 * HIGH, docs), BF16),
            jax.ShapeDtypeStruct((LEAVES // LANES, 2 * LANES), F32),
        ),
        in_specs=[vmem()] * 4,
        out_specs=(vmem(), vmem(), vmem()),
        compiler_params=pltpu.CompilerParams(vmem_limit_bytes=VMEM_LIMIT),
        cost_estimate=pl.CostEstimate(flops=200_000_000, bytes_accessed=3_000_000, transcendentals=0),
        name="leaf_terms",
    )(perm, bins, leaves, lambdas)


def histogram_kernel(first, groups, tile_ref, bins_ref, *refs):
    out_ref = refs[-1]
    docs = tile_ref.shape[1]
    depth = docs
    rows = 16
    row = iota((rows, depth), 0)
    low_level = [(row + rows * k).astype(F32).astype(BF16) for k in range(LOW // rows)]
    high_level = (row % HIGH).astype(F32).astype(BF16)
    upper = jnp.where(row < HIGH, 1.0, 0.0).astype(BF16) > 0
    zero = jnp.zeros((rows, depth), BF16)
    one = jnp.ones((rows, depth), BF16)
    lane_owner = iota((1, GROUP * LOW), 1) // LOW

    def one_group(g, carry):
        base = pl.multiple_of((first + g) * GROUP, GROUP)
        acc = None
        for k in range(docs // depth):
            span = slice(k * depth, (k + 1) * depth)
            code = bins_ref[pl.ds(base, GROUP), span]
            high = jnp.floor(code * (1.0 / LOW))
            low = code - high * LOW
            left, right, count = [], [], []
            wide = []
            for f in range(GROUP):
                high_f = jnp.broadcast_to(high[f:f + 1, :], (rows, depth))
                low_f = jnp.broadcast_to(low[f:f + 1, :], (rows, depth)).astype(BF16)
                high_f = high_f.astype(BF16)
                wide.append(high_f)
                match = high_f == high_level
                for c in range(2):
                    left.append(jnp.where(match, tile_ref[c * rows:(c + 1) * rows, span], zero))
                for level in low_level:
                    right.append(jnp.where(low_f == level, one, zero))
            for f in range(0, GROUP, 2):
                both = jnp.where(upper, wide[f], wide[f + 1])
                count.append(jnp.where(both == high_level, one, zero))
            part = lax.dot_general(
                jnp.concatenate(left + count, axis=0), jnp.concatenate(right, axis=0), NT,
                preferred_element_type=F32,
            )
            acc = part if acc is None else acc + part
        stats = jnp.zeros((2 * rows, GROUP * LOW), F32)
        counts = jnp.zeros((HIGH, GROUP * LOW), F32)
        for f in range(GROUP):
            mine = lane_owner == f
            stats = jnp.where(mine, acc[f * 2 * rows:(f + 1) * 2 * rows], stats)
            at = GROUP * 2 * rows + f * HIGH
            counts = jnp.where(mine, acc[at:at + HIGH], counts)
        out_ref[pl.ds(pl.multiple_of(g * 3 * HIGH, 3 * HIGH), 3 * HIGH), :] = jnp.concatenate(
            [stats[0:HIGH] + stats[HIGH:2 * HIGH], stats[2 * HIGH:3 * HIGH] + stats[3 * HIGH:4 * HIGH], counts], axis=0)
        return carry

    if len(refs) > 1:
        out_ref[groups * 3 * HIGH:, :] = refs[0][...]
    lax.fori_loop(0, groups, one_group, 0, unroll=min(groups, 8))


def histogram_part(first, groups, tiles, bins_t, *tail):
    rows = groups * 3 * HIGH + sum(piece.shape[0] for piece in tail)
    return pl.pallas_call(
        functools.partial(histogram_kernel, first, groups),
        out_shape=jax.ShapeDtypeStruct((rows, GROUP * LOW), F32),
        in_specs=[vmem()] * (2 + len(tail)),
        out_specs=vmem(),
        compiler_params=pltpu.CompilerParams(vmem_limit_bytes=VMEM_LIMIT),
        cost_estimate=pl.CostEstimate(flops=groups * 1_000_000, bytes_accessed=groups * 1_000, transcendentals=0),
        name="histogram_part",
    )(tiles, bins_t, *tail)


def finish_kernel(per_dev, lam_ref, leaf_ref, kept_ref, sums_ref, *refs):
    arrived = list(refs[1::-1]) + list(refs[2:-4])
    lam_out, value_ref, step_ref, hist_ref = refs[-4:]
    lam_out[...] = lam_ref[...]
    unit = kept_ref.shape[0]
    totals = add_up([sums_ref[...]] + [ref[unit:, :] for ref in arrived])
    highs = LEAVES // LANES
    grad, curv = totals[:, :LANES], totals[:, LANES:]
    shrunk = jnp.maximum(jnp.abs(grad) - lasso_penalty, 0.0)
    values = jnp.where(grad > 0.0, -shrunk, shrunk) / (curv + ridge_penalty)
    value_ref[...] = values
    leaf = leaf_ref[...]
    top, spot = leaf // LANES, leaf % LANES
    step = jnp.zeros(leaf.shape, F32)
    for h in range(highs):
        row = jnp.broadcast_to(values[h:h + 1, :], leaf.shape)
        step = jnp.where(top == h, jnp.take_along_axis(row, spot, axis=1), step)
    step_ref[...] = shrinkage * step
    hist = add_up([kept_ref[...]] + [ref[:unit, :] for ref in arrived])
    if per_dev == GROUP:
        shape = hist.shape
        line, place = iota(shape, 0), iota(shape, 1) // LOW
        step = 1
        while step < GROUP:
            down, across = (line // step) % 2, (place // step) % 2
            shift = step * LOW
            ahead = pltpu.roll(pltpu.roll(hist, shape[0] - step, 0), shift, 1)
            behind = pltpu.roll(pltpu.roll(hist, step, 0), shape[1] - shift, 1)
            hist = jnp.where(down == across, hist, jnp.where(across == 1, ahead, behind))
            step *= 2
        for c in range(3):
            for f in range(GROUP):
                hist_ref[c:c + 1, f * BINS:(f + 1) * BINS] = hist[c * HIGH + f:c * HIGH + f + 1, :]
    else:
        hist_ref[...] = hist


def finish(per_dev, lambdas, leaves, kept, sums, arrived):
    out = (3, per_dev * BINS) if per_dev == GROUP else kept.shape
    return pl.pallas_call(
        functools.partial(finish_kernel, per_dev),
        out_shape=(
            jax.ShapeDtypeStruct(lambdas.shape, F32),
            jax.ShapeDtypeStruct((LEAVES // LANES, LANES), F32),
            jax.ShapeDtypeStruct(leaves.shape, F32),
            jax.ShapeDtypeStruct(out, F32),
        ),
        in_specs=[vmem()] * (4 + len(arrived)),
        out_specs=(vmem(),) * 4,
        compiler_params=pltpu.CompilerParams(vmem_limit_bytes=VMEM_LIMIT),
        name="finish",
    )(lambdas, leaves, kept, sums, *arrived)


def add_up(parts):
    while len(parts) > 1:
        parts = [parts[k] + parts[k + 1] for k in range(0, len(parts), 2)]
    return parts[0]


def local(scores, labels, leaves, bins, lengths, owner):
    query_count = lax.axis_size("query")
    feat_count = lax.axis_size("feat")
    count = query_count * feat_count
    place = lax.axis_index("query").astype(jnp.int32) * feat_count + lax.axis_index("feat").astype(jnp.int32)
    docs = scores.shape[0]
    own = docs // LANES
    features = owner.shape[0]
    per_dev = features // count
    unit = 3 * per_dev
    axes = ("query", "feat")
    feat_masks = [1 << b for b in range(feat_count.bit_length() - 1)]
    query_masks = [feat_count << b for b in range(query_count.bit_length() - 1)]

    def swap(value, mask):
        return lax.ppermute(value, axes, [(p, p ^ mask) for p in range(count)])

    pos = place.reshape(1)
    leaf_rows = leaves.reshape(own, LANES)
    own_scores = scores.reshape(own, LANES)
    score_parts = [own_scores]
    def inner_partner(p):
        z = p % feat_count
        if z in (0, feat_count - 1):
            return p ^ query_masks[0]
        return p + 1 if z % 2 else p - 1

    score_parts.append(lax.ppermute(own_scores, axes, [(p, inner_partner(p)) for p in range(count)]))
    score_parts.append(swap(own_scores, 1))
    masks = feat_masks + query_masks[:0:-1] + query_masks[:1]
    score_parts[0], leaf_rows, qid, worth, inverse, perm, bounds = prepare(
        feat_count, masks, lengths, pos, labels.reshape(-1, LANES), owner.reshape(-1, LANES), own_scores, leaf_rows)
    lambdas = pair_terms(feat_count, bounds, pos, score_parts, worth, qid, inverse)
    bins_t, tiles, sums = leaf_terms(perm, bins, leaf_rows, lambdas)

    def part(tiles, low, high, *tail):
        if per_dev == GROUP:
            return histogram_part(low, high - low, tiles, bins_t, *tail)
        groups = high - low
        wide = histogram_part(low, groups, tiles, bins_t)
        wide = wide.reshape(groups, 3, HIGH, GROUP // per_dev, per_dev, LOW).transpose(0, 3, 1, 4, 2, 5)
        return jnp.concatenate([wide.reshape(groups * GROUP // per_dev * unit, BINS), *tail], axis=0)

    def join(block, total):
        return jnp.concatenate([block, total], axis=0)

    eighth = features // GROUP // 8
    edge = count // 8 * unit
    arrived = swap(part(tiles, 7 * eighth, 8 * eighth, sums), query_masks[0])
    block = part(tiles, 3 * eighth, 4 * eighth) + arrived[:edge]
    sums = sums + arrived[edge:]
    message, tiles = lax.optimization_barrier((join(block, sums), tiles))
    crossed_far = swap(message, query_masks[1])
    arrived = swap(part(tiles, 5 * eighth, 7 * eighth), query_masks[0])
    both = part(tiles, eighth, 3 * eighth) + arrived
    sums = sums + crossed_far[edge:]
    message, rest, tiles = lax.optimization_barrier(
        (join(both[:edge] + crossed_far[:edge], sums), join(both[edge:], sums), tiles))
    turned = swap(message, query_masks[2])
    crossed_near = swap(rest, query_masks[1])
    arrived = swap(part(tiles, 4 * eighth, 5 * eighth), query_masks[0])
    kept = part(tiles, 0, eighth) + arrived + crossed_near[:edge] + turned[:edge]
    sums = sums + turned[edge:]
    for mask in query_masks[3:]:
        edge = edge // 2
        arrived = swap(join(kept[edge:], sums), mask)
        kept = kept[:edge] + arrived[:edge]
        sums = sums + arrived[edge:]
    arrived = [swap(join(kept[m * unit:(m + 1) * unit], sums), m) for m in range(1, feat_count)]
    arrived[:2] = arrived[1::-1]
    lambdas, values, step, histograms = finish(per_dev, lambdas, leaf_rows, kept[:unit], sums, arrived)
    return lambdas, values.reshape(LEAVES), step.reshape(docs), histograms.reshape(3, per_dev * BINS)


def solution(mesh):
    in_specs = (
        P(("query", "feat")),
        P("query"),
        P(("query", "feat")),
        P(("query", "feat"), None),
        P("query", None),
        P(),
    )
    out_specs = (P(None, ("query", "feat")), P(), P(("query", "feat")), P(None, ("query", "feat")))
    return jax.shard_map(local, mesh=mesh, in_specs=in_specs, out_specs=out_specs, check_vma=False)
```
